32 devices in a mesh: ctx: 4 (over z), exp: 8 (over y, x, core).
Axes of the slice: x: 2, y: 2, z: 4, core: 2. Of those that a mesh axis runs over, the one named last changes fastest.
Arguments:
- queries: bfloat16 [1024, 4096], P('ctx', 'exp'), may hold values from -6 to 6
- keys: bfloat16 [1024, 256], P('ctx'), may hold values from -6 to 6
- values: bfloat16 [1024, 256], P('ctx'), may hold values from -6 to 6
- attn_out: bfloat16 [1024, 4096], P('ctx', 'exp'), may hold values from -0.59765625 to 0.59765625
- attn_out_grad: bfloat16 [1024, 4096], P('ctx', 'exp'), may hold values from -6 to 6
- lse_excess: float32 [32, 1024], P('exp', 'ctx'), may hold values from 1 to 2.5
- block_mask: int32 [4, 4], replicated, may hold values from 0 to 1, as said below
- expert_ids: int32 [1024, 8], P('exp'), may hold values from 0 to 15, all different within a row; in each aligned block of 128 rows (0 to 127, 128 to 255, ...) at most 65 rows name the same one
- route_probs: bfloat16 [1024, 8], P('exp'), may hold values from 0.019897461 to 0.5
- moe_grad: bfloat16 [1024, 4096], P('exp'), may hold values from -6 to 6
- shadow_list: int32 [16], replicated, may hold values from -1 to 7, as said below
- stored_hidden_state: bfloat16 [8, 3, 8, 65, 1536], P('exp', None, None, None, 'ctx'), may hold values from -6 to 6
Outputs:
- query_grad: bfloat16 [1024, 4096], P('ctx', 'exp')
- key_grad: bfloat16 [1024, 256], P(('ctx', 'exp'))
- value_grad: bfloat16 [1024, 256], P(('ctx', 'exp'))
- expert_grad: float32 [16, 1536, 4096], P('exp', 'ctx')
The draws below stay inside these ranges and needn't reach their ends.
Inputs may be any that keep to these rules, and one draw needn't show every extreme that they name: block_mask[i, j] is 1 on the diagonal and 0 above it. `expert_ids`: each token names 8 different experts; among the tokens of one exp index no expert is named more than 65 times, a bound that some block reaches. `shadow_list`: every exp index holds the shadow of exactly one expert, never of one it owns, and exactly one of the 2 experts of each exp index has a shadow.
All inputs are finite; a program needn't handle non-finite values.
Results may differ from the reference program's by a relative error of at most 0.015.
Values may be sent and summed in bfloat16 or wider, within the bound.
No kernel may reach another device: no remote copies, remote signals or barrier semaphores. Data moves between devices by JAX's collectives and lax.ppermute only.
A program may use at most 192 MiB of HBM per device.

```python
import math
import jax
import jax.numpy as jnp
import numpy as np
from jax import lax

D = 4096
HD = 128
KVH = 2
HIDDEN_UNITS = 1536
TOP = 8
HEADS_DEV = 4
EXP_DEV = 2
TOK_DEV = 256
MTOK = 128
NBLK = 4
SEQ = 1024
QH = 32
EXPERTS = 16
SLOT_COUNT = 3
MT = 1024
TOKEN_LIMIT = 65
N_EXP = 8


def draw_block_mask(key, part):
    key = jax.random.fold_in(key, 5)
    coins = jax.random.randint(key, (NBLK, NBLK), 0, 4)
    place = jnp.arange(NBLK, dtype=jnp.int32)
    below = place[None, :] < place[:, None]
    live = jnp.logical_or(jnp.logical_and(below, coins == 0), place[None, :] == place[:, None])
    return live.astype(jnp.int32)


def draw_shadow_list(key, part):
    key = jax.random.fold_in(key, 11)
    first, second = jax.random.split(key)
    shuffled = jax.random.permutation(first, N_EXP).astype(jnp.int32)
    place = jnp.arange(N_EXP, dtype=jnp.int32)
    wanted = (shuffled[0] + 1) % N_EXP
    where_wanted = jnp.sum(jnp.where(shuffled == wanted, place, 0)).astype(jnp.int32)
    second_value = shuffled[1]
    order = jnp.where(place == 1, wanted, jnp.where(place == where_wanted, second_value, shuffled)).astype(jnp.int32)
    hosts = jnp.roll(order, -1)
    picks = jax.random.randint(second, (N_EXP,), 0, EXP_DEV).astype(jnp.int32)
    chosen = hosts * EXP_DEV + picks
    table = jnp.full((EXPERTS,), -1, jnp.int32)
    return table.at[chosen].set(order)


def levels(rng, dims, cuts, least, top_value):
    def one(axis_at, blocks):
        draws = jax.random.uniform(jax.random.fold_in(jax.random.fold_in(rng, 6), axis_at), (blocks,), jnp.float32, least / len(cuts), top_value / len(cuts))
        return jnp.repeat(jnp.exp(draws), dims[axis_at] // blocks).reshape((-1,) + (1,) * (len(dims) - axis_at - 1))

    gain = one(*cuts[0])
    for cut in cuts[1:]:
        gain = gain * one(*cut)
    return gain


def deal_out(own_key, own, number, rows, amount, top, limit, skew):
    sequence = jax.random.permutation(own_key, amount)
    heavy_load, ordinary = portions_of(amount, rows * top, limit, skew, True), portions_of(amount, rows * top, limit, skew, False)
    places = jnp.arange(amount)

    def named(sizes, offset_by):
        used = int((sizes > 0).sum())
        fixed = max(1, used // 4)
        shifted = fixed + (places - fixed + offset_by * (used - fixed)) % max(1, amount - fixed)
        return jnp.zeros((amount,), jnp.int32).at[sequence[jnp.where(places < fixed, places, shifted)]].set(jnp.asarray(sizes, jnp.int32))

    sizes = jnp.where(number % 4 == 0, named(heavy_load, number // 4), named(ordinary, number - number // 4 - 1))
    mixed = jax.random.permutation(jax.random.fold_in(own, 3), amount)
    source_of, taker = mixed[0:amount // 2 * 2:2], mixed[1:amount // 2 * 2:2]
    margin = jnp.minimum(sizes[source_of] - 1, limit - sizes[taker]) // 2
    margin = jnp.where((source_of == sequence[0]) | (taker == sequence[0]) | (sizes[taker] == 0), 0, jnp.maximum(margin, 0))
    shifted = jax.random.randint(jax.random.fold_in(own, 4), (amount // 2,), 0, 1 << 20) % (margin + 1)
    sizes = sizes.at[source_of].add(-shifted).at[taker].add(shifted)
    items = jnp.searchsorted(jnp.cumsum(sizes), jnp.arange(rows * top), side="right").astype(jnp.int32)
    grid = items.reshape(top, rows).T
    grid = grid[jax.random.permutation(jax.random.fold_in(own, 1), rows)]
    offset_by = jax.random.randint(jax.random.fold_in(own, 2), (rows, 1), 0, top)
    return jnp.take_along_axis(grid, (jnp.arange(top)[None, :] + offset_by) % top, axis=1)


def portions_of(number_of, total, reach, skew, full):
    loads = [(1 << 20) // math.isqrt(standing ** skew) + 1 for standing in range(1, number_of + 1)]
    largest = reach if full else min(reach, max(-(-total // number_of), total * loads[0] // sum(loads)))
    least = 1 if total - largest >= number_of - 1 else 0
    given, surplus = [largest] + [least] * (number_of - 1), total - largest - least * (number_of - 1)
    while surplus > 0:
        free = [i for i in range(1, number_of) if given[i] < largest] or [i for i in range(1, number_of) if given[i] < reach]
        pool, budget = sum([loads[i] for i in free]), surplus
        for i in free:
            more = min(reach - given[i], max(1, budget * loads[i] // pool), surplus)
            given[i] = given[i] + more
            surplus = surplus - more
    return np.array(given)


def noise(own_key, shape, spread, reach, cuts=(), kind=jnp.bfloat16):
    result = spread * jax.random.normal(own_key, shape, jnp.float32)
    if cuts:
        result = result * levels(own_key, shape, cuts, -0.22, 0.18)
    return jnp.clip(result, -reach, reach).astype(kind)


def setup_inputs(seed: int = 0) -> dict:
    streams_of = jax.random.split(jax.random.key(seed), 13)
    queries = noise(streams_of[0], (SEQ, QH * HD), 1.0, 6.0, ((0, 4), (1, 8)))
    keys = noise(streams_of[1], (SEQ, KVH * HD), 1.0, 6.0, ((0, 4),))
    values = noise(streams_of[2], (SEQ, KVH * HD), 1.0, 6.0, ((0, 4),))
    attn_out = noise(streams_of[3], (SEQ, QH * HD), 0.1, 0.59765625, ((0, 4), (1, 8)))
    attn_out_grad = noise(streams_of[4], (SEQ, QH * HD), 1.0, 6.0, ((0, 4), (1, 8)))
    lse_excess = jnp.clip(1.0 + 1.5 * jax.random.uniform(streams_of[5], (QH, SEQ), jnp.float32) ** levels(streams_of[5], (QH, SEQ), ((0, 8), (1, 4)), -0.2, 0.2), 1.0, 2.5)
    block_mask = draw_block_mask(jax.random.fold_in(streams_of[12], 71), 0)
    expert_ids_keys = jax.random.split(jax.random.fold_in(streams_of[7], 1), MT // MTOK)
    expert_ids_turns = jax.random.permutation(jax.random.fold_in(streams_of[7], 3), MT // MTOK)
    expert_ids = jax.vmap(lambda own, number: deal_out(jax.random.fold_in(streams_of[7], 2), own, number, MTOK, EXPERTS, TOP, TOKEN_LIMIT, 2))(expert_ids_keys, expert_ids_turns).reshape((MT, TOP))
    route_probs = jnp.clip(0.019897461 + 0.48010254 * jax.random.uniform(streams_of[8], (MT, TOP), jnp.float32) ** levels(streams_of[8], (MT, TOP), ((0, 8),), -0.2, 0.2), 0.019897461, 0.5).astype(jnp.bfloat16)
    moe_grad = noise(streams_of[9], (MT, D), 1.0, 6.0, ((0, 8),))
    shadow_list = draw_shadow_list(jax.random.fold_in(streams_of[12], 71), 0)
    stored_hidden_state = noise(streams_of[11], (N_EXP, SLOT_COUNT, N_EXP, TOKEN_LIMIT, HIDDEN_UNITS), 1.0, 6.0, ((0, 8), (4, 4)))
    return {"queries": queries, "keys": keys, "values": values, "attn_out": attn_out, "attn_out_grad": attn_out_grad, "lse_excess": lse_excess, "block_mask": block_mask, "expert_ids": expert_ids, "route_probs": route_probs, "moe_grad": moe_grad, "shadow_list": shadow_list, "stored_hidden_state": stored_hidden_state}


def pair_terms(query_heads, grad_heads, delta, offset, key_block, value_block, diagonal):
    rows = query_heads.shape[0]
    scale = 1.0 / math.sqrt(query_heads.shape[2])
    high = lax.Precision.HIGHEST
    scores = jnp.einsum('qhd,kd->hqk', query_heads, key_block, precision=high) * scale
    place = jnp.arange(rows, dtype=jnp.int32)
    allowed = jnp.logical_or(jnp.logical_not(diagonal), place[:, None] >= place[None, :])
    prob = jnp.where(allowed[None], jnp.exp(scores - offset[:, :, None]), 0.0)
    prob_low = lax.optimization_barrier(prob.astype(jnp.bfloat16)).astype(jnp.float32)
    value_term = jnp.einsum('hqk,qhd->kd', prob_low, grad_heads, precision=high)
    prob_grad = jnp.einsum('qhd,kd->hqk', grad_heads, value_block, precision=high)
    score_grad = lax.optimization_barrier((prob * (prob_grad - delta[:, :, None]) * scale).astype(jnp.bfloat16)).astype(jnp.float32)
    query_term = jnp.einsum('hqk,kd->qhd', score_grad, key_block, precision=high)
    key_term = jnp.einsum('hqk,qhd->kd', score_grad, query_heads, precision=high)
    return (query_term, key_term, value_term)

def group_grads(group, queries, keys, values, attn_out, attn_out_grad, lse_excess, block_mask):
    cols = HEADS_DEV * HD
    query_part = lax.dynamic_slice_in_dim(queries, group * cols, cols, 1).astype(jnp.float32).reshape(NBLK, TOK_DEV, HEADS_DEV, HD)
    gradient_piece = lax.dynamic_slice_in_dim(attn_out_grad, group * cols, cols, 1).astype(jnp.float32).reshape(NBLK, TOK_DEV, HEADS_DEV, HD)
    out_part = lax.dynamic_slice_in_dim(attn_out, group * cols, cols, 1).astype(jnp.float32).reshape(NBLK, TOK_DEV, HEADS_DEV, HD)
    delta = jnp.transpose(lax.optimization_barrier(jnp.sum(gradient_piece * out_part, axis=3)), (0, 2, 1))
    excess = lax.dynamic_slice_in_dim(lse_excess, group * HEADS_DEV, HEADS_DEV, 0).reshape(HEADS_DEV, NBLK, TOK_DEV)
    offset = 0.5 * math.log(TOK_DEV) + jnp.transpose(excess, (1, 0, 2))
    kv_head = group * KVH // N_EXP
    key_all = lax.dynamic_slice_in_dim(keys, kv_head * HD, HD, 1).astype(jnp.float32).reshape(NBLK, TOK_DEV, HD)
    value_all = lax.dynamic_slice_in_dim(values, kv_head * HD, HD, 1).astype(jnp.float32).reshape(NBLK, TOK_DEV, HD)
    zero_query = jnp.zeros((TOK_DEV, HEADS_DEV, HD), jnp.float32)
    zero_pair = jnp.zeros((TOK_DEV, HD), jnp.float32)

    def query_block(carry, index):
        key_sum, value_sum = carry

        def visit(source):
            live = block_mask[index, source] > 0
            return lax.cond(live, lambda: pair_terms(query_part[index], gradient_piece[index], delta[index], offset[index], key_all[source], value_all[source], index == source), lambda: (zero_query, zero_pair, zero_pair))
        query_terms, key_terms, value_terms = lax.map(visit, jnp.arange(NBLK, dtype=jnp.int32))
        key_sum = (key_sum.astype(jnp.float32) + key_terms).astype(jnp.bfloat16)
        value_sum = (value_sum.astype(jnp.float32) + value_terms).astype(jnp.bfloat16)
        return ((key_sum, value_sum), lax.optimization_barrier(jnp.sum(query_terms, axis=0)))
    start = (jnp.zeros((NBLK, TOK_DEV, HD), jnp.bfloat16), jnp.zeros((NBLK, TOK_DEV, HD), jnp.bfloat16))
    (key_sum, value_sum), query_sum = lax.scan(query_block, start, jnp.arange(NBLK, dtype=jnp.int32))
    return (query_sum.reshape(SEQ, cols).astype(jnp.bfloat16), key_sum, value_sum)

def route_slots(expert_ids, shadow_list, per_dev, capacity, to_shadow):
    tokens, top = expert_ids.shape
    count = tokens * top
    experts_all = shadow_list.shape[0]
    flat = expert_ids.reshape(count)
    table = flat[:, None] == jnp.arange(experts_all, dtype=jnp.int32)[None, :]
    shadow = lax.optimization_barrier(jnp.sum(jnp.where(table, shadow_list[None, :], 0), axis=1)).astype(jnp.int32)
    order = jnp.arange(count, dtype=jnp.int32)
    side = jnp.logical_and(shadow >= 0, order // top % 2 == 1)
    owner = flat // per_dev
    target_dev = jnp.where(side, shadow, owner) if to_shadow else owner
    slot = jnp.where(side, per_dev, flat % per_dev)
    label = flat * 2 + side.astype(jnp.int32)
    earlier = jnp.logical_and(label[:, None] == label[None, :], order[:, None] > order[None, :])
    rank = lax.optimization_barrier(jnp.sum(earlier.astype(jnp.int32), axis=1))
    return ((target_dev * (per_dev + 1) + slot) * capacity + rank).astype(jnp.int32)

def packed_rows(expert_ids, route_probs, moe_grad, destination, owners, slots, capacity):
    tokens, top = expert_ids.shape
    total = owners * slots * capacity
    place = jnp.arange(total, dtype=jnp.int32)[:, None] == destination[None, :]
    place_tok = lax.optimization_barrier(jnp.sum(place.reshape(total, tokens, top).astype(jnp.int32), axis=2))
    rows_out = jnp.dot(place_tok.astype(jnp.bfloat16), moe_grad, preferred_element_type=jnp.float32).astype(jnp.bfloat16)
    weight_out = jnp.dot(place.astype(jnp.bfloat16), route_probs.reshape(tokens * top, 1), preferred_element_type=jnp.float32).astype(jnp.bfloat16)
    return (rows_out.reshape(owners, slots, capacity, moe_grad.shape[1]), weight_out.reshape(owners, slots, capacity))

def slot_tiles(hidden, rows_in, weight_in):
    scaled = hidden.astype(jnp.float32) * jnp.transpose(weight_in, (1, 0, 2))[..., None].astype(jnp.float32)
    weighted = lax.optimization_barrier(scaled.astype(jnp.bfloat16)).astype(jnp.float32)
    return jnp.einsum('ascf,sacd->afd', weighted, rows_in.astype(jnp.float32), precision=lax.Precision.HIGHEST)

def reference(queries, keys, values, attn_out, attn_out_grad, lse_excess, block_mask, expert_ids, route_probs, moe_grad, shadow_list, stored_hidden_state):
    groups = jnp.arange(N_EXP, dtype=jnp.int32)
    query_all, key_all, value_all = lax.map(lambda group: group_grads(group, queries, keys, values, attn_out, attn_out_grad, lse_excess, block_mask), groups)
    query_grad = jnp.transpose(query_all, (1, 0, 2)).reshape(SEQ, QH * HD)
    pick = (groups[:, None] * KVH // N_EXP == jnp.arange(KVH, dtype=jnp.int32)[None, :]).astype(jnp.float32)
    key_wide = lax.optimization_barrier(jnp.sum(key_all.reshape(N_EXP, SEQ, 1, HD).astype(jnp.float32) * pick[:, None, :, None], axis=0))
    value_wide = lax.optimization_barrier(jnp.sum(value_all.reshape(N_EXP, SEQ, 1, HD).astype(jnp.float32) * pick[:, None, :, None], axis=0))
    key_grad = key_wide.reshape(SEQ, KVH * HD).astype(jnp.bfloat16)
    value_grad = value_wide.reshape(SEQ, KVH * HD).astype(jnp.bfloat16)

    def source_rows(source):
        expert_index_piece = lax.dynamic_slice_in_dim(expert_ids, source * MTOK, MTOK, 0)
        probability_piece = lax.dynamic_slice_in_dim(route_probs, source * MTOK, MTOK, 0)
        gradient_piece = lax.dynamic_slice_in_dim(moe_grad, source * MTOK, MTOK, 0)
        destination = route_slots(expert_index_piece, shadow_list, EXP_DEV, TOKEN_LIMIT, True)
        return packed_rows(expert_index_piece, probability_piece, gradient_piece, destination, N_EXP, SLOT_COUNT, TOKEN_LIMIT)
    rows_all, weight_all = lax.map(source_rows, groups)

    def copy_tiles(copy):
        rows_here = lax.dynamic_index_in_dim(rows_all, copy, 1, keepdims=False)
        weight_here = lax.dynamic_index_in_dim(weight_all, copy, 1, keepdims=False)
        hidden = lax.dynamic_index_in_dim(stored_hidden_state, copy, 0, keepdims=False)
        tiles = slot_tiles(hidden, rows_here, weight_here)
        return (tiles[:EXP_DEV], tiles[EXP_DEV].astype(jnp.bfloat16))
    own_all, helper_all = lax.map(copy_tiles, groups)
    own_all = own_all.reshape(EXPERTS, HIDDEN_UNITS, D)

    def finish(expert):
        helper = shadow_list[expert]
        extra = lax.dynamic_index_in_dim(helper_all, jnp.maximum(helper, 0), 0, keepdims=False).astype(jnp.float32)
        return own_all[expert] + jnp.where(helper >= 0, extra, 0.0)
    expert_grad = lax.map(finish, jnp.arange(EXPERTS, dtype=jnp.int32))
    return (query_grad, key_grad, value_grad, expert_grad)
```

```python
import functools
import math

import jax
import jax.numpy as jnp
from jax import lax
from jax.experimental import pallas as pl
from jax.experimental.pallas import tpu as pltpu
from jax.sharding import PartitionSpec as P

LAST = (((1,), (1,)), ((), ()))
FIRST = (((0,), (0,)), ((), ()))


def attention_kernel(
    live_ref, query_ref, grad_ref, out_ref, lse_ref, pairs_ref, query_grad_ref, terms_ref, sums_ref
):
    rows, width = pairs_ref.shape[1], pairs_ref.shape[2] // 2
    heads = lse_ref.shape[0]
    scale = 1.0 / math.sqrt(width)
    offset = 0.5 * math.log(rows) + lse_ref[...]
    spans = [slice(h * width, (h + 1) * width) for h in range(heads)]
    delta = []
    for span in spans:
        both = grad_ref[:, span].astype(jnp.float32) * out_ref[:, span].astype(jnp.float32)
        delta.append(jnp.sum(both.T, axis=0, keepdims=True))

    def block(step, diagonal):
        key, value = pairs_ref[step, :, :width], pairs_ref[step, :, width:]
        probs, slopes = [], []
        for h, span in enumerate(spans):
            query, grad = query_ref[:, span], grad_ref[:, span]
            scores = lax.dot_general(key, query, LAST, preferred_element_type=jnp.float32)
            prob = jnp.exp(scores * scale - offset[h : h + 1])
            if diagonal:
                at_key = lax.broadcasted_iota(jnp.int32, (rows, rows), 0)
                at_query = lax.broadcasted_iota(jnp.int32, (rows, rows), 1)
                prob = jnp.where(at_key <= at_query, prob, 0.0)
            prob_grad = lax.dot_general(value, grad, LAST, preferred_element_type=jnp.float32)
            slope = (prob * (prob_grad - delta[h]) * scale).astype(jnp.bfloat16)
            probs.append(prob.astype(jnp.bfloat16))
            slopes.append(slope)
            query_term = lax.dot_general(slope, key, FIRST, preferred_element_type=jnp.float32)
            if diagonal:
                sums_ref[:, span] = query_term
            else:
                sums_ref[:, span] += query_term
        queries = jnp.concatenate([query_ref[:, span] for span in spans], axis=0)
        grads = jnp.concatenate([grad_ref[:, span] for span in spans], axis=0)
        terms_ref[step, :, :width] = jnp.dot(
            jnp.concatenate(slopes, axis=1), queries, preferred_element_type=jnp.float32
        ).astype(jnp.bfloat16)
        terms_ref[step, :, width:] = jnp.dot(
            jnp.concatenate(probs, axis=1), grads, preferred_element_type=jnp.float32
        ).astype(jnp.bfloat16)

    block(0, True)

    @pl.loop(1, pairs_ref.shape[0])
    def _(step):
        @pl.when(live_ref[step] > 0)
        def _():
            block(step, False)

        @pl.when(live_ref[step] <= 0)
        def _():
            terms_ref[step] = jnp.zeros_like(terms_ref[step])

    query_grad_ref[...] = sums_ref[...].astype(jnp.bfloat16)


def attention(queries, keys, values, attn_out, attn_out_grad, lse_excess, block_mask):
    rows = queries.shape[0]
    heads = lse_excess.shape[0]
    width = queries.shape[1] // heads
    cycle = lax.axis_size("ctx")
    mine = lax.axis_index("ctx")
    owners = lax.axis_size("exp")
    kv_count = keys.shape[1] // width
    kv_head = lax.axis_index("exp") * kv_count // owners
    pair = jnp.concatenate(
        [
            lax.dynamic_slice_in_dim(keys, kv_head * width, width, 1),
            lax.dynamic_slice_in_dim(values, kv_head * width, width, 1),
        ],
        axis=1,
    )
    arrived = [pair] + [
        lax.ppermute(pair, "ctx", [(c, c + step) for c in range(cycle - step)])
        for step in range(1, cycle)
    ]
    source = mine - jnp.arange(cycle, dtype=jnp.int32)
    live = jnp.where(source >= 0, block_mask[mine, jnp.maximum(source, 0)], 0)
    whole = pl.BlockSpec(memory_space=pltpu.VMEM)
    query_grad, terms = pl.pallas_call(
        attention_kernel,
        out_shape=(
            jax.ShapeDtypeStruct(queries.shape, jnp.bfloat16),
            jax.ShapeDtypeStruct((cycle, rows, 2 * width), jnp.bfloat16),
        ),
        in_specs=[pl.BlockSpec(memory_space=pltpu.SMEM)] + [whole] * 5,
        out_specs=(whole, whole),
        scratch_shapes=[pltpu.VMEM(queries.shape, jnp.float32)],
        compiler_params=pltpu.CompilerParams(vmem_limit_bytes=40 * 2**20),
        name="attention",
    )(live, queries, attn_out_grad, attn_out, lse_excess, jnp.stack(arrived))
    total = terms[0].astype(jnp.float32)
    for step in range(1, cycle):
        total = total + lax.ppermute(
            terms[step], "ctx", [(c, c - step) for c in range(step, cycle)]
        ).astype(jnp.float32)
    parts = lax.all_to_all(
        total.astype(jnp.bfloat16), "exp", split_axis=0, concat_axis=0, tiled=True
    )
    kv_sum = jnp.sum(
        parts.reshape(kv_count, owners // kv_count, rows // owners, 2, width).astype(jnp.float32),
        axis=1,
    )
    final = jnp.transpose(kv_sum, (2, 1, 0, 3)).reshape(2, rows // owners, kv_count * width)
    final = final.astype(jnp.bfloat16)
    return (query_grad, final[0], final[1])


def rows_of_pairs(named, capacity):
    tokens = named.shape[-1]
    ones = named.astype(jnp.bfloat16)
    before = (
        lax.broadcasted_iota(jnp.int32, (tokens, tokens), 0)
        < lax.broadcasted_iota(jnp.int32, (tokens, tokens), 1)
    ).astype(jnp.bfloat16)
    rank = jnp.einsum("...u,ut->...t", ones, before, preferred_element_type=jnp.float32)
    place = jnp.arange(capacity, dtype=jnp.int32)
    return jnp.where(
        named[..., None] & (rank.astype(jnp.int32)[..., None] == place), 1.0, 0.0
    ).astype(jnp.bfloat16)


def experts(expert_ids, route_probs, moe_grad, shadow_list, stored_hidden_state):
    owners = lax.axis_size("exp")
    own_index = lax.axis_index("exp")
    tokens = expert_ids.shape[0]
    count = shadow_list.shape[0]
    per_dev = count // owners
    hidden = stored_hidden_state[0]
    units = hidden.shape[-1]
    swap = functools.partial(
        lax.all_to_all, axis_name="exp", split_axis=0, concat_axis=0, tiled=True
    )
    gathered = lax.all_gather(moe_grad, "exp", tiled=True)

    hit = expert_ids[:, None, :] == jnp.arange(count, dtype=jnp.int32)[None, :, None]
    table = jnp.sum(
        jnp.where(hit, route_probs[:, None, :].astype(jnp.float32), 0.0), axis=2
    ).astype(jnp.bfloat16)
    probs = swap(table.T).reshape(owners, per_dev, tokens)

    limit = min(hidden.shape[2], tokens // 2)
    by_source = swap(hidden[per_dev, :, :limit])
    hosts = jnp.max(shadow_list.reshape(owners, per_dev), axis=1)
    shadow_rows = swap(by_source[hosts])

    flags = lax.dynamic_slice_in_dim(shadow_list, own_index * per_dev, per_dev) >= 0
    odd = jnp.arange(tokens, dtype=jnp.int32) % 2 == 1
    named = probs > 0
    side = named & odd & flags[None, :, None]
    own_place = rows_of_pairs(named & ~side, hidden.shape[2])
    side_place = rows_of_pairs(side, limit)
    rows = jnp.einsum(
        "sjtr,jsrf->stjf", own_place, hidden[:per_dev], preferred_element_type=jnp.float32
    ) + jnp.einsum("sjtr,srf->stjf", side_place, shadow_rows, preferred_element_type=jnp.float32)
    weight = jnp.transpose(probs, (0, 2, 1))[..., None].astype(jnp.float32)
    weighted = (rows * weight).astype(jnp.bfloat16)
    tiles = lax.dot_general(
        weighted.reshape(owners * tokens, per_dev * units),
        gathered,
        FIRST,
        preferred_element_type=jnp.float32,
    )
    return tiles.reshape(per_dev, units, moe_grad.shape[1])


def local(
    queries,
    keys,
    values,
    attn_out,
    attn_out_grad,
    lse_excess,
    block_mask,
    expert_ids,
    route_probs,
    moe_grad,
    shadow_list,
    stored_hidden_state,
):
    query_grad, key_grad, value_grad = attention(
        queries, keys, values, attn_out, attn_out_grad, lse_excess, block_mask
    )
    expert_grad = experts(expert_ids, route_probs, moe_grad, shadow_list, stored_hidden_state)
    return (query_grad, key_grad, value_grad, expert_grad)


def solution(mesh):
    placed = (
        P("ctx", "exp"),
        P("ctx", None),
        P("ctx", None),
        P("ctx", "exp"),
        P("ctx", "exp"),
        P("exp", "ctx"),
        P(),
        P("exp", None),
        P("exp", None),
        P("exp", None),
        P(),
        P("exp", None, None, None, "ctx"),
    )
    return jax.shard_map(
        local,
        mesh=mesh,
        in_specs=placed,
        out_specs=(
            P("ctx", "exp"),
            P(("ctx", "exp"), None),
            P(("ctx", "exp"), None),
            P("exp", "ctx", None),
        ),
        check_vma=False,
    )
```

```python
import functools
import math

import jax
import jax.numpy as jnp
from jax import lax
from jax.experimental import pallas as pl
from jax.experimental.pallas import tpu as pltpu
from jax.sharding import PartitionSpec as P

LAST = (((1,), (1,)), ((), ()))
FIRST = (((0,), (0,)), ((), ()))


def attention_kernel(
    live_ref, query_ref, grad_ref, out_ref, lse_ref, pairs_ref, query_grad_ref, terms_ref, sums_ref
):
    rows, width = pairs_ref.shape[1], pairs_ref.shape[2] // 2
    heads = lse_ref.shape[0]
    scale = 1.0 / math.sqrt(width)
    offset = 0.5 * math.log(rows) + lse_ref[...]
    spans = [slice(h * width, (h + 1) * width) for h in range(heads)]
    delta = []
    for span in spans:
        both = grad_ref[:, span].astype(jnp.float32) * out_ref[:, span].astype(jnp.float32)
        delta.append(jnp.sum(both.T, axis=0, keepdims=True))

    def block(step, diagonal):
        key, value = pairs_ref[step, :, :width], pairs_ref[step, :, width:]
        probs, slopes = [], []
        for h, span in enumerate(spans):
            query, grad = query_ref[:, span], grad_ref[:, span]
            scores = lax.dot_general(key, query, LAST, preferred_element_type=jnp.float32)
            prob = jnp.exp(scores * scale - offset[h : h + 1])
            if diagonal:
                at_key = lax.broadcasted_iota(jnp.int32, (rows, rows), 0)
                at_query = lax.broadcasted_iota(jnp.int32, (rows, rows), 1)
                prob = jnp.where(at_key <= at_query, prob, 0.0)
            prob_grad = lax.dot_general(value, grad, LAST, preferred_element_type=jnp.float32)
            slope = (prob * (prob_grad - delta[h]) * scale).astype(jnp.bfloat16)
            probs.append(prob.astype(jnp.bfloat16))
            slopes.append(slope)
            query_term = lax.dot_general(slope, key, FIRST, preferred_element_type=jnp.float32)
            if diagonal:
                sums_ref[:, span] = query_term
            else:
                sums_ref[:, span] += query_term
        queries = jnp.concatenate([query_ref[:, span] for span in spans], axis=0)
        grads = jnp.concatenate([grad_ref[:, span] for span in spans], axis=0)
        terms_ref[step, :, :width] = jnp.dot(
            jnp.concatenate(slopes, axis=1), queries, preferred_element_type=jnp.float32
        ).astype(jnp.bfloat16)
        terms_ref[step, :, width:] = jnp.dot(
            jnp.concatenate(probs, axis=1), grads, preferred_element_type=jnp.float32
        ).astype(jnp.bfloat16)

    block(0, True)

    @pl.loop(1, pairs_ref.shape[0])
    def _(step):
        @pl.when(live_ref[step] > 0)
        def _():
            block(step, False)

        @pl.when(live_ref[step] <= 0)
        def _():
            terms_ref[step] = jnp.zeros_like(terms_ref[step])

    query_grad_ref[...] = sums_ref[...].astype(jnp.bfloat16)


def attention(queries, keys, values, attn_out, attn_out_grad, lse_excess, block_mask):
    rows = queries.shape[0]
    heads = lse_excess.shape[0]
    width = queries.shape[1] // heads
    cycle = lax.axis_size("ctx")
    mine = lax.axis_index("ctx")
    owners = lax.axis_size("exp")
    kv_count = keys.shape[1] // width
    kv_head = lax.axis_index("exp") * kv_count // owners
    pair = jnp.concatenate(
        [
            lax.dynamic_slice_in_dim(keys, kv_head * width, width, 1),
            lax.dynamic_slice_in_dim(values, kv_head * width, width, 1),
        ],
        axis=1,
    )
    arrived = [pair] + [
        lax.ppermute(pair, "ctx", [(c, c + step) for c in range(cycle - step)])
        for step in range(1, cycle)
    ]
    source = mine - jnp.arange(cycle, dtype=jnp.int32)
    live = jnp.where(source >= 0, block_mask[mine, jnp.maximum(source, 0)], 0)
    whole = pl.BlockSpec(memory_space=pltpu.VMEM)
    query_grad, terms = pl.pallas_call(
        attention_kernel,
        out_shape=(
            jax.ShapeDtypeStruct(queries.shape, jnp.bfloat16),
            jax.ShapeDtypeStruct((cycle, rows, 2 * width), jnp.bfloat16),
        ),
        in_specs=[pl.BlockSpec(memory_space=pltpu.SMEM)] + [whole] * 5,
        out_specs=(whole, whole),
        scratch_shapes=[pltpu.VMEM(queries.shape, jnp.float32)],
        compiler_params=pltpu.CompilerParams(vmem_limit_bytes=40 * 2**20),
        name="attention",
    )(live, queries, attn_out_grad, attn_out, lse_excess, jnp.stack(arrived))
    total = terms[0].astype(jnp.float32)
    for step in range(1, cycle):
        total = total + lax.ppermute(
            terms[step], "ctx", [(c, c - step) for c in range(step, cycle)]
        ).astype(jnp.float32)
    parts = lax.all_to_all(
        total.astype(jnp.bfloat16), "exp", split_axis=0, concat_axis=0, tiled=True
    )
    kv_sum = jnp.sum(
        parts.reshape(kv_count, owners // kv_count, rows // owners, 2, width).astype(jnp.float32),
        axis=1,
    )
    final = jnp.transpose(kv_sum, (2, 1, 0, 3)).reshape(2, rows // owners, kv_count * width)
    final = final.astype(jnp.bfloat16)
    return (query_grad, final[0], final[1])


def weight_kernel(order_ref, flag_ref, probs_ref, hidden_ref, shadow_ref, weight_ref):
    per_dev, tokens = probs_ref.shape[1:]
    units = hidden_ref.shape[4]
    earlier = (
        lax.broadcasted_iota(jnp.int32, (tokens, tokens), 0)
        < lax.broadcasted_iota(jnp.int32, (tokens, tokens), 1)
    ).astype(jnp.bfloat16)
    odd = lax.broadcasted_iota(jnp.int32, (1, tokens), 1) % 2 == 1

    def rows_at(named, rows):
        rank = jnp.dot(
            jnp.broadcast_to(named.astype(jnp.float32), (8, tokens)).astype(jnp.bfloat16),
            earlier,
            preferred_element_type=jnp.float32,
        )[:1]
        place = lax.broadcasted_iota(jnp.int32, (rows.shape[0], tokens), 0).astype(jnp.float32)
        chosen = jnp.where(jnp.logical_and(named, rank == place), 1.0, 0.0).astype(jnp.bfloat16)
        return lax.dot_general(rows, chosen, FIRST, preferred_element_type=jnp.float32)

    for j in range(per_dev):
        prob = probs_ref[0, j : j + 1].astype(jnp.float32)
        named = prob > 0
        side = jnp.logical_and(jnp.logical_and(named, odd), flag_ref[j] > 0)
        own = jnp.logical_and(named, jnp.logical_not(side))
        rows = rows_at(own, hidden_ref[0, j, 0]) + rows_at(side, shadow_ref[0])
        weight_ref[j * units : (j + 1) * units] = (rows * prob).astype(jnp.bfloat16)


def weighted_rows(probs, hidden, shadow_rows, flags, order):
    owners, per_dev, tokens = probs.shape
    units = hidden.shape[4]
    return pl.pallas_call(
        weight_kernel,
        out_shape=jax.ShapeDtypeStruct((per_dev * units, owners * tokens), jnp.bfloat16),
        grid_spec=pltpu.PrefetchScalarGridSpec(
            num_scalar_prefetch=2,
            grid=(owners,),
            in_specs=[
                pl.BlockSpec((1, per_dev, tokens), lambda i, order, flag: (order[i], 0, 0)),
                pl.BlockSpec(
                    (1, per_dev, 1) + hidden.shape[3:],
                    lambda i, order, flag: (0, 0, order[i], 0, 0),
                ),
                pl.BlockSpec(
                    (1,) + shadow_rows.shape[1:], lambda i, order, flag: (order[i], 0, 0)
                ),
            ],
            out_specs=pl.BlockSpec((per_dev * units, tokens), lambda i, order, flag: (0, i)),
        ),
        compiler_params=pltpu.CompilerParams(vmem_limit_bytes=40 * 2**20),
        name="weighted",
    )(order, flags, probs, hidden, shadow_rows)


def tile_kernel(weight_ref, first_ref, second_ref, *rest):
    tile_ref = rest[-1]
    depth = first_ref.shape[0]
    tile_ref[...] = jnp.dot(
        weight_ref[:, :depth], first_ref[...], preferred_element_type=jnp.float32
    ) + jnp.dot(weight_ref[:, depth:], second_ref[...], preferred_element_type=jnp.float32)


def tile_columns(weighted, first, second, width, start, tiles):
    depth, columns = first.shape
    rows = weighted.shape[0]
    step = min(512, columns)
    shift = start // step
    gathered = pl.BlockSpec((depth, step), lambda i: (0, i))
    earlier = [] if tiles is None else [tiles]
    return pl.pallas_call(
        tile_kernel,
        out_shape=jax.ShapeDtypeStruct((rows, width), jnp.float32),
        grid=(columns // step,),
        in_specs=[pl.BlockSpec(weighted.shape, lambda i: (0, 0)), gathered, gathered]
        + [pl.BlockSpec(memory_space=pl.ANY)] * len(earlier),
        out_specs=pl.BlockSpec((rows, step), lambda i: (0, i + shift)),
        input_output_aliases={3: 0} if earlier else {},
        compiler_params=pltpu.CompilerParams(vmem_limit_bytes=40 * 2**20),
        name="tiles",
    )(weighted, first, second, *earlier)


def experts(expert_ids, route_probs, moe_grad, shadow_list, stored_hidden_state):
    owners = lax.axis_size("exp")
    own_index = lax.axis_index("exp")
    tokens, model = moe_grad.shape
    count = shadow_list.shape[0]
    per_dev = count // owners
    units = stored_hidden_state.shape[4]
    chips = owners // 2
    alike = [[2 * chip + core for chip in range(chips)] for core in range(2)]
    swap = functools.partial(
        lax.all_to_all, axis_name="exp", split_axis=0, concat_axis=0, tiled=True
    )
    parts = 2
    gathered = [
        lax.all_gather(columns, "exp", axis_index_groups=alike, tiled=True)
        for columns in jnp.split(moe_grad, parts, axis=1)
    ]

    hit = expert_ids[:, None, :] == jnp.arange(count, dtype=jnp.int32)[None, :, None]
    table = jnp.sum(
        jnp.where(hit, route_probs[:, None, :].astype(jnp.float32), 0.0), axis=2
    ).astype(jnp.bfloat16)
    table = table.T.reshape(owners, per_dev * tokens)
    extra = -(-table.shape[1] // units)
    table = jnp.pad(table, ((0, 0), (0, extra * units - table.shape[1])))
    limit = min(stored_hidden_state.shape[3], tokens // 2)
    mixed = swap(
        jnp.concatenate(
            [stored_hidden_state[0, per_dev, :, :limit], table.reshape(owners, extra, units)],
            axis=1,
        )
    )
    probs = mixed[:, limit:].reshape(owners, extra * units)[:, : per_dev * tokens]
    probs = probs.reshape(owners, per_dev, tokens)
    hosts = jnp.max(shadow_list.reshape(owners, per_dev), axis=1)
    shadow_rows = swap(mixed[:, :limit][hosts])
    flags = lax.dynamic_slice_in_dim(shadow_list, own_index * per_dev, per_dev) >= 0
    place = jnp.arange(owners, dtype=jnp.int32)
    order = 2 * (place % chips) + (place // chips + own_index) % 2
    weighted = weighted_rows(
        probs, stored_hidden_state, shadow_rows, flags.astype(jnp.int32), order
    )
    return weighted, gathered


def expert_tiles(weighted, gathered, anchors, per_dev):
    owners = lax.axis_size("exp")
    model = sum(first.shape[1] for first in gathered)
    pairs, second = [], None
    for first, anchor in zip(gathered, anchors):
        first, _ = lax.optimization_barrier((first, (anchor, second)))
        second = lax.ppermute(first, "exp", [(e, e ^ 1) for e in range(owners)])
        pairs.append((first, second))
    tiles, start = None, 0
    for first, second in pairs:
        tiles = tile_columns(weighted, first, second, model, start, tiles)
        start += first.shape[1]
    return tiles.reshape(per_dev, weighted.shape[0] // per_dev, model)


def local(
    queries,
    keys,
    values,
    attn_out,
    attn_out_grad,
    lse_excess,
    block_mask,
    expert_ids,
    route_probs,
    moe_grad,
    shadow_list,
    stored_hidden_state,
):
    query_grad, key_grad, value_grad = attention(
        queries, keys, values, attn_out, attn_out_grad, lse_excess, block_mask
    )
    weighted, gathered = experts(
        expert_ids, route_probs, moe_grad, shadow_list, stored_hidden_state
    )
    per_dev = shadow_list.shape[0] // lax.axis_size("exp")
    expert_grad = expert_tiles(weighted, gathered, (weighted, (key_grad, value_grad)), per_dev)
    return (query_grad, key_grad, value_grad, expert_grad)


def solution(mesh):
    placed = (
        P("ctx", "exp"),
        P("ctx", None),
        P("ctx", None),
        P("ctx", "exp"),
        P("ctx", "exp"),
        P("exp", "ctx"),
        P(),
        P("exp", None),
        P("exp", None),
        P("exp", None),
        P(),
        P("exp", None, None, None, "ctx"),
    )
    return jax.shard_map(
        local,
        mesh=mesh,
        in_specs=placed,
        out_specs=(
            P("ctx", "exp"),
            P(("ctx", "exp"), None),
            P(("ctx", "exp"), None),
            P("exp", "ctx", None),
        ),
        check_vma=False,
    )
```

```python
import functools
import math

import jax
import jax.numpy as jnp
from jax import lax
from jax.experimental import pallas as pl
from jax.experimental.pallas import tpu as pltpu
from jax.sharding import PartitionSpec as P

LAST = (((1,), (1,)), ((), ()))
FIRST = (((0,), (0,)), ((), ()))


def attention_kernel(
    place_ref, mask_ref, query_ref, grad_ref, out_ref, lse_ref, *rest
):
    cycle = mask_ref.shape[0]
    pair_refs, (query_grad_ref, terms_ref, sums_ref, pairs_ref) = rest[:cycle], rest[cycle:]
    rows, width = pairs_ref.shape[1], pairs_ref.shape[2] // 2
    heads = lse_ref.shape[0]
    kv_count = terms_ref.shape[2] // (2 * width)
    scale = 1.0 / math.sqrt(width)
    mine, kv_head = place_ref[0], place_ref[1]
    offset = 0.5 * math.log(rows) + lse_ref[...]
    spans = [slice(h * width, (h + 1) * width) for h in range(heads)]
    for step, pair_ref in enumerate(pair_refs):
        pairs_ref[step] = pair_ref[...]
    delta = []
    for span in spans:
        both = grad_ref[:, span].astype(jnp.float32) * out_ref[:, span].astype(jnp.float32)
        delta.append(jnp.sum(both.T, axis=0, keepdims=True))

    def block(step, diagonal):
        key, value = pairs_ref[step, :, :width], pairs_ref[step, :, width:]
        probs, slopes = [], []
        for h, span in enumerate(spans):
            query, grad = query_ref[:, span], grad_ref[:, span]
            scores = lax.dot_general(key, query, LAST, preferred_element_type=jnp.float32)
            prob = jnp.exp(scores * scale - offset[h : h + 1])
            if diagonal:
                at_key = lax.broadcasted_iota(jnp.int32, (rows, rows), 0)
                at_query = lax.broadcasted_iota(jnp.int32, (rows, rows), 1)
                prob = jnp.where(at_key <= at_query, prob, 0.0)
            prob_grad = lax.dot_general(value, grad, LAST, preferred_element_type=jnp.float32)
            slope = (prob * (prob_grad - delta[h]) * scale).astype(jnp.bfloat16)
            probs.append(prob.astype(jnp.bfloat16))
            slopes.append(slope)
            query_term = lax.dot_general(slope, key, FIRST, preferred_element_type=jnp.float32)
            if diagonal:
                sums_ref[:, span] = query_term
            else:
                sums_ref[:, span] += query_term
        queries = jnp.concatenate([query_ref[:, span] for span in spans], axis=0)
        grads = jnp.concatenate([grad_ref[:, span] for span in spans], axis=0)
        key_term = jnp.dot(
            jnp.concatenate(slopes, axis=1), queries, preferred_element_type=jnp.float32
        )
        value_term = jnp.dot(
            jnp.concatenate(probs, axis=1), grads, preferred_element_type=jnp.float32
        )
        for n, term in enumerate((key_term, value_term)):
            for k in range(kv_count):
                at = (n * kv_count + k) * width
                terms_ref[mine - step, :, at : at + width] = jnp.where(
                    kv_head == k, term, 0.0
                ).astype(jnp.bfloat16)

    block(0, True)

    @pl.loop(0, cycle)
    def _(source):
        seen = jnp.logical_and(source < mine, mask_ref[mine, source] > 0)

        @pl.when(seen)
        def _():
            block(mine - source, False)

        @pl.when(jnp.logical_and(source != mine, jnp.logical_not(seen)))
        def _():
            terms_ref[source] = jnp.zeros_like(terms_ref[source])

    query_grad_ref[...] = sums_ref[...].astype(jnp.bfloat16)


def attention(queries, keys, values, attn_out, attn_out_grad, lse_excess, block_mask):
    rows = queries.shape[0]
    heads = lse_excess.shape[0]
    width = queries.shape[1] // heads
    cycle = lax.axis_size("ctx")
    mine = lax.axis_index("ctx")
    owners = lax.axis_size("exp")
    kv_count = keys.shape[1] // width
    kv_head = lax.axis_index("exp") * kv_count // owners
    pair = jnp.concatenate(
        [
            lax.dynamic_slice_in_dim(keys, kv_head * width, width, 1),
            lax.dynamic_slice_in_dim(values, kv_head * width, width, 1),
        ],
        axis=1,
    )
    arrived = [pair] + [
        lax.ppermute(pair, "ctx", [(c, c + step) for c in range(cycle - step)])
        for step in range(1, cycle)
    ]
    whole = pl.BlockSpec(memory_space=pltpu.VMEM)
    scalars = pl.BlockSpec(memory_space=pltpu.SMEM)
    query_grad, terms = pl.pallas_call(
        attention_kernel,
        out_shape=(
            jax.ShapeDtypeStruct(queries.shape, jnp.bfloat16),
            jax.ShapeDtypeStruct((cycle, rows, 2 * kv_count * width), jnp.bfloat16),
        ),
        in_specs=[scalars] * 2 + [whole] * (4 + cycle),
        out_specs=(whole, whole),
        scratch_shapes=[
            pltpu.VMEM(queries.shape, jnp.float32),
            pltpu.VMEM((cycle,) + pair.shape, jnp.bfloat16),
        ],
        compiler_params=pltpu.CompilerParams(vmem_limit_bytes=40 * 2**20),
        name="attention",
    )(
        jnp.stack([mine, kv_head]).astype(jnp.int32),
        block_mask,
        queries,
        attn_out_grad,
        attn_out,
        lse_excess,
        *arrived,
    )
    total = lax.psum_scatter(
        terms.reshape(cycle * rows, 2 * kv_count * width),
        ("ctx", "exp"),
        scatter_dimension=0,
        tiled=True,
    )
    return query_grad, total


def weight_kernel(order_ref, flag_ref, probs_ref, hidden_ref, shadow_ref, weight_ref):
    per_dev, tokens = probs_ref.shape[1:]
    units = hidden_ref.shape[4]
    earlier = (
        lax.broadcasted_iota(jnp.int32, (tokens, tokens), 0)
        < lax.broadcasted_iota(jnp.int32, (tokens, tokens), 1)
    ).astype(jnp.bfloat16)
    odd = lax.broadcasted_iota(jnp.int32, (1, tokens), 1) % 2 == 1

    def rows_at(named, rows):
        rank = jnp.dot(
            jnp.broadcast_to(named.astype(jnp.float32), (8, tokens)).astype(jnp.bfloat16),
            earlier,
            preferred_element_type=jnp.float32,
        )[:1]
        place = lax.broadcasted_iota(jnp.int32, (rows.shape[0], tokens), 0).astype(jnp.float32)
        chosen = jnp.where(jnp.logical_and(named, rank == place), 1.0, 0.0).astype(jnp.bfloat16)
        return lax.dot_general(rows, chosen, FIRST, preferred_element_type=jnp.float32)

    for j in range(per_dev):
        prob = probs_ref[0, j : j + 1].astype(jnp.float32)
        named = prob > 0
        side = jnp.logical_and(jnp.logical_and(named, odd), flag_ref[j] > 0)
        own = jnp.logical_and(named, jnp.logical_not(side))
        rows = rows_at(own, hidden_ref[0, j, 0]) + rows_at(side, shadow_ref[0])
        weight_ref[j * units : (j + 1) * units] = (rows * prob).astype(jnp.bfloat16)


def weighted_rows(probs, hidden, shadow_rows, flags, order):
    owners, per_dev, tokens = probs.shape
    units = hidden.shape[4]
    return pl.pallas_call(
        weight_kernel,
        out_shape=jax.ShapeDtypeStruct((per_dev * units, owners * tokens), jnp.bfloat16),
        grid_spec=pltpu.PrefetchScalarGridSpec(
            num_scalar_prefetch=2,
            grid=(owners,),
            in_specs=[
                pl.BlockSpec((1, per_dev, tokens), lambda i, order, flag: (order[i], 0, 0)),
                pl.BlockSpec(
                    (1, per_dev, 1) + hidden.shape[3:],
                    lambda i, order, flag: (0, 0, order[i], 0, 0),
                ),
                pl.BlockSpec(
                    (1,) + shadow_rows.shape[1:], lambda i, order, flag: (order[i], 0, 0)
                ),
            ],
            out_specs=pl.BlockSpec((per_dev * units, tokens), lambda i, order, flag: (0, i)),
        ),
        compiler_params=pltpu.CompilerParams(vmem_limit_bytes=40 * 2**20),
        name="weighted",
    )(order, flags, probs, hidden, shadow_rows)


def tile_kernel(weight_ref, first_ref, second_ref, *rest):
    tile_ref = rest[-1]
    depth = first_ref.shape[0]
    tile_ref[...] = jnp.dot(
        weight_ref[:, :depth], first_ref[...], preferred_element_type=jnp.float32
    ) + jnp.dot(weight_ref[:, depth:], second_ref[...], preferred_element_type=jnp.float32)


def tile_columns(weighted, first, second, width, start, tiles):
    depth, columns = first.shape
    rows = weighted.shape[0]
    step = min(512, columns)
    shift = start // step
    gathered = pl.BlockSpec((depth, step), lambda i: (0, i))
    earlier = [] if tiles is None else [tiles]
    return pl.pallas_call(
        tile_kernel,
        out_shape=jax.ShapeDtypeStruct((rows, width), jnp.float32),
        grid=(columns // step,),
        in_specs=[pl.BlockSpec(weighted.shape, lambda i: (0, 0)), gathered, gathered]
        + [pl.BlockSpec(memory_space=pl.ANY)] * len(earlier),
        out_specs=pl.BlockSpec((rows, step), lambda i: (0, i + shift)),
        input_output_aliases={3: 0} if earlier else {},
        compiler_params=pltpu.CompilerParams(vmem_limit_bytes=40 * 2**20),
        name="tiles",
    )(weighted, first, second, *earlier)


def experts(expert_ids, route_probs, moe_grad, shadow_list, stored_hidden_state):
    owners = lax.axis_size("exp")
    own_index = lax.axis_index("exp")
    tokens, model = moe_grad.shape
    count = shadow_list.shape[0]
    per_dev = count // owners
    units = stored_hidden_state.shape[4]
    chips = owners // 2
    ring = [chip ^ (chip >> 1) for chip in range(chips)]
    alike = [[2 * chip for chip in ring], [2 * chip + 1 for chip in ring[::-1]]]
    swap = functools.partial(
        lax.all_to_all, axis_name="exp", split_axis=0, concat_axis=0, tiled=True
    )
    parts = 2
    gathered = [
        lax.all_gather(columns, "exp", axis_index_groups=alike, tiled=True)
        for columns in jnp.split(moe_grad, parts, axis=1)
    ]

    hit = expert_ids[:, None, :] == jnp.arange(count, dtype=jnp.int32)[None, :, None]
    table = jnp.sum(
        jnp.where(hit, route_probs[:, None, :].astype(jnp.float32), 0.0), axis=2
    ).astype(jnp.bfloat16)
    table = table.T.reshape(owners, per_dev * tokens)
    extra = -(-table.shape[1] // units)
    table = jnp.pad(table, ((0, 0), (0, extra * units - table.shape[1])))
    limit = min(stored_hidden_state.shape[3], tokens // 2)
    mixed = swap(
        jnp.concatenate(
            [stored_hidden_state[0, per_dev, :, :limit], table.reshape(owners, extra, units)],
            axis=1,
        )
    )
    probs = mixed[:, limit:].reshape(owners, extra * units)[:, : per_dev * tokens]
    probs = probs.reshape(owners, per_dev, tokens)
    hosts = jnp.max(shadow_list.reshape(owners, per_dev), axis=1)
    shadow_rows = swap(mixed[:, :limit][hosts])
    flags = lax.dynamic_slice_in_dim(shadow_list, own_index * per_dev, per_dev) >= 0
    order = jnp.where(
        own_index % 2 == 0,
        jnp.array(alike[0] + alike[1], jnp.int32),
        jnp.array(alike[1] + alike[0], jnp.int32),
    )
    weighted = weighted_rows(
        probs, stored_hidden_state, shadow_rows, flags.astype(jnp.int32), order
    )
    return weighted, gathered


def expert_tiles(weighted, gathered, anchors, per_dev):
    owners = lax.axis_size("exp")
    model = sum(first.shape[1] for first in gathered)
    pairs, second = [], None
    for first, anchor in zip(gathered, anchors):
        first, _ = lax.optimization_barrier((first, (anchor, second)))
        second = lax.ppermute(first, "exp", [(e, e ^ 1) for e in range(owners)])
        pairs.append((first, second))
    tiles, start = None, 0
    for first, second in pairs:
        tiles = tile_columns(weighted, first, second, model, start, tiles)
        start += first.shape[1]
    return tiles.reshape(per_dev, weighted.shape[0] // per_dev, model)


def local(
    queries,
    keys,
    values,
    attn_out,
    attn_out_grad,
    lse_excess,
    block_mask,
    expert_ids,
    route_probs,
    moe_grad,
    shadow_list,
    stored_hidden_state,
):
    query_grad, kv_grad = attention(
        queries, keys, values, attn_out, attn_out_grad, lse_excess, block_mask
    )
    weighted, gathered = experts(
        expert_ids, route_probs, moe_grad, shadow_list, stored_hidden_state
    )
    per_dev = shadow_list.shape[0] // lax.axis_size("exp")
    expert_grad = expert_tiles(weighted, gathered, ((weighted, query_grad), None), per_dev)
    kv_grad, expert_grad = lax.optimization_barrier((kv_grad, expert_grad))
    key_grad, value_grad = jnp.split(kv_grad, 2, axis=1)
    return (query_grad, key_grad, value_grad, expert_grad)


def solution(mesh):
    placed = (
        P("ctx", "exp"),
        P("ctx", None),
        P("ctx", None),
        P("ctx", "exp"),
        P("ctx", "exp"),
        P("exp", "ctx"),
        P(),
        P("exp", None),
        P("exp", None),
        P("exp", None),
        P(),
        P("exp", None, None, None, "ctx"),
    )
    return jax.shard_map(
        local,
        mesh=mesh,
        in_specs=placed,
        out_specs=(
            P("ctx", "exp"),
            P(("ctx", "exp"), None),
            P(("ctx", "exp"), None),
            P("exp", "ctx", None),
        ),
        check_vma=False,
    )
```

```python
import functools
import math

import jax
import jax.numpy as jnp
from jax import lax
from jax.experimental import pallas as pl
from jax.experimental.pallas import tpu as pltpu
from jax.sharding import PartitionSpec as P

LAST = (((1,), (1,)), ((), ()))
FIRST = (((0,), (0,)), ((), ()))


def attention_kernel(
    place_ref, mask_ref, query_ref, grad_ref, out_ref, lse_ref, *rest
):
    cycle = mask_ref.shape[0]
    pair_refs, (query_grad_ref, terms_ref, sums_ref, pairs_ref) = rest[:cycle], rest[cycle:]
    rows, width = pairs_ref.shape[1], pairs_ref.shape[2] // 2
    heads = lse_ref.shape[0]
    scale = 1.0 / math.sqrt(width)
    mine = place_ref[0]
    offset = 0.5 * math.log(rows) + lse_ref[...]
    spans = [slice(h * width, (h + 1) * width) for h in range(heads)]
    for step, pair_ref in enumerate(pair_refs):
        pairs_ref[step] = pair_ref[...]
    delta = []
    for span in spans:
        both = grad_ref[:, span].astype(jnp.float32) * out_ref[:, span].astype(jnp.float32)
        delta.append(jnp.sum(both.T, axis=0, keepdims=True))

    def block(step, diagonal):
        key, value = pairs_ref[step, :, :width], pairs_ref[step, :, width:]
        probs, slopes = [], []
        for h, span in enumerate(spans):
            query, grad = query_ref[:, span], grad_ref[:, span]
            scores = lax.dot_general(key, query, LAST, preferred_element_type=jnp.float32)
            prob = jnp.exp(scores * scale - offset[h : h + 1])
            if diagonal:
                at_key = lax.broadcasted_iota(jnp.int32, (rows, rows), 0)
                at_query = lax.broadcasted_iota(jnp.int32, (rows, rows), 1)
                prob = jnp.where(at_key <= at_query, prob, 0.0)
            prob_grad = lax.dot_general(value, grad, LAST, preferred_element_type=jnp.float32)
            slope = (prob * (prob_grad - delta[h]) * scale).astype(jnp.bfloat16)
            probs.append(prob.astype(jnp.bfloat16))
            slopes.append(slope)
            query_term = lax.dot_general(slope, key, FIRST, preferred_element_type=jnp.float32)
            if diagonal:
                sums_ref[:, span] = query_term
            else:
                sums_ref[:, span] += query_term
        queries = jnp.concatenate([query_ref[:, span] for span in spans], axis=0)
        grads = jnp.concatenate([grad_ref[:, span] for span in spans], axis=0)
        key_term = jnp.dot(
            jnp.concatenate(slopes, axis=1), queries, preferred_element_type=jnp.float32
        )
        value_term = jnp.dot(
            jnp.concatenate(probs, axis=1), grads, preferred_element_type=jnp.float32
        )
        terms_ref[mine - step, :, :width] = key_term.astype(jnp.bfloat16)
        terms_ref[mine - step, :, width:] = value_term.astype(jnp.bfloat16)

    block(0, True)

    @pl.loop(0, cycle)
    def _(source):
        seen = jnp.logical_and(source < mine, mask_ref[mine, source] > 0)

        @pl.when(seen)
        def _():
            block(mine - source, False)

        @pl.when(jnp.logical_and(source != mine, jnp.logical_not(seen)))
        def _():
            terms_ref[source] = jnp.zeros_like(terms_ref[source])

    query_grad_ref[...] = sums_ref[...].astype(jnp.bfloat16)


def attention(queries, keys, values, attn_out, attn_out_grad, lse_excess, block_mask):
    rows = queries.shape[0]
    heads = lse_excess.shape[0]
    width = queries.shape[1] // heads
    cycle = lax.axis_size("ctx")
    mine = lax.axis_index("ctx")
    owners = lax.axis_size("exp")
    kv_count = keys.shape[1] // width
    kv_head = lax.axis_index("exp") * kv_count // owners
    pair = jnp.concatenate(
        [
            lax.dynamic_slice_in_dim(keys, kv_head * width, width, 1),
            lax.dynamic_slice_in_dim(values, kv_head * width, width, 1),
        ],
        axis=1,
    )
    arrived = [pair] + [
        lax.ppermute(pair, "ctx", [(c, c + step) for c in range(cycle - step)])
        for step in range(1, cycle)
    ]
    whole = pl.BlockSpec(memory_space=pltpu.VMEM)
    scalars = pl.BlockSpec(memory_space=pltpu.SMEM)
    query_grad, terms = pl.pallas_call(
        attention_kernel,
        out_shape=(
            jax.ShapeDtypeStruct(queries.shape, jnp.bfloat16),
            jax.ShapeDtypeStruct((cycle, rows, 2 * width), jnp.bfloat16),
        ),
        in_specs=[scalars] * 2 + [whole] * (4 + cycle),
        out_specs=(whole, whole),
        scratch_shapes=[
            pltpu.VMEM(queries.shape, jnp.float32),
            pltpu.VMEM((cycle,) + pair.shape, jnp.bfloat16),
        ],
        compiler_params=pltpu.CompilerParams(vmem_limit_bytes=40 * 2**20),
        name="attention",
    )(
        mine.astype(jnp.int32)[None],
        block_mask,
        queries,
        attn_out_grad,
        attn_out,
        lse_excess,
        *arrived,
    )
    return query_grad, terms


def sum_kernel(parts_ref, key_ref, value_ref):
    cycle, owners, rows, columns = parts_ref.shape
    kv_count = key_ref.shape[1] * 2 // columns
    group = owners // kv_count
    width = columns // 2
    for k in range(kv_count):
        total = jnp.zeros((rows, columns), jnp.float32)
        for c in range(cycle):
            for e in range(k * group, (k + 1) * group):
                total += parts_ref[c, e].astype(jnp.float32)
        key_ref[:, k * width : (k + 1) * width] = total[:, :width].astype(jnp.bfloat16)
        value_ref[:, k * width : (k + 1) * width] = total[:, width:].astype(jnp.bfloat16)


def summed_terms(terms, kv_columns):
    cycle, owners = lax.axis_size("ctx"), lax.axis_size("exp")
    rows, columns = terms.shape[1] // owners, terms.shape[2]
    parts = lax.all_to_all(
        terms.reshape(cycle * owners, rows, columns),
        ("ctx", "exp"),
        split_axis=0,
        concat_axis=0,
        tiled=True,
    )
    whole = pl.BlockSpec(memory_space=pltpu.VMEM)
    out = jax.ShapeDtypeStruct((rows, kv_columns), jnp.bfloat16)
    return pl.pallas_call(
        sum_kernel,
        out_shape=(out, out),
        in_specs=[whole],
        out_specs=(whole, whole),
        compiler_params=pltpu.CompilerParams(vmem_limit_bytes=40 * 2**20),
        name="sums",
    )(parts.reshape(cycle, owners, rows, columns))


def weight_kernel(order_ref, flag_ref, probs_ref, hidden_ref, shadow_ref, weight_ref):
    per_dev, tokens = probs_ref.shape[1:]
    units = hidden_ref.shape[4]
    earlier = (
        lax.broadcasted_iota(jnp.int32, (tokens, tokens), 0)
        < lax.broadcasted_iota(jnp.int32, (tokens, tokens), 1)
    ).astype(jnp.bfloat16)
    odd = lax.broadcasted_iota(jnp.int32, (1, tokens), 1) % 2 == 1

    def rows_at(named, rows):
        rank = jnp.dot(
            jnp.broadcast_to(named.astype(jnp.float32), (8, tokens)).astype(jnp.bfloat16),
            earlier,
            preferred_element_type=jnp.float32,
        )[:1]
        place = lax.broadcasted_iota(jnp.int32, (rows.shape[0], tokens), 0).astype(jnp.float32)
        chosen = jnp.where(jnp.logical_and(named, rank == place), 1.0, 0.0).astype(jnp.bfloat16)
        return lax.dot_general(rows, chosen, FIRST, preferred_element_type=jnp.float32)

    for j in range(per_dev):
        prob = probs_ref[0, j : j + 1].astype(jnp.float32)
        named = prob > 0
        side = jnp.logical_and(jnp.logical_and(named, odd), flag_ref[j] > 0)
        own = jnp.logical_and(named, jnp.logical_not(side))
        rows = rows_at(own, hidden_ref[0, j, 0]) + rows_at(side, shadow_ref[0])
        weight_ref[j * units : (j + 1) * units] = (rows * prob).astype(jnp.bfloat16)


def weighted_rows(probs, hidden, shadow_rows, flags, order):
    owners, per_dev, tokens = probs.shape
    units = hidden.shape[4]
    return pl.pallas_call(
        weight_kernel,
        out_shape=jax.ShapeDtypeStruct((per_dev * units, owners * tokens), jnp.bfloat16),
        grid_spec=pltpu.PrefetchScalarGridSpec(
            num_scalar_prefetch=2,
            grid=(owners,),
            in_specs=[
                pl.BlockSpec((1, per_dev, tokens), lambda i, order, flag: (order[i], 0, 0)),
                pl.BlockSpec(
                    (1, per_dev, 1) + hidden.shape[3:],
                    lambda i, order, flag: (0, 0, order[i], 0, 0),
                ),
                pl.BlockSpec(
                    (1,) + shadow_rows.shape[1:], lambda i, order, flag: (order[i], 0, 0)
                ),
            ],
            out_specs=pl.BlockSpec((per_dev * units, tokens), lambda i, order, flag: (0, i)),
        ),
        compiler_params=pltpu.CompilerParams(vmem_limit_bytes=40 * 2**20),
        name="weighted",
    )(order, flags, probs, hidden, shadow_rows)


def tile_kernel(start, count, weight_ref, *refs):
    tile_ref = refs[-1]
    blocks = jnp.concatenate([ref[...] for ref in refs[:count]], axis=0)
    tile = jnp.dot(
        weight_ref[:, start : start + blocks.shape[0]], blocks, preferred_element_type=jnp.float32
    )
    for ref in refs[count:-1]:
        tile += ref[...]
    tile_ref[...] = tile


def tile_sum(weighted, blocks, start, partial):
    tokens, model = blocks[0].shape
    rows = weighted.shape[0]
    step = 512
    column = lambda i: (0, i)
    earlier = [] if partial is None else [partial]
    depth = len(blocks) * tokens
    return pl.pallas_call(
        functools.partial(tile_kernel, start, len(blocks)),
        out_shape=jax.ShapeDtypeStruct((rows, model), jnp.float32),
        grid=(model // step,),
        in_specs=[pl.BlockSpec(weighted.shape, lambda i: (0, 0))]
        + [pl.BlockSpec((tokens, step), column)] * len(blocks)
        + [pl.BlockSpec((rows, step), column)] * len(earlier),
        out_specs=pl.BlockSpec((rows, step), column),
        compiler_params=pltpu.CompilerParams(vmem_limit_bytes=50 * 2**20),
        cost_estimate=pl.CostEstimate(
            flops=2 * rows * depth * model,
            bytes_accessed=4 * rows * model * (1 + len(earlier)) + 2 * depth * model,
            transcendentals=0,
        ),
        name="tiles",
    )(weighted, *blocks, *earlier)


def experts(expert_ids, route_probs, moe_grad, shadow_list, stored_hidden_state, anchor):
    owners = lax.axis_size("exp")
    own_index = lax.axis_index("exp")
    swap = functools.partial(
        lax.all_to_all, axis_name="exp", split_axis=0, concat_axis=0, tiled=True
    )
    tokens, model = moe_grad.shape
    count = shadow_list.shape[0]
    per_dev = count // owners
    units = stored_hidden_state.shape[4]
    hit = expert_ids[:, None, :] == jnp.arange(count, dtype=jnp.int32)[None, :, None]
    table = jnp.sum(
        jnp.where(hit, route_probs[:, None, :].astype(jnp.float32), 0.0), axis=2
    ).astype(jnp.bfloat16)
    table = table.T.reshape(owners, per_dev * tokens)
    extra = -(-table.shape[1] // units)
    table = jnp.pad(table, ((0, 0), (0, extra * units - table.shape[1])))
    limit = min(stored_hidden_state.shape[3], tokens // 2)
    mixed = swap(
        jnp.concatenate(
            [stored_hidden_state[0, per_dev, :, :limit], table.reshape(owners, extra, units)],
            axis=1,
        )
    )
    probs = mixed[:, limit:].reshape(owners, extra * units)[:, : per_dev * tokens]
    probs = probs.reshape(owners, per_dev, tokens)
    hosts = jnp.max(shadow_list.reshape(owners, per_dev), axis=1)
    sent, _ = lax.optimization_barrier((mixed[:, :limit][hosts], anchor))
    shadow_rows = swap(sent)
    flags = lax.dynamic_slice_in_dim(shadow_list, own_index * per_dev, per_dev) >= 0
    steps = block_steps(owners)
    orders = [
        [step ^ turn for pair in zip(steps[core], steps[1 - core]) for step, turn in zip(pair, (0, 1))]
        for core in range(2)
    ]
    order = own_index ^ jnp.where(
        own_index % 2 == 0, jnp.array(orders[0], jnp.int32), jnp.array(orders[1], jnp.int32)
    )
    weighted = weighted_rows(
        probs, stored_hidden_state, shadow_rows, flags.astype(jnp.int32), order
    )
    return weighted, probs


def block_steps(owners):
    masks = [1 << bit for bit in range(1, owners.bit_length() - 1)]
    steps = []
    for core in range(2):
        first, second = masks[1 - core], masks[core]
        held = [0, first, second, first ^ second]
        for mask in masks[2:]:
            held = held + [step ^ mask for step in held]
        steps.append(held)
    return steps


def moved(value, steps):
    owners = lax.axis_size("exp")
    return lax.ppermute(value, "exp", [(e, e ^ steps[e % 2]) for e in range(owners)])


def near_blocks(moe_grad):
    steps = block_steps(lax.axis_size("exp"))
    first = moved(moe_grad, [held[1] for held in steps])
    second = moved(moe_grad, [held[2] for held in steps])
    return first, second, moved(moe_grad, (1, 1))


def expert_tiles(weighted, moe_grad, near, anchor, per_dev):
    owners = lax.axis_size("exp")
    steps = block_steps(owners)
    first, second, beside = near
    first, _ = lax.optimization_barrier((first, anchor))
    far = moved(first, [held[2] for held in steps])
    second, _ = lax.optimization_barrier((second, anchor))
    held = [moe_grad, first, second]
    blocks = [moe_grad, beside] + [
        block for part in held[1:] for block in (part, moved(part, (1, 1)))
    ]
    tiles = tile_sum(weighted, blocks, 0, None)
    far, _ = lax.optimization_barrier((far, weighted))
    held = held + [far]
    rest = [far]
    for turn in range(len(steps[0]).bit_length() - 3):
        mask = steps[0][4 << turn]
        more = [moved(part, (mask, mask)) for part in held]
        held, rest = held + more, rest + more
    rest = [block for part in rest for block in (part, moved(part, (1, 1)))]
    tiles = tile_sum(weighted, rest, len(blocks) * moe_grad.shape[0], tiles)
    return tiles.reshape(per_dev, weighted.shape[0] // per_dev, moe_grad.shape[1])


def local(
    queries,
    keys,
    values,
    attn_out,
    attn_out_grad,
    lse_excess,
    block_mask,
    expert_ids,
    route_probs,
    moe_grad,
    shadow_list,
    stored_hidden_state,
):
    near = near_blocks(moe_grad)
    query_grad, terms = attention(
        queries, keys, values, attn_out, attn_out_grad, lse_excess, block_mask
    )
    weighted, probs = experts(
        expert_ids, route_probs, moe_grad, shadow_list, stored_hidden_state, query_grad
    )
    key_grad, value_grad = summed_terms(terms, keys.shape[1])
    per_dev = shadow_list.shape[0] // lax.axis_size("exp")
    expert_grad = expert_tiles(weighted, moe_grad, near, (query_grad, probs), per_dev)
    return (query_grad, key_grad, value_grad, expert_grad)


def solution(mesh):
    placed = (
        P("ctx", "exp"),
        P("ctx", None),
        P("ctx", None),
        P("ctx", "exp"),
        P("ctx", "exp"),
        P("exp", "ctx"),
        P(),
        P("exp", None),
        P("exp", None),
        P("exp", None),
        P(),
        P("exp", None, None, None, "ctx"),
    )
    return jax.shard_map(
        local,
        mesh=mesh,
        in_specs=placed,
        out_specs=(
            P("ctx", "exp"),
            P(("ctx", "exp"), None),
            P(("ctx", "exp"), None),
            P("exp", "ctx", None),
        ),
        check_vma=False,
    )
```

```python
import functools
import math

import jax
import jax.numpy as jnp
from jax import lax
from jax.experimental import pallas as pl
from jax.experimental.pallas import tpu as pltpu
from jax.sharding import PartitionSpec as P

LAST = (((1,), (1,)), ((), ()))
FIRST = (((0,), (0,)), ((), ()))


def attention_kernel(
    place_ref, mask_ref, query_ref, grad_ref, out_ref, lse_ref, *rest
):
    cycle = mask_ref.shape[0]
    pair_refs, query_grad_ref, term_refs = rest[:cycle], rest[cycle], rest[cycle + 1 : -3]
    sums_ref, pairs_ref, terms_ref = rest[-3:]
    rows, width = pairs_ref.shape[1], pairs_ref.shape[2] // 2
    heads = lse_ref.shape[0]
    scale = 1.0 / math.sqrt(width)
    mine = place_ref[0]
    offset = 0.5 * math.log(rows) + lse_ref[...]
    spans = [slice(h * width, (h + 1) * width) for h in range(heads)]
    for step, pair_ref in enumerate(pair_refs):
        pairs_ref[step] = pair_ref[...]
    delta = []
    for span in spans:
        both = grad_ref[:, span].astype(jnp.float32) * out_ref[:, span].astype(jnp.float32)
        delta.append(jnp.sum(both.T, axis=0, keepdims=True))

    def block(step, diagonal):
        key, value = pairs_ref[step, :, :width], pairs_ref[step, :, width:]
        probs, slopes = [], []
        for h, span in enumerate(spans):
            query, grad = query_ref[:, span], grad_ref[:, span]
            scores = lax.dot_general(key, query, LAST, preferred_element_type=jnp.float32)
            prob = jnp.exp(scores * scale - offset[h : h + 1])
            if diagonal:
                at_key = lax.broadcasted_iota(jnp.int32, (rows, rows), 0)
                at_query = lax.broadcasted_iota(jnp.int32, (rows, rows), 1)
                prob = jnp.where(at_key <= at_query, prob, 0.0)
            prob_grad = lax.dot_general(value, grad, LAST, preferred_element_type=jnp.float32)
            slope = (prob * (prob_grad - delta[h]) * scale).astype(jnp.bfloat16)
            probs.append(prob.astype(jnp.bfloat16))
            slopes.append(slope)
            query_term = lax.dot_general(slope, key, FIRST, preferred_element_type=jnp.float32)
            if diagonal:
                sums_ref[:, span] = query_term
            else:
                sums_ref[:, span] += query_term
        queries = jnp.concatenate([query_ref[:, span] for span in spans], axis=0)
        grads = jnp.concatenate([grad_ref[:, span] for span in spans], axis=0)
        key_term = jnp.dot(
            jnp.concatenate(slopes, axis=1), queries, preferred_element_type=jnp.float32
        )
        value_term = jnp.dot(
            jnp.concatenate(probs, axis=1), grads, preferred_element_type=jnp.float32
        )
        terms_ref[step, :, :width] = key_term.astype(jnp.bfloat16)
        terms_ref[step, :, width:] = value_term.astype(jnp.bfloat16)

    block(0, True)

    @pl.loop(1, cycle)
    def _(step):
        source = mine - step
        seen = jnp.logical_and(source >= 0, mask_ref[mine, jnp.maximum(source, 0)] > 0)

        @pl.when(seen)
        def _():
            block(step, False)

        @pl.when(jnp.logical_not(seen))
        def _():
            terms_ref[step] = jnp.zeros_like(terms_ref[step])

    for step, term_ref in enumerate(term_refs):
        term_ref[...] = terms_ref[step]
    query_grad_ref[...] = sums_ref[...].astype(jnp.bfloat16)


def attention(queries, keys, values, attn_out, attn_out_grad, lse_excess, block_mask):
    rows = queries.shape[0]
    heads = lse_excess.shape[0]
    width = queries.shape[1] // heads
    cycle = lax.axis_size("ctx")
    mine = lax.axis_index("ctx")
    owners = lax.axis_size("exp")
    kv_count = keys.shape[1] // width
    kv_head = lax.axis_index("exp") * kv_count // owners
    pair = jnp.concatenate(
        [
            lax.dynamic_slice_in_dim(keys, kv_head * width, width, 1),
            lax.dynamic_slice_in_dim(values, kv_head * width, width, 1),
        ],
        axis=1,
    )
    arrived = [pair] + [
        lax.ppermute(pair, "ctx", [(c, c + step) for c in range(cycle - step)])
        for step in range(1, cycle)
    ]
    whole = pl.BlockSpec(memory_space=pltpu.VMEM)
    scalars = pl.BlockSpec(memory_space=pltpu.SMEM)
    query_grad, *terms = pl.pallas_call(
        attention_kernel,
        out_shape=[jax.ShapeDtypeStruct(queries.shape, jnp.bfloat16)]
        + [jax.ShapeDtypeStruct(pair.shape, jnp.bfloat16)] * cycle,
        in_specs=[scalars] * 2 + [whole] * (4 + cycle),
        out_specs=[whole] * (1 + cycle),
        scratch_shapes=[
            pltpu.VMEM(queries.shape, jnp.float32),
            pltpu.VMEM((cycle,) + pair.shape, jnp.bfloat16),
            pltpu.VMEM((cycle,) + pair.shape, jnp.bfloat16),
        ],
        compiler_params=pltpu.CompilerParams(vmem_limit_bytes=24 * 2**20),
        name="attention",
    )(
        mine.astype(jnp.int32)[None],
        block_mask,
        queries,
        attn_out_grad,
        attn_out,
        lse_excess,
        *arrived,
    )
    return query_grad, terms


def sum_kernel(parts_ref, key_ref, value_ref):
    owners, rows, columns = parts_ref.shape
    kv_count = key_ref.shape[1] * 2 // columns
    group = owners // kv_count
    width = columns // 2
    for k in range(kv_count):
        total = jnp.zeros((rows, columns), jnp.float32)
        for e in range(k * group, (k + 1) * group):
            total += parts_ref[e].astype(jnp.float32)
        key_ref[:, k * width : (k + 1) * width] = total[:, :width].astype(jnp.bfloat16)
        value_ref[:, k * width : (k + 1) * width] = total[:, width:].astype(jnp.bfloat16)


def block_terms(terms):
    cycle = lax.axis_size("ctx")
    total = terms[0].astype(jnp.float32)
    for step in range(1, cycle):
        pairs = [(c, c - step) for c in range(step, cycle)]
        total = total + lax.ppermute(terms[step], "ctx", pairs).astype(jnp.float32)
    return total.astype(jnp.bfloat16)


def summed_terms(total, kv_columns):
    owners = lax.axis_size("exp")
    rows, columns = total.shape
    parts = lax.all_to_all(
        total.reshape(owners, rows // owners, columns),
        "exp",
        split_axis=0,
        concat_axis=0,
        tiled=True,
    )
    whole = pl.BlockSpec(memory_space=pltpu.VMEM)
    out = jax.ShapeDtypeStruct((rows // owners, kv_columns), jnp.bfloat16)
    return pl.pallas_call(
        sum_kernel,
        out_shape=(out, out),
        in_specs=[whole],
        out_specs=(whole, whole),
        compiler_params=pltpu.CompilerParams(vmem_limit_bytes=16 * 2**20),
        name="sums",
    )(parts)


def weight_kernel(order_ref, flag_ref, probs_ref, hidden_ref, shadow_ref, weight_ref):
    owners, per_dev, tokens = probs_ref.shape
    units = hidden_ref.shape[4]
    earlier = (
        lax.broadcasted_iota(jnp.int32, (tokens, tokens), 0)
        < lax.broadcasted_iota(jnp.int32, (tokens, tokens), 1)
    ).astype(jnp.bfloat16)
    odd = lax.broadcasted_iota(jnp.int32, (1, tokens), 1) % 2 == 1

    def rows_at(named, rows):
        rank = jnp.dot(
            jnp.broadcast_to(named.astype(jnp.float32), (8, tokens)).astype(jnp.bfloat16),
            earlier,
            preferred_element_type=jnp.float32,
        )[:1]
        place = lax.broadcasted_iota(jnp.int32, (rows.shape[0], tokens), 0).astype(jnp.float32)
        chosen = jnp.where(jnp.logical_and(named, rank == place), 1.0, 0.0).astype(jnp.bfloat16)
        return lax.dot_general(rows, chosen, FIRST, preferred_element_type=jnp.float32)

    for i in range(owners):
        source = order_ref[i]
        for j in range(per_dev):
            prob = probs_ref[source, j : j + 1].astype(jnp.float32)
            named = prob > 0
            side = jnp.logical_and(jnp.logical_and(named, odd), flag_ref[j] > 0)
            own = jnp.logical_and(named, jnp.logical_not(side))
            rows = rows_at(own, hidden_ref[0, j, source]) + rows_at(side, shadow_ref[source])
            weight_ref[j * units : (j + 1) * units, i * tokens : (i + 1) * tokens] = (
                rows * prob
            ).astype(jnp.bfloat16)


def weighted_rows(probs, hidden, shadow_rows, flags, order):
    owners, per_dev, tokens = probs.shape
    units = hidden.shape[4]
    whole = pl.BlockSpec(memory_space=pltpu.VMEM)
    scalars = pl.BlockSpec(memory_space=pltpu.SMEM)
    return pl.pallas_call(
        weight_kernel,
        out_shape=jax.ShapeDtypeStruct((per_dev * units, owners * tokens), jnp.bfloat16),
        in_specs=[scalars] * 2 + [whole] * 3,
        out_specs=whole,
        compiler_params=pltpu.CompilerParams(vmem_limit_bytes=24 * 2**20),
        name="weighted",
    )(order, flags, probs, hidden, shadow_rows)


def tile_kernel(weight_ref, *refs):
    *block_refs, tile_ref, held_ref, sems = refs
    per_dev, units, model = tile_ref.shape
    steps = sems.shape[0]
    step = model // steps
    copies = []
    for i in range(steps):
        columns = slice(i * step, (i + 1) * step)
        blocks = jnp.concatenate([ref[:, columns] for ref in block_refs], axis=0)
        held_ref[:, columns] = jnp.dot(
            weight_ref[...], blocks, preferred_element_type=jnp.float32
        )
        for j in range(per_dev):
            copies.append(
                pltpu.make_async_copy(
                    held_ref.at[pl.ds(j * units, units), pl.ds(i * step, step)],
                    tile_ref.at[j, :, pl.ds(i * step, step)],
                    sems.at[i, j],
                )
            )
            copies[-1].start()
    for copy in copies:
        copy.wait()


def tile_sums(weighted, blocks, per_dev):
    model = blocks[0].shape[1]
    rows = weighted.shape[0]
    steps = model // 512
    whole = pl.BlockSpec(memory_space=pltpu.VMEM)
    return pl.pallas_call(
        tile_kernel,
        out_shape=jax.ShapeDtypeStruct((per_dev, rows // per_dev, model), jnp.float32),
        in_specs=[whole] * (1 + len(blocks)),
        out_specs=pl.BlockSpec(memory_space=pl.ANY),
        scratch_shapes=[
            pltpu.VMEM((rows, model), jnp.float32),
            pltpu.SemaphoreType.DMA((steps, per_dev)),
        ],
        compiler_params=pltpu.CompilerParams(vmem_limit_bytes=24 * 2**20),
        name="tiles",
    )(weighted, *blocks)


def experts(expert_ids, route_probs, moe_grad, shadow_list, stored_hidden_state, anchor, later):
    owners = lax.axis_size("exp")
    own_index = lax.axis_index("exp")
    swap = functools.partial(
        lax.all_to_all, axis_name="exp", split_axis=0, concat_axis=0, tiled=True
    )
    tokens, model = moe_grad.shape
    count = shadow_list.shape[0]
    per_dev = count // owners
    units = stored_hidden_state.shape[4]
    hit = expert_ids[:, None, :] == jnp.arange(count, dtype=jnp.int32)[None, :, None]
    table = jnp.sum(
        jnp.where(hit, route_probs[:, None, :].astype(jnp.float32), 0.0), axis=2
    ).astype(jnp.bfloat16)
    table = table.T.reshape(owners, per_dev * tokens)
    extra = -(-table.shape[1] // units)
    table = jnp.pad(table, ((0, 0), (0, extra * units - table.shape[1])))
    limit = min(stored_hidden_state.shape[3], tokens // 2)
    mixed = jnp.concatenate(
        [stored_hidden_state[0, per_dev, :, :limit], table.reshape(owners, extra, units)],
        axis=1,
    )
    mixed, _ = lax.optimization_barrier((mixed, anchor))
    mixed = swap(mixed)
    probs = mixed[:, limit:].reshape(owners, extra * units)[:, : per_dev * tokens]
    probs = probs.reshape(owners, per_dev, tokens)
    hosts = jnp.max(shadow_list.reshape(owners, per_dev), axis=1)
    shadow_rows = swap(mixed[:, :limit][hosts])
    shadow_rows, later = lax.optimization_barrier((shadow_rows, later))
    flags = lax.dynamic_slice_in_dim(shadow_list, own_index * per_dev, per_dev) >= 0
    steps = block_steps(owners)
    orders = [
        [step ^ turn for pair in zip(steps[core], steps[1 - core]) for step, turn in zip(pair, (0, 1))]
        for core in range(2)
    ]
    order = own_index ^ jnp.where(
        own_index % 2 == 0, jnp.array(orders[0], jnp.int32), jnp.array(orders[1], jnp.int32)
    )
    weighted = weighted_rows(
        probs, stored_hidden_state, shadow_rows, flags.astype(jnp.int32), order
    )
    return weighted, probs, later


def block_steps(owners):
    masks = [1 << bit for bit in range(1, owners.bit_length() - 1)]
    steps = []
    for core in range(2):
        first, second = masks[1 - core], masks[core]
        held = [0, first, second, first ^ second]
        for mask in masks[2:]:
            held = held + [step ^ mask for step in held]
        steps.append(held)
    return steps


def moved(value, steps):
    owners = lax.axis_size("exp")
    return lax.ppermute(value, "exp", [(e, e ^ steps[e % 2]) for e in range(owners)])


def near_blocks(moe_grad):
    steps = block_steps(lax.axis_size("exp"))
    first = moved(moe_grad, [held[1] for held in steps])
    second = moved(moe_grad, [held[2] for held in steps])
    return first, second, moved(moe_grad, (1, 1))


def expert_tiles(weighted, moe_grad, near, anchor, per_dev):
    owners = lax.axis_size("exp")
    steps = block_steps(owners)
    first, second, beside = near
    first, _ = lax.optimization_barrier((first, anchor))
    far = moved(first, [held[2] for held in steps])
    second, _ = lax.optimization_barrier((second, anchor))
    held = [moe_grad, first, second]
    blocks = [moe_grad, beside] + [
        block for part in held[1:] for block in (part, moved(part, (1, 1)))
    ]
    far, _ = lax.optimization_barrier((far, weighted))
    held = held + [far]
    rest = [far]
    for turn in range(len(steps[0]).bit_length() - 3):
        mask = steps[0][4 << turn]
        more = [moved(part, (mask, mask)) for part in held]
        held, rest = held + more, rest + more
    rest = [block for part in rest for block in (part, moved(part, (1, 1)))]
    return tile_sums(weighted, blocks + rest, per_dev)


def local(
    queries,
    keys,
    values,
    attn_out,
    attn_out_grad,
    lse_excess,
    block_mask,
    expert_ids,
    route_probs,
    moe_grad,
    shadow_list,
    stored_hidden_state,
):
    near = near_blocks(moe_grad)
    query_grad, terms = attention(
        queries, keys, values, attn_out, attn_out_grad, lse_excess, block_mask
    )
    total = block_terms(terms)
    weighted, probs, total = experts(
        expert_ids, route_probs, moe_grad, shadow_list, stored_hidden_state, query_grad, total
    )
    key_grad, value_grad = summed_terms(total, keys.shape[1])
    per_dev = shadow_list.shape[0] // lax.axis_size("exp")
    expert_grad = expert_tiles(weighted, moe_grad, near, (query_grad, probs), per_dev)
    return (query_grad, key_grad, value_grad, expert_grad)


def solution(mesh):
    placed = (
        P("ctx", "exp"),
        P("ctx", None),
        P("ctx", None),
        P("ctx", "exp"),
        P("ctx", "exp"),
        P("exp", "ctx"),
        P(),
        P("exp", None),
        P("exp", None),
        P("exp", None),
        P(),
        P("exp", None, None, None, "ctx"),
    )
    return jax.shard_map(
        local,
        mesh=mesh,
        in_specs=placed,
        out_specs=(
            P("ctx", "exp"),
            P(("ctx", "exp"), None),
            P(("ctx", "exp"), None),
            P("exp", "ctx", None),
        ),
        check_vma=False,
    )
```

```python
import functools
import math

import jax
import jax.numpy as jnp
from jax import lax
from jax.experimental import pallas as pl
from jax.experimental.pallas import tpu as pltpu
from jax.sharding import PartitionSpec as P

LAST = (((1,), (1,)), ((), ()))
FIRST = (((0,), (0,)), ((), ()))


def full(shape):
    return pl.BlockSpec(shape, lambda *at: (0,) * len(shape))


def attention_kernel(
    place_ref, mask_ref, query_ref, grad_ref, out_ref, lse_ref, *rest
):
    cycle = mask_ref.shape[0]
    pair_refs, query_grad_ref, term_refs = rest[:cycle], rest[cycle], rest[cycle + 1 : -3]
    sums_ref, pairs_ref, terms_ref = rest[-3:]
    rows, width = pairs_ref.shape[1], pairs_ref.shape[2] // 2
    heads = lse_ref.shape[0]
    scale = 1.0 / math.sqrt(width)
    mine = place_ref[0]
    offset = 0.5 * math.log(rows) + lse_ref[...]
    spans = [slice(h * width, (h + 1) * width) for h in range(heads)]
    for step, pair_ref in enumerate(pair_refs):
        pairs_ref[step] = pair_ref[...]
    delta = []
    for span in spans:
        both = grad_ref[:, span].astype(jnp.float32) * out_ref[:, span].astype(jnp.float32)
        delta.append(jnp.sum(both.T, axis=0, keepdims=True))

    def block(step, diagonal):
        key, value = pairs_ref[step, :, :width], pairs_ref[step, :, width:]
        probs, slopes = [], []
        for h, span in enumerate(spans):
            query, grad = query_ref[:, span], grad_ref[:, span]
            scores = lax.dot_general(key, query, LAST, preferred_element_type=jnp.float32)
            prob = jnp.exp(scores * scale - offset[h : h + 1])
            if diagonal:
                at_key = lax.broadcasted_iota(jnp.int32, (rows, rows), 0)
                at_query = lax.broadcasted_iota(jnp.int32, (rows, rows), 1)
                prob = jnp.where(at_key <= at_query, prob, 0.0)
            prob_grad = lax.dot_general(value, grad, LAST, preferred_element_type=jnp.float32)
            slope = (prob * (prob_grad - delta[h]) * scale).astype(jnp.bfloat16)
            probs.append(prob.astype(jnp.bfloat16))
            slopes.append(slope)
            query_term = lax.dot_general(slope, key, FIRST, preferred_element_type=jnp.float32)
            if diagonal:
                sums_ref[:, span] = query_term
            else:
                sums_ref[:, span] += query_term
        queries = jnp.concatenate([query_ref[:, span] for span in spans], axis=0)
        grads = jnp.concatenate([grad_ref[:, span] for span in spans], axis=0)
        key_term = jnp.dot(
            jnp.concatenate(slopes, axis=1), queries, preferred_element_type=jnp.float32
        )
        value_term = jnp.dot(
            jnp.concatenate(probs, axis=1), grads, preferred_element_type=jnp.float32
        )
        terms_ref[step, :, :width] = key_term.astype(jnp.bfloat16)
        terms_ref[step, :, width:] = value_term.astype(jnp.bfloat16)

    block(0, True)

    @pl.loop(1, cycle)
    def _(step):
        source = mine - step
        seen = jnp.logical_and(source >= 0, mask_ref[mine, jnp.maximum(source, 0)] > 0)

        @pl.when(seen)
        def _():
            block(step, False)

        @pl.when(jnp.logical_not(seen))
        def _():
            terms_ref[step] = jnp.zeros_like(terms_ref[step])

    for step, term_ref in enumerate(term_refs):
        term_ref[...] = terms_ref[step]
    query_grad_ref[...] = sums_ref[...].astype(jnp.bfloat16)


def attention(queries, keys, values, attn_out, attn_out_grad, lse_excess, block_mask):
    rows = queries.shape[0]
    heads = lse_excess.shape[0]
    width = queries.shape[1] // heads
    cycle = lax.axis_size("ctx")
    mine = lax.axis_index("ctx")
    owners = lax.axis_size("exp")
    kv_count = keys.shape[1] // width
    kv_head = lax.axis_index("exp") * kv_count // owners
    pair = jnp.concatenate(
        [
            lax.dynamic_slice_in_dim(keys, kv_head * width, width, 1),
            lax.dynamic_slice_in_dim(values, kv_head * width, width, 1),
        ],
        axis=1,
    )
    arrived = [pair] + [
        lax.ppermute(pair, "ctx", [(c, c + step) for c in range(cycle - step)])
        for step in range(1, cycle)
    ]
    operands = (queries, attn_out_grad, attn_out, lse_excess, *arrived)
    query_grad, *terms = pl.pallas_call(
        attention_kernel,
        out_shape=[jax.ShapeDtypeStruct(queries.shape, jnp.bfloat16)]
        + [jax.ShapeDtypeStruct(pair.shape, jnp.bfloat16)] * cycle,
        grid_spec=pltpu.PrefetchScalarGridSpec(
            num_scalar_prefetch=2,
            grid=(1,),
            in_specs=[full(operand.shape) for operand in operands],
            out_specs=[full(queries.shape)] + [full(pair.shape)] * cycle,
            scratch_shapes=[
                pltpu.VMEM(queries.shape, jnp.float32),
                pltpu.VMEM((cycle,) + pair.shape, jnp.bfloat16),
                pltpu.VMEM((cycle,) + pair.shape, jnp.bfloat16),
            ],
        ),
        compiler_params=pltpu.CompilerParams(vmem_limit_bytes=32 * 2**20),
        name="attention",
    )(mine.astype(jnp.int32)[None], block_mask, *operands)
    return query_grad, terms, arrived


def sum_kernel(parts_ref, key_ref, value_ref):
    owners, rows, columns = parts_ref.shape
    kv_count = key_ref.shape[1] * 2 // columns
    group = owners // kv_count
    width = columns // 2
    for k in range(kv_count):
        total = jnp.zeros((rows, columns), jnp.float32)
        for e in range(k * group, (k + 1) * group):
            total += parts_ref[e].astype(jnp.float32)
        key_ref[:, k * width : (k + 1) * width] = total[:, :width].astype(jnp.bfloat16)
        value_ref[:, k * width : (k + 1) * width] = total[:, width:].astype(jnp.bfloat16)


def block_terms(terms):
    cycle = lax.axis_size("ctx")
    total = terms[0].astype(jnp.float32)
    for step in range(1, cycle):
        pairs = [(c, c - step) for c in range(step, cycle)]
        total = total + lax.ppermute(terms[step], "ctx", pairs).astype(jnp.float32)
    return total.astype(jnp.bfloat16)


def summed_terms(total, kv_columns, tiles):
    owners = lax.axis_size("exp")
    rows, columns = total.shape
    parts = lax.all_to_all(
        total.reshape(owners, rows // owners, columns),
        "exp",
        split_axis=0,
        concat_axis=0,
        tiled=True,
    )
    parts, tiles = lax.optimization_barrier((parts, tiles))
    shape = (rows // owners, kv_columns)
    out = jax.ShapeDtypeStruct(shape, jnp.bfloat16)
    key_grad, value_grad = pl.pallas_call(
        sum_kernel,
        out_shape=(out, out),
        grid=(1,),
        in_specs=[full(parts.shape)],
        out_specs=(full(shape), full(shape)),
        compiler_params=pltpu.CompilerParams(vmem_limit_bytes=16 * 2**20),
        name="sums",
    )(parts)
    return key_grad, value_grad, tiles


def pick_kernel(per_dev, shadow_ref, mixed_ref, sent_ref, sems):
    copies = []
    for owner in range(sent_ref.shape[0]):
        host = shadow_ref[owner * per_dev]
        for j in range(1, per_dev):
            host = jnp.maximum(host, shadow_ref[owner * per_dev + j])
        copies.append(
            pltpu.make_async_copy(
                mixed_ref.at[host, pl.ds(0, sent_ref.shape[1])], sent_ref.at[owner], sems.at[owner]
            )
        )
        copies[-1].start()
    for copy in copies:
        copy.wait()


def picked_rows(shadow_list, mixed, limit):
    owners = mixed.shape[0]
    anywhere = pl.BlockSpec(memory_space=pl.ANY)
    return pl.pallas_call(
        functools.partial(pick_kernel, shadow_list.shape[0] // owners),
        out_shape=jax.ShapeDtypeStruct((owners, limit, mixed.shape[2]), jnp.bfloat16),
        grid_spec=pltpu.PrefetchScalarGridSpec(
            num_scalar_prefetch=1,
            grid=(1,),
            in_specs=[anywhere],
            out_specs=anywhere,
            scratch_shapes=[pltpu.SemaphoreType.DMA((owners,))],
        ),
        name="picked",
    )(shadow_list, mixed)


def weight_kernel(orders, own_ref, shadow_ref, mixed_ref, hidden_ref, side_ref, weight_ref):
    owners = mixed_ref.shape[0]
    per_dev, units = hidden_ref.shape[1], hidden_ref.shape[4]
    tokens = weight_ref.shape[1] // owners
    limit = side_ref.shape[1]
    own = own_ref[0]
    earlier = (
        lax.broadcasted_iota(jnp.int32, (tokens, tokens), 0)
        < lax.broadcasted_iota(jnp.int32, (tokens, tokens), 1)
    ).astype(jnp.bfloat16)
    odd = lax.broadcasted_iota(jnp.int32, (1, tokens), 1) % 2 == 1

    def rows_at(named, rows):
        rank = jnp.dot(
            jnp.broadcast_to(named.astype(jnp.float32), (8, tokens)).astype(jnp.bfloat16),
            earlier,
            preferred_element_type=jnp.float32,
        )[:1]
        place = lax.broadcasted_iota(jnp.int32, (rows.shape[0], tokens), 0).astype(jnp.float32)
        chosen = jnp.where(jnp.logical_and(named, rank == place), 1.0, 0.0).astype(jnp.bfloat16)
        return lax.dot_general(rows, chosen, FIRST, preferred_element_type=jnp.float32)

    for i in range(owners):
        source = own ^ jnp.where(own % 2 == 0, orders[0][i], orders[1][i])
        for j in range(per_dev):
            prob = mixed_ref[source, limit + j : limit + j + 1, :tokens].astype(jnp.float32)
            named = prob > 0
            flag = shadow_ref[own * per_dev + j] >= 0
            side = jnp.logical_and(jnp.logical_and(named, odd), flag)
            here = jnp.logical_and(named, jnp.logical_not(side))
            rows = rows_at(here, hidden_ref[0, j, source]) + rows_at(
                side, side_ref[source, :, :units]
            )
            weight_ref[j * units : (j + 1) * units, i * tokens : (i + 1) * tokens] = (
                rows * prob
            ).astype(jnp.bfloat16)


def weighted_rows(own_index, shadow_list, mixed, hidden, shadow_rows, tokens, orders):
    owners = mixed.shape[0]
    per_dev, units = shadow_list.shape[0] // owners, hidden.shape[4]
    shape = (per_dev * units, owners * tokens)
    return pl.pallas_call(
        functools.partial(weight_kernel, orders),
        out_shape=jax.ShapeDtypeStruct(shape, jnp.bfloat16),
        grid_spec=pltpu.PrefetchScalarGridSpec(
            num_scalar_prefetch=2,
            grid=(1,),
            in_specs=[
                full(mixed.shape),
                full((1, per_dev) + hidden.shape[2:]),
                full(shadow_rows.shape),
            ],
            out_specs=full(shape),
        ),
        compiler_params=pltpu.CompilerParams(vmem_limit_bytes=32 * 2**20),
        name="weighted",
    )(own_index.astype(jnp.int32)[None], shadow_list, mixed, hidden, shadow_rows)


def tile_kernel(weight_ref, *refs):
    *block_refs, tile_ref, gathered_ref, held_ref, in_sems, out_sems = refs
    per_dev, units, model = tile_ref.shape
    tokens = block_refs[0].shape[0]
    steps = in_sems.shape[0]
    step = model // steps
    arriving, leaving = [], []
    for i in range(steps):
        columns = pl.ds(i * step, step)
        arriving.append(
            [
                pltpu.make_async_copy(
                    ref.at[:, columns],
                    gathered_ref.at[pl.ds(n * tokens, tokens), columns],
                    in_sems.at[i, n],
                )
                for n, ref in enumerate(block_refs)
            ]
        )
        for copy in arriving[-1]:
            copy.start()
    for i in range(steps):
        for copy in arriving[i]:
            copy.wait()
        columns = slice(i * step, (i + 1) * step)
        held_ref[:, columns] = jnp.dot(
            weight_ref[...], gathered_ref[:, columns], preferred_element_type=jnp.float32
        )
        for j in range(per_dev):
            leaving.append(
                pltpu.make_async_copy(
                    held_ref.at[pl.ds(j * units, units), pl.ds(i * step, step)],
                    tile_ref.at[j, :, pl.ds(i * step, step)],
                    out_sems.at[i, j],
                )
            )
            leaving[-1].start()
    for copy in leaving:
        copy.wait()


def tile_sums(weighted, blocks, per_dev):
    tokens, model = blocks[0].shape
    rows = weighted.shape[0]
    steps = model // 512
    anywhere = pl.BlockSpec(memory_space=pl.ANY)
    return pl.pallas_call(
        tile_kernel,
        out_shape=jax.ShapeDtypeStruct((per_dev, rows // per_dev, model), jnp.float32),
        in_specs=[pl.BlockSpec(memory_space=pltpu.VMEM)] + [anywhere] * len(blocks),
        out_specs=anywhere,
        scratch_shapes=[
            pltpu.VMEM((len(blocks) * tokens, model), jnp.bfloat16),
            pltpu.VMEM((rows, model), jnp.float32),
            pltpu.SemaphoreType.DMA((steps, len(blocks))),
            pltpu.SemaphoreType.DMA((steps, per_dev)),
        ],
        compiler_params=pltpu.CompilerParams(vmem_limit_bytes=32 * 2**20),
        name="tiles",
    )(weighted, *blocks)


def experts(expert_ids, route_probs, shadow_list, stored_hidden_state, first_anchor, near, later):
    owners = lax.axis_size("exp")
    own_index = lax.axis_index("exp")
    swap = functools.partial(
        lax.all_to_all, axis_name="exp", split_axis=0, concat_axis=0, tiled=True
    )
    tokens = expert_ids.shape[0]
    count = shadow_list.shape[0]
    per_dev = count // owners
    capacity, units = stored_hidden_state.shape[3:]
    hit = expert_ids[:, None, :] == jnp.arange(count, dtype=jnp.int32)[None, :, None]
    table = jnp.sum(
        jnp.where(hit, route_probs[:, None, :].astype(jnp.float32), 0.0), axis=2
    ).astype(jnp.bfloat16)
    table = table.T.reshape(owners, per_dev, tokens)
    used = min(capacity, tokens // 2)
    limit = -(-used // 16) * 16
    lanes = max(units, tokens)
    rows = jnp.pad(
        stored_hidden_state[0, per_dev, :, :used],
        ((0, 0), (0, limit - used), (0, lanes - units)),
    )
    mixed = jnp.concatenate([rows, jnp.pad(table, ((0, 0), (0, 0), (0, lanes - tokens)))], axis=1)
    mixed, _ = lax.optimization_barrier((mixed, first_anchor))
    mixed = swap(mixed)
    mixed, near = lax.optimization_barrier((mixed, near))
    shadow_rows = swap(picked_rows(shadow_list, mixed, limit))
    shadow_rows, later = lax.optimization_barrier((shadow_rows, later))
    steps = block_steps(owners)
    orders = [
        [step ^ turn for pair in zip(steps[core], steps[1 - core]) for step, turn in zip(pair, (0, 1))]
        for core in range(2)
    ]
    weighted = weighted_rows(
        own_index, shadow_list, mixed, stored_hidden_state, shadow_rows, tokens, orders
    )
    return weighted, near, later


def block_steps(owners):
    masks = [1 << bit for bit in range(1, owners.bit_length() - 1)]
    steps = []
    for core in range(2):
        first, second = masks[1 - core], masks[core]
        held = [0, first, second, first ^ second]
        for mask in masks[2:]:
            held = held + [step ^ mask for step in held]
        steps.append(held)
    return steps


def moved(value, steps):
    owners = lax.axis_size("exp")
    return lax.ppermute(value, "exp", [(e, e ^ steps[e % 2]) for e in range(owners)])


def near_blocks(moe_grad):
    steps = block_steps(lax.axis_size("exp"))
    first = moved(moe_grad, [held[1] for held in steps])
    second = moved(moe_grad, [held[2] for held in steps])
    return first, second, moved(moe_grad, (1, 1))


def expert_tiles(weighted, moe_grad, near, per_dev):
    owners = lax.axis_size("exp")
    steps = block_steps(owners)
    first, second, beside = near
    far = moved(first, [held[2] for held in steps])
    held = [moe_grad, first, second]
    blocks = [moe_grad, beside] + [
        block for part in held[1:] for block in (part, moved(part, (1, 1)))
    ]
    far, _ = lax.optimization_barrier((far, weighted))
    held = held + [far]
    rest = [far]
    for turn in range(len(steps[0]).bit_length() - 3):
        mask = steps[0][4 << turn]
        more = [moved(part, (mask, mask)) for part in held]
        held, rest = held + more, rest + more
    rest = [block for part in rest for block in (part, moved(part, (1, 1)))]
    return tile_sums(weighted, blocks + rest, per_dev)


def local(
    queries,
    keys,
    values,
    attn_out,
    attn_out_grad,
    lse_excess,
    block_mask,
    expert_ids,
    route_probs,
    moe_grad,
    shadow_list,
    stored_hidden_state,
):
    near = near_blocks(moe_grad)
    query_grad, terms, arrived = attention(
        queries, keys, values, attn_out, attn_out_grad, lse_excess, block_mask
    )
    total = block_terms(terms)
    first, second, beside = near
    weighted, (first, second, _), total = experts(
        expert_ids,
        route_probs,
        shadow_list,
        stored_hidden_state,
        arrived[1],
        (first, second, query_grad),
        total,
    )
    per_dev = shadow_list.shape[0] // lax.axis_size("exp")
    tiles = expert_tiles(weighted, moe_grad, (first, second, beside), per_dev)
    key_grad, value_grad, expert_grad = summed_terms(total, keys.shape[1], tiles)
    return (query_grad, key_grad, value_grad, expert_grad)


def solution(mesh):
    placed = (
        P("ctx", "exp"),
        P("ctx", None),
        P("ctx", None),
        P("ctx", "exp"),
        P("ctx", "exp"),
        P("exp", "ctx"),
        P(),
        P("exp", None),
        P("exp", None),
        P("exp", None),
        P(),
        P("exp", None, None, None, "ctx"),
    )
    return jax.shard_map(
        local,
        mesh=mesh,
        in_specs=placed,
        out_specs=(
            P("ctx", "exp"),
            P(("ctx", "exp"), None),
            P(("ctx", "exp"), None),
            P("exp", "ctx", None),
        ),
        check_vma=False,
    )
```

```python
import functools
import math

import jax
import jax.numpy as jnp
from jax import lax
from jax.experimental import pallas as pl
from jax.experimental.pallas import tpu as pltpu
from jax.sharding import PartitionSpec as P

LAST = (((1,), (1,)), ((), ()))
FIRST = (((0,), (0,)), ((), ()))


def full(shape):
    return pl.BlockSpec(shape, lambda *at: (0,) * len(shape))


def attention_kernel(
    place_ref, mask_ref, query_ref, grad_ref, out_ref, lse_ref, *rest
):
    cycle = mask_ref.shape[0]
    pair_refs, (query_grad_ref, terms_ref, sums_ref, pairs_ref) = rest[:cycle], rest[cycle:]
    rows, width = pairs_ref.shape[1], pairs_ref.shape[2] // 2
    heads = lse_ref.shape[0]
    scale = 1.0 / math.sqrt(width)
    mine = place_ref[0]
    offset = 0.5 * math.log(rows) + lse_ref[...]
    spans = [slice(h * width, (h + 1) * width) for h in range(heads)]
    for step, pair_ref in enumerate(pair_refs):
        pairs_ref[step] = pair_ref[...]
    delta = []
    for span in spans:
        both = grad_ref[:, span].astype(jnp.float32) * out_ref[:, span].astype(jnp.float32)
        delta.append(jnp.sum(both.T, axis=0, keepdims=True))

    def block(step, diagonal):
        key, value = pairs_ref[step, :, :width], pairs_ref[step, :, width:]
        probs, slopes = [], []
        for h, span in enumerate(spans):
            query, grad = query_ref[:, span], grad_ref[:, span]
            scores = lax.dot_general(key, query, LAST, preferred_element_type=jnp.float32)
            prob = jnp.exp(scores * scale - offset[h : h + 1])
            if diagonal:
                at_key = lax.broadcasted_iota(jnp.int32, (rows, rows), 0)
                at_query = lax.broadcasted_iota(jnp.int32, (rows, rows), 1)
                prob = jnp.where(at_key <= at_query, prob, 0.0)
            prob_grad = lax.dot_general(value, grad, LAST, preferred_element_type=jnp.float32)
            slope = (prob * (prob_grad - delta[h]) * scale).astype(jnp.bfloat16)
            probs.append(prob.astype(jnp.bfloat16))
            slopes.append(slope)
            query_term = lax.dot_general(slope, key, FIRST, preferred_element_type=jnp.float32)
            if diagonal:
                sums_ref[:, span] = query_term
            else:
                sums_ref[:, span] += query_term
        queries = jnp.concatenate([query_ref[:, span] for span in spans], axis=0)
        grads = jnp.concatenate([grad_ref[:, span] for span in spans], axis=0)
        key_term = jnp.dot(
            jnp.concatenate(slopes, axis=1), queries, preferred_element_type=jnp.float32
        )
        value_term = jnp.dot(
            jnp.concatenate(probs, axis=1), grads, preferred_element_type=jnp.float32
        )
        terms_ref[mine - step, :, :width] = key_term.astype(jnp.bfloat16)
        terms_ref[mine - step, :, width:] = value_term.astype(jnp.bfloat16)

    block(0, True)

    @pl.loop(0, cycle)
    def _(source):
        seen = jnp.logical_and(source < mine, mask_ref[mine, source] > 0)

        @pl.when(seen)
        def _():
            block(mine - source, False)

        @pl.when(jnp.logical_and(source != mine, jnp.logical_not(seen)))
        def _():
            terms_ref[source] = jnp.zeros_like(terms_ref[source])

    query_grad_ref[...] = sums_ref[...].astype(jnp.bfloat16)


def key_blocks(keys, values, width):
    cycle = lax.axis_size("ctx")
    owners = lax.axis_size("exp")
    kv_count = keys.shape[1] // width
    kv_head = lax.axis_index("exp") * kv_count // owners
    pair = jnp.concatenate(
        [
            lax.dynamic_slice_in_dim(keys, kv_head * width, width, 1),
            lax.dynamic_slice_in_dim(values, kv_head * width, width, 1),
        ],
        axis=1,
    )
    return [pair] + [
        lax.ppermute(pair, "ctx", [(c, c + step) for c in range(cycle - step)])
        for step in range(1, cycle)
    ]


def attention(queries, arrived, attn_out, attn_out_grad, lse_excess, block_mask):
    cycle = lax.axis_size("ctx")
    mine = lax.axis_index("ctx")
    pair = arrived[0]
    operands = (queries, attn_out_grad, attn_out, lse_excess, *arrived)
    return pl.pallas_call(
        attention_kernel,
        out_shape=(
            jax.ShapeDtypeStruct(queries.shape, jnp.bfloat16),
            jax.ShapeDtypeStruct((cycle,) + pair.shape, jnp.bfloat16),
        ),
        grid_spec=pltpu.PrefetchScalarGridSpec(
            num_scalar_prefetch=2,
            grid=(1,),
            in_specs=[full(operand.shape) for operand in operands],
            out_specs=(full(queries.shape), full((cycle,) + pair.shape)),
            scratch_shapes=[
                pltpu.VMEM(queries.shape, jnp.float32),
                pltpu.VMEM((cycle,) + pair.shape, jnp.bfloat16),
            ],
        ),
        compiler_params=pltpu.CompilerParams(vmem_limit_bytes=32 * 2**20),
        name="attention",
    )(mine.astype(jnp.int32)[None], block_mask, *operands)


def sum_kernel(parts_ref, key_ref, value_ref):
    cycle, owners, rows, columns = parts_ref.shape
    kv_count = key_ref.shape[1] * 2 // columns
    group = owners // kv_count
    width = columns // 2
    for k in range(kv_count):
        total = jnp.zeros((rows, columns), jnp.float32)
        for c in range(cycle):
            for e in range(k * group, (k + 1) * group):
                total += parts_ref[c, e].astype(jnp.float32)
        key_ref[:, k * width : (k + 1) * width] = total[:, :width].astype(jnp.bfloat16)
        value_ref[:, k * width : (k + 1) * width] = total[:, width:].astype(jnp.bfloat16)


def summed_terms(terms, kv_columns, tiles):
    cycle, owners = lax.axis_size("ctx"), lax.axis_size("exp")
    rows, columns = terms.shape[1:]
    parts = lax.all_to_all(
        terms.reshape(cycle * owners, rows // owners, columns),
        ("ctx", "exp"),
        split_axis=0,
        concat_axis=0,
        tiled=True,
    ).reshape(cycle, owners, rows // owners, columns)
    parts, tiles = lax.optimization_barrier((parts, tiles))
    shape = (rows // owners, kv_columns)
    out = jax.ShapeDtypeStruct(shape, jnp.bfloat16)
    key_grad, value_grad = pl.pallas_call(
        sum_kernel,
        out_shape=(out, out),
        grid=(1,),
        in_specs=[full(parts.shape)],
        out_specs=(full(shape), full(shape)),
        compiler_params=pltpu.CompilerParams(vmem_limit_bytes=16 * 2**20),
        name="sums",
    )(parts)
    return key_grad, value_grad, tiles


def pick_kernel(per_dev, shadow_ref, mixed_ref, sent_ref):
    for owner in range(sent_ref.shape[0]):
        host = shadow_ref[owner * per_dev]
        for j in range(1, per_dev):
            host = jnp.maximum(host, shadow_ref[owner * per_dev + j])
        sent_ref[owner] = mixed_ref[host, : sent_ref.shape[1]]


def picked_rows(shadow_list, mixed, limit):
    owners = mixed.shape[0]
    whole = pl.BlockSpec(memory_space=pltpu.VMEM)
    return pl.pallas_call(
        functools.partial(pick_kernel, shadow_list.shape[0] // owners),
        out_shape=jax.ShapeDtypeStruct((owners, limit, mixed.shape[2]), jnp.bfloat16),
        in_specs=[pl.BlockSpec(memory_space=pltpu.SMEM), whole],
        out_specs=whole,
        compiler_params=pltpu.CompilerParams(vmem_limit_bytes=4 * 2**20),
        name="picked",
    )(shadow_list, mixed)


def weight_kernel(orders, own_ref, shadow_ref, mixed_ref, hidden_ref, side_ref, weight_ref):
    owners = mixed_ref.shape[0]
    per_dev, units = hidden_ref.shape[1], hidden_ref.shape[4]
    tokens = weight_ref.shape[1] // owners
    limit = side_ref.shape[1]
    own = own_ref[0]
    earlier = (
        lax.broadcasted_iota(jnp.int32, (tokens, tokens), 0)
        < lax.broadcasted_iota(jnp.int32, (tokens, tokens), 1)
    ).astype(jnp.bfloat16)
    odd = lax.broadcasted_iota(jnp.int32, (1, tokens), 1) % 2 == 1

    def rows_at(named, rows):
        rank = jnp.dot(
            jnp.broadcast_to(named.astype(jnp.float32), (8, tokens)).astype(jnp.bfloat16),
            earlier,
            preferred_element_type=jnp.float32,
        )[:1]
        place = lax.broadcasted_iota(jnp.int32, (rows.shape[0], tokens), 0).astype(jnp.float32)
        chosen = jnp.where(jnp.logical_and(named, rank == place), 1.0, 0.0).astype(jnp.bfloat16)
        return lax.dot_general(rows, chosen, FIRST, preferred_element_type=jnp.float32)

    for i in range(owners):
        source = own ^ jnp.where(own % 2 == 0, orders[0][i], orders[1][i])
        for j in range(per_dev):
            prob = mixed_ref[source, limit + j : limit + j + 1, :tokens].astype(jnp.float32)
            named = prob > 0
            flag = shadow_ref[own * per_dev + j] >= 0
            side = jnp.logical_and(jnp.logical_and(named, odd), flag)
            here = jnp.logical_and(named, jnp.logical_not(side))
            rows = rows_at(here, hidden_ref[0, j, source]) + rows_at(
                side, side_ref[source, :, :units]
            )
            weight_ref[j * units : (j + 1) * units, i * tokens : (i + 1) * tokens] = (
                rows * prob
            ).astype(jnp.bfloat16)


def weighted_rows(own_index, shadow_list, mixed, hidden, shadow_rows, tokens, orders):
    owners = mixed.shape[0]
    per_dev, units = shadow_list.shape[0] // owners, hidden.shape[4]
    shape = (per_dev * units, owners * tokens)
    return pl.pallas_call(
        functools.partial(weight_kernel, orders),
        out_shape=jax.ShapeDtypeStruct(shape, jnp.bfloat16),
        grid_spec=pltpu.PrefetchScalarGridSpec(
            num_scalar_prefetch=2,
            grid=(1,),
            in_specs=[
                full(mixed.shape),
                full((1, per_dev) + hidden.shape[2:]),
                full(shadow_rows.shape),
            ],
            out_specs=full(shape),
        ),
        compiler_params=pltpu.CompilerParams(vmem_limit_bytes=32 * 2**20),
        name="weighted",
    )(own_index.astype(jnp.int32)[None], shadow_list, mixed, hidden, shadow_rows)


def tile_kernel(weight_ref, *refs):
    *block_refs, tile_ref, gathered_ref, held_ref, in_sems, out_sems = refs
    per_dev, units, model = tile_ref.shape
    tokens = block_refs[0].shape[0]
    steps = in_sems.shape[0]
    step = model // steps
    arriving, leaving = [], []
    for i in range(steps):
        columns = pl.ds(i * step, step)
        arriving.append(
            [
                pltpu.make_async_copy(
                    ref.at[:, columns],
                    gathered_ref.at[pl.ds(n * tokens, tokens), columns],
                    in_sems.at[i, n],
                )
                for n, ref in enumerate(block_refs)
            ]
        )
    for copy in arriving[0] + arriving[1]:
        copy.start()
    for i in range(steps):
        for copy in arriving[i]:
            copy.wait()
        for copy in arriving[i + 2] if i + 2 < steps else []:
            copy.start()
        columns = slice(i * step, (i + 1) * step)
        held_ref[:, columns] = jnp.dot(
            weight_ref[...], gathered_ref[:, columns], preferred_element_type=jnp.float32
        )
        for j in range(per_dev):
            leaving.append(
                pltpu.make_async_copy(
                    held_ref.at[pl.ds(j * units, units), pl.ds(i * step, step)],
                    tile_ref.at[j, :, pl.ds(i * step, step)],
                    out_sems.at[i, j],
                )
            )
            leaving[-1].start()
    for copy in leaving:
        copy.wait()


def tile_sums(weighted, blocks, per_dev):
    tokens, model = blocks[0].shape
    rows = weighted.shape[0]
    steps = model // 512
    anywhere = pl.BlockSpec(memory_space=pl.ANY)
    return pl.pallas_call(
        tile_kernel,
        out_shape=jax.ShapeDtypeStruct((per_dev, rows // per_dev, model), jnp.float32),
        in_specs=[pl.BlockSpec(memory_space=pltpu.VMEM)] + [anywhere] * len(blocks),
        out_specs=anywhere,
        scratch_shapes=[
            pltpu.VMEM((len(blocks) * tokens, model), jnp.bfloat16),
            pltpu.VMEM((rows, model), jnp.float32),
            pltpu.SemaphoreType.DMA((steps, len(blocks))),
            pltpu.SemaphoreType.DMA((steps, per_dev)),
        ],
        compiler_params=pltpu.CompilerParams(vmem_limit_bytes=32 * 2**20),
        name="tiles",
    )(weighted, *blocks)


def swapped(value):
    return lax.all_to_all(value, "exp", split_axis=0, concat_axis=0, tiled=True)


def source_rows(expert_ids, route_probs, shadow_list, stored_hidden_state):
    owners = lax.axis_size("exp")
    tokens = expert_ids.shape[0]
    count = shadow_list.shape[0]
    per_dev = count // owners
    capacity, units = stored_hidden_state.shape[3:]
    hit = expert_ids[:, None, :] == jnp.arange(count, dtype=jnp.int32)[None, :, None]
    table = jnp.sum(
        jnp.where(hit, route_probs[:, None, :].astype(jnp.float32), 0.0), axis=2
    ).astype(jnp.bfloat16)
    table = table.T.reshape(owners, per_dev, tokens)
    used = min(capacity, tokens // 2)
    limit = -(-used // 16) * 16
    lanes = max(units, tokens)
    rows = jnp.pad(
        stored_hidden_state[0, per_dev, :, :used],
        ((0, 0), (0, limit - used), (0, lanes - units)),
    )
    mixed = jnp.concatenate([rows, jnp.pad(table, ((0, 0), (0, 0), (0, lanes - tokens)))], axis=1)
    mixed = swapped(mixed)
    return mixed, picked_rows(shadow_list, mixed, limit)


def expert_rows(mixed, shadow_rows, shadow_list, stored_hidden_state, tokens):
    steps = block_steps(lax.axis_size("exp"))
    orders = [
        [step ^ turn for pair in zip(steps[core], steps[1 - core]) for step, turn in zip(pair, (0, 1))]
        for core in range(2)
    ]
    own_index = lax.axis_index("exp")
    return weighted_rows(
        own_index, shadow_list, mixed, stored_hidden_state, shadow_rows, tokens, orders
    )


def block_steps(owners):
    masks = [1 << bit for bit in range(1, owners.bit_length() - 1)]
    steps = []
    for core in range(2):
        first, second = masks[1 - core], masks[core]
        held = [0, first, second, first ^ second]
        for mask in masks[2:]:
            held = held + [step ^ mask for step in held]
        steps.append(held)
    return steps


def moved(value, steps):
    owners = lax.axis_size("exp")
    return lax.ppermute(value, "exp", [(e, e ^ steps[e % 2]) for e in range(owners)])


def near_blocks(moe_grad):
    steps = block_steps(lax.axis_size("exp"))
    first = moved(moe_grad, [held[1] for held in steps])
    second = moved(moe_grad, [held[2] for held in steps])
    return first, second, moved(moe_grad, (1, 1))


def expert_tiles(weighted, moe_grad, near, per_dev):
    owners = lax.axis_size("exp")
    steps = block_steps(owners)
    first, second, beside = near
    far = moved(first, [held[2] for held in steps])
    held = [moe_grad, first, second]
    blocks = [moe_grad, beside] + [
        block for part in held[1:] for block in (part, moved(part, (1, 1)))
    ]
    far, _ = lax.optimization_barrier((far, weighted))
    held = held + [far]
    rest = [far]
    for turn in range(len(steps[0]).bit_length() - 3):
        mask = steps[0][4 << turn]
        more = [moved(part, (mask, mask)) for part in held]
        held, rest = held + more, rest + more
    rest = [block for part in rest for block in (part, moved(part, (1, 1)))]
    return tile_sums(weighted, blocks + rest, per_dev)


def local(
    queries,
    keys,
    values,
    attn_out,
    attn_out_grad,
    lse_excess,
    block_mask,
    expert_ids,
    route_probs,
    moe_grad,
    shadow_list,
    stored_hidden_state,
):
    first, second, beside = near_blocks(moe_grad)
    arrived = key_blocks(keys, values, queries.shape[1] // lse_excess.shape[0])
    mixed, sent = source_rows(expert_ids, route_probs, shadow_list, stored_hidden_state)
    sent, first, second, arrived = lax.optimization_barrier((sent, first, second, arrived))
    shadow_rows = swapped(sent)
    query_grad, terms = attention(
        queries, arrived, attn_out, attn_out_grad, lse_excess, block_mask
    )
    shadow_rows, _ = lax.optimization_barrier((shadow_rows, query_grad))
    weighted = expert_rows(
        mixed, shadow_rows, shadow_list, stored_hidden_state, expert_ids.shape[0]
    )
    per_dev = shadow_list.shape[0] // lax.axis_size("exp")
    tiles = expert_tiles(weighted, moe_grad, (first, second, beside), per_dev)
    key_grad, value_grad, expert_grad = summed_terms(terms, keys.shape[1], tiles)
    return (query_grad, key_grad, value_grad, expert_grad)


def solution(mesh):
    placed = (
        P("ctx", "exp"),
        P("ctx", None),
        P("ctx", None),
        P("ctx", "exp"),
        P("ctx", "exp"),
        P("exp", "ctx"),
        P(),
        P("exp", None),
        P("exp", None),
        P("exp", None),
        P(),
        P("exp", None, None, None, "ctx"),
    )
    return jax.shard_map(
        local,
        mesh=mesh,
        in_specs=placed,
        out_specs=(
            P("ctx", "exp"),
            P(("ctx", "exp"), None),
            P(("ctx", "exp"), None),
            P("exp", "ctx", None),
        ),
        check_vma=False,
    )
```

```python
import functools
import math

import jax
import jax.numpy as jnp
from jax import lax
from jax.experimental import pallas as pl
from jax.experimental.pallas import tpu as pltpu
from jax.sharding import PartitionSpec as P

LAST = (((1,), (1,)), ((), ()))
FIRST = (((0,), (0,)), ((), ()))


def full(shape):
    return pl.BlockSpec(shape, lambda *at: (0,) * len(shape))


def attention_kernel(
    place_ref, mask_ref, query_ref, grad_ref, out_ref, lse_ref, *rest
):
    cycle = mask_ref.shape[0]
    pair_refs, (query_grad_ref, terms_ref, sums_ref, pairs_ref) = rest[:cycle], rest[cycle:]
    rows, width = pairs_ref.shape[1], pairs_ref.shape[2] // 2
    heads = lse_ref.shape[0]
    scale = 1.0 / math.sqrt(width)
    mine = place_ref[0]
    offset = 0.5 * math.log(rows) + lse_ref[...]
    spans = [slice(h * width, (h + 1) * width) for h in range(heads)]
    for step, pair_ref in enumerate(pair_refs):
        pairs_ref[step] = pair_ref[...]
    delta = []
    for span in spans:
        both = grad_ref[:, span].astype(jnp.float32) * out_ref[:, span].astype(jnp.float32)
        delta.append(jnp.sum(both.T, axis=0, keepdims=True))

    def block(step, diagonal):
        key, value = pairs_ref[step, :, :width], pairs_ref[step, :, width:]
        probs, slopes = [], []
        for h, span in enumerate(spans):
            query, grad = query_ref[:, span], grad_ref[:, span]
            scores = lax.dot_general(key, query, LAST, preferred_element_type=jnp.float32)
            prob = jnp.exp(scores * scale - offset[h : h + 1])
            if diagonal:
                at_key = lax.broadcasted_iota(jnp.int32, (rows, rows), 0)
                at_query = lax.broadcasted_iota(jnp.int32, (rows, rows), 1)
                prob = jnp.where(at_key <= at_query, prob, 0.0)
            prob_grad = lax.dot_general(value, grad, LAST, preferred_element_type=jnp.float32)
            slope = (prob * (prob_grad - delta[h]) * scale).astype(jnp.bfloat16)
            probs.append(prob.astype(jnp.bfloat16))
            slopes.append(slope)
            query_term = lax.dot_general(slope, key, FIRST, preferred_element_type=jnp.float32)
            if diagonal:
                sums_ref[:, span] = query_term
            else:
                sums_ref[:, span] += query_term
        queries = jnp.concatenate([query_ref[:, span] for span in spans], axis=0)
        grads = jnp.concatenate([grad_ref[:, span] for span in spans], axis=0)
        key_term = jnp.dot(
            jnp.concatenate(slopes, axis=1), queries, preferred_element_type=jnp.float32
        )
        value_term = jnp.dot(
            jnp.concatenate(probs, axis=1), grads, preferred_element_type=jnp.float32
        )
        terms_ref[mine - step, :, :width] = key_term.astype(jnp.bfloat16)
        terms_ref[mine - step, :, width:] = value_term.astype(jnp.bfloat16)

    block(0, True)

    @pl.loop(0, cycle)
    def _(source):
        seen = jnp.logical_and(source < mine, mask_ref[mine, source] > 0)

        @pl.when(seen)
        def _():
            block(mine - source, False)

        @pl.when(jnp.logical_and(source != mine, jnp.logical_not(seen)))
        def _():
            terms_ref[source] = jnp.zeros_like(terms_ref[source])

    query_grad_ref[...] = sums_ref[...].astype(jnp.bfloat16)


def key_blocks(keys, values, width):
    cycle = lax.axis_size("ctx")
    owners = lax.axis_size("exp")
    kv_count = keys.shape[1] // width
    kv_head = lax.axis_index("exp") * kv_count // owners
    pair = jnp.concatenate(
        [
            lax.dynamic_slice_in_dim(keys, kv_head * width, width, 1),
            lax.dynamic_slice_in_dim(values, kv_head * width, width, 1),
        ],
        axis=1,
    )
    return [pair] + [
        lax.ppermute(pair, "ctx", [(c, c + step) for c in range(cycle - step)])
        for step in range(1, cycle)
    ]


def attention(queries, arrived, attn_out, attn_out_grad, lse_excess, block_mask):
    cycle = lax.axis_size("ctx")
    mine = lax.axis_index("ctx")
    pair = arrived[0]
    operands = (queries, attn_out_grad, attn_out, lse_excess, *arrived)
    return pl.pallas_call(
        attention_kernel,
        out_shape=(
            jax.ShapeDtypeStruct(queries.shape, jnp.bfloat16),
            jax.ShapeDtypeStruct((cycle,) + pair.shape, jnp.bfloat16),
        ),
        grid_spec=pltpu.PrefetchScalarGridSpec(
            num_scalar_prefetch=2,
            grid=(1,),
            in_specs=[full(operand.shape) for operand in operands],
            out_specs=(full(queries.shape), full((cycle,) + pair.shape)),
            scratch_shapes=[
                pltpu.VMEM(queries.shape, jnp.float32),
                pltpu.VMEM((cycle,) + pair.shape, jnp.bfloat16),
            ],
        ),
        compiler_params=pltpu.CompilerParams(vmem_limit_bytes=32 * 2**20),
        name="attention",
    )(mine.astype(jnp.int32)[None], block_mask, *operands)


def sum_kernel(parts_ref, key_ref, value_ref):
    cycle, owners, rows, columns = parts_ref.shape
    kv_count = key_ref.shape[1] * 2 // columns
    group = owners // kv_count
    width = columns // 2
    for k in range(kv_count):
        total = jnp.zeros((rows, columns), jnp.float32)
        for c in range(cycle):
            for e in range(k * group, (k + 1) * group):
                total += parts_ref[c, e].astype(jnp.float32)
        key_ref[:, k * width : (k + 1) * width] = total[:, :width].astype(jnp.bfloat16)
        value_ref[:, k * width : (k + 1) * width] = total[:, width:].astype(jnp.bfloat16)


def summed_terms(terms, kv_columns, tiles):
    cycle, owners = lax.axis_size("ctx"), lax.axis_size("exp")
    rows, columns = terms.shape[1:]
    parts = lax.all_to_all(
        terms.reshape(cycle * owners, rows // owners, columns),
        ("ctx", "exp"),
        split_axis=0,
        concat_axis=0,
        tiled=True,
    ).reshape(cycle, owners, rows // owners, columns)
    parts, tiles = lax.optimization_barrier((parts, tiles))
    shape = (rows // owners, kv_columns)
    out = jax.ShapeDtypeStruct(shape, jnp.bfloat16)
    key_grad, value_grad = pl.pallas_call(
        sum_kernel,
        out_shape=(out, out),
        grid=(1,),
        in_specs=[full(parts.shape)],
        out_specs=(full(shape), full(shape)),
        compiler_params=pltpu.CompilerParams(vmem_limit_bytes=16 * 2**20),
        name="sums",
    )(parts)
    return key_grad, value_grad, tiles


def pick_kernel(per_dev, shadow_ref, mixed_ref, sent_ref):
    for owner in range(sent_ref.shape[0]):
        host = shadow_ref[owner * per_dev]
        for j in range(1, per_dev):
            host = jnp.maximum(host, shadow_ref[owner * per_dev + j])
        sent_ref[owner] = mixed_ref[host, : sent_ref.shape[1]]


def picked_rows(shadow_list, mixed, limit):
    owners = mixed.shape[0]
    whole = pl.BlockSpec(memory_space=pltpu.VMEM)
    return pl.pallas_call(
        functools.partial(pick_kernel, shadow_list.shape[0] // owners),
        out_shape=jax.ShapeDtypeStruct((owners, limit, mixed.shape[2]), jnp.bfloat16),
        in_specs=[pl.BlockSpec(memory_space=pltpu.SMEM), whole],
        out_specs=whole,
        compiler_params=pltpu.CompilerParams(vmem_limit_bytes=4 * 2**20),
        name="picked",
    )(shadow_list, mixed)


def weight_kernel(orders, own_ref, shadow_ref, mixed_ref, hidden_ref, side_ref, weight_ref):
    owners = mixed_ref.shape[0]
    per_dev, units = hidden_ref.shape[1], hidden_ref.shape[4]
    tokens = weight_ref.shape[1] // owners
    limit = side_ref.shape[1]
    own = own_ref[0]
    earlier = (
        lax.broadcasted_iota(jnp.int32, (tokens, tokens), 0)
        < lax.broadcasted_iota(jnp.int32, (tokens, tokens), 1)
    ).astype(jnp.bfloat16)
    odd = lax.broadcasted_iota(jnp.int32, (1, tokens), 1) % 2 == 1

    def rows_at(named, rows):
        rank = jnp.dot(
            jnp.broadcast_to(named.astype(jnp.float32), (8, tokens)).astype(jnp.bfloat16),
            earlier,
            preferred_element_type=jnp.float32,
        )[:1]
        place = lax.broadcasted_iota(jnp.int32, (rows.shape[0], tokens), 0).astype(jnp.float32)
        chosen = jnp.where(jnp.logical_and(named, rank == place), 1.0, 0.0).astype(jnp.bfloat16)
        return lax.dot_general(rows, chosen, FIRST, preferred_element_type=jnp.float32)

    for i in range(owners):
        source = own ^ jnp.where(own % 2 == 0, orders[0][i], orders[1][i])
        for j in range(per_dev):
            prob = mixed_ref[source, limit + j : limit + j + 1, :tokens].astype(jnp.float32)
            named = prob > 0
            flag = shadow_ref[own * per_dev + j] >= 0
            side = jnp.logical_and(jnp.logical_and(named, odd), flag)
            here = jnp.logical_and(named, jnp.logical_not(side))
            rows = rows_at(here, hidden_ref[0, j, source]) + rows_at(
                side, side_ref[source, :, :units]
            )
            weight_ref[j * units : (j + 1) * units, i * tokens : (i + 1) * tokens] = (
                rows * prob
            ).astype(jnp.bfloat16)


def weighted_rows(own_index, shadow_list, mixed, hidden, shadow_rows, tokens, orders):
    owners = mixed.shape[0]
    per_dev, units = shadow_list.shape[0] // owners, hidden.shape[4]
    shape = (per_dev * units, owners * tokens)
    return pl.pallas_call(
        functools.partial(weight_kernel, orders),
        out_shape=jax.ShapeDtypeStruct(shape, jnp.bfloat16),
        grid_spec=pltpu.PrefetchScalarGridSpec(
            num_scalar_prefetch=2,
            grid=(1,),
            in_specs=[
                full(mixed.shape),
                full((1, per_dev) + hidden.shape[2:]),
                full(shadow_rows.shape),
            ],
            out_specs=full(shape),
        ),
        compiler_params=pltpu.CompilerParams(vmem_limit_bytes=32 * 2**20),
        name="weighted",
    )(own_index.astype(jnp.int32)[None], shadow_list, mixed, hidden, shadow_rows)


def tile_kernel(weight_ref, *refs):
    *block_refs, tile_ref, gathered_ref, held_ref, in_sems, out_sems = refs
    per_dev, units, model = tile_ref.shape
    tokens = block_refs[0].shape[0]
    steps = in_sems.shape[0]
    step = model // steps
    arriving, leaving = [], []
    for i in range(steps):
        columns = pl.ds(i * step, step)
        arriving.append(
            [
                pltpu.make_async_copy(
                    ref.at[:, columns],
                    gathered_ref.at[pl.ds(n * tokens, tokens), columns],
                    in_sems.at[i, n],
                )
                for n, ref in enumerate(block_refs)
            ]
        )
    for copy in arriving[0] + arriving[1]:
        copy.start()
    for i in range(steps):
        for copy in arriving[i]:
            copy.wait()
        for copy in arriving[i + 2] if i + 2 < steps else []:
            copy.start()
        columns = slice(i * step, (i + 1) * step)
        held_ref[:, columns] = jnp.dot(
            weight_ref[...], gathered_ref[:, columns], preferred_element_type=jnp.float32
        )
        for j in range(per_dev):
            leaving.append(
                pltpu.make_async_copy(
                    held_ref.at[pl.ds(j * units, units), pl.ds(i * step, step)],
                    tile_ref.at[j, :, pl.ds(i * step, step)],
                    out_sems.at[i, j],
                )
            )
            leaving[-1].start()
    for copy in leaving:
        copy.wait()


def tile_sums(weighted, blocks, per_dev):
    tokens, model = blocks[0].shape
    rows = weighted.shape[0]
    steps = model // 1024
    anywhere = pl.BlockSpec(memory_space=pl.ANY)
    return pl.pallas_call(
        tile_kernel,
        out_shape=jax.ShapeDtypeStruct((per_dev, rows // per_dev, model), jnp.float32),
        in_specs=[pl.BlockSpec(memory_space=pltpu.VMEM)] + [anywhere] * len(blocks),
        out_specs=anywhere,
        scratch_shapes=[
            pltpu.VMEM((len(blocks) * tokens, model), jnp.bfloat16),
            pltpu.VMEM((rows, model), jnp.float32),
            pltpu.SemaphoreType.DMA((steps, len(blocks))),
            pltpu.SemaphoreType.DMA((steps, per_dev)),
        ],
        compiler_params=pltpu.CompilerParams(vmem_limit_bytes=32 * 2**20),
        name="tiles",
    )(weighted, *blocks)


def swapped(value):
    return lax.all_to_all(value, "exp", split_axis=0, concat_axis=0, tiled=True)


def source_rows(expert_ids, route_probs, shadow_list, stored_hidden_state):
    owners = lax.axis_size("exp")
    tokens = expert_ids.shape[0]
    count = shadow_list.shape[0]
    per_dev = count // owners
    capacity, units = stored_hidden_state.shape[3:]
    hit = expert_ids[:, None, :] == jnp.arange(count, dtype=jnp.int32)[None, :, None]
    table = jnp.sum(
        jnp.where(hit, route_probs[:, None, :].astype(jnp.float32), 0.0), axis=2
    ).astype(jnp.bfloat16)
    table = table.T.reshape(owners, per_dev, tokens)
    used = min(capacity, tokens // 2)
    limit = -(-used // 16) * 16
    lanes = max(units, tokens)
    rows = jnp.pad(
        stored_hidden_state[0, per_dev, :, :used],
        ((0, 0), (0, limit - used), (0, lanes - units)),
    )
    mixed = jnp.concatenate([rows, jnp.pad(table, ((0, 0), (0, 0), (0, lanes - tokens)))], axis=1)
    mixed = swapped(mixed)
    return mixed, picked_rows(shadow_list, mixed, limit)


def expert_rows(mixed, shadow_rows, shadow_list, stored_hidden_state, tokens):
    steps = block_steps(lax.axis_size("exp"))
    orders = [
        [step ^ turn for pair in zip(steps[core], steps[1 - core]) for step, turn in zip(pair, (0, 1))]
        for core in range(2)
    ]
    own_index = lax.axis_index("exp")
    return weighted_rows(
        own_index, shadow_list, mixed, stored_hidden_state, shadow_rows, tokens, orders
    )


def block_steps(owners):
    masks = [1 << bit for bit in range(1, owners.bit_length() - 1)]
    steps = []
    for core in range(2):
        first, second = masks[1 - core], masks[core]
        held = [0, first, second, first ^ second]
        for mask in masks[2:]:
            held = held + [step ^ mask for step in held]
        steps.append(held)
    return steps


def moved(value, steps):
    owners = lax.axis_size("exp")
    return lax.ppermute(value, "exp", [(e, e ^ steps[e % 2]) for e in range(owners)])


def expert_tiles(weighted, near, per_dev):
    owners = lax.axis_size("exp")
    steps = block_steps(owners)
    far = moved(near[1], [held[2] for held in steps])
    held = list(near)
    blocks = [block for part in held for block in (part, moved(part, (1, 1)))]
    far, _ = lax.optimization_barrier((far, weighted))
    held = held + [far]
    rest = [far]
    for turn in range(len(steps[0]).bit_length() - 3):
        mask = steps[0][4 << turn]
        more = [moved(part, (mask, mask)) for part in held]
        held, rest = held + more, rest + more
    rest = [block for part in rest for block in (part, moved(part, (1, 1)))]
    return tile_sums(weighted, blocks + rest, per_dev)


def local(
    queries,
    keys,
    values,
    attn_out,
    attn_out_grad,
    lse_excess,
    block_mask,
    expert_ids,
    route_probs,
    moe_grad,
    shadow_list,
    stored_hidden_state,
):
    steps = block_steps(lax.axis_size("exp"))
    first = moved(moe_grad, [held[1] for held in steps])
    arrived = key_blocks(keys, values, queries.shape[1] // lse_excess.shape[0])
    mixed, sent = source_rows(expert_ids, route_probs, shadow_list, stored_hidden_state)
    moe_grad, _ = lax.optimization_barrier((moe_grad, mixed))
    second = moved(moe_grad, [held[2] for held in steps])
    sent, arrived = lax.optimization_barrier((sent, arrived))
    shadow_rows = swapped(sent)
    query_grad, terms = attention(
        queries, arrived, attn_out, attn_out_grad, lse_excess, block_mask
    )
    first, _ = lax.optimization_barrier((first, query_grad))
    shadow_rows, _ = lax.optimization_barrier((shadow_rows, query_grad))
    weighted = expert_rows(
        mixed, shadow_rows, shadow_list, stored_hidden_state, expert_ids.shape[0]
    )
    per_dev = shadow_list.shape[0] // lax.axis_size("exp")
    tiles = expert_tiles(weighted, (moe_grad, first, second), per_dev)
    key_grad, value_grad, expert_grad = summed_terms(terms, keys.shape[1], tiles)
    return (query_grad, key_grad, value_grad, expert_grad)


def solution(mesh):
    placed = (
        P("ctx", "exp"),
        P("ctx", None),
        P("ctx", None),
        P("ctx", "exp"),
        P("ctx", "exp"),
        P("exp", "ctx"),
        P(),
        P("exp", None),
        P("exp", None),
        P("exp", None),
        P(),
        P("exp", None, None, None, "ctx"),
    )
    return jax.shard_map(
        local,
        mesh=mesh,
        in_specs=placed,
        out_specs=(
            P("ctx", "exp"),
            P(("ctx", "exp"), None),
            P(("ctx", "exp"), None),
            P("exp", "ctx", None),
        ),
        check_vma=False,
    )
```

```python
import functools
import math

import jax
import jax.numpy as jnp
from jax import lax
from jax.experimental import pallas as pl
from jax.experimental.pallas import tpu as pltpu
from jax.sharding import PartitionSpec as P

LAST = (((1,), (1,)), ((), ()))
FIRST = (((0,), (0,)), ((), ()))


def full(shape):
    return pl.BlockSpec(shape, lambda *at: (0,) * len(shape))


def attention_kernel(
    place_ref, mask_ref, query_ref, grad_ref, out_ref, lse_ref, *rest
):
    cycle = mask_ref.shape[0]
    pair_refs, (query_grad_ref, terms_ref, sums_ref, pairs_ref) = rest[:cycle], rest[cycle:]
    rows, width = pairs_ref.shape[1], pairs_ref.shape[2] // 2
    heads = lse_ref.shape[0]
    scale = 1.0 / math.sqrt(width)
    mine = place_ref[0]
    offset = 0.5 * math.log(rows) + lse_ref[...]
    spans = [slice(h * width, (h + 1) * width) for h in range(heads)]
    for step, pair_ref in enumerate(pair_refs):
        pairs_ref[step] = pair_ref[...]
    delta = []
    for span in spans:
        both = grad_ref[:, span].astype(jnp.float32) * out_ref[:, span].astype(jnp.float32)
        delta.append(jnp.sum(both.T, axis=0, keepdims=True))

    def block(step, diagonal):
        key, value = pairs_ref[step, :, :width], pairs_ref[step, :, width:]
        probs, slopes = [], []
        for h, span in enumerate(spans):
            query, grad = query_ref[:, span], grad_ref[:, span]
            scores = lax.dot_general(key, query, LAST, preferred_element_type=jnp.float32)
            prob = jnp.exp(scores * scale - offset[h : h + 1])
            if diagonal:
                at_key = lax.broadcasted_iota(jnp.int32, (rows, rows), 0)
                at_query = lax.broadcasted_iota(jnp.int32, (rows, rows), 1)
                prob = jnp.where(at_key <= at_query, prob, 0.0)
            prob_grad = lax.dot_general(value, grad, LAST, preferred_element_type=jnp.float32)
            slope = (prob * (prob_grad - delta[h]) * scale).astype(jnp.bfloat16)
            probs.append(prob.astype(jnp.bfloat16))
            slopes.append(slope)
            query_term = lax.dot_general(slope, key, FIRST, preferred_element_type=jnp.float32)
            if diagonal:
                sums_ref[:, span] = query_term
            else:
                sums_ref[:, span] += query_term
        queries = jnp.concatenate([query_ref[:, span] for span in spans], axis=0)
        grads = jnp.concatenate([grad_ref[:, span] for span in spans], axis=0)
        key_term = jnp.dot(
            jnp.concatenate(slopes, axis=1), queries, preferred_element_type=jnp.float32
        )
        value_term = jnp.dot(
            jnp.concatenate(probs, axis=1), grads, preferred_element_type=jnp.float32
        )
        terms_ref[mine - step, :, :width] = key_term.astype(jnp.bfloat16)
        terms_ref[mine - step, :, width:] = value_term.astype(jnp.bfloat16)

    block(0, True)

    @pl.loop(0, cycle)
    def _(source):
        seen = jnp.logical_and(source < mine, mask_ref[mine, source] > 0)

        @pl.when(seen)
        def _():
            block(mine - source, False)

        @pl.when(jnp.logical_and(source != mine, jnp.logical_not(seen)))
        def _():
            terms_ref[source] = jnp.zeros_like(terms_ref[source])

    query_grad_ref[...] = sums_ref[...].astype(jnp.bfloat16)


def key_blocks(keys, values, width):
    cycle = lax.axis_size("ctx")
    owners = lax.axis_size("exp")
    kv_count = keys.shape[1] // width
    kv_head = lax.axis_index("exp") * kv_count // owners
    pair = jnp.concatenate(
        [
            lax.dynamic_slice_in_dim(keys, kv_head * width, width, 1),
            lax.dynamic_slice_in_dim(values, kv_head * width, width, 1),
        ],
        axis=1,
    )
    return [pair] + [
        lax.ppermute(pair, "ctx", [(c, c + step) for c in range(cycle - step)])
        for step in range(1, cycle)
    ]


def attention(queries, arrived, attn_out, attn_out_grad, lse_excess, block_mask):
    cycle = lax.axis_size("ctx")
    mine = lax.axis_index("ctx")
    pair = arrived[0]
    operands = (queries, attn_out_grad, attn_out, lse_excess, *arrived)
    return pl.pallas_call(
        attention_kernel,
        out_shape=(
            jax.ShapeDtypeStruct(queries.shape, jnp.bfloat16),
            jax.ShapeDtypeStruct((cycle,) + pair.shape, jnp.bfloat16),
        ),
        grid_spec=pltpu.PrefetchScalarGridSpec(
            num_scalar_prefetch=2,
            grid=(1,),
            in_specs=[full(operand.shape) for operand in operands],
            out_specs=(full(queries.shape), full((cycle,) + pair.shape)),
            scratch_shapes=[
                pltpu.VMEM(queries.shape, jnp.float32),
                pltpu.VMEM((cycle,) + pair.shape, jnp.bfloat16),
            ],
        ),
        compiler_params=pltpu.CompilerParams(vmem_limit_bytes=32 * 2**20),
        name="attention",
    )(mine.astype(jnp.int32)[None], block_mask, *operands)


def sum_kernel(parts_ref, key_ref, value_ref):
    cycle, owners, rows, columns = parts_ref.shape
    kv_count = key_ref.shape[1] * 2 // columns
    group = owners // kv_count
    width = columns // 2
    for k in range(kv_count):
        total = jnp.zeros((rows, columns), jnp.float32)
        for c in range(cycle):
            for e in range(k * group, (k + 1) * group):
                total += parts_ref[c, e].astype(jnp.float32)
        key_ref[:, k * width : (k + 1) * width] = total[:, :width].astype(jnp.bfloat16)
        value_ref[:, k * width : (k + 1) * width] = total[:, width:].astype(jnp.bfloat16)


def summed_terms(terms, kv_columns, tiles):
    cycle, owners = lax.axis_size("ctx"), lax.axis_size("exp")
    rows, columns = terms.shape[1:]
    parts = lax.all_to_all(
        terms.reshape(cycle * owners, rows // owners, columns),
        ("ctx", "exp"),
        split_axis=0,
        concat_axis=0,
        tiled=True,
    ).reshape(cycle, owners, rows // owners, columns)
    parts, tiles = lax.optimization_barrier((parts, tiles))
    shape = (rows // owners, kv_columns)
    out = jax.ShapeDtypeStruct(shape, jnp.bfloat16)
    key_grad, value_grad = pl.pallas_call(
        sum_kernel,
        out_shape=(out, out),
        grid=(1,),
        in_specs=[full(parts.shape)],
        out_specs=(full(shape), full(shape)),
        compiler_params=pltpu.CompilerParams(vmem_limit_bytes=16 * 2**20),
        name="sums",
    )(parts)
    return key_grad, value_grad, tiles


def pick_kernel(per_dev, shadow_ref, mixed_ref, sent_ref):
    for owner in range(sent_ref.shape[0]):
        host = shadow_ref[owner * per_dev]
        for j in range(1, per_dev):
            host = jnp.maximum(host, shadow_ref[owner * per_dev + j])
        sent_ref[owner] = mixed_ref[host, : sent_ref.shape[1]]


def picked_rows(shadow_list, mixed, limit):
    owners = mixed.shape[0]
    whole = pl.BlockSpec(memory_space=pltpu.VMEM)
    return pl.pallas_call(
        functools.partial(pick_kernel, shadow_list.shape[0] // owners),
        out_shape=jax.ShapeDtypeStruct((owners, limit, mixed.shape[2]), jnp.bfloat16),
        in_specs=[pl.BlockSpec(memory_space=pltpu.SMEM), whole],
        out_specs=whole,
        compiler_params=pltpu.CompilerParams(vmem_limit_bytes=4 * 2**20),
        name="picked",
    )(shadow_list, mixed)


def weight_kernel(orders, own_ref, shadow_ref, mixed_ref, hidden_ref, side_ref, weight_ref):
    owners = mixed_ref.shape[0]
    per_dev, units = hidden_ref.shape[1], hidden_ref.shape[4]
    tokens = weight_ref.shape[1] // owners
    limit = side_ref.shape[1]
    own = own_ref[0]
    earlier = (
        lax.broadcasted_iota(jnp.int32, (tokens, tokens), 0)
        < lax.broadcasted_iota(jnp.int32, (tokens, tokens), 1)
    ).astype(jnp.bfloat16)
    odd = lax.broadcasted_iota(jnp.int32, (1, tokens), 1) % 2 == 1

    def rows_at(named, rows):
        rank = jnp.dot(
            jnp.broadcast_to(named.astype(jnp.float32), (8, tokens)).astype(jnp.bfloat16),
            earlier,
            preferred_element_type=jnp.float32,
        )[:1]
        place = lax.broadcasted_iota(jnp.int32, (rows.shape[0], tokens), 0).astype(jnp.float32)
        chosen = jnp.where(jnp.logical_and(named, rank == place), 1.0, 0.0).astype(jnp.bfloat16)
        return lax.dot_general(rows, chosen, FIRST, preferred_element_type=jnp.float32)

    for i in range(owners):
        source = own ^ jnp.where(own % 2 == 0, orders[0][i], orders[1][i])
        for j in range(per_dev):
            prob = mixed_ref[source, limit + j : limit + j + 1, :tokens].astype(jnp.float32)
            named = prob > 0
            flag = shadow_ref[own * per_dev + j] >= 0
            side = jnp.logical_and(jnp.logical_and(named, odd), flag)
            here = jnp.logical_and(named, jnp.logical_not(side))
            rows = rows_at(here, hidden_ref[0, j, source]) + rows_at(
                side, side_ref[source, :, :units]
            )
            weight_ref[j * units : (j + 1) * units, i * tokens : (i + 1) * tokens] = (
                rows * prob
            ).astype(jnp.bfloat16)


def weighted_rows(own_index, shadow_list, mixed, hidden, shadow_rows, tokens, orders):
    owners = mixed.shape[0]
    per_dev, units = shadow_list.shape[0] // owners, hidden.shape[4]
    shape = (per_dev * units, owners * tokens)
    return pl.pallas_call(
        functools.partial(weight_kernel, orders),
        out_shape=jax.ShapeDtypeStruct(shape, jnp.bfloat16),
        grid_spec=pltpu.PrefetchScalarGridSpec(
            num_scalar_prefetch=2,
            grid=(1,),
            in_specs=[
                full(mixed.shape),
                full((1, per_dev) + hidden.shape[2:]),
                full(shadow_rows.shape),
            ],
            out_specs=full(shape),
        ),
        compiler_params=pltpu.CompilerParams(vmem_limit_bytes=32 * 2**20),
        name="weighted",
    )(own_index.astype(jnp.int32)[None], shadow_list, mixed, hidden, shadow_rows)


def tile_kernel(weight_ref, *refs):
    *block_refs, tile_ref, gathered_ref, held_ref, in_sems, out_sems = refs
    per_dev, units, model = tile_ref.shape
    tokens = block_refs[0].shape[0]
    steps = in_sems.shape[0]
    step = model // steps
    arriving, leaving = [], []
    for i in range(steps):
        columns = pl.ds(i * step, step)
        arriving.append(
            [
                pltpu.make_async_copy(
                    ref.at[:, columns],
                    gathered_ref.at[pl.ds(n * tokens, tokens), columns],
                    in_sems.at[i, n],
                )
                for n, ref in enumerate(block_refs)
            ]
        )
    for copy in arriving[0] + arriving[1]:
        copy.start()
    for i in range(steps):
        for copy in arriving[i]:
            copy.wait()
        for copy in arriving[i + 2] if i + 2 < steps else []:
            copy.start()
        columns = slice(i * step, (i + 1) * step)
        held_ref[:, columns] = jnp.dot(
            weight_ref[...], gathered_ref[:, columns], preferred_element_type=jnp.float32
        )
        for j in range(per_dev):
            leaving.append(
                pltpu.make_async_copy(
                    held_ref.at[pl.ds(j * units, units), pl.ds(i * step, step)],
                    tile_ref.at[j, :, pl.ds(i * step, step)],
                    out_sems.at[i, j],
                )
            )
            leaving[-1].start()
    for copy in leaving:
        copy.wait()


def tile_sums(weighted, blocks, per_dev):
    tokens, model = blocks[0].shape
    rows = weighted.shape[0]
    steps = model // 1024
    anywhere = pl.BlockSpec(memory_space=pl.ANY)
    return pl.pallas_call(
        tile_kernel,
        out_shape=jax.ShapeDtypeStruct((per_dev, rows // per_dev, model), jnp.float32),
        in_specs=[pl.BlockSpec(memory_space=pltpu.VMEM)] + [anywhere] * len(blocks),
        out_specs=anywhere,
        scratch_shapes=[
            pltpu.VMEM((len(blocks) * tokens, model), jnp.bfloat16),
            pltpu.VMEM((rows, model), jnp.float32),
            pltpu.SemaphoreType.DMA((steps, len(blocks))),
            pltpu.SemaphoreType.DMA((steps, per_dev)),
        ],
        compiler_params=pltpu.CompilerParams(vmem_limit_bytes=32 * 2**20),
        name="tiles",
    )(weighted, *blocks)


def swapped(value):
    return lax.all_to_all(value, "exp", split_axis=0, concat_axis=0, tiled=True)


def source_rows(expert_ids, route_probs, shadow_list, stored_hidden_state):
    owners = lax.axis_size("exp")
    tokens = expert_ids.shape[0]
    count = shadow_list.shape[0]
    per_dev = count // owners
    capacity, units = stored_hidden_state.shape[3:]
    hit = expert_ids[:, None, :] == jnp.arange(count, dtype=jnp.int32)[None, :, None]
    table = jnp.sum(
        jnp.where(hit, route_probs[:, None, :].astype(jnp.float32), 0.0), axis=2
    ).astype(jnp.bfloat16)
    table = table.T.reshape(owners, per_dev, tokens)
    used = min(capacity, tokens // 2)
    limit = -(-used // 16) * 16
    lanes = max(units, tokens)
    rows = jnp.pad(
        stored_hidden_state[0, per_dev, :, :used],
        ((0, 0), (0, limit - used), (0, lanes - units)),
    )
    mixed = jnp.concatenate([rows, jnp.pad(table, ((0, 0), (0, 0), (0, lanes - tokens)))], axis=1)
    mixed = swapped(mixed)
    return mixed, picked_rows(shadow_list, mixed, limit)


def expert_rows(mixed, shadow_rows, shadow_list, stored_hidden_state, tokens):
    steps = block_steps(lax.axis_size("exp"))
    orders = [
        [step ^ turn for pair in zip(steps[core], steps[1 - core]) for step, turn in zip(pair, (0, 1))]
        for core in range(2)
    ]
    own_index = lax.axis_index("exp")
    return weighted_rows(
        own_index, shadow_list, mixed, stored_hidden_state, shadow_rows, tokens, orders
    )


def block_steps(owners):
    masks = [1 << bit for bit in range(1, owners.bit_length() - 1)]
    steps = []
    for core in range(2):
        first, second = masks[1 - core], masks[core]
        held = [0, first, second, first ^ second]
        for mask in masks[2:]:
            held = held + [step ^ mask for step in held]
        steps.append(held)
    return steps


def moved(value, steps):
    owners = lax.axis_size("exp")
    return lax.ppermute(value, "exp", [(e, e ^ steps[e % 2]) for e in range(owners)])


def expert_tiles(weighted, near, per_dev):
    owners = lax.axis_size("exp")
    steps = block_steps(owners)
    far = moved(near[1], [held[2] for held in steps])
    held = list(near)
    blocks = [block for part in held for block in (part, moved(part, (1, 1)))]
    far, _ = lax.optimization_barrier((far, weighted))
    held = held + [far]
    rest = [far]
    for turn in range(len(steps[0]).bit_length() - 3):
        mask = steps[0][4 << turn]
        more = [moved(part, (mask, mask)) for part in held]
        held, rest = held + more, rest + more
    rest = [block for part in rest for block in (part, moved(part, (1, 1)))]
    return tile_sums(weighted, blocks + rest, per_dev)


def local(
    queries,
    keys,
    values,
    attn_out,
    attn_out_grad,
    lse_excess,
    block_mask,
    expert_ids,
    route_probs,
    moe_grad,
    shadow_list,
    stored_hidden_state,
):
    steps = block_steps(lax.axis_size("exp"))
    first = moved(moe_grad, [held[1] for held in steps])
    arrived = key_blocks(keys, values, queries.shape[1] // lse_excess.shape[0])
    mixed, sent = source_rows(expert_ids, route_probs, shadow_list, stored_hidden_state)
    moe_grad, first = lax.optimization_barrier((moe_grad, first))
    second = moved(moe_grad, [held[2] for held in steps])
    sent, arrived = lax.optimization_barrier((sent, arrived))
    shadow_rows = swapped(sent)
    query_grad, terms = attention(
        queries, arrived, attn_out, attn_out_grad, lse_excess, block_mask
    )
    first, shadow_rows, query_grad = lax.optimization_barrier((first, shadow_rows, query_grad))
    weighted = expert_rows(
        mixed, shadow_rows, shadow_list, stored_hidden_state, expert_ids.shape[0]
    )
    per_dev = shadow_list.shape[0] // lax.axis_size("exp")
    tiles = expert_tiles(weighted, (moe_grad, first, second), per_dev)
    key_grad, value_grad, expert_grad = summed_terms(terms, keys.shape[1], tiles)
    return (query_grad, key_grad, value_grad, expert_grad)


def solution(mesh):
    placed = (
        P("ctx", "exp"),
        P("ctx", None),
        P("ctx", None),
        P("ctx", "exp"),
        P("ctx", "exp"),
        P("exp", "ctx"),
        P(),
        P("exp", None),
        P("exp", None),
        P("exp", None),
        P(),
        P("exp", None, None, None, "ctx"),
    )
    return jax.shard_map(
        local,
        mesh=mesh,
        in_specs=placed,
        out_specs=(
            P("ctx", "exp"),
            P(("ctx", "exp"), None),
            P(("ctx", "exp"), None),
            P("exp", "ctx", None),
        ),
        check_vma=False,
    )
```

```python
import functools
import math

import jax
import jax.numpy as jnp
from jax import lax
from jax.experimental import pallas as pl
from jax.experimental.pallas import tpu as pltpu
from jax.sharding import PartitionSpec as P

LAST = (((1,), (1,)), ((), ()))
FIRST = (((0,), (0,)), ((), ()))


def full(shape):
    return pl.BlockSpec(shape, lambda *at: (0,) * len(shape))


def attention_kernel(
    place_ref, mask_ref, query_ref, grad_ref, out_ref, lse_ref, *rest
):
    cycle = mask_ref.shape[0]
    pair_refs, (query_grad_ref, terms_ref, sums_ref, pairs_ref) = rest[:cycle], rest[cycle:]
    rows, width = pairs_ref.shape[1], pairs_ref.shape[2] // 2
    heads = lse_ref.shape[0]
    scale = 1.0 / math.sqrt(width)
    mine = place_ref[0]
    offset = 0.5 * math.log(rows) + lse_ref[...]
    spans = [slice(h * width, (h + 1) * width) for h in range(heads)]
    for step, pair_ref in enumerate(pair_refs):
        pairs_ref[step] = pair_ref[...]
    delta = []
    for span in spans:
        both = grad_ref[:, span].astype(jnp.float32) * out_ref[:, span].astype(jnp.float32)
        delta.append(jnp.sum(both.T, axis=0, keepdims=True))

    def block(step, diagonal):
        key, value = pairs_ref[step, :, :width], pairs_ref[step, :, width:]
        probs, slopes = [], []
        for h, span in enumerate(spans):
            query, grad = query_ref[:, span], grad_ref[:, span]
            scores = lax.dot_general(key, query, LAST, preferred_element_type=jnp.float32)
            prob = jnp.exp(scores * scale - offset[h : h + 1])
            if diagonal:
                at_key = lax.broadcasted_iota(jnp.int32, (rows, rows), 0)
                at_query = lax.broadcasted_iota(jnp.int32, (rows, rows), 1)
                prob = jnp.where(at_key <= at_query, prob, 0.0)
            prob_grad = lax.dot_general(value, grad, LAST, preferred_element_type=jnp.float32)
            slope = (prob * (prob_grad - delta[h]) * scale).astype(jnp.bfloat16)
            probs.append(prob.astype(jnp.bfloat16))
            slopes.append(slope)
            query_term = lax.dot_general(slope, key, FIRST, preferred_element_type=jnp.float32)
            if diagonal:
                sums_ref[:, span] = query_term
            else:
                sums_ref[:, span] += query_term
        queries = jnp.concatenate([query_ref[:, span] for span in spans], axis=0)
        grads = jnp.concatenate([grad_ref[:, span] for span in spans], axis=0)
        key_term = jnp.dot(
            jnp.concatenate(slopes, axis=1), queries, preferred_element_type=jnp.float32
        )
        value_term = jnp.dot(
            jnp.concatenate(probs, axis=1), grads, preferred_element_type=jnp.float32
        )
        terms_ref[mine - step, :, :width] = key_term.astype(jnp.bfloat16)
        terms_ref[mine - step, :, width:] = value_term.astype(jnp.bfloat16)

    block(0, True)

    @pl.loop(0, cycle)
    def _(source):
        seen = jnp.logical_and(source < mine, mask_ref[mine, source] > 0)

        @pl.when(seen)
        def _():
            block(mine - source, False)

        @pl.when(jnp.logical_and(source != mine, jnp.logical_not(seen)))
        def _():
            terms_ref[source] = jnp.zeros_like(terms_ref[source])

    query_grad_ref[...] = sums_ref[...].astype(jnp.bfloat16)


def key_blocks(keys, values, width):
    cycle = lax.axis_size("ctx")
    owners = lax.axis_size("exp")
    kv_count = keys.shape[1] // width
    kv_head = lax.axis_index("exp") * kv_count // owners
    pair = jnp.concatenate(
        [
            lax.dynamic_slice_in_dim(keys, kv_head * width, width, 1),
            lax.dynamic_slice_in_dim(values, kv_head * width, width, 1),
        ],
        axis=1,
    )
    return [pair] + [
        lax.ppermute(pair, "ctx", [(c, c + step) for c in range(cycle - step)])
        for step in range(1, cycle)
    ]


def attention(queries, arrived, attn_out, attn_out_grad, lse_excess, block_mask):
    cycle = lax.axis_size("ctx")
    mine = lax.axis_index("ctx")
    pair = arrived[0]
    operands = (queries, attn_out_grad, attn_out, lse_excess, *arrived)
    return pl.pallas_call(
        attention_kernel,
        out_shape=(
            jax.ShapeDtypeStruct(queries.shape, jnp.bfloat16),
            jax.ShapeDtypeStruct((cycle,) + pair.shape, jnp.bfloat16),
        ),
        grid_spec=pltpu.PrefetchScalarGridSpec(
            num_scalar_prefetch=2,
            grid=(1,),
            in_specs=[full(operand.shape) for operand in operands],
            out_specs=(full(queries.shape), full((cycle,) + pair.shape)),
            scratch_shapes=[
                pltpu.VMEM(queries.shape, jnp.float32),
                pltpu.VMEM((cycle,) + pair.shape, jnp.bfloat16),
            ],
        ),
        compiler_params=pltpu.CompilerParams(vmem_limit_bytes=32 * 2**20),
        name="attention",
    )(mine.astype(jnp.int32)[None], block_mask, *operands)


def sum_kernel(parts_ref, key_ref, value_ref):
    cycle, owners, rows, columns = parts_ref.shape
    kv_count = key_ref.shape[1] * 2 // columns
    group = owners // kv_count
    width = columns // 2
    for k in range(kv_count):
        total = jnp.zeros((rows, columns), jnp.float32)
        for c in range(cycle):
            for e in range(k * group, (k + 1) * group):
                total += parts_ref[c, e].astype(jnp.float32)
        key_ref[:, k * width : (k + 1) * width] = total[:, :width].astype(jnp.bfloat16)
        value_ref[:, k * width : (k + 1) * width] = total[:, width:].astype(jnp.bfloat16)


def summed_terms(terms, kv_columns, tiles):
    cycle, owners = lax.axis_size("ctx"), lax.axis_size("exp")
    rows, columns = terms.shape[1:]
    parts = lax.all_to_all(
        terms.reshape(cycle * owners, rows // owners, columns),
        ("ctx", "exp"),
        split_axis=0,
        concat_axis=0,
        tiled=True,
    ).reshape(cycle, owners, rows // owners, columns)
    parts, tiles = lax.optimization_barrier((parts, tiles))
    shape = (rows // owners, kv_columns)
    out = jax.ShapeDtypeStruct(shape, jnp.bfloat16)
    key_grad, value_grad = pl.pallas_call(
        sum_kernel,
        out_shape=(out, out),
        grid=(1,),
        in_specs=[full(parts.shape)],
        out_specs=(full(shape), full(shape)),
        compiler_params=pltpu.CompilerParams(vmem_limit_bytes=16 * 2**20),
        name="sums",
    )(parts)
    return key_grad, value_grad, tiles


def pick_kernel(per_dev, shadow_ref, mixed_ref, sent_ref):
    for owner in range(sent_ref.shape[0]):
        host = shadow_ref[owner * per_dev]
        for j in range(1, per_dev):
            host = jnp.maximum(host, shadow_ref[owner * per_dev + j])
        sent_ref[owner] = mixed_ref[host, : sent_ref.shape[1]]


def picked_rows(shadow_list, mixed, limit):
    owners = mixed.shape[0]
    whole = pl.BlockSpec(memory_space=pltpu.VMEM)
    return pl.pallas_call(
        functools.partial(pick_kernel, shadow_list.shape[0] // owners),
        out_shape=jax.ShapeDtypeStruct((owners, limit, mixed.shape[2]), jnp.bfloat16),
        in_specs=[pl.BlockSpec(memory_space=pltpu.SMEM), whole],
        out_specs=whole,
        compiler_params=pltpu.CompilerParams(vmem_limit_bytes=4 * 2**20),
        name="picked",
    )(shadow_list, mixed)


def weight_kernel(orders, own_ref, shadow_ref, mixed_ref, hidden_ref, side_ref, weight_ref):
    owners = mixed_ref.shape[0]
    per_dev, units = hidden_ref.shape[1], hidden_ref.shape[4]
    tokens = weight_ref.shape[1] // owners
    limit = side_ref.shape[1]
    own = own_ref[0]
    earlier = (
        lax.broadcasted_iota(jnp.int32, (tokens, tokens), 0)
        < lax.broadcasted_iota(jnp.int32, (tokens, tokens), 1)
    ).astype(jnp.bfloat16)
    odd = lax.broadcasted_iota(jnp.int32, (1, tokens), 1) % 2 == 1

    def rows_at(named, rows):
        rank = jnp.dot(
            jnp.broadcast_to(named.astype(jnp.float32), (8, tokens)).astype(jnp.bfloat16),
            earlier,
            preferred_element_type=jnp.float32,
        )[:1]
        place = lax.broadcasted_iota(jnp.int32, (rows.shape[0], tokens), 0).astype(jnp.float32)
        chosen = jnp.where(jnp.logical_and(named, rank == place), 1.0, 0.0).astype(jnp.bfloat16)
        return lax.dot_general(rows, chosen, FIRST, preferred_element_type=jnp.float32)

    for i in range(owners):
        source = own ^ jnp.where(own % 2 == 0, orders[0][i], orders[1][i])
        for j in range(per_dev):
            prob = mixed_ref[source, limit + j : limit + j + 1, :tokens].astype(jnp.float32)
            named = prob > 0
            flag = shadow_ref[own * per_dev + j] >= 0
            side = jnp.logical_and(jnp.logical_and(named, odd), flag)
            here = jnp.logical_and(named, jnp.logical_not(side))
            rows = rows_at(here, hidden_ref[0, j, source]) + rows_at(
                side, side_ref[source, :, :units]
            )
            weight_ref[j * units : (j + 1) * units, i * tokens : (i + 1) * tokens] = (
                rows * prob
            ).astype(jnp.bfloat16)


def weighted_rows(own_index, shadow_list, mixed, hidden, shadow_rows, tokens, orders):
    owners = mixed.shape[0]
    per_dev, units = shadow_list.shape[0] // owners, hidden.shape[4]
    shape = (per_dev * units, owners * tokens)
    return pl.pallas_call(
        functools.partial(weight_kernel, orders),
        out_shape=jax.ShapeDtypeStruct(shape, jnp.bfloat16),
        grid_spec=pltpu.PrefetchScalarGridSpec(
            num_scalar_prefetch=2,
            grid=(1,),
            in_specs=[
                full(mixed.shape),
                full((1, per_dev) + hidden.shape[2:]),
                full(shadow_rows.shape),
            ],
            out_specs=full(shape),
        ),
        compiler_params=pltpu.CompilerParams(vmem_limit_bytes=32 * 2**20),
        name="weighted",
    )(own_index.astype(jnp.int32)[None], shadow_list, mixed, hidden, shadow_rows)


def tile_kernel(weight_ref, *refs):
    *block_refs, tile_ref, gathered_ref, held_ref, in_sems, out_sems = refs
    per_dev, units, model = tile_ref.shape
    tokens = block_refs[0].shape[0]
    steps = in_sems.shape[0]
    step = model // steps
    arriving, leaving = [], []
    for i in range(steps):
        columns = pl.ds(i * step, step)
        arriving.append(
            [
                pltpu.make_async_copy(
                    ref.at[:, columns],
                    gathered_ref.at[pl.ds(n * tokens, tokens), columns],
                    in_sems.at[i, n],
                )
                for n, ref in enumerate(block_refs)
            ]
        )
    for copy in arriving[0] + arriving[1]:
        copy.start()
    for i in range(steps):
        for copy in arriving[i]:
            copy.wait()
        for copy in arriving[i + 2] if i + 2 < steps else []:
            copy.start()
        columns = slice(i * step, (i + 1) * step)
        held_ref[:, columns] = jnp.dot(
            weight_ref[...], gathered_ref[:, columns], preferred_element_type=jnp.float32
        )
        for j in range(per_dev):
            leaving.append(
                pltpu.make_async_copy(
                    held_ref.at[pl.ds(j * units, units), pl.ds(i * step, step)],
                    tile_ref.at[j, :, pl.ds(i * step, step)],
                    out_sems.at[i, j],
                )
            )
            leaving[-1].start()
    for copy in leaving:
        copy.wait()


def tile_sums(weighted, blocks, per_dev):
    tokens, model = blocks[0].shape
    rows = weighted.shape[0]
    steps = model // 1024
    anywhere = pl.BlockSpec(memory_space=pl.ANY)
    return pl.pallas_call(
        tile_kernel,
        out_shape=jax.ShapeDtypeStruct((per_dev, rows // per_dev, model), jnp.float32),
        in_specs=[pl.BlockSpec(memory_space=pltpu.VMEM)] + [anywhere] * len(blocks),
        out_specs=anywhere,
        scratch_shapes=[
            pltpu.VMEM((len(blocks) * tokens, model), jnp.bfloat16),
            pltpu.VMEM((rows, model), jnp.float32),
            pltpu.SemaphoreType.DMA((steps, len(blocks))),
            pltpu.SemaphoreType.DMA((steps, per_dev)),
        ],
        compiler_params=pltpu.CompilerParams(vmem_limit_bytes=32 * 2**20),
        name="tiles",
    )(weighted, *blocks)


def swapped(value):
    return lax.all_to_all(value, "exp", split_axis=0, concat_axis=0, tiled=True)


def source_rows(expert_ids, route_probs, shadow_list, stored_hidden_state):
    owners = lax.axis_size("exp")
    tokens = expert_ids.shape[0]
    count = shadow_list.shape[0]
    per_dev = count // owners
    capacity, units = stored_hidden_state.shape[3:]
    hit = expert_ids[:, None, :] == jnp.arange(count, dtype=jnp.int32)[None, :, None]
    table = jnp.sum(
        jnp.where(hit, route_probs[:, None, :].astype(jnp.float32), 0.0), axis=2
    ).astype(jnp.bfloat16)
    table = table.T.reshape(owners, per_dev, tokens)
    used = min(capacity, tokens // 2)
    limit = -(-used // 16) * 16
    lanes = max(units, tokens)
    rows = jnp.pad(
        stored_hidden_state[0, per_dev, :, :used],
        ((0, 0), (0, limit - used), (0, lanes - units)),
    )
    return jnp.concatenate([rows, jnp.pad(table, ((0, 0), (0, 0), (0, lanes - tokens)))], axis=1)


def expert_rows(mixed, shadow_rows, shadow_list, stored_hidden_state, tokens):
    steps = block_steps(lax.axis_size("exp"))
    orders = [
        [step ^ turn for pair in zip(steps[core], steps[1 - core]) for step, turn in zip(pair, (0, 1))]
        for core in range(2)
    ]
    own_index = lax.axis_index("exp")
    return weighted_rows(
        own_index, shadow_list, mixed, stored_hidden_state, shadow_rows, tokens, orders
    )


def block_steps(owners):
    masks = [1 << bit for bit in range(1, owners.bit_length() - 1)]
    steps = []
    for core in range(2):
        first, second = masks[1 - core], masks[core]
        held = [0, first, second, first ^ second]
        for mask in masks[2:]:
            held = held + [step ^ mask for step in held]
        steps.append(held)
    return steps


def moved(value, steps):
    owners = lax.axis_size("exp")
    return lax.ppermute(value, "exp", [(e, e ^ steps[e % 2]) for e in range(owners)])


def after(value, *others):
    return lax.optimization_barrier((value, others))[0]


def beside(block):
    return moved(block, (1, 1))


def all_blocks(held):
    steps = block_steps(lax.axis_size("exp"))[0]
    for turn in range(len(steps).bit_length() - 3):
        mask = steps[4 << turn]
        more = [moved(part, (mask, mask)) for part, _ in held]
        held = held + [(part, beside(part)) for part in more]
    return [block for pair in held for block in pair]


def local(
    queries,
    keys,
    values,
    attn_out,
    attn_out_grad,
    lse_excess,
    block_mask,
    expert_ids,
    route_probs,
    moe_grad,
    shadow_list,
    stored_hidden_state,
):
    steps = block_steps(lax.axis_size("exp"))
    tokens = expert_ids.shape[0]
    first = moved(moe_grad, [held[1] for held in steps])
    arrived = key_blocks(keys, values, queries.shape[1] // lse_excess.shape[0])
    payload = source_rows(expert_ids, route_probs, shadow_list, stored_hidden_state)
    own_beside = beside(after(moe_grad, payload))
    mixed = swapped(payload)
    second = moved(after(moe_grad, own_beside), [held[2] for held in steps])
    per_dev = shadow_list.shape[0] // lax.axis_size("exp")
    sent = after(picked_rows(shadow_list, mixed, payload.shape[1] - per_dev), arrived)
    first_beside = beside(after(first, sent))
    shadow_rows = swapped(sent)
    far = moved(after(first, first_beside), [held[2] for held in steps])
    query_grad, terms = attention(
        queries, after(arrived, first_beside), attn_out, attn_out_grad, lse_excess, block_mask
    )
    weighted = expert_rows(
        mixed, after(shadow_rows, query_grad), shadow_list, stored_hidden_state, tokens
    )
    second_beside = beside(after(second, weighted))
    far = after(far, second_beside)
    blocks = all_blocks(
        [(moe_grad, own_beside), (first, first_beside), (second, second_beside), (far, beside(far))]
    )
    tiles = tile_sums(weighted, blocks, per_dev)
    key_grad, value_grad, expert_grad = summed_terms(terms, keys.shape[1], tiles)
    return (query_grad, key_grad, value_grad, expert_grad)


def solution(mesh):
    placed = (
        P("ctx", "exp"),
        P("ctx", None),
        P("ctx", None),
        P("ctx", "exp"),
        P("ctx", "exp"),
        P("exp", "ctx"),
        P(),
        P("exp", None),
        P("exp", None),
        P("exp", None),
        P(),
        P("exp", None, None, None, "ctx"),
    )
    return jax.shard_map(
        local,
        mesh=mesh,
        in_specs=placed,
        out_specs=(
            P("ctx", "exp"),
            P(("ctx", "exp"), None),
            P(("ctx", "exp"), None),
            P("exp", "ctx", None),
        ),
        check_vma=False,
    )
```

```python
import functools
import math

import jax
import jax.numpy as jnp
from jax import lax
from jax.experimental import pallas as pl
from jax.experimental.pallas import tpu as pltpu
from jax.sharding import PartitionSpec as P

LAST = (((1,), (1,)), ((), ()))
FIRST = (((0,), (0,)), ((), ()))


def full(shape):
    return pl.BlockSpec(shape, lambda *at: (0,) * len(shape))


def attention_kernel(
    place_ref, mask_ref, query_ref, grad_ref, out_ref, lse_ref, *rest
):
    cycle = mask_ref.shape[0]
    pair_refs, (query_grad_ref, terms_ref, sums_ref, pairs_ref) = rest[:cycle], rest[cycle:]
    rows, width = pairs_ref.shape[1], pairs_ref.shape[2] // 2
    heads = lse_ref.shape[0]
    scale = 1.0 / math.sqrt(width)
    mine = place_ref[0]
    offset = 0.5 * math.log(rows) + lse_ref[...]
    spans = [slice(h * width, (h + 1) * width) for h in range(heads)]
    for step, pair_ref in enumerate(pair_refs):
        pairs_ref[step] = pair_ref[...]
    delta = []
    for span in spans:
        both = grad_ref[:, span].astype(jnp.float32) * out_ref[:, span].astype(jnp.float32)
        delta.append(jnp.sum(both.T, axis=0, keepdims=True))

    def block(step, diagonal):
        key, value = pairs_ref[step, :, :width], pairs_ref[step, :, width:]
        probs, slopes = [], []
        for h, span in enumerate(spans):
            query, grad = query_ref[:, span], grad_ref[:, span]
            scores = lax.dot_general(key, query, LAST, preferred_element_type=jnp.float32)
            prob = jnp.exp(scores * scale - offset[h : h + 1])
            if diagonal:
                at_key = lax.broadcasted_iota(jnp.int32, (rows, rows), 0)
                at_query = lax.broadcasted_iota(jnp.int32, (rows, rows), 1)
                prob = jnp.where(at_key <= at_query, prob, 0.0)
            prob_grad = lax.dot_general(value, grad, LAST, preferred_element_type=jnp.float32)
            slope = (prob * (prob_grad - delta[h]) * scale).astype(jnp.bfloat16)
            probs.append(prob.astype(jnp.bfloat16))
            slopes.append(slope)
            query_term = lax.dot_general(slope, key, FIRST, preferred_element_type=jnp.float32)
            if diagonal:
                sums_ref[:, span] = query_term
            else:
                sums_ref[:, span] += query_term
        queries = jnp.concatenate([query_ref[:, span] for span in spans], axis=0)
        grads = jnp.concatenate([grad_ref[:, span] for span in spans], axis=0)
        key_term = jnp.dot(
            jnp.concatenate(slopes, axis=1), queries, preferred_element_type=jnp.float32
        )
        value_term = jnp.dot(
            jnp.concatenate(probs, axis=1), grads, preferred_element_type=jnp.float32
        )
        terms_ref[mine - step, :, :width] = key_term.astype(jnp.bfloat16)
        terms_ref[mine - step, :, width:] = value_term.astype(jnp.bfloat16)

    block(0, True)

    @pl.loop(0, cycle)
    def _(source):
        seen = jnp.logical_and(source < mine, mask_ref[mine, source] > 0)

        @pl.when(seen)
        def _():
            block(mine - source, False)

        @pl.when(jnp.logical_and(source != mine, jnp.logical_not(seen)))
        def _():
            terms_ref[source] = jnp.zeros_like(terms_ref[source])

    query_grad_ref[...] = sums_ref[...].astype(jnp.bfloat16)


def key_blocks(keys, values, width):
    cycle = lax.axis_size("ctx")
    owners = lax.axis_size("exp")
    kv_count = keys.shape[1] // width
    kv_head = lax.axis_index("exp") * kv_count // owners
    pair = jnp.concatenate(
        [
            lax.dynamic_slice_in_dim(keys, kv_head * width, width, 1),
            lax.dynamic_slice_in_dim(values, kv_head * width, width, 1),
        ],
        axis=1,
    )
    return [pair] + [
        lax.ppermute(pair, "ctx", [(c, c + step) for c in range(cycle - step)])
        for step in range(1, cycle)
    ]


def attention(queries, arrived, attn_out, attn_out_grad, lse_excess, block_mask):
    cycle = lax.axis_size("ctx")
    mine = lax.axis_index("ctx")
    pair = arrived[0]
    operands = (queries, attn_out_grad, attn_out, lse_excess, *arrived)
    return pl.pallas_call(
        attention_kernel,
        out_shape=(
            jax.ShapeDtypeStruct(queries.shape, jnp.bfloat16),
            jax.ShapeDtypeStruct((cycle,) + pair.shape, jnp.bfloat16),
        ),
        grid_spec=pltpu.PrefetchScalarGridSpec(
            num_scalar_prefetch=2,
            grid=(1,),
            in_specs=[full(operand.shape) for operand in operands],
            out_specs=(full(queries.shape), full((cycle,) + pair.shape)),
            scratch_shapes=[
                pltpu.VMEM(queries.shape, jnp.float32),
                pltpu.VMEM((cycle,) + pair.shape, jnp.bfloat16),
            ],
        ),
        compiler_params=pltpu.CompilerParams(vmem_limit_bytes=32 * 2**20),
        name="attention",
    )(mine.astype(jnp.int32)[None], block_mask, *operands)


def sum_kernel(parts_ref, key_ref, value_ref):
    cycle, owners, rows, columns = parts_ref.shape
    kv_count = key_ref.shape[1] * 2 // columns
    group = owners // kv_count
    width = columns // 2
    for k in range(kv_count):
        total = jnp.zeros((rows, columns), jnp.float32)
        for c in range(cycle):
            for e in range(k * group, (k + 1) * group):
                total += parts_ref[c, e].astype(jnp.float32)
        key_ref[:, k * width : (k + 1) * width] = total[:, :width].astype(jnp.bfloat16)
        value_ref[:, k * width : (k + 1) * width] = total[:, width:].astype(jnp.bfloat16)


def summed_terms(terms, kv_columns):
    cycle, owners = lax.axis_size("ctx"), lax.axis_size("exp")
    rows, columns = terms.shape[1:]
    parts = lax.all_to_all(
        terms.reshape(cycle * owners, rows // owners, columns),
        ("ctx", "exp"),
        split_axis=0,
        concat_axis=0,
        tiled=True,
    ).reshape(cycle, owners, rows // owners, columns)
    shape = (rows // owners, kv_columns)
    out = jax.ShapeDtypeStruct(shape, jnp.bfloat16)
    return pl.pallas_call(
        sum_kernel,
        out_shape=(out, out),
        grid=(1,),
        in_specs=[full(parts.shape)],
        out_specs=(full(shape), full(shape)),
        compiler_params=pltpu.CompilerParams(vmem_limit_bytes=16 * 2**20),
        name="sums",
    )(parts)


def weight_kernel(orders, own_ref, shadow_ref, hidden_ref, *refs):
    *payload_refs, weight_ref, side_ref = refs
    owners = len(payload_refs)
    per_dev, units = hidden_ref.shape[1], hidden_ref.shape[4]
    tokens = weight_ref.shape[1] // owners
    limit = side_ref.shape[1]
    own = own_ref[0]
    sources = [
        own ^ jnp.where(own % 2 == 0, orders[0][i], orders[1][i]) for i in range(owners)
    ]
    host = shadow_ref[own * per_dev]
    for j in range(1, per_dev):
        host = jnp.maximum(host, shadow_ref[own * per_dev + j])
    for source, payload_ref in zip(sources, payload_refs):

        @pl.when(source == host)
        def _(payload_ref=payload_ref):
            side_ref[...] = payload_ref[:, :limit]

    earlier = (
        lax.broadcasted_iota(jnp.int32, (tokens, tokens), 0)
        < lax.broadcasted_iota(jnp.int32, (tokens, tokens), 1)
    ).astype(jnp.bfloat16)
    odd = lax.broadcasted_iota(jnp.int32, (1, tokens), 1) % 2 == 1

    def rows_at(named, rows):
        rank = jnp.dot(
            jnp.broadcast_to(named.astype(jnp.float32), (8, tokens)).astype(jnp.bfloat16),
            earlier,
            preferred_element_type=jnp.float32,
        )[:1]
        place = lax.broadcasted_iota(jnp.int32, (rows.shape[0], tokens), 0).astype(jnp.float32)
        chosen = jnp.where(jnp.logical_and(named, rank == place), 1.0, 0.0).astype(jnp.bfloat16)
        return lax.dot_general(rows, chosen, FIRST, preferred_element_type=jnp.float32)

    for i, (source, payload_ref) in enumerate(zip(sources, payload_refs)):
        for j in range(per_dev):
            prob = payload_ref[own, limit + j : limit + j + 1, :tokens].astype(jnp.float32)
            named = prob > 0
            flag = shadow_ref[own * per_dev + j] >= 0
            side = jnp.logical_and(jnp.logical_and(named, odd), flag)
            here = jnp.logical_and(named, jnp.logical_not(side))
            rows = rows_at(here, hidden_ref[0, j, source]) + rows_at(
                side, side_ref[source, :, :units]
            )
            weight_ref[j * units : (j + 1) * units, i * tokens : (i + 1) * tokens] = (
                rows * prob
            ).astype(jnp.bfloat16)


def weighted_rows(shadow_list, hidden, payloads, tokens, anchors):
    owners = len(payloads)
    own_index = lax.axis_index("exp")
    per_dev, units = shadow_list.shape[0] // owners, hidden.shape[4]
    shape = (per_dev * units, owners * tokens)
    steps = block_steps(owners)
    orders = [
        [step ^ turn for pair in zip(steps[core], steps[1 - core]) for step, turn in zip(pair, (0, 1))]
        for core in range(2)
    ]
    blocks, rows, lanes = payloads[0].shape
    return pl.pallas_call(
        functools.partial(weight_kernel, orders),
        out_shape=jax.ShapeDtypeStruct(shape, jnp.bfloat16),
        grid_spec=pltpu.PrefetchScalarGridSpec(
            num_scalar_prefetch=2,
            grid=(1,),
            in_specs=[full((1, per_dev) + hidden.shape[2:])]
            + [full(payload.shape) for payload in payloads],
            out_specs=full(shape),
            scratch_shapes=[pltpu.VMEM((blocks, rows - per_dev, lanes), jnp.bfloat16)],
        ),
        compiler_params=pltpu.CompilerParams(vmem_limit_bytes=32 * 2**20),
        name="weighted",
    )(own_index.astype(jnp.int32)[None], shadow_list, after(hidden, anchors), *payloads)


def tile_kernel(weight_ref, *refs):
    *block_refs, tile_ref, gathered_ref, held_ref, in_sems, out_sems = refs
    per_dev, units, model = tile_ref.shape
    tokens = block_refs[0].shape[0]
    steps = in_sems.shape[0]
    step = model // steps
    arriving, leaving = [], []
    for i in range(steps):
        columns = pl.ds(i * step, step)
        arriving.append(
            [
                pltpu.make_async_copy(
                    ref.at[:, columns],
                    gathered_ref.at[pl.ds(n * tokens, tokens), columns],
                    in_sems.at[i, n],
                )
                for n, ref in enumerate(block_refs)
            ]
        )
    for copy in arriving[0] + arriving[1]:
        copy.start()
    for i in range(steps):
        for copy in arriving[i]:
            copy.wait()
        for copy in arriving[i + 2] if i + 2 < steps else []:
            copy.start()
        columns = slice(i * step, (i + 1) * step)
        held_ref[:, columns] = jnp.dot(
            weight_ref[...], gathered_ref[:, columns], preferred_element_type=jnp.float32
        )
        for j in range(per_dev):
            leaving.append(
                pltpu.make_async_copy(
                    held_ref.at[pl.ds(j * units, units), pl.ds(i * step, step)],
                    tile_ref.at[j, :, pl.ds(i * step, step)],
                    out_sems.at[i, j],
                )
            )
            leaving[-1].start()
    for copy in leaving:
        copy.wait()


def tile_sums(weighted, blocks, per_dev):
    tokens, model = blocks[0].shape
    rows = weighted.shape[0]
    steps = model // 1024
    anywhere = pl.BlockSpec(memory_space=pl.ANY)
    return pl.pallas_call(
        tile_kernel,
        out_shape=jax.ShapeDtypeStruct((per_dev, rows // per_dev, model), jnp.float32),
        in_specs=[pl.BlockSpec(memory_space=pltpu.VMEM)] + [anywhere] * len(blocks),
        out_specs=anywhere,
        scratch_shapes=[
            pltpu.VMEM((len(blocks) * tokens, model), jnp.bfloat16),
            pltpu.VMEM((rows, model), jnp.float32),
            pltpu.SemaphoreType.DMA((steps, len(blocks))),
            pltpu.SemaphoreType.DMA((steps, per_dev)),
        ],
        compiler_params=pltpu.CompilerParams(vmem_limit_bytes=32 * 2**20),
        name="tiles",
    )(weighted, *blocks)


def source_rows(expert_ids, route_probs, shadow_list, stored_hidden_state):
    owners = lax.axis_size("exp")
    tokens = expert_ids.shape[0]
    count = shadow_list.shape[0]
    per_dev = count // owners
    capacity, units = stored_hidden_state.shape[3:]
    hit = expert_ids[:, None, :] == jnp.arange(count, dtype=jnp.int32)[None, :, None]
    table = jnp.sum(
        jnp.where(hit, route_probs[:, None, :].astype(jnp.float32), 0.0), axis=2
    ).astype(jnp.bfloat16)
    table = table.T.reshape(owners, per_dev, tokens)
    used = min(capacity, tokens // 2)
    limit = -(-used // 16) * 16
    lanes = max(units, tokens)
    rows = jnp.pad(
        stored_hidden_state[0, per_dev, :, :used],
        ((0, 0), (0, limit - used), (0, lanes - units)),
    )
    return jnp.concatenate([rows, jnp.pad(table, ((0, 0), (0, 0), (0, lanes - tokens)))], axis=1)


def block_steps(owners):
    masks = [1 << bit for bit in range(1, owners.bit_length() - 1)]
    steps = []
    for core in range(2):
        first, second = masks[1 - core], masks[core]
        held = [0, first, second, first ^ second]
        for mask in masks[2:]:
            held = held + [step ^ mask for step in held]
        steps.append(held)
    return steps


def moved(value, steps):
    owners = lax.axis_size("exp")
    return lax.ppermute(value, "exp", [(e, e ^ steps[e % 2]) for e in range(owners)])


def after(value, *others):
    return lax.optimization_barrier((value, others))[0]


def beside(block):
    return moved(block, (1, 1))


def near_and_far(block, anchor=None):
    steps = block_steps(lax.axis_size("exp"))
    first = moved(block, [held[1] for held in steps])
    second = moved(block, [held[2] for held in steps])
    far = moved(first if anchor is None else after(first, anchor), [held[2] for held in steps])
    return [block, first, second, far]


def all_blocks(held):
    steps = block_steps(lax.axis_size("exp"))[0]
    for turn in range(len(steps).bit_length() - 3):
        mask = steps[4 << turn]
        more = [moved(part, (mask, mask)) for part, _ in held]
        held = held + [(part, beside(part)) for part in more]
    return [block for pair in held for block in pair]


def local(
    queries,
    keys,
    values,
    attn_out,
    attn_out_grad,
    lse_excess,
    block_mask,
    expert_ids,
    route_probs,
    moe_grad,
    shadow_list,
    stored_hidden_state,
):
    arrived = key_blocks(keys, values, queries.shape[1] // lse_excess.shape[0])
    query_grad, terms = attention(
        queries, arrived, attn_out, attn_out_grad, lse_excess, block_mask
    )
    key_grad, value_grad = summed_terms(terms, keys.shape[1])
    *near, far = near_and_far(moe_grad, query_grad)
    held = [(block, beside(after(block, query_grad))) for block in near]
    payload = source_rows(expert_ids, route_probs, shadow_list, stored_hidden_state)
    payloads = all_blocks([(block, beside(block)) for block in near_and_far(payload)])
    weighted = weighted_rows(
        shadow_list,
        stored_hidden_state,
        payloads,
        expert_ids.shape[0],
        [block for _, block in held],
    )
    far = after(far, weighted, key_grad, value_grad)
    blocks = all_blocks(held + [(far, beside(far))])
    per_dev = shadow_list.shape[0] // lax.axis_size("exp")
    expert_grad = tile_sums(weighted, blocks, per_dev)
    return (query_grad, key_grad, value_grad, expert_grad)


def solution(mesh):
    placed = (
        P("ctx", "exp"),
        P("ctx", None),
        P("ctx", None),
        P("ctx", "exp"),
        P("ctx", "exp"),
        P("exp", "ctx"),
        P(),
        P("exp", None),
        P("exp", None),
        P("exp", None),
        P(),
        P("exp", None, None, None, "ctx"),
    )
    return jax.shard_map(
        local,
        mesh=mesh,
        in_specs=placed,
        out_specs=(
            P("ctx", "exp"),
            P(("ctx", "exp"), None),
            P(("ctx", "exp"), None),
            P("exp", "ctx", None),
        ),
        check_vma=False,
    )
```

```python
import functools
import math

import jax
import jax.numpy as jnp
from jax import lax
from jax.experimental import pallas as pl
from jax.experimental.pallas import tpu as pltpu
from jax.sharding import PartitionSpec as P

LAST = (((1,), (1,)), ((), ()))
FIRST = (((0,), (0,)), ((), ()))


def full(shape):
    return pl.BlockSpec(shape, lambda *at: (0,) * len(shape))


def attention_kernel(
    place_ref, mask_ref, query_ref, grad_ref, out_ref, lse_ref, *rest
):
    cycle = mask_ref.shape[0]
    pair_refs, query_grad_ref, term_refs = rest[:cycle], rest[cycle], rest[cycle + 1 : -3]
    sums_ref, pairs_ref, terms_ref = rest[-3:]
    rows, width = pairs_ref.shape[1], pairs_ref.shape[2] // 2
    heads = lse_ref.shape[0]
    scale = 1.0 / math.sqrt(width)
    mine = place_ref[0]
    offset = 0.5 * math.log(rows) + lse_ref[...]
    spans = [slice(h * width, (h + 1) * width) for h in range(heads)]
    for step, pair_ref in enumerate(pair_refs):
        pairs_ref[step] = pair_ref[...]
    delta = []
    for span in spans:
        both = grad_ref[:, span].astype(jnp.float32) * out_ref[:, span].astype(jnp.float32)
        delta.append(jnp.sum(both.T, axis=0, keepdims=True))

    def block(step, diagonal):
        key, value = pairs_ref[step, :, :width], pairs_ref[step, :, width:]
        probs, slopes = [], []
        for h, span in enumerate(spans):
            query, grad = query_ref[:, span], grad_ref[:, span]
            scores = lax.dot_general(key, query, LAST, preferred_element_type=jnp.float32)
            prob = jnp.exp(scores * scale - offset[h : h + 1])
            if diagonal:
                at_key = lax.broadcasted_iota(jnp.int32, (rows, rows), 0)
                at_query = lax.broadcasted_iota(jnp.int32, (rows, rows), 1)
                prob = jnp.where(at_key <= at_query, prob, 0.0)
            prob_grad = lax.dot_general(value, grad, LAST, preferred_element_type=jnp.float32)
            slope = (prob * (prob_grad - delta[h]) * scale).astype(jnp.bfloat16)
            probs.append(prob.astype(jnp.bfloat16))
            slopes.append(slope)
            query_term = lax.dot_general(slope, key, FIRST, preferred_element_type=jnp.float32)
            if diagonal:
                sums_ref[:, span] = query_term
            else:
                sums_ref[:, span] += query_term
        queries = jnp.concatenate([query_ref[:, span] for span in spans], axis=0)
        grads = jnp.concatenate([grad_ref[:, span] for span in spans], axis=0)
        key_term = jnp.dot(
            jnp.concatenate(slopes, axis=1), queries, preferred_element_type=jnp.float32
        )
        value_term = jnp.dot(
            jnp.concatenate(probs, axis=1), grads, preferred_element_type=jnp.float32
        )
        terms_ref[step, :, :width] = key_term.astype(jnp.bfloat16)
        terms_ref[step, :, width:] = value_term.astype(jnp.bfloat16)

    block(0, True)

    @pl.loop(1, cycle)
    def _(step):
        source = mine - step
        seen = jnp.logical_and(source >= 0, mask_ref[mine, jnp.maximum(source, 0)] > 0)

        @pl.when(seen)
        def _():
            block(step, False)

        @pl.when(jnp.logical_not(seen))
        def _():
            terms_ref[step] = jnp.zeros_like(terms_ref[step])

    for step, term_ref in enumerate(term_refs):
        term_ref[...] = terms_ref[step]
    query_grad_ref[...] = sums_ref[...].astype(jnp.bfloat16)


def key_blocks(keys, values, width):
    cycle = lax.axis_size("ctx")
    owners = lax.axis_size("exp")
    kv_count = keys.shape[1] // width
    kv_head = lax.axis_index("exp") * kv_count // owners
    pair = jnp.concatenate(
        [
            lax.dynamic_slice_in_dim(keys, kv_head * width, width, 1),
            lax.dynamic_slice_in_dim(values, kv_head * width, width, 1),
        ],
        axis=1,
    )
    return [pair] + [
        lax.ppermute(pair, "ctx", [(c, c + step) for c in range(cycle - step)])
        for step in range(1, cycle)
    ]


def attention(queries, arrived, attn_out, attn_out_grad, lse_excess, block_mask):
    cycle = lax.axis_size("ctx")
    mine = lax.axis_index("ctx")
    pair = arrived[0]
    operands = (queries, attn_out_grad, attn_out, lse_excess, *arrived)
    query_grad, *terms = pl.pallas_call(
        attention_kernel,
        out_shape=[jax.ShapeDtypeStruct(queries.shape, jnp.bfloat16)]
        + [jax.ShapeDtypeStruct(pair.shape, jnp.bfloat16)] * cycle,
        grid_spec=pltpu.PrefetchScalarGridSpec(
            num_scalar_prefetch=2,
            grid=(1,),
            in_specs=[full(operand.shape) for operand in operands],
            out_specs=[full(queries.shape)] + [full(pair.shape)] * cycle,
            scratch_shapes=[
                pltpu.VMEM(queries.shape, jnp.float32),
                pltpu.VMEM((cycle,) + pair.shape, jnp.bfloat16),
                pltpu.VMEM((cycle,) + pair.shape, jnp.bfloat16),
            ],
        ),
        compiler_params=pltpu.CompilerParams(vmem_limit_bytes=32 * 2**20),
        name="attention",
    )(mine.astype(jnp.int32)[None], block_mask, *operands)
    return query_grad, terms


def sum_kernel(parts_ref, key_ref, value_ref):
    owners, rows, columns = parts_ref.shape
    kv_count = key_ref.shape[1] * 2 // columns
    group = owners // kv_count
    width = columns // 2
    for k in range(kv_count):
        total = jnp.zeros((rows, columns), jnp.float32)
        for e in range(k * group, (k + 1) * group):
            total += parts_ref[e].astype(jnp.float32)
        key_ref[:, k * width : (k + 1) * width] = total[:, :width].astype(jnp.bfloat16)
        value_ref[:, k * width : (k + 1) * width] = total[:, width:].astype(jnp.bfloat16)


def block_terms(terms):
    cycle = lax.axis_size("ctx")
    total = terms[0].astype(jnp.float32)
    for step in range(1, cycle):
        pairs = [(c, c - step) for c in range(step, cycle)]
        total = total + lax.ppermute(terms[step], "ctx", pairs).astype(jnp.float32)
    return total.astype(jnp.bfloat16)


def summed_terms(total, kv_columns, tiles):
    owners = lax.axis_size("exp")
    rows, columns = total.shape
    parts = lax.all_to_all(
        total.reshape(owners, rows // owners, columns),
        "exp",
        split_axis=0,
        concat_axis=0,
        tiled=True,
    )
    parts, tiles = lax.optimization_barrier((parts, tiles))
    shape = (rows // owners, kv_columns)
    out = jax.ShapeDtypeStruct(shape, jnp.bfloat16)
    key_grad, value_grad = pl.pallas_call(
        sum_kernel,
        out_shape=(out, out),
        grid=(1,),
        in_specs=[full(parts.shape)],
        out_specs=(full(shape), full(shape)),
        compiler_params=pltpu.CompilerParams(vmem_limit_bytes=16 * 2**20),
        name="sums",
    )(parts)
    return key_grad, value_grad, tiles


def pick_kernel(per_dev, shadow_ref, mixed_ref, sent_ref):
    for owner in range(sent_ref.shape[0]):
        host = shadow_ref[owner * per_dev]
        for j in range(1, per_dev):
            host = jnp.maximum(host, shadow_ref[owner * per_dev + j])
        sent_ref[owner] = mixed_ref[host, : sent_ref.shape[1]]


def picked_rows(shadow_list, mixed, limit):
    owners = mixed.shape[0]
    whole = pl.BlockSpec(memory_space=pltpu.VMEM)
    return pl.pallas_call(
        functools.partial(pick_kernel, shadow_list.shape[0] // owners),
        out_shape=jax.ShapeDtypeStruct((owners, limit, mixed.shape[2]), jnp.bfloat16),
        in_specs=[pl.BlockSpec(memory_space=pltpu.SMEM), whole],
        out_specs=whole,
        compiler_params=pltpu.CompilerParams(vmem_limit_bytes=4 * 2**20),
        name="picked",
    )(shadow_list, mixed)


def weight_kernel(orders, own_ref, shadow_ref, mixed_ref, hidden_ref, side_ref, weight_ref):
    owners = mixed_ref.shape[0]
    per_dev, units = hidden_ref.shape[1], hidden_ref.shape[4]
    tokens = weight_ref.shape[1] // owners
    limit = side_ref.shape[1]
    own = own_ref[0]
    earlier = (
        lax.broadcasted_iota(jnp.int32, (tokens, tokens), 0)
        < lax.broadcasted_iota(jnp.int32, (tokens, tokens), 1)
    ).astype(jnp.bfloat16)
    odd = lax.broadcasted_iota(jnp.int32, (1, tokens), 1) % 2 == 1

    def rows_at(named, rows):
        rank = jnp.dot(
            jnp.broadcast_to(named.astype(jnp.float32), (8, tokens)).astype(jnp.bfloat16),
            earlier,
            preferred_element_type=jnp.float32,
        )[:1]
        place = lax.broadcasted_iota(jnp.int32, (rows.shape[0], tokens), 0).astype(jnp.float32)
        chosen = jnp.where(jnp.logical_and(named, rank == place), 1.0, 0.0).astype(jnp.bfloat16)
        return lax.dot_general(rows, chosen, FIRST, preferred_element_type=jnp.float32)

    for i in range(owners):
        source = own ^ jnp.where(own % 2 == 0, orders[0][i], orders[1][i])
        for j in range(per_dev):
            prob = mixed_ref[source, limit + j : limit + j + 1, :tokens].astype(jnp.float32)
            named = prob > 0
            flag = shadow_ref[own * per_dev + j] >= 0
            side = jnp.logical_and(jnp.logical_and(named, odd), flag)
            here = jnp.logical_and(named, jnp.logical_not(side))
            rows = rows_at(here, hidden_ref[0, j, source]) + rows_at(
                side, side_ref[source, :, :units]
            )
            weight_ref[j * units : (j + 1) * units, i * tokens : (i + 1) * tokens] = (
                rows * prob
            ).astype(jnp.bfloat16)


def weighted_rows(own_index, shadow_list, mixed, hidden, shadow_rows, tokens, orders):
    owners = mixed.shape[0]
    per_dev, units = shadow_list.shape[0] // owners, hidden.shape[4]
    shape = (per_dev * units, owners * tokens)
    return pl.pallas_call(
        functools.partial(weight_kernel, orders),
        out_shape=jax.ShapeDtypeStruct(shape, jnp.bfloat16),
        grid_spec=pltpu.PrefetchScalarGridSpec(
            num_scalar_prefetch=2,
            grid=(1,),
            in_specs=[
                full(mixed.shape),
                full((1, per_dev) + hidden.shape[2:]),
                full(shadow_rows.shape),
            ],
            out_specs=full(shape),
        ),
        compiler_params=pltpu.CompilerParams(vmem_limit_bytes=32 * 2**20),
        name="weighted",
    )(own_index.astype(jnp.int32)[None], shadow_list, mixed, hidden, shadow_rows)


def tile_kernel(start, count, weight_ref, *refs):
    block_refs = refs[:count]
    tile_ref, gathered_ref, held_ref, in_sems, out_sems = refs[-5:]
    per_dev, units, _ = tile_ref.shape
    tokens = block_refs[0].shape[0]
    steps = in_sems.shape[0]
    width = held_ref.shape[1]
    step = width // steps
    arriving, leaving = [], []
    for i in range(steps):
        arriving.append(
            [
                pltpu.make_async_copy(
                    ref.at[:, pl.ds(i * step + (start if ref.shape[1] > width else 0), step)],
                    gathered_ref.at[pl.ds(n * tokens, tokens), pl.ds(i * step, step)],
                    in_sems.at[i, n],
                )
                for n, ref in enumerate(block_refs)
            ]
        )
    for copy in arriving[0] + arriving[1]:
        copy.start()
    for i in range(steps):
        for copy in arriving[i]:
            copy.wait()
        for copy in arriving[i + 2] if i + 2 < steps else []:
            copy.start()
        columns = slice(i * step, (i + 1) * step)
        held_ref[:, columns] = jnp.dot(
            weight_ref[...], gathered_ref[:, columns], preferred_element_type=jnp.float32
        )
        for j in range(per_dev):
            leaving.append(
                pltpu.make_async_copy(
                    held_ref.at[pl.ds(j * units, units), pl.ds(i * step, step)],
                    tile_ref.at[j, :, pl.ds(start + i * step, step)],
                    out_sems.at[i, j],
                )
            )
            leaving[-1].start()
    for copy in leaving:
        copy.wait()


def tile_sums(weighted, blocks, per_dev, start, tiles):
    tokens, model = blocks[0].shape
    width = min(block.shape[1] for block in blocks)
    rows = weighted.shape[0]
    steps = width // 512
    anywhere = pl.BlockSpec(memory_space=pl.ANY)
    earlier = [] if tiles is None else [tiles]
    return pl.pallas_call(
        functools.partial(tile_kernel, start, len(blocks)),
        out_shape=jax.ShapeDtypeStruct((per_dev, rows // per_dev, model), jnp.float32),
        in_specs=[pl.BlockSpec(memory_space=pltpu.VMEM)] + [anywhere] * (len(blocks) + len(earlier)),
        out_specs=anywhere,
        scratch_shapes=[
            pltpu.VMEM((len(blocks) * tokens, width), jnp.bfloat16),
            pltpu.VMEM((rows, width), jnp.float32),
            pltpu.SemaphoreType.DMA((steps, len(blocks))),
            pltpu.SemaphoreType.DMA((steps, per_dev)),
        ],
        input_output_aliases={1 + len(blocks): 0} if earlier else {},
        compiler_params=pltpu.CompilerParams(vmem_limit_bytes=20 * 2**20),
        name="tiles",
    )(weighted, *blocks, *earlier)


def swapped(value):
    return lax.all_to_all(value, "exp", split_axis=0, concat_axis=0, tiled=True)


def source_rows(expert_ids, route_probs, shadow_list, stored_hidden_state):
    owners = lax.axis_size("exp")
    tokens = expert_ids.shape[0]
    count = shadow_list.shape[0]
    per_dev = count // owners
    capacity, units = stored_hidden_state.shape[3:]
    hit = expert_ids[:, None, :] == jnp.arange(count, dtype=jnp.int32)[None, :, None]
    table = jnp.sum(
        jnp.where(hit, route_probs[:, None, :].astype(jnp.float32), 0.0), axis=2
    ).astype(jnp.bfloat16)
    table = table.T.reshape(owners, per_dev, tokens)
    used = min(capacity, tokens // 2)
    limit = -(-used // 16) * 16
    lanes = max(units, tokens)
    rows = jnp.pad(
        stored_hidden_state[0, per_dev, :, :used],
        ((0, 0), (0, limit - used), (0, lanes - units)),
    )
    return jnp.concatenate([rows, jnp.pad(table, ((0, 0), (0, 0), (0, lanes - tokens)))], axis=1)


def expert_rows(mixed, shadow_rows, shadow_list, stored_hidden_state, tokens):
    steps = block_steps(lax.axis_size("exp"))
    orders = [
        [step ^ turn for pair in zip(steps[core], steps[1 - core]) for step, turn in zip(pair, (0, 1))]
        for core in range(2)
    ]
    own_index = lax.axis_index("exp")
    return weighted_rows(
        own_index, shadow_list, mixed, stored_hidden_state, shadow_rows, tokens, orders
    )


def block_steps(owners):
    masks = [1 << bit for bit in range(1, owners.bit_length() - 1)]
    steps = []
    for core in range(2):
        first, second = masks[1 - core], masks[core]
        held = [0, first, second, first ^ second]
        for mask in masks[2:]:
            held = held + [step ^ mask for step in held]
        steps.append(held)
    return steps


def moved(value, steps):
    owners = lax.axis_size("exp")
    return lax.ppermute(value, "exp", [(e, e ^ steps[e % 2]) for e in range(owners)])


def after(value, *others):
    return lax.optimization_barrier((value, others))[0]


def beside(block):
    return moved(block, (1, 1))


def all_blocks(held):
    steps = block_steps(lax.axis_size("exp"))[0]
    for turn in range(len(steps).bit_length() - 3):
        mask = steps[4 << turn]
        more = [moved(part, (mask, mask)) for part, _ in held]
        held = held + [(part, beside(part)) for part in more]
    return [block for pair in held for block in pair]


def local(
    queries,
    keys,
    values,
    attn_out,
    attn_out_grad,
    lse_excess,
    block_mask,
    expert_ids,
    route_probs,
    moe_grad,
    shadow_list,
    stored_hidden_state,
):
    steps = block_steps(lax.axis_size("exp"))
    tokens = expert_ids.shape[0]
    per_dev = shadow_list.shape[0] // lax.axis_size("exp")
    first = moved(moe_grad, [held[1] for held in steps])
    own_beside = beside(moe_grad)
    arrived = key_blocks(keys, values, queries.shape[1] // lse_excess.shape[0])
    payload = source_rows(expert_ids, route_probs, shadow_list, stored_hidden_state)
    mixed = swapped(payload)
    second = moved(after(moe_grad, mixed), [held[2] for held in steps])
    sent = picked_rows(shadow_list, mixed, payload.shape[1] - per_dev)
    sent = after(sent, arrived, own_beside)
    first_beside = beside(after(first, sent))
    shadow_rows = swapped(sent)
    query_grad, terms = attention(
        queries, arrived, attn_out, attn_out_grad, lse_excess, block_mask
    )
    total = block_terms(terms)
    parts = 2
    first, second, shadow_rows, query_grad, first_beside = lax.optimization_barrier(
        (first, second, shadow_rows, query_grad, first_beside)
    )
    far = [moved(part, [held[2] for held in steps]) for part in jnp.split(first, parts, axis=1)]
    shadow_rows, total = lax.optimization_barrier((shadow_rows, total))
    weighted = expert_rows(mixed, shadow_rows, shadow_list, stored_hidden_state, tokens)
    second_beside = beside(after(second, weighted))
    near = [(moe_grad, own_beside), (first, first_beside), (second, second_beside)]
    tiles, start = None, 0
    for part in far:
        part, _ = lax.optimization_barrier((part, weighted if tiles is None else tiles))
        blocks = all_blocks(near + [(part, beside(part))])
        tiles = tile_sums(weighted, blocks, per_dev, start, tiles)
        start += part.shape[1]
    key_grad, value_grad, expert_grad = summed_terms(total, keys.shape[1], tiles)
    return (query_grad, key_grad, value_grad, expert_grad)


def solution(mesh):
    placed = (
        P("ctx", "exp"),
        P("ctx", None),
        P("ctx", None),
        P("ctx", "exp"),
        P("ctx", "exp"),
        P("exp", "ctx"),
        P(),
        P("exp", None),
        P("exp", None),
        P("exp", None),
        P(),
        P("exp", None, None, None, "ctx"),
    )
    return jax.shard_map(
        local,
        mesh=mesh,
        in_specs=placed,
        out_specs=(
            P("ctx", "exp"),
            P(("ctx", "exp"), None),
            P(("ctx", "exp"), None),
            P("exp", "ctx", None),
        ),
        check_vma=False,
    )
```

```python
import functools
import math

import jax
import jax.numpy as jnp
from jax import lax
from jax.experimental import pallas as pl
from jax.experimental.pallas import tpu as pltpu
from jax.sharding import PartitionSpec as P

LAST = (((1,), (1,)), ((), ()))
FIRST = (((0,), (0,)), ((), ()))


def full(shape):
    return pl.BlockSpec(shape, lambda *at: (0,) * len(shape))


def attention_kernel(
    place_ref, mask_ref, query_ref, grad_ref, out_ref, lse_ref, *rest
):
    cycle = mask_ref.shape[0]
    pair_refs, query_grad_ref, term_refs = rest[:cycle], rest[cycle], rest[cycle + 1 : -3]
    sums_ref, pairs_ref, terms_ref = rest[-3:]
    rows, width = pairs_ref.shape[1], pairs_ref.shape[2] // 2
    heads = lse_ref.shape[0]
    scale = 1.0 / math.sqrt(width)
    mine = place_ref[0]
    offset = 0.5 * math.log(rows) + lse_ref[...]
    spans = [slice(h * width, (h + 1) * width) for h in range(heads)]
    for step, pair_ref in enumerate(pair_refs):
        pairs_ref[step] = pair_ref[...]
    delta = []
    for span in spans:
        both = grad_ref[:, span].astype(jnp.float32) * out_ref[:, span].astype(jnp.float32)
        delta.append(jnp.sum(both.T, axis=0, keepdims=True))

    def block(step, diagonal):
        key, value = pairs_ref[step, :, :width], pairs_ref[step, :, width:]
        probs, slopes = [], []
        for h, span in enumerate(spans):
            query, grad = query_ref[:, span], grad_ref[:, span]
            scores = lax.dot_general(key, query, LAST, preferred_element_type=jnp.float32)
            prob = jnp.exp(scores * scale - offset[h : h + 1])
            if diagonal:
                at_key = lax.broadcasted_iota(jnp.int32, (rows, rows), 0)
                at_query = lax.broadcasted_iota(jnp.int32, (rows, rows), 1)
                prob = jnp.where(at_key <= at_query, prob, 0.0)
            prob_grad = lax.dot_general(value, grad, LAST, preferred_element_type=jnp.float32)
            slope = (prob * (prob_grad - delta[h]) * scale).astype(jnp.bfloat16)
            probs.append(prob.astype(jnp.bfloat16))
            slopes.append(slope)
            query_term = lax.dot_general(slope, key, FIRST, preferred_element_type=jnp.float32)
            if diagonal:
                sums_ref[:, span] = query_term
            else:
                sums_ref[:, span] += query_term
        queries = jnp.concatenate([query_ref[:, span] for span in spans], axis=0)
        grads = jnp.concatenate([grad_ref[:, span] for span in spans], axis=0)
        key_term = jnp.dot(
            jnp.concatenate(slopes, axis=1), queries, preferred_element_type=jnp.float32
        )
        value_term = jnp.dot(
            jnp.concatenate(probs, axis=1), grads, preferred_element_type=jnp.float32
        )
        terms_ref[step, :, :width] = key_term.astype(jnp.bfloat16)
        terms_ref[step, :, width:] = value_term.astype(jnp.bfloat16)

    block(0, True)

    @pl.loop(1, cycle)
    def _(step):
        source = mine - step
        seen = jnp.logical_and(source >= 0, mask_ref[mine, jnp.maximum(source, 0)] > 0)

        @pl.when(seen)
        def _():
            block(step, False)

        @pl.when(jnp.logical_not(seen))
        def _():
            terms_ref[step] = jnp.zeros_like(terms_ref[step])

    for step, term_ref in enumerate(term_refs):
        term_ref[...] = terms_ref[step]
    query_grad_ref[...] = sums_ref[...].astype(jnp.bfloat16)


def key_blocks(keys, values, width):
    cycle = lax.axis_size("ctx")
    owners = lax.axis_size("exp")
    kv_count = keys.shape[1] // width
    kv_head = lax.axis_index("exp") * kv_count // owners
    pair = jnp.concatenate(
        [
            lax.dynamic_slice_in_dim(keys, kv_head * width, width, 1),
            lax.dynamic_slice_in_dim(values, kv_head * width, width, 1),
        ],
        axis=1,
    )
    return [pair] + [
        lax.ppermute(pair, "ctx", [(c, c + step) for c in range(cycle - step)])
        for step in range(1, cycle)
    ]


def attention(queries, arrived, attn_out, attn_out_grad, lse_excess, block_mask):
    cycle = lax.axis_size("ctx")
    mine = lax.axis_index("ctx")
    pair = arrived[0]
    operands = (queries, attn_out_grad, attn_out, lse_excess, *arrived)
    query_grad, *terms = pl.pallas_call(
        attention_kernel,
        out_shape=[jax.ShapeDtypeStruct(queries.shape, jnp.bfloat16)]
        + [jax.ShapeDtypeStruct(pair.shape, jnp.bfloat16)] * cycle,
        grid_spec=pltpu.PrefetchScalarGridSpec(
            num_scalar_prefetch=2,
            grid=(1,),
            in_specs=[full(operand.shape) for operand in operands],
            out_specs=[full(queries.shape)] + [full(pair.shape)] * cycle,
            scratch_shapes=[
                pltpu.VMEM(queries.shape, jnp.float32),
                pltpu.VMEM((cycle,) + pair.shape, jnp.bfloat16),
                pltpu.VMEM((cycle,) + pair.shape, jnp.bfloat16),
            ],
        ),
        compiler_params=pltpu.CompilerParams(vmem_limit_bytes=32 * 2**20),
        name="attention",
    )(mine.astype(jnp.int32)[None], block_mask, *operands)
    return query_grad, terms


def sum_kernel(parts_ref, key_ref, value_ref):
    owners, rows, columns = parts_ref.shape
    kv_count = key_ref.shape[1] * 2 // columns
    group = owners // kv_count
    width = columns // 2
    for k in range(kv_count):
        total = jnp.zeros((rows, columns), jnp.float32)
        for e in range(k * group, (k + 1) * group):
            total += parts_ref[e].astype(jnp.float32)
        key_ref[:, k * width : (k + 1) * width] = total[:, :width].astype(jnp.bfloat16)
        value_ref[:, k * width : (k + 1) * width] = total[:, width:].astype(jnp.bfloat16)


def block_terms(terms):
    cycle = lax.axis_size("ctx")
    total = terms[0].astype(jnp.float32)
    for step in range(1, cycle):
        pairs = [(c, c - step) for c in range(step, cycle)]
        total = total + lax.ppermute(terms[step], "ctx", pairs).astype(jnp.float32)
    return total.astype(jnp.bfloat16)


def summed_terms(total, kv_columns, tiles):
    owners = lax.axis_size("exp")
    rows, columns = total.shape
    parts = lax.all_to_all(
        total.reshape(owners, rows // owners, columns),
        "exp",
        split_axis=0,
        concat_axis=0,
        tiled=True,
    )
    parts, tiles = lax.optimization_barrier((parts, tiles))
    shape = (rows // owners, kv_columns)
    out = jax.ShapeDtypeStruct(shape, jnp.bfloat16)
    key_grad, value_grad = pl.pallas_call(
        sum_kernel,
        out_shape=(out, out),
        grid=(1,),
        in_specs=[full(parts.shape)],
        out_specs=(full(shape), full(shape)),
        compiler_params=pltpu.CompilerParams(vmem_limit_bytes=16 * 2**20),
        name="sums",
    )(parts)
    return key_grad, value_grad, tiles


def pick_kernel(per_dev, shadow_ref, mixed_ref, sent_ref):
    for owner in range(sent_ref.shape[0]):
        host = shadow_ref[owner * per_dev]
        for j in range(1, per_dev):
            host = jnp.maximum(host, shadow_ref[owner * per_dev + j])
        sent_ref[owner] = mixed_ref[host, : sent_ref.shape[1]]


def picked_rows(shadow_list, mixed, limit):
    owners = mixed.shape[0]
    whole = pl.BlockSpec(memory_space=pltpu.VMEM)
    return pl.pallas_call(
        functools.partial(pick_kernel, shadow_list.shape[0] // owners),
        out_shape=jax.ShapeDtypeStruct((owners, limit, mixed.shape[2]), jnp.bfloat16),
        in_specs=[pl.BlockSpec(memory_space=pltpu.SMEM), whole],
        out_specs=whole,
        compiler_params=pltpu.CompilerParams(vmem_limit_bytes=4 * 2**20),
        name="picked",
    )(shadow_list, mixed)


def weight_kernel(orders, own_ref, shadow_ref, mixed_ref, hidden_ref, side_ref, weight_ref):
    owners = mixed_ref.shape[0]
    per_dev, units = hidden_ref.shape[1], hidden_ref.shape[4]
    tokens = weight_ref.shape[1] // owners
    limit = side_ref.shape[1]
    own = own_ref[0]
    earlier = (
        lax.broadcasted_iota(jnp.int32, (tokens, tokens), 0)
        < lax.broadcasted_iota(jnp.int32, (tokens, tokens), 1)
    ).astype(jnp.bfloat16)
    odd = lax.broadcasted_iota(jnp.int32, (1, tokens), 1) % 2 == 1

    def rows_at(named, rows):
        rank = jnp.dot(
            jnp.broadcast_to(named.astype(jnp.float32), (8, tokens)).astype(jnp.bfloat16),
            earlier,
            preferred_element_type=jnp.float32,
        )[:1]
        place = lax.broadcasted_iota(jnp.int32, (rows.shape[0], tokens), 0).astype(jnp.float32)
        chosen = jnp.where(jnp.logical_and(named, rank == place), 1.0, 0.0).astype(jnp.bfloat16)
        return lax.dot_general(rows, chosen, FIRST, preferred_element_type=jnp.float32)

    for i in range(owners):
        source = own ^ jnp.where(own % 2 == 0, orders[0][i], orders[1][i])
        for j in range(per_dev):
            prob = mixed_ref[source, limit + j : limit + j + 1, :tokens].astype(jnp.float32)
            named = prob > 0
            flag = shadow_ref[own * per_dev + j] >= 0
            side = jnp.logical_and(jnp.logical_and(named, odd), flag)
            here = jnp.logical_and(named, jnp.logical_not(side))
            rows = rows_at(here, hidden_ref[0, j, source]) + rows_at(
                side, side_ref[source, :, :units]
            )
            weight_ref[j * units : (j + 1) * units, i * tokens : (i + 1) * tokens] = (
                rows * prob
            ).astype(jnp.bfloat16)


def weighted_rows(own_index, shadow_list, mixed, hidden, shadow_rows, tokens, orders):
    owners = mixed.shape[0]
    per_dev, units = shadow_list.shape[0] // owners, hidden.shape[4]
    shape = (per_dev * units, owners * tokens)
    return pl.pallas_call(
        functools.partial(weight_kernel, orders),
        out_shape=jax.ShapeDtypeStruct(shape, jnp.bfloat16),
        grid_spec=pltpu.PrefetchScalarGridSpec(
            num_scalar_prefetch=2,
            grid=(1,),
            in_specs=[
                full(mixed.shape),
                full((1, per_dev) + hidden.shape[2:]),
                full(shadow_rows.shape),
            ],
            out_specs=full(shape),
        ),
        compiler_params=pltpu.CompilerParams(vmem_limit_bytes=32 * 2**20),
        name="weighted",
    )(own_index.astype(jnp.int32)[None], shadow_list, mixed, hidden, shadow_rows)


def tile_kernel(weight_ref, *refs):
    *block_refs, tile_ref, gathered_ref, held_ref, in_sems, out_sems = refs
    per_dev, units, model = tile_ref.shape
    tokens = block_refs[0].shape[0]
    steps = in_sems.shape[0]
    step = model // steps
    arriving, leaving = [], []
    for i in range(steps):
        columns = pl.ds(i * step, step)
        arriving.append(
            [
                pltpu.make_async_copy(
                    ref.at[:, columns],
                    gathered_ref.at[pl.ds(n * tokens, tokens), columns],
                    in_sems.at[i, n],
                )
                for n, ref in enumerate(block_refs)
            ]
        )
    for copy in arriving[0] + arriving[1]:
        copy.start()
    for i in range(steps):
        for copy in arriving[i]:
            copy.wait()
        for copy in arriving[i + 2] if i + 2 < steps else []:
            copy.start()
        columns = slice(i * step, (i + 1) * step)
        held_ref[:, columns] = jnp.dot(
            weight_ref[...], gathered_ref[:, columns], preferred_element_type=jnp.float32
        )
        for j in range(per_dev):
            leaving.append(
                pltpu.make_async_copy(
                    held_ref.at[pl.ds(j * units, units), pl.ds(i * step, step)],
                    tile_ref.at[j, :, pl.ds(i * step, step)],
                    out_sems.at[i, j],
                )
            )
            leaving[-1].start()
    for copy in leaving:
        copy.wait()


def tile_sums(weighted, blocks, per_dev):
    tokens, model = blocks[0].shape
    rows = weighted.shape[0]
    steps = model // 1024
    anywhere = pl.BlockSpec(memory_space=pl.ANY)
    return pl.pallas_call(
        tile_kernel,
        out_shape=jax.ShapeDtypeStruct((per_dev, rows // per_dev, model), jnp.float32),
        in_specs=[pl.BlockSpec(memory_space=pltpu.VMEM)] + [anywhere] * len(blocks),
        out_specs=anywhere,
        scratch_shapes=[
            pltpu.VMEM((len(blocks) * tokens, model), jnp.bfloat16),
            pltpu.VMEM((rows, model), jnp.float32),
            pltpu.SemaphoreType.DMA((steps, len(blocks))),
            pltpu.SemaphoreType.DMA((steps, per_dev)),
        ],
        compiler_params=pltpu.CompilerParams(vmem_limit_bytes=32 * 2**20),
        name="tiles",
    )(weighted, *blocks)


def swapped(value):
    return lax.all_to_all(value, "exp", split_axis=0, concat_axis=0, tiled=True)


def source_rows(expert_ids, route_probs, shadow_list, stored_hidden_state):
    owners = lax.axis_size("exp")
    tokens = expert_ids.shape[0]
    count = shadow_list.shape[0]
    per_dev = count // owners
    capacity, units = stored_hidden_state.shape[3:]
    hit = expert_ids[:, None, :] == jnp.arange(count, dtype=jnp.int32)[None, :, None]
    table = jnp.sum(
        jnp.where(hit, route_probs[:, None, :].astype(jnp.float32), 0.0), axis=2
    ).astype(jnp.bfloat16)
    table = table.T.reshape(owners, per_dev, tokens)
    used = min(capacity, tokens // 2)
    limit = -(-used // 16) * 16
    lanes = max(units, tokens)
    rows = jnp.pad(
        stored_hidden_state[0, per_dev, :, :used],
        ((0, 0), (0, limit - used), (0, lanes - units)),
    )
    return jnp.concatenate([rows, jnp.pad(table, ((0, 0), (0, 0), (0, lanes - tokens)))], axis=1)


def expert_rows(mixed, shadow_rows, shadow_list, stored_hidden_state, tokens):
    steps = block_steps(lax.axis_size("exp"))
    orders = [
        [step ^ turn for pair in zip(steps[core], steps[1 - core]) for step, turn in zip(pair, (0, 1))]
        for core in range(2)
    ]
    own_index = lax.axis_index("exp")
    return weighted_rows(
        own_index, shadow_list, mixed, stored_hidden_state, shadow_rows, tokens, orders
    )


def block_steps(owners):
    masks = [1 << bit for bit in range(1, owners.bit_length() - 1)]
    steps = []
    for core in range(2):
        first, second = masks[1 - core], masks[core]
        held = [0, first, second, first ^ second]
        for mask in masks[2:]:
            held = held + [step ^ mask for step in held]
        steps.append(held)
    return steps


def moved(value, steps):
    owners = lax.axis_size("exp")
    return lax.ppermute(value, "exp", [(e, e ^ steps[e % 2]) for e in range(owners)])


def after(value, *others):
    return lax.optimization_barrier((value, others))[0]


def beside(block):
    return moved(block, (1, 1))


def all_blocks(held):
    steps = block_steps(lax.axis_size("exp"))[0]
    for turn in range(len(steps).bit_length() - 3):
        mask = steps[4 << turn]
        more = [moved(part, (mask, mask)) for part, _ in held]
        held = held + [(part, beside(part)) for part in more]
    return [block for pair in held for block in pair]


def local(
    queries,
    keys,
    values,
    attn_out,
    attn_out_grad,
    lse_excess,
    block_mask,
    expert_ids,
    route_probs,
    moe_grad,
    shadow_list,
    stored_hidden_state,
):
    steps = block_steps(lax.axis_size("exp"))
    tokens = expert_ids.shape[0]
    per_dev = shadow_list.shape[0] // lax.axis_size("exp")
    first = moved(moe_grad, [held[1] for held in steps])
    second = moved(moe_grad, [held[2] for held in steps])
    payload = source_rows(expert_ids, route_probs, shadow_list, stored_hidden_state)
    mixed = swapped(payload)
    arrived = key_blocks(after(keys, payload), values, queries.shape[1] // lse_excess.shape[0])
    query_grad, terms = attention(
        queries, arrived, attn_out, attn_out_grad, lse_excess, block_mask
    )
    total = block_terms(terms)
    far = moved(after(first, query_grad), [held[2] for held in steps])
    mixed, _ = lax.optimization_barrier((mixed, query_grad))
    sent = picked_rows(shadow_list, mixed, payload.shape[1] - per_dev)
    sent, first, second = lax.optimization_barrier((sent, first, second))
    shadow_rows = swapped(sent)
    shadow_rows, total = lax.optimization_barrier((shadow_rows, total))
    weighted = expert_rows(mixed, shadow_rows, shadow_list, stored_hidden_state, tokens)
    far = after(far, weighted)
    blocks = all_blocks([(block, beside(block)) for block in (moe_grad, first, second, far)])
    tiles = tile_sums(weighted, blocks, per_dev)
    key_grad, value_grad, expert_grad = summed_terms(total, keys.shape[1], tiles)
    return (query_grad, key_grad, value_grad, expert_grad)


def solution(mesh):
    placed = (
        P("ctx", "exp"),
        P("ctx", None),
        P("ctx", None),
        P("ctx", "exp"),
        P("ctx", "exp"),
        P("exp", "ctx"),
        P(),
        P("exp", None),
        P("exp", None),
        P("exp", None),
        P(),
        P("exp", None, None, None, "ctx"),
    )
    return jax.shard_map(
        local,
        mesh=mesh,
        in_specs=placed,
        out_specs=(
            P("ctx", "exp"),
            P(("ctx", "exp"), None),
            P(("ctx", "exp"), None),
            P("exp", "ctx", None),
        ),
        check_vma=False,
    )
```

```python
import functools
import math

import jax
import jax.numpy as jnp
from jax import lax
from jax.experimental import pallas as pl
from jax.experimental.pallas import tpu as pltpu
from jax.sharding import PartitionSpec as P

LAST = (((1,), (1,)), ((), ()))
FIRST = (((0,), (0,)), ((), ()))


def full(shape):
    return pl.BlockSpec(shape, lambda *at: (0,) * len(shape))


def attention_kernel(
    place_ref, mask_ref, query_ref, grad_ref, out_ref, lse_ref, *rest
):
    cycle = mask_ref.shape[0]
    pair_refs, (query_grad_ref, terms_ref, sums_ref, pairs_ref) = rest[:cycle], rest[cycle:]
    rows, width = pairs_ref.shape[1], pairs_ref.shape[2] // 2
    heads = lse_ref.shape[0]
    scale = 1.0 / math.sqrt(width)
    mine = place_ref[0]
    offset = 0.5 * math.log(rows) + lse_ref[...]
    spans = [slice(h * width, (h + 1) * width) for h in range(heads)]
    for step, pair_ref in enumerate(pair_refs):
        pairs_ref[step] = pair_ref[...]
    delta = []
    for span in spans:
        both = grad_ref[:, span].astype(jnp.float32) * out_ref[:, span].astype(jnp.float32)
        delta.append(jnp.sum(both.T, axis=0, keepdims=True))

    def block(step, diagonal):
        key, value = pairs_ref[step, :, :width], pairs_ref[step, :, width:]
        probs, slopes = [], []
        for h, span in enumerate(spans):
            query, grad = query_ref[:, span], grad_ref[:, span]
            scores = lax.dot_general(key, query, LAST, preferred_element_type=jnp.float32)
            prob = jnp.exp(scores * scale - offset[h : h + 1])
            if diagonal:
                at_key = lax.broadcasted_iota(jnp.int32, (rows, rows), 0)
                at_query = lax.broadcasted_iota(jnp.int32, (rows, rows), 1)
                prob = jnp.where(at_key <= at_query, prob, 0.0)
            prob_grad = lax.dot_general(value, grad, LAST, preferred_element_type=jnp.float32)
            slope = (prob * (prob_grad - delta[h]) * scale).astype(jnp.bfloat16)
            probs.append(prob.astype(jnp.bfloat16))
            slopes.append(slope)
            query_term = lax.dot_general(slope, key, FIRST, preferred_element_type=jnp.float32)
            if diagonal:
                sums_ref[:, span] = query_term
            else:
                sums_ref[:, span] += query_term
        queries = jnp.concatenate([query_ref[:, span] for span in spans], axis=0)
        grads = jnp.concatenate([grad_ref[:, span] for span in spans], axis=0)
        key_term = jnp.dot(
            jnp.concatenate(slopes, axis=1), queries, preferred_element_type=jnp.float32
        )
        value_term = jnp.dot(
            jnp.concatenate(probs, axis=1), grads, preferred_element_type=jnp.float32
        )
        terms_ref[mine - step, :, :width] = key_term.astype(jnp.bfloat16)
        terms_ref[mine - step, :, width:] = value_term.astype(jnp.bfloat16)

    block(0, True)

    @pl.loop(0, cycle)
    def _(source):
        seen = jnp.logical_and(source < mine, mask_ref[mine, source] > 0)

        @pl.when(seen)
        def _():
            block(mine - source, False)

        @pl.when(jnp.logical_and(source != mine, jnp.logical_not(seen)))
        def _():
            terms_ref[source] = jnp.zeros_like(terms_ref[source])

    query_grad_ref[...] = sums_ref[...].astype(jnp.bfloat16)


def key_blocks(keys, values, width):
    cycle = lax.axis_size("ctx")
    owners = lax.axis_size("exp")
    kv_count = keys.shape[1] // width
    kv_head = lax.axis_index("exp") * kv_count // owners
    pair = jnp.concatenate(
        [
            lax.dynamic_slice_in_dim(keys, kv_head * width, width, 1),
            lax.dynamic_slice_in_dim(values, kv_head * width, width, 1),
        ],
        axis=1,
    )
    return [pair] + [
        lax.ppermute(pair, "ctx", [(c, c + step) for c in range(cycle - step)])
        for step in range(1, cycle)
    ]


def attention(queries, arrived, attn_out, attn_out_grad, lse_excess, block_mask):
    cycle = lax.axis_size("ctx")
    mine = lax.axis_index("ctx")
    pair = arrived[0]
    operands = (queries, attn_out_grad, attn_out, lse_excess, *arrived)
    return pl.pallas_call(
        attention_kernel,
        out_shape=(
            jax.ShapeDtypeStruct(queries.shape, jnp.bfloat16),
            jax.ShapeDtypeStruct((cycle,) + pair.shape, jnp.bfloat16),
        ),
        grid_spec=pltpu.PrefetchScalarGridSpec(
            num_scalar_prefetch=2,
            grid=(1,),
            in_specs=[full(operand.shape) for operand in operands],
            out_specs=(full(queries.shape), full((cycle,) + pair.shape)),
            scratch_shapes=[
                pltpu.VMEM(queries.shape, jnp.float32),
                pltpu.VMEM((cycle,) + pair.shape, jnp.bfloat16),
            ],
        ),
        compiler_params=pltpu.CompilerParams(vmem_limit_bytes=32 * 2**20),
        name="attention",
    )(mine.astype(jnp.int32)[None], block_mask, *operands)


def sum_kernel(parts_ref, key_ref, value_ref):
    cycle, owners, rows, columns = parts_ref.shape
    kv_count = key_ref.shape[1] * 2 // columns
    group = owners // kv_count
    width = columns // 2
    for k in range(kv_count):
        total = jnp.zeros((rows, columns), jnp.float32)
        for c in range(cycle):
            for e in range(k * group, (k + 1) * group):
                total += parts_ref[c, e].astype(jnp.float32)
        key_ref[:, k * width : (k + 1) * width] = total[:, :width].astype(jnp.bfloat16)
        value_ref[:, k * width : (k + 1) * width] = total[:, width:].astype(jnp.bfloat16)


def summed_terms(terms, kv_columns, tiles):
    cycle, owners = lax.axis_size("ctx"), lax.axis_size("exp")
    rows, columns = terms.shape[1:]
    parts = lax.all_to_all(
        terms.reshape(cycle * owners, rows // owners, columns),
        ("ctx", "exp"),
        split_axis=0,
        concat_axis=0,
        tiled=True,
    ).reshape(cycle, owners, rows // owners, columns)
    parts, tiles = lax.optimization_barrier((parts, tiles))
    shape = (rows // owners, kv_columns)
    out = jax.ShapeDtypeStruct(shape, jnp.bfloat16)
    key_grad, value_grad = pl.pallas_call(
        sum_kernel,
        out_shape=(out, out),
        grid=(1,),
        in_specs=[full(parts.shape)],
        out_specs=(full(shape), full(shape)),
        compiler_params=pltpu.CompilerParams(vmem_limit_bytes=16 * 2**20),
        name="sums",
    )(parts)
    return key_grad, value_grad, tiles


def pick_kernel(per_dev, shadow_ref, mixed_ref, sent_ref):
    for owner in range(sent_ref.shape[0]):
        host = shadow_ref[owner * per_dev]
        for j in range(1, per_dev):
            host = jnp.maximum(host, shadow_ref[owner * per_dev + j])
        sent_ref[owner] = mixed_ref[host, : sent_ref.shape[1]]


def picked_rows(shadow_list, mixed, limit):
    owners = mixed.shape[0]
    whole = pl.BlockSpec(memory_space=pltpu.VMEM)
    return pl.pallas_call(
        functools.partial(pick_kernel, shadow_list.shape[0] // owners),
        out_shape=jax.ShapeDtypeStruct((owners, limit, mixed.shape[2]), jnp.bfloat16),
        in_specs=[pl.BlockSpec(memory_space=pltpu.SMEM), whole],
        out_specs=whole,
        compiler_params=pltpu.CompilerParams(vmem_limit_bytes=4 * 2**20),
        name="picked",
    )(shadow_list, mixed)


def weight_kernel(orders, own_ref, shadow_ref, mixed_ref, hidden_ref, side_ref, weight_ref):
    owners = mixed_ref.shape[0]
    per_dev, units = hidden_ref.shape[1], hidden_ref.shape[4]
    tokens = weight_ref.shape[1] // owners
    limit = side_ref.shape[1]
    own = own_ref[0]
    earlier = (
        lax.broadcasted_iota(jnp.int32, (tokens, tokens), 0)
        < lax.broadcasted_iota(jnp.int32, (tokens, tokens), 1)
    ).astype(jnp.bfloat16)
    odd = lax.broadcasted_iota(jnp.int32, (1, tokens), 1) % 2 == 1

    def rows_at(named, rows):
        rank = jnp.dot(
            jnp.broadcast_to(named.astype(jnp.float32), (8, tokens)).astype(jnp.bfloat16),
            earlier,
            preferred_element_type=jnp.float32,
        )[:1]
        place = lax.broadcasted_iota(jnp.int32, (rows.shape[0], tokens), 0).astype(jnp.float32)
        chosen = jnp.where(jnp.logical_and(named, rank == place), 1.0, 0.0).astype(jnp.bfloat16)
        return lax.dot_general(rows, chosen, FIRST, preferred_element_type=jnp.float32)

    for i in range(owners):
        source = own ^ jnp.where(own % 2 == 0, orders[0][i], orders[1][i])
        for j in range(per_dev):
            prob = mixed_ref[source, limit + j : limit + j + 1, :tokens].astype(jnp.float32)
            named = prob > 0
            flag = shadow_ref[own * per_dev + j] >= 0
            side = jnp.logical_and(jnp.logical_and(named, odd), flag)
            here = jnp.logical_and(named, jnp.logical_not(side))
            rows = rows_at(here, hidden_ref[0, j, source]) + rows_at(
                side, side_ref[source, :, :units]
            )
            weight_ref[j * units : (j + 1) * units, i * tokens : (i + 1) * tokens] = (
                rows * prob
            ).astype(jnp.bfloat16)


def weighted_rows(own_index, shadow_list, mixed, hidden, shadow_rows, tokens, orders):
    owners = mixed.shape[0]
    per_dev, units = shadow_list.shape[0] // owners, hidden.shape[4]
    shape = (per_dev * units, owners * tokens)
    return pl.pallas_call(
        functools.partial(weight_kernel, orders),
        out_shape=jax.ShapeDtypeStruct(shape, jnp.bfloat16),
        grid_spec=pltpu.PrefetchScalarGridSpec(
            num_scalar_prefetch=2,
            grid=(1,),
            in_specs=[
                full(mixed.shape),
                full((1, per_dev) + hidden.shape[2:]),
                full(shadow_rows.shape),
            ],
            out_specs=full(shape),
        ),
        compiler_params=pltpu.CompilerParams(vmem_limit_bytes=32 * 2**20),
        name="weighted",
    )(own_index.astype(jnp.int32)[None], shadow_list, mixed, hidden, shadow_rows)


def tile_kernel(weight_ref, *refs):
    *block_refs, tile_ref, gathered_ref, held_ref, in_sems, out_sems = refs
    per_dev, units, model = tile_ref.shape
    tokens = block_refs[0].shape[0]
    steps = in_sems.shape[0]
    step = model // steps
    arriving, leaving = [], []
    for i in range(steps):
        columns = pl.ds(i * step, step)
        arriving.append(
            [
                pltpu.make_async_copy(
                    ref.at[:, columns],
                    gathered_ref.at[pl.ds(n * tokens, tokens), columns],
                    in_sems.at[i, n],
                )
                for n, ref in enumerate(block_refs)
            ]
        )
    for copy in arriving[0] + arriving[1]:
        copy.start()
    for i in range(steps):
        for copy in arriving[i]:
            copy.wait()
        for copy in arriving[i + 2] if i + 2 < steps else []:
            copy.start()
        columns = slice(i * step, (i + 1) * step)
        held_ref[:, columns] = jnp.dot(
            weight_ref[...], gathered_ref[:, columns], preferred_element_type=jnp.float32
        )
        for j in range(per_dev):
            leaving.append(
                pltpu.make_async_copy(
                    held_ref.at[pl.ds(j * units, units), pl.ds(i * step, step)],
                    tile_ref.at[j, :, pl.ds(i * step, step)],
                    out_sems.at[i, j],
                )
            )
            leaving[-1].start()
    for copy in leaving:
        copy.wait()


def tile_sums(weighted, blocks, per_dev):
    tokens, model = blocks[0].shape
    rows = weighted.shape[0]
    steps = model // 1024
    anywhere = pl.BlockSpec(memory_space=pl.ANY)
    return pl.pallas_call(
        tile_kernel,
        out_shape=jax.ShapeDtypeStruct((per_dev, rows // per_dev, model), jnp.float32),
        in_specs=[pl.BlockSpec(memory_space=pltpu.VMEM)] + [anywhere] * len(blocks),
        out_specs=anywhere,
        scratch_shapes=[
            pltpu.VMEM((len(blocks) * tokens, model), jnp.bfloat16),
            pltpu.VMEM((rows, model), jnp.float32),
            pltpu.SemaphoreType.DMA((steps, len(blocks))),
            pltpu.SemaphoreType.DMA((steps, per_dev)),
        ],
        compiler_params=pltpu.CompilerParams(vmem_limit_bytes=32 * 2**20),
        name="tiles",
    )(weighted, *blocks)


def swapped(value):
    return lax.all_to_all(value, "exp", split_axis=0, concat_axis=0, tiled=True)


def source_rows(expert_ids, route_probs, shadow_list, stored_hidden_state):
    owners = lax.axis_size("exp")
    tokens = expert_ids.shape[0]
    count = shadow_list.shape[0]
    per_dev = count // owners
    capacity, units = stored_hidden_state.shape[3:]
    hit = expert_ids[:, None, :] == jnp.arange(count, dtype=jnp.int32)[None, :, None]
    table = jnp.sum(
        jnp.where(hit, route_probs[:, None, :].astype(jnp.float32), 0.0), axis=2
    ).astype(jnp.bfloat16)
    table = table.T.reshape(owners, per_dev, tokens)
    used = min(capacity, tokens // 2)
    limit = -(-used // 16) * 16
    lanes = max(units, tokens)
    rows = jnp.pad(
        stored_hidden_state[0, per_dev, :, :used],
        ((0, 0), (0, limit - used), (0, lanes - units)),
    )
    mixed = jnp.concatenate([rows, jnp.pad(table, ((0, 0), (0, 0), (0, lanes - tokens)))], axis=1)
    mixed = swapped(mixed)
    return mixed, picked_rows(shadow_list, mixed, limit)


def expert_rows(mixed, shadow_rows, shadow_list, stored_hidden_state, tokens):
    steps = block_steps(lax.axis_size("exp"))
    orders = [
        [step ^ turn for pair in zip(steps[core], steps[1 - core]) for step, turn in zip(pair, (0, 1))]
        for core in range(2)
    ]
    own_index = lax.axis_index("exp")
    return weighted_rows(
        own_index, shadow_list, mixed, stored_hidden_state, shadow_rows, tokens, orders
    )


def block_steps(owners):
    masks = [1 << bit for bit in range(1, owners.bit_length() - 1)]
    steps = []
    for core in range(2):
        first, second = masks[1 - core], masks[core]
        held = [0, first, second, first ^ second]
        for mask in masks[2:]:
            held = held + [step ^ mask for step in held]
        steps.append(held)
    return steps


def moved(value, steps):
    owners = lax.axis_size("exp")
    return lax.ppermute(value, "exp", [(e, e ^ steps[e % 2]) for e in range(owners)])


def expert_tiles(weighted, near, per_dev):
    owners = lax.axis_size("exp")
    steps = block_steps(owners)
    far = moved(near[1], [held[2] for held in steps])
    held = list(near)
    blocks = [block for part in held for block in (part, moved(part, (1, 1)))]
    far, _ = lax.optimization_barrier((far, weighted))
    held = held + [far]
    rest = [far]
    for turn in range(len(steps[0]).bit_length() - 3):
        mask = steps[0][4 << turn]
        more = [moved(part, (mask, mask)) for part in held]
        held, rest = held + more, rest + more
    rest = [block for part in rest for block in (part, moved(part, (1, 1)))]
    return tile_sums(weighted, blocks + rest, per_dev)


def local(
    queries,
    keys,
    values,
    attn_out,
    attn_out_grad,
    lse_excess,
    block_mask,
    expert_ids,
    route_probs,
    moe_grad,
    shadow_list,
    stored_hidden_state,
):
    steps = block_steps(lax.axis_size("exp"))
    first = moved(moe_grad, [held[1] for held in steps])
    arrived = key_blocks(keys, values, queries.shape[1] // lse_excess.shape[0])
    mixed, sent = source_rows(expert_ids, route_probs, shadow_list, stored_hidden_state)
    ready, mixed = lax.optimization_barrier((moe_grad, mixed))
    second = moved(ready, [held[2] for held in steps])
    sent, arrived = lax.optimization_barrier((sent, arrived))
    shadow_rows = swapped(sent)
    query_grad, terms = attention(
        queries, arrived, attn_out, attn_out_grad, lse_excess, block_mask
    )
    first, second, shadow_rows, query_grad = lax.optimization_barrier(
        (first, second, shadow_rows, query_grad)
    )
    weighted = expert_rows(
        mixed, shadow_rows, shadow_list, stored_hidden_state, expert_ids.shape[0]
    )
    per_dev = shadow_list.shape[0] // lax.axis_size("exp")
    tiles = expert_tiles(weighted, (moe_grad, first, second), per_dev)
    key_grad, value_grad, expert_grad = summed_terms(terms, keys.shape[1], tiles)
    return (query_grad, key_grad, value_grad, expert_grad)


def solution(mesh):
    placed = (
        P("ctx", "exp"),
        P("ctx", None),
        P("ctx", None),
        P("ctx", "exp"),
        P("ctx", "exp"),
        P("exp", "ctx"),
        P(),
        P("exp", None),
        P("exp", None),
        P("exp", None),
        P(),
        P("exp", None, None, None, "ctx"),
    )
    return jax.shard_map(
        local,
        mesh=mesh,
        in_specs=placed,
        out_specs=(
            P("ctx", "exp"),
            P(("ctx", "exp"), None),
            P(("ctx", "exp"), None),
            P("exp", "ctx", None),
        ),
        check_vma=False,
    )
```

```python
import functools
import math

import jax
import jax.numpy as jnp
from jax import lax
from jax.experimental import pallas as pl
from jax.experimental.pallas import tpu as pltpu
from jax.sharding import PartitionSpec as P

LAST = (((1,), (1,)), ((), ()))
FIRST = (((0,), (0,)), ((), ()))


def full(shape):
    return pl.BlockSpec(shape, lambda *at: (0,) * len(shape))


def attention_kernel(
    place_ref, mask_ref, query_ref, grad_ref, out_ref, lse_ref, *rest
):
    cycle = mask_ref.shape[0]
    pair_refs, (query_grad_ref, terms_ref, sums_ref, pairs_ref) = rest[:cycle], rest[cycle:]
    rows, width = pairs_ref.shape[1], pairs_ref.shape[2] // 2
    heads = lse_ref.shape[0]
    scale = 1.0 / math.sqrt(width)
    mine = place_ref[0]
    offset = 0.5 * math.log(rows) + lse_ref[...]
    spans = [slice(h * width, (h + 1) * width) for h in range(heads)]
    for step, pair_ref in enumerate(pair_refs):
        pairs_ref[step] = pair_ref[...]
    delta = []
    for span in spans:
        both = grad_ref[:, span].astype(jnp.float32) * out_ref[:, span].astype(jnp.float32)
        delta.append(jnp.sum(both.T, axis=0, keepdims=True))

    def block(step, diagonal):
        key, value = pairs_ref[step, :, :width], pairs_ref[step, :, width:]
        probs, slopes = [], []
        for h, span in enumerate(spans):
            query, grad = query_ref[:, span], grad_ref[:, span]
            scores = lax.dot_general(key, query, LAST, preferred_element_type=jnp.float32)
            prob = jnp.exp(scores * scale - offset[h : h + 1])
            if diagonal:
                at_key = lax.broadcasted_iota(jnp.int32, (rows, rows), 0)
                at_query = lax.broadcasted_iota(jnp.int32, (rows, rows), 1)
                prob = jnp.where(at_key <= at_query, prob, 0.0)
            prob_grad = lax.dot_general(value, grad, LAST, preferred_element_type=jnp.float32)
            slope = (prob * (prob_grad - delta[h]) * scale).astype(jnp.bfloat16)
            probs.append(prob.astype(jnp.bfloat16))
            slopes.append(slope)
            query_term = lax.dot_general(slope, key, FIRST, preferred_element_type=jnp.float32)
            if diagonal:
                sums_ref[:, span] = query_term
            else:
                sums_ref[:, span] += query_term
        queries = jnp.concatenate([query_ref[:, span] for span in spans], axis=0)
        grads = jnp.concatenate([grad_ref[:, span] for span in spans], axis=0)
        key_term = jnp.dot(
            jnp.concatenate(slopes, axis=1), queries, preferred_element_type=jnp.float32
        )
        value_term = jnp.dot(
            jnp.concatenate(probs, axis=1), grads, preferred_element_type=jnp.float32
        )
        terms_ref[mine - step, :, :width] = key_term.astype(jnp.bfloat16)
        terms_ref[mine - step, :, width:] = value_term.astype(jnp.bfloat16)

    block(0, True)

    @pl.loop(0, cycle)
    def _(source):
        seen = jnp.logical_and(source < mine, mask_ref[mine, source] > 0)

        @pl.when(seen)
        def _():
            block(mine - source, False)

        @pl.when(jnp.logical_and(source != mine, jnp.logical_not(seen)))
        def _():
            terms_ref[source] = jnp.zeros_like(terms_ref[source])

    query_grad_ref[...] = sums_ref[...].astype(jnp.bfloat16)


def key_blocks(keys, values, width):
    cycle = lax.axis_size("ctx")
    owners = lax.axis_size("exp")
    kv_count = keys.shape[1] // width
    kv_head = lax.axis_index("exp") * kv_count // owners
    pair = jnp.concatenate(
        [
            lax.dynamic_slice_in_dim(keys, kv_head * width, width, 1),
            lax.dynamic_slice_in_dim(values, kv_head * width, width, 1),
        ],
        axis=1,
    )
    return [pair] + [
        lax.ppermute(pair, "ctx", [(c, c + step) for c in range(cycle - step)])
        for step in range(1, cycle)
    ]


def attention(queries, arrived, attn_out, attn_out_grad, lse_excess, block_mask):
    cycle = lax.axis_size("ctx")
    mine = lax.axis_index("ctx")
    pair = arrived[0]
    operands = (queries, attn_out_grad, attn_out, lse_excess, *arrived)
    return pl.pallas_call(
        attention_kernel,
        out_shape=(
            jax.ShapeDtypeStruct(queries.shape, jnp.bfloat16),
            jax.ShapeDtypeStruct((cycle,) + pair.shape, jnp.bfloat16),
        ),
        grid_spec=pltpu.PrefetchScalarGridSpec(
            num_scalar_prefetch=2,
            grid=(1,),
            in_specs=[full(operand.shape) for operand in operands],
            out_specs=(full(queries.shape), full((cycle,) + pair.shape)),
            scratch_shapes=[
                pltpu.VMEM(queries.shape, jnp.float32),
                pltpu.VMEM((cycle,) + pair.shape, jnp.bfloat16),
            ],
        ),
        compiler_params=pltpu.CompilerParams(vmem_limit_bytes=32 * 2**20),
        name="attention",
    )(mine.astype(jnp.int32)[None], block_mask, *operands)


def sum_kernel(parts_ref, key_ref, value_ref):
    cycle, owners, rows, columns = parts_ref.shape
    kv_count = key_ref.shape[1] * 2 // columns
    group = owners // kv_count
    width = columns // 2
    for k in range(kv_count):
        total = jnp.zeros((rows, columns), jnp.float32)
        for c in range(cycle):
            for e in range(k * group, (k + 1) * group):
                total += parts_ref[c, e].astype(jnp.float32)
        key_ref[:, k * width : (k + 1) * width] = total[:, :width].astype(jnp.bfloat16)
        value_ref[:, k * width : (k + 1) * width] = total[:, width:].astype(jnp.bfloat16)


def summed_terms(terms, kv_columns, tiles):
    cycle, owners = lax.axis_size("ctx"), lax.axis_size("exp")
    rows, columns = terms.shape[1:]
    parts = lax.all_to_all(
        terms.reshape(cycle * owners, rows // owners, columns),
        ("ctx", "exp"),
        split_axis=0,
        concat_axis=0,
        tiled=True,
    ).reshape(cycle, owners, rows // owners, columns)
    parts, tiles = lax.optimization_barrier((parts, tiles))
    shape = (rows // owners, kv_columns)
    out = jax.ShapeDtypeStruct(shape, jnp.bfloat16)
    key_grad, value_grad = pl.pallas_call(
        sum_kernel,
        out_shape=(out, out),
        grid=(1,),
        in_specs=[full(parts.shape)],
        out_specs=(full(shape), full(shape)),
        compiler_params=pltpu.CompilerParams(vmem_limit_bytes=16 * 2**20),
        name="sums",
    )(parts)
    return key_grad, value_grad, tiles


def pick_kernel(per_dev, shadow_ref, mixed_ref, sent_ref):
    for owner in range(sent_ref.shape[0]):
        host = shadow_ref[owner * per_dev]
        for j in range(1, per_dev):
            host = jnp.maximum(host, shadow_ref[owner * per_dev + j])
        sent_ref[owner] = mixed_ref[host, : sent_ref.shape[1]]


def picked_rows(shadow_list, mixed, limit):
    owners = mixed.shape[0]
    whole = pl.BlockSpec(memory_space=pltpu.VMEM)
    return pl.pallas_call(
        functools.partial(pick_kernel, shadow_list.shape[0] // owners),
        out_shape=jax.ShapeDtypeStruct((owners, limit, mixed.shape[2]), jnp.bfloat16),
        in_specs=[pl.BlockSpec(memory_space=pltpu.SMEM), whole],
        out_specs=whole,
        compiler_params=pltpu.CompilerParams(vmem_limit_bytes=4 * 2**20),
        name="picked",
    )(shadow_list, mixed)


def weight_kernel(orders, own_ref, shadow_ref, mixed_ref, hidden_ref, side_ref, weight_ref):
    owners = mixed_ref.shape[0]
    per_dev, units = hidden_ref.shape[1], hidden_ref.shape[4]
    tokens = weight_ref.shape[1] // owners
    limit = side_ref.shape[1]
    own = own_ref[0]
    earlier = (
        lax.broadcasted_iota(jnp.int32, (tokens, tokens), 0)
        < lax.broadcasted_iota(jnp.int32, (tokens, tokens), 1)
    ).astype(jnp.bfloat16)
    odd = lax.broadcasted_iota(jnp.int32, (1, tokens), 1) % 2 == 1

    def rows_at(named, rows):
        rank = jnp.dot(
            jnp.broadcast_to(named.astype(jnp.float32), (8, tokens)).astype(jnp.bfloat16),
            earlier,
            preferred_element_type=jnp.float32,
        )[:1]
        place = lax.broadcasted_iota(jnp.int32, (rows.shape[0], tokens), 0).astype(jnp.float32)
        chosen = jnp.where(jnp.logical_and(named, rank == place), 1.0, 0.0).astype(jnp.bfloat16)
        return lax.dot_general(rows, chosen, FIRST, preferred_element_type=jnp.float32)

    for i in range(owners):
        source = own ^ jnp.where(own % 2 == 0, orders[0][i], orders[1][i])
        for j in range(per_dev):
            prob = mixed_ref[source, limit + j : limit + j + 1, :tokens].astype(jnp.float32)
            named = prob > 0
            flag = shadow_ref[own * per_dev + j] >= 0
            side = jnp.logical_and(jnp.logical_and(named, odd), flag)
            here = jnp.logical_and(named, jnp.logical_not(side))
            rows = rows_at(here, hidden_ref[0, j, source]) + rows_at(
                side, side_ref[source, :, :units]
            )
            weight_ref[j * units : (j + 1) * units, i * tokens : (i + 1) * tokens] = (
                rows * prob
            ).astype(jnp.bfloat16)


def weighted_rows(own_index, shadow_list, mixed, hidden, shadow_rows, tokens, orders):
    owners = mixed.shape[0]
    per_dev, units = shadow_list.shape[0] // owners, hidden.shape[4]
    shape = (per_dev * units, owners * tokens)
    return pl.pallas_call(
        functools.partial(weight_kernel, orders),
        out_shape=jax.ShapeDtypeStruct(shape, jnp.bfloat16),
        grid_spec=pltpu.PrefetchScalarGridSpec(
            num_scalar_prefetch=2,
            grid=(1,),
            in_specs=[
                full(mixed.shape),
                full((1, per_dev) + hidden.shape[2:]),
                full(shadow_rows.shape),
            ],
            out_specs=full(shape),
        ),
        compiler_params=pltpu.CompilerParams(vmem_limit_bytes=32 * 2**20),
        name="weighted",
    )(own_index.astype(jnp.int32)[None], shadow_list, mixed, hidden, shadow_rows)


def tile_kernel(weight_ref, *refs):
    *block_refs, tile_ref, gathered_ref, held_ref, in_sems, out_sems = refs
    per_dev, units, model = tile_ref.shape
    tokens = block_refs[0].shape[0]
    steps = in_sems.shape[0]
    step = model // steps
    arriving, leaving = [], []
    for i in range(steps):
        columns = pl.ds(i * step, step)
        arriving.append(
            [
                pltpu.make_async_copy(
                    ref.at[:, columns],
                    gathered_ref.at[pl.ds(n * tokens, tokens), columns],
                    in_sems.at[i, n],
                )
                for n, ref in enumerate(block_refs)
            ]
        )
    for copy in arriving[0] + arriving[1]:
        copy.start()
    for i in range(steps):
        for copy in arriving[i]:
            copy.wait()
        for copy in arriving[i + 2] if i + 2 < steps else []:
            copy.start()
        columns = slice(i * step, (i + 1) * step)
        held_ref[:, columns] = jnp.dot(
            weight_ref[...], gathered_ref[:, columns], preferred_element_type=jnp.float32
        )
        for j in range(per_dev):
            leaving.append(
                pltpu.make_async_copy(
                    held_ref.at[pl.ds(j * units, units), pl.ds(i * step, step)],
                    tile_ref.at[j, :, pl.ds(i * step, step)],
                    out_sems.at[i, j],
                )
            )
            leaving[-1].start()
    for copy in leaving:
        copy.wait()


def tile_sums(weighted, blocks, per_dev):
    tokens, model = blocks[0].shape
    rows = weighted.shape[0]
    steps = model // 1024
    anywhere = pl.BlockSpec(memory_space=pl.ANY)
    return pl.pallas_call(
        tile_kernel,
        out_shape=jax.ShapeDtypeStruct((per_dev, rows // per_dev, model), jnp.float32),
        in_specs=[pl.BlockSpec(memory_space=pltpu.VMEM)] + [anywhere] * len(blocks),
        out_specs=anywhere,
        scratch_shapes=[
            pltpu.VMEM((len(blocks) * tokens, model), jnp.bfloat16),
            pltpu.VMEM((rows, model), jnp.float32),
            pltpu.SemaphoreType.DMA((steps, len(blocks))),
            pltpu.SemaphoreType.DMA((steps, per_dev)),
        ],
        compiler_params=pltpu.CompilerParams(vmem_limit_bytes=32 * 2**20),
        name="tiles",
    )(weighted, *blocks)


def swapped(value):
    return lax.all_to_all(value, "exp", split_axis=0, concat_axis=0, tiled=True)


def source_rows(expert_ids, route_probs, shadow_list, stored_hidden_state):
    owners = lax.axis_size("exp")
    tokens = expert_ids.shape[0]
    count = shadow_list.shape[0]
    per_dev = count // owners
    capacity, units = stored_hidden_state.shape[3:]
    hit = expert_ids[:, None, :] == jnp.arange(count, dtype=jnp.int32)[None, :, None]
    table = jnp.sum(
        jnp.where(hit, route_probs[:, None, :].astype(jnp.float32), 0.0), axis=2
    ).astype(jnp.bfloat16)
    table = table.T.reshape(owners, per_dev, tokens)
    used = min(capacity, tokens // 2)
    limit = -(-used // 16) * 16
    lanes = max(units, tokens)
    rows = jnp.pad(
        stored_hidden_state[0, per_dev, :, :used],
        ((0, 0), (0, limit - used), (0, lanes - units)),
    )
    mixed = jnp.concatenate([rows, jnp.pad(table, ((0, 0), (0, 0), (0, lanes - tokens)))], axis=1)
    mixed = swapped(mixed)
    return mixed, picked_rows(shadow_list, mixed, limit)


def expert_rows(mixed, shadow_rows, shadow_list, stored_hidden_state, tokens):
    steps = block_steps(lax.axis_size("exp"))
    orders = [
        [step ^ turn for pair in zip(steps[core], steps[1 - core]) for step, turn in zip(pair, (0, 1))]
        for core in range(2)
    ]
    own_index = lax.axis_index("exp")
    return weighted_rows(
        own_index, shadow_list, mixed, stored_hidden_state, shadow_rows, tokens, orders
    )


def block_steps(owners):
    masks = [1 << bit for bit in range(1, owners.bit_length() - 1)]
    steps = []
    for core in range(2):
        first, second = masks[1 - core], masks[core]
        held = [0, first, second, first ^ second]
        for mask in masks[2:]:
            held = held + [step ^ mask for step in held]
        steps.append(held)
    return steps


def moved(value, steps):
    owners = lax.axis_size("exp")
    return lax.ppermute(value, "exp", [(e, e ^ steps[e % 2]) for e in range(owners)])


def expert_tiles(weighted, near, per_dev):
    owners = lax.axis_size("exp")
    steps = block_steps(owners)
    far = moved(near[1], [held[2] for held in steps])
    held = list(near)
    blocks = [block for part in held for block in (part, moved(part, (1, 1)))]
    far, _ = lax.optimization_barrier((far, weighted))
    held = held + [far]
    rest = [far]
    for turn in range(len(steps[0]).bit_length() - 3):
        mask = steps[0][4 << turn]
        more = [moved(part, (mask, mask)) for part in held]
        held, rest = held + more, rest + more
    rest = [block for part in rest for block in (part, moved(part, (1, 1)))]
    return tile_sums(weighted, blocks + rest, per_dev)


def local(
    queries,
    keys,
    values,
    attn_out,
    attn_out_grad,
    lse_excess,
    block_mask,
    expert_ids,
    route_probs,
    moe_grad,
    shadow_list,
    stored_hidden_state,
):
    steps = block_steps(lax.axis_size("exp"))
    first = moved(moe_grad, [held[1] for held in steps])
    arrived = key_blocks(keys, values, queries.shape[1] // lse_excess.shape[0])
    mixed, sent = source_rows(expert_ids, route_probs, shadow_list, stored_hidden_state)
    ready, mixed = lax.optimization_barrier((moe_grad, mixed))
    second = moved(ready, [held[2] for held in steps])
    shadow_rows = swapped(sent)
    arrived, _ = lax.optimization_barrier((arrived, sent))
    query_grad, terms = attention(
        queries, arrived, attn_out, attn_out_grad, lse_excess, block_mask
    )
    first, second, shadow_rows, query_grad = lax.optimization_barrier(
        (first, second, shadow_rows, query_grad)
    )
    weighted = expert_rows(
        mixed, shadow_rows, shadow_list, stored_hidden_state, expert_ids.shape[0]
    )
    per_dev = shadow_list.shape[0] // lax.axis_size("exp")
    tiles = expert_tiles(weighted, (moe_grad, first, second), per_dev)
    key_grad, value_grad, expert_grad = summed_terms(terms, keys.shape[1], tiles)
    return (query_grad, key_grad, value_grad, expert_grad)


def solution(mesh):
    placed = (
        P("ctx", "exp"),
        P("ctx", None),
        P("ctx", None),
        P("ctx", "exp"),
        P("ctx", "exp"),
        P("exp", "ctx"),
        P(),
        P("exp", None),
        P("exp", None),
        P("exp", None),
        P(),
        P("exp", None, None, None, "ctx"),
    )
    return jax.shard_map(
        local,
        mesh=mesh,
        in_specs=placed,
        out_specs=(
            P("ctx", "exp"),
            P(("ctx", "exp"), None),
            P(("ctx", "exp"), None),
            P("exp", "ctx", None),
        ),
        check_vma=False,
    )
```

```python
import functools
import math

import jax
import jax.numpy as jnp
from jax import lax
from jax.experimental import pallas as pl
from jax.experimental.pallas import tpu as pltpu
from jax.sharding import PartitionSpec as P

LAST = (((1,), (1,)), ((), ()))
FIRST = (((0,), (0,)), ((), ()))


def full(shape):
    return pl.BlockSpec(shape, lambda *at: (0,) * len(shape))


def attention_kernel(
    place_ref, mask_ref, query_ref, grad_ref, out_ref, lse_ref, *rest
):
    cycle = mask_ref.shape[0]
    pair_refs, (query_grad_ref, terms_ref, sums_ref, pairs_ref) = rest[:cycle], rest[cycle:]
    rows, width = pairs_ref.shape[1], pairs_ref.shape[2] // 2
    heads = lse_ref.shape[0]
    scale = 1.0 / math.sqrt(width)
    mine = place_ref[0]
    offset = 0.5 * math.log(rows) + lse_ref[...]
    spans = [slice(h * width, (h + 1) * width) for h in range(heads)]
    for step, pair_ref in enumerate(pair_refs):
        pairs_ref[step] = pair_ref[...]
    delta = []
    for span in spans:
        both = grad_ref[:, span].astype(jnp.float32) * out_ref[:, span].astype(jnp.float32)
        delta.append(jnp.sum(both.T, axis=0, keepdims=True))

    def block(step, diagonal):
        key, value = pairs_ref[step, :, :width], pairs_ref[step, :, width:]
        probs, slopes = [], []
        for h, span in enumerate(spans):
            query, grad = query_ref[:, span], grad_ref[:, span]
            scores = lax.dot_general(key, query, LAST, preferred_element_type=jnp.float32)
            prob = jnp.exp(scores * scale - offset[h : h + 1])
            if diagonal:
                at_key = lax.broadcasted_iota(jnp.int32, (rows, rows), 0)
                at_query = lax.broadcasted_iota(jnp.int32, (rows, rows), 1)
                prob = jnp.where(at_key <= at_query, prob, 0.0)
            prob_grad = lax.dot_general(value, grad, LAST, preferred_element_type=jnp.float32)
            slope = (prob * (prob_grad - delta[h]) * scale).astype(jnp.bfloat16)
            probs.append(prob.astype(jnp.bfloat16))
            slopes.append(slope)
            query_term = lax.dot_general(slope, key, FIRST, preferred_element_type=jnp.float32)
            if diagonal:
                sums_ref[:, span] = query_term
            else:
                sums_ref[:, span] += query_term
        queries = jnp.concatenate([query_ref[:, span] for span in spans], axis=0)
        grads = jnp.concatenate([grad_ref[:, span] for span in spans], axis=0)
        key_term = jnp.dot(
            jnp.concatenate(slopes, axis=1), queries, preferred_element_type=jnp.float32
        )
        value_term = jnp.dot(
            jnp.concatenate(probs, axis=1), grads, preferred_element_type=jnp.float32
        )
        terms_ref[mine - step, :, :width] = key_term.astype(jnp.bfloat16)
        terms_ref[mine - step, :, width:] = value_term.astype(jnp.bfloat16)

    block(0, True)

    @pl.loop(0, cycle)
    def _(source):
        seen = jnp.logical_and(source < mine, mask_ref[mine, source] > 0)

        @pl.when(seen)
        def _():
            block(mine - source, False)

        @pl.when(jnp.logical_and(source != mine, jnp.logical_not(seen)))
        def _():
            terms_ref[source] = jnp.zeros_like(terms_ref[source])

    query_grad_ref[...] = sums_ref[...].astype(jnp.bfloat16)


def key_blocks(keys, values, width):
    cycle = lax.axis_size("ctx")
    owners = lax.axis_size("exp")
    kv_count = keys.shape[1] // width
    kv_head = lax.axis_index("exp") * kv_count // owners
    pair = jnp.concatenate(
        [
            lax.dynamic_slice_in_dim(keys, kv_head * width, width, 1),
            lax.dynamic_slice_in_dim(values, kv_head * width, width, 1),
        ],
        axis=1,
    )
    return [pair] + [
        lax.ppermute(pair, "ctx", [(c, c + step) for c in range(cycle - step)])
        for step in range(1, cycle)
    ]


def attention(queries, arrived, attn_out, attn_out_grad, lse_excess, block_mask):
    cycle = lax.axis_size("ctx")
    mine = lax.axis_index("ctx")
    pair = arrived[0]
    operands = (queries, attn_out_grad, attn_out, lse_excess, *arrived)
    return pl.pallas_call(
        attention_kernel,
        out_shape=(
            jax.ShapeDtypeStruct(queries.shape, jnp.bfloat16),
            jax.ShapeDtypeStruct((cycle,) + pair.shape, jnp.bfloat16),
        ),
        grid_spec=pltpu.PrefetchScalarGridSpec(
            num_scalar_prefetch=2,
            grid=(1,),
            in_specs=[full(operand.shape) for operand in operands],
            out_specs=(full(queries.shape), full((cycle,) + pair.shape)),
            scratch_shapes=[
                pltpu.VMEM(queries.shape, jnp.float32),
                pltpu.VMEM((cycle,) + pair.shape, jnp.bfloat16),
            ],
        ),
        compiler_params=pltpu.CompilerParams(vmem_limit_bytes=32 * 2**20),
        name="attention",
    )(mine.astype(jnp.int32)[None], block_mask, *operands)


def sum_kernel(parts_ref, key_ref, value_ref):
    cycle, owners, rows, columns = parts_ref.shape
    kv_count = key_ref.shape[1] * 2 // columns
    group = owners // kv_count
    width = columns // 2
    for k in range(kv_count):
        total = jnp.zeros((rows, columns), jnp.float32)
        for c in range(cycle):
            for e in range(k * group, (k + 1) * group):
                total += parts_ref[c, e].astype(jnp.float32)
        key_ref[:, k * width : (k + 1) * width] = total[:, :width].astype(jnp.bfloat16)
        value_ref[:, k * width : (k + 1) * width] = total[:, width:].astype(jnp.bfloat16)


def summed_terms(terms, kv_columns, tiles):
    cycle, owners = lax.axis_size("ctx"), lax.axis_size("exp")
    rows, columns = terms.shape[1:]
    parts = lax.all_to_all(
        terms.reshape(cycle * owners, rows // owners, columns),
        ("ctx", "exp"),
        split_axis=0,
        concat_axis=0,
        tiled=True,
    ).reshape(cycle, owners, rows // owners, columns)
    parts, tiles = lax.optimization_barrier((parts, tiles))
    shape = (rows // owners, kv_columns)
    out = jax.ShapeDtypeStruct(shape, jnp.bfloat16)
    key_grad, value_grad = pl.pallas_call(
        sum_kernel,
        out_shape=(out, out),
        grid=(1,),
        in_specs=[full(parts.shape)],
        out_specs=(full(shape), full(shape)),
        compiler_params=pltpu.CompilerParams(vmem_limit_bytes=16 * 2**20),
        name="sums",
    )(parts)
    return key_grad, value_grad, tiles


def pick_kernel(per_dev, shadow_ref, mixed_ref, sent_ref):
    for owner in range(sent_ref.shape[0]):
        host = shadow_ref[owner * per_dev]
        for j in range(1, per_dev):
            host = jnp.maximum(host, shadow_ref[owner * per_dev + j])
        sent_ref[owner] = mixed_ref[host, : sent_ref.shape[1]]


def picked_rows(shadow_list, mixed, limit):
    owners = mixed.shape[0]
    whole = pl.BlockSpec(memory_space=pltpu.VMEM)
    return pl.pallas_call(
        functools.partial(pick_kernel, shadow_list.shape[0] // owners),
        out_shape=jax.ShapeDtypeStruct((owners, limit, mixed.shape[2]), jnp.bfloat16),
        in_specs=[pl.BlockSpec(memory_space=pltpu.SMEM), whole],
        out_specs=whole,
        compiler_params=pltpu.CompilerParams(vmem_limit_bytes=4 * 2**20),
        name="picked",
    )(shadow_list, mixed)


def weight_kernel(orders, own_ref, shadow_ref, mixed_ref, hidden_ref, side_ref, weight_ref):
    owners = mixed_ref.shape[0]
    per_dev, units = hidden_ref.shape[1], hidden_ref.shape[4]
    tokens = weight_ref.shape[1] // owners
    limit = side_ref.shape[1]
    own = own_ref[0]
    earlier = (
        lax.broadcasted_iota(jnp.int32, (tokens, tokens), 0)
        < lax.broadcasted_iota(jnp.int32, (tokens, tokens), 1)
    ).astype(jnp.bfloat16)
    odd = lax.broadcasted_iota(jnp.int32, (1, tokens), 1) % 2 == 1

    def rows_at(named, rows):
        rank = jnp.dot(
            jnp.broadcast_to(named.astype(jnp.float32), (8, tokens)).astype(jnp.bfloat16),
            earlier,
            preferred_element_type=jnp.float32,
        )[:1]
        place = lax.broadcasted_iota(jnp.int32, (rows.shape[0], tokens), 0).astype(jnp.float32)
        chosen = jnp.where(jnp.logical_and(named, rank == place), 1.0, 0.0).astype(jnp.bfloat16)
        return lax.dot_general(rows, chosen, FIRST, preferred_element_type=jnp.float32)

    for i in range(owners):
        source = own ^ jnp.where(own % 2 == 0, orders[0][i], orders[1][i])
        for j in range(per_dev):
            prob = mixed_ref[source, limit + j : limit + j + 1, :tokens].astype(jnp.float32)
            named = prob > 0
            flag = shadow_ref[own * per_dev + j] >= 0
            side = jnp.logical_and(jnp.logical_and(named, odd), flag)
            here = jnp.logical_and(named, jnp.logical_not(side))
            rows = rows_at(here, hidden_ref[0, j, source]) + rows_at(
                side, side_ref[source, :, :units]
            )
            weight_ref[j * units : (j + 1) * units, i * tokens : (i + 1) * tokens] = (
                rows * prob
            ).astype(jnp.bfloat16)


def weighted_rows(own_index, shadow_list, mixed, hidden, shadow_rows, tokens, orders):
    owners = mixed.shape[0]
    per_dev, units = shadow_list.shape[0] // owners, hidden.shape[4]
    shape = (per_dev * units, owners * tokens)
    return pl.pallas_call(
        functools.partial(weight_kernel, orders),
        out_shape=jax.ShapeDtypeStruct(shape, jnp.bfloat16),
        grid_spec=pltpu.PrefetchScalarGridSpec(
            num_scalar_prefetch=2,
            grid=(1,),
            in_specs=[
                full(mixed.shape),
                full((1, per_dev) + hidden.shape[2:]),
                full(shadow_rows.shape),
            ],
            out_specs=full(shape),
        ),
        compiler_params=pltpu.CompilerParams(vmem_limit_bytes=32 * 2**20),
        name="weighted",
    )(own_index.astype(jnp.int32)[None], shadow_list, mixed, hidden, shadow_rows)


def tile_kernel(weight_ref, *refs):
    *block_refs, tile_ref, gathered_ref, held_ref, in_sems, out_sems = refs
    per_dev, units, model = tile_ref.shape
    tokens = block_refs[0].shape[0]
    steps = in_sems.shape[0]
    step = model // steps
    arriving, leaving = [], []
    for i in range(steps):
        columns = pl.ds(i * step, step)
        arriving.append(
            [
                pltpu.make_async_copy(
                    ref.at[:, columns],
                    gathered_ref.at[pl.ds(n * tokens, tokens), columns],
                    in_sems.at[i, n],
                )
                for n, ref in enumerate(block_refs)
            ]
        )
    for copy in arriving[0] + arriving[1]:
        copy.start()
    for i in range(steps):
        for copy in arriving[i]:
            copy.wait()
        for copy in arriving[i + 2] if i + 2 < steps else []:
            copy.start()
        columns = slice(i * step, (i + 1) * step)
        held_ref[:, columns] = jnp.dot(
            weight_ref[...], gathered_ref[:, columns], preferred_element_type=jnp.float32
        )
        for j in range(per_dev):
            leaving.append(
                pltpu.make_async_copy(
                    held_ref.at[pl.ds(j * units, units), pl.ds(i * step, step)],
                    tile_ref.at[j, :, pl.ds(i * step, step)],
                    out_sems.at[i, j],
                )
            )
            leaving[-1].start()
    for copy in leaving:
        copy.wait()


def tile_sums(weighted, blocks, per_dev):
    tokens, model = blocks[0].shape
    rows = weighted.shape[0]
    steps = model // 1024
    anywhere = pl.BlockSpec(memory_space=pl.ANY)
    return pl.pallas_call(
        tile_kernel,
        out_shape=jax.ShapeDtypeStruct((per_dev, rows // per_dev, model), jnp.float32),
        in_specs=[pl.BlockSpec(memory_space=pltpu.VMEM)] + [anywhere] * len(blocks),
        out_specs=anywhere,
        scratch_shapes=[
            pltpu.VMEM((len(blocks) * tokens, model), jnp.bfloat16),
            pltpu.VMEM((rows, model), jnp.float32),
            pltpu.SemaphoreType.DMA((steps, len(blocks))),
            pltpu.SemaphoreType.DMA((steps, per_dev)),
        ],
        compiler_params=pltpu.CompilerParams(vmem_limit_bytes=32 * 2**20),
        name="tiles",
    )(weighted, *blocks)


def swapped(value):
    return lax.all_to_all(value, "exp", split_axis=0, concat_axis=0, tiled=True)


def source_rows(expert_ids, route_probs, shadow_list, stored_hidden_state):
    owners = lax.axis_size("exp")
    tokens = expert_ids.shape[0]
    count = shadow_list.shape[0]
    per_dev = count // owners
    capacity, units = stored_hidden_state.shape[3:]
    hit = expert_ids[:, None, :] == jnp.arange(count, dtype=jnp.int32)[None, :, None]
    table = jnp.sum(
        jnp.where(hit, route_probs[:, None, :].astype(jnp.float32), 0.0), axis=2
    ).astype(jnp.bfloat16)
    table = table.T.reshape(owners, per_dev, tokens)
    used = min(capacity, tokens // 2)
    limit = -(-used // 16) * 16
    lanes = max(units, tokens)
    rows = jnp.pad(
        stored_hidden_state[0, per_dev, :, :used],
        ((0, 0), (0, limit - used), (0, lanes - units)),
    )
    mixed = jnp.concatenate([rows, jnp.pad(table, ((0, 0), (0, 0), (0, lanes - tokens)))], axis=1)
    mixed = swapped(mixed)
    return mixed, picked_rows(shadow_list, mixed, limit)


def expert_rows(mixed, shadow_rows, shadow_list, stored_hidden_state, tokens):
    steps = block_steps(lax.axis_size("exp"))
    orders = [
        [step ^ turn for pair in zip(steps[core], steps[1 - core]) for step, turn in zip(pair, (0, 1))]
        for core in range(2)
    ]
    own_index = lax.axis_index("exp")
    return weighted_rows(
        own_index, shadow_list, mixed, stored_hidden_state, shadow_rows, tokens, orders
    )


def block_steps(owners):
    masks = [1 << bit for bit in range(1, owners.bit_length() - 1)]
    steps = []
    for core in range(2):
        first, second = masks[1 - core], masks[core]
        held = [0, first, second, first ^ second]
        for mask in masks[2:]:
            held = held + [step ^ mask for step in held]
        steps.append(held)
    return steps


def moved(value, steps):
    owners = lax.axis_size("exp")
    return lax.ppermute(value, "exp", [(e, e ^ steps[e % 2]) for e in range(owners)])


def expert_tiles(weighted, near, anchor, per_dev):
    owners = lax.axis_size("exp")
    steps = block_steps(owners)
    far = moved(near[1], [held[2] for held in steps])
    held = list(near)
    blocks = [block for part in held for block in (part, moved(part, (1, 1)))]
    far, _ = lax.optimization_barrier((far, (weighted, anchor)))
    held = held + [far]
    rest = [far]
    for turn in range(len(steps[0]).bit_length() - 3):
        mask = steps[0][4 << turn]
        more = [moved(part, (mask, mask)) for part in held]
        held, rest = held + more, rest + more
    rest = [block for part in rest for block in (part, moved(part, (1, 1)))]
    return tile_sums(weighted, blocks + rest, per_dev)


def local(
    queries,
    keys,
    values,
    attn_out,
    attn_out_grad,
    lse_excess,
    block_mask,
    expert_ids,
    route_probs,
    moe_grad,
    shadow_list,
    stored_hidden_state,
):
    steps = block_steps(lax.axis_size("exp"))
    first = moved(moe_grad, [held[1] for held in steps])
    arrived = key_blocks(keys, values, queries.shape[1] // lse_excess.shape[0])
    mixed, sent = source_rows(expert_ids, route_probs, shadow_list, stored_hidden_state)
    ready, mixed = lax.optimization_barrier((moe_grad, mixed))
    second = moved(ready, [held[2] for held in steps])
    shadow_rows = swapped(sent)
    first, second, shadow_rows = lax.optimization_barrier((first, second, shadow_rows))
    arrived, _ = lax.optimization_barrier((arrived, shadow_rows))
    query_grad, terms = attention(
        queries, arrived, attn_out, attn_out_grad, lse_excess, block_mask
    )
    weighted = expert_rows(
        mixed, shadow_rows, shadow_list, stored_hidden_state, expert_ids.shape[0]
    )
    per_dev = shadow_list.shape[0] // lax.axis_size("exp")
    tiles = expert_tiles(weighted, (moe_grad, first, second), query_grad, per_dev)
    key_grad, value_grad, expert_grad = summed_terms(terms, keys.shape[1], tiles)
    return (query_grad, key_grad, value_grad, expert_grad)


def solution(mesh):
    placed = (
        P("ctx", "exp"),
        P("ctx", None),
        P("ctx", None),
        P("ctx", "exp"),
        P("ctx", "exp"),
        P("exp", "ctx"),
        P(),
        P("exp", None),
        P("exp", None),
        P("exp", None),
        P(),
        P("exp", None, None, None, "ctx"),
    )
    return jax.shard_map(
        local,
        mesh=mesh,
        in_specs=placed,
        out_specs=(
            P("ctx", "exp"),
            P(("ctx", "exp"), None),
            P(("ctx", "exp"), None),
            P("exp", "ctx", None),
        ),
        check_vma=False,
    )
```

```python
import functools
import math

import jax
import jax.numpy as jnp
from jax import lax
from jax.experimental import pallas as pl
from jax.experimental.pallas import tpu as pltpu
from jax.sharding import PartitionSpec as P

LAST = (((1,), (1,)), ((), ()))
FIRST = (((0,), (0,)), ((), ()))


def full(shape):
    return pl.BlockSpec(shape, lambda *at: (0,) * len(shape))


def attention_kernel(
    place_ref, mask_ref, query_ref, grad_ref, out_ref, lse_ref, *rest
):
    cycle = mask_ref.shape[0]
    pair_refs, (query_grad_ref, terms_ref, sums_ref, pairs_ref) = rest[:cycle], rest[cycle:]
    rows, width = pairs_ref.shape[1], pairs_ref.shape[2] // 2
    heads = lse_ref.shape[0]
    scale = 1.0 / math.sqrt(width)
    mine = place_ref[0]
    offset = 0.5 * math.log(rows) + lse_ref[...]
    spans = [slice(h * width, (h + 1) * width) for h in range(heads)]
    for step, pair_ref in enumerate(pair_refs):
        pairs_ref[step] = pair_ref[...]
    delta = []
    for span in spans:
        both = grad_ref[:, span].astype(jnp.float32) * out_ref[:, span].astype(jnp.float32)
        delta.append(jnp.sum(both.T, axis=0, keepdims=True))

    def block(step, diagonal):
        key, value = pairs_ref[step, :, :width], pairs_ref[step, :, width:]
        probs, slopes = [], []
        for h, span in enumerate(spans):
            query, grad = query_ref[:, span], grad_ref[:, span]
            scores = lax.dot_general(key, query, LAST, preferred_element_type=jnp.float32)
            prob = jnp.exp(scores * scale - offset[h : h + 1])
            if diagonal:
                at_key = lax.broadcasted_iota(jnp.int32, (rows, rows), 0)
                at_query = lax.broadcasted_iota(jnp.int32, (rows, rows), 1)
                prob = jnp.where(at_key <= at_query, prob, 0.0)
            prob_grad = lax.dot_general(value, grad, LAST, preferred_element_type=jnp.float32)
            slope = (prob * (prob_grad - delta[h]) * scale).astype(jnp.bfloat16)
            probs.append(prob.astype(jnp.bfloat16))
            slopes.append(slope)
            query_term = lax.dot_general(slope, key, FIRST, preferred_element_type=jnp.float32)
            if diagonal:
                sums_ref[:, span] = query_term
            else:
                sums_ref[:, span] += query_term
        queries = jnp.concatenate([query_ref[:, span] for span in spans], axis=0)
        grads = jnp.concatenate([grad_ref[:, span] for span in spans], axis=0)
        key_term = jnp.dot(
            jnp.concatenate(slopes, axis=1), queries, preferred_element_type=jnp.float32
        )
        value_term = jnp.dot(
            jnp.concatenate(probs, axis=1), grads, preferred_element_type=jnp.float32
        )
        terms_ref[mine - step, :, :width] = key_term.astype(jnp.bfloat16)
        terms_ref[mine - step, :, width:] = value_term.astype(jnp.bfloat16)

    block(0, True)

    @pl.loop(0, cycle)
    def _(source):
        seen = jnp.logical_and(source < mine, mask_ref[mine, source] > 0)

        @pl.when(seen)
        def _():
            block(mine - source, False)

        @pl.when(jnp.logical_and(source != mine, jnp.logical_not(seen)))
        def _():
            terms_ref[source] = jnp.zeros_like(terms_ref[source])

    query_grad_ref[...] = sums_ref[...].astype(jnp.bfloat16)


def key_blocks(keys, values, width):
    cycle = lax.axis_size("ctx")
    owners = lax.axis_size("exp")
    kv_count = keys.shape[1] // width
    kv_head = lax.axis_index("exp") * kv_count // owners
    pair = jnp.concatenate(
        [
            lax.dynamic_slice_in_dim(keys, kv_head * width, width, 1),
            lax.dynamic_slice_in_dim(values, kv_head * width, width, 1),
        ],
        axis=1,
    )
    return [pair] + [
        lax.ppermute(pair, "ctx", [(c, c + step) for c in range(cycle - step)])
        for step in range(1, cycle)
    ]


def attention(queries, arrived, attn_out, attn_out_grad, lse_excess, block_mask):
    cycle = lax.axis_size("ctx")
    mine = lax.axis_index("ctx")
    pair = arrived[0]
    operands = (queries, attn_out_grad, attn_out, lse_excess, *arrived)
    return pl.pallas_call(
        attention_kernel,
        out_shape=(
            jax.ShapeDtypeStruct(queries.shape, jnp.bfloat16),
            jax.ShapeDtypeStruct((cycle,) + pair.shape, jnp.bfloat16),
        ),
        grid_spec=pltpu.PrefetchScalarGridSpec(
            num_scalar_prefetch=2,
            grid=(1,),
            in_specs=[full(operand.shape) for operand in operands],
            out_specs=(full(queries.shape), full((cycle,) + pair.shape)),
            scratch_shapes=[
                pltpu.VMEM(queries.shape, jnp.float32),
                pltpu.VMEM((cycle,) + pair.shape, jnp.bfloat16),
            ],
        ),
        compiler_params=pltpu.CompilerParams(vmem_limit_bytes=32 * 2**20),
        name="attention",
    )(mine.astype(jnp.int32)[None], block_mask, *operands)


def sum_kernel(parts_ref, key_ref, value_ref):
    cycle, owners, rows, columns = parts_ref.shape
    kv_count = key_ref.shape[1] * 2 // columns
    group = owners // kv_count
    width = columns // 2
    for k in range(kv_count):
        total = jnp.zeros((rows, columns), jnp.float32)
        for c in range(cycle):
            for e in range(k * group, (k + 1) * group):
                total += parts_ref[c, e].astype(jnp.float32)
        key_ref[:, k * width : (k + 1) * width] = total[:, :width].astype(jnp.bfloat16)
        value_ref[:, k * width : (k + 1) * width] = total[:, width:].astype(jnp.bfloat16)


def summed_terms(terms, kv_columns, tiles):
    cycle, owners = lax.axis_size("ctx"), lax.axis_size("exp")
    rows, columns = terms.shape[1:]
    parts = lax.all_to_all(
        terms.reshape(cycle * owners, rows // owners, columns),
        ("ctx", "exp"),
        split_axis=0,
        concat_axis=0,
        tiled=True,
    ).reshape(cycle, owners, rows // owners, columns)
    parts, tiles = lax.optimization_barrier((parts, tiles))
    shape = (rows // owners, kv_columns)
    out = jax.ShapeDtypeStruct(shape, jnp.bfloat16)
    key_grad, value_grad = pl.pallas_call(
        sum_kernel,
        out_shape=(out, out),
        grid=(1,),
        in_specs=[full(parts.shape)],
        out_specs=(full(shape), full(shape)),
        compiler_params=pltpu.CompilerParams(vmem_limit_bytes=16 * 2**20),
        name="sums",
    )(parts)
    return key_grad, value_grad, tiles


def pick_kernel(per_dev, shadow_ref, mixed_ref, sent_ref):
    for owner in range(sent_ref.shape[0]):
        host = shadow_ref[owner * per_dev]
        for j in range(1, per_dev):
            host = jnp.maximum(host, shadow_ref[owner * per_dev + j])
        sent_ref[owner] = mixed_ref[host, : sent_ref.shape[1]]


def picked_rows(shadow_list, mixed, limit):
    owners = mixed.shape[0]
    whole = pl.BlockSpec(memory_space=pltpu.VMEM)
    return pl.pallas_call(
        functools.partial(pick_kernel, shadow_list.shape[0] // owners),
        out_shape=jax.ShapeDtypeStruct((owners, limit, mixed.shape[2]), jnp.bfloat16),
        in_specs=[pl.BlockSpec(memory_space=pltpu.SMEM), whole],
        out_specs=whole,
        compiler_params=pltpu.CompilerParams(vmem_limit_bytes=4 * 2**20),
        name="picked",
    )(shadow_list, mixed)


def weight_kernel(orders, own_ref, shadow_ref, mixed_ref, hidden_ref, side_ref, weight_ref):
    owners = mixed_ref.shape[0]
    per_dev, units = hidden_ref.shape[1], hidden_ref.shape[4]
    tokens = weight_ref.shape[1] // owners
    limit = side_ref.shape[1]
    own = own_ref[0]
    earlier = (
        lax.broadcasted_iota(jnp.int32, (tokens, tokens), 0)
        < lax.broadcasted_iota(jnp.int32, (tokens, tokens), 1)
    ).astype(jnp.bfloat16)
    odd = lax.broadcasted_iota(jnp.int32, (1, tokens), 1) % 2 == 1

    def rows_at(named, rows):
        rank = jnp.dot(
            jnp.broadcast_to(named.astype(jnp.float32), (8, tokens)).astype(jnp.bfloat16),
            earlier,
            preferred_element_type=jnp.float32,
        )[:1]
        place = lax.broadcasted_iota(jnp.int32, (rows.shape[0], tokens), 0).astype(jnp.float32)
        chosen = jnp.where(jnp.logical_and(named, rank == place), 1.0, 0.0).astype(jnp.bfloat16)
        return lax.dot_general(rows, chosen, FIRST, preferred_element_type=jnp.float32)

    for i in range(owners):
        source = own ^ jnp.where(own % 2 == 0, orders[0][i], orders[1][i])
        for j in range(per_dev):
            prob = mixed_ref[source, limit + j : limit + j + 1, :tokens].astype(jnp.float32)
            named = prob > 0
            flag = shadow_ref[own * per_dev + j] >= 0
            side = jnp.logical_and(jnp.logical_and(named, odd), flag)
            here = jnp.logical_and(named, jnp.logical_not(side))
            rows = rows_at(here, hidden_ref[0, j, source]) + rows_at(
                side, side_ref[source, :, :units]
            )
            weight_ref[j * units : (j + 1) * units, i * tokens : (i + 1) * tokens] = (
                rows * prob
            ).astype(jnp.bfloat16)


def weighted_rows(own_index, shadow_list, mixed, hidden, shadow_rows, tokens, orders):
    owners = mixed.shape[0]
    per_dev, units = shadow_list.shape[0] // owners, hidden.shape[4]
    shape = (per_dev * units, owners * tokens)
    return pl.pallas_call(
        functools.partial(weight_kernel, orders),
        out_shape=jax.ShapeDtypeStruct(shape, jnp.bfloat16),
        grid_spec=pltpu.PrefetchScalarGridSpec(
            num_scalar_prefetch=2,
            grid=(1,),
            in_specs=[
                full(mixed.shape),
                full((1, per_dev) + hidden.shape[2:]),
                full(shadow_rows.shape),
            ],
            out_specs=full(shape),
        ),
        compiler_params=pltpu.CompilerParams(vmem_limit_bytes=32 * 2**20),
        name="weighted",
    )(own_index.astype(jnp.int32)[None], shadow_list, mixed, hidden, shadow_rows)


def tile_kernel(weight_ref, *refs):
    *block_refs, tile_ref, gathered_ref, held_ref, in_sems, out_sems = refs
    per_dev, units, model = tile_ref.shape
    tokens = block_refs[0].shape[0]
    steps = in_sems.shape[0]
    step = model // steps
    arriving, leaving = [], []
    for i in range(steps):
        columns = pl.ds(i * step, step)
        arriving.append(
            [
                pltpu.make_async_copy(
                    ref.at[:, columns],
                    gathered_ref.at[pl.ds(n * tokens, tokens), columns],
                    in_sems.at[i, n],
                )
                for n, ref in enumerate(block_refs)
            ]
        )
    for copy in arriving[0] + arriving[1]:
        copy.start()
    for i in range(steps):
        for copy in arriving[i]:
            copy.wait()
        for copy in arriving[i + 2] if i + 2 < steps else []:
            copy.start()
        columns = slice(i * step, (i + 1) * step)
        held_ref[:, columns] = jnp.dot(
            weight_ref[...], gathered_ref[:, columns], preferred_element_type=jnp.float32
        )
        for j in range(per_dev):
            leaving.append(
                pltpu.make_async_copy(
                    held_ref.at[pl.ds(j * units, units), pl.ds(i * step, step)],
                    tile_ref.at[j, :, pl.ds(i * step, step)],
                    out_sems.at[i, j],
                )
            )
            leaving[-1].start()
    for copy in leaving:
        copy.wait()


def tile_sums(weighted, blocks, per_dev):
    tokens, model = blocks[0].shape
    rows = weighted.shape[0]
    steps = model // 1024
    anywhere = pl.BlockSpec(memory_space=pl.ANY)
    return pl.pallas_call(
        tile_kernel,
        out_shape=jax.ShapeDtypeStruct((per_dev, rows // per_dev, model), jnp.float32),
        in_specs=[pl.BlockSpec(memory_space=pltpu.VMEM)] + [anywhere] * len(blocks),
        out_specs=anywhere,
        scratch_shapes=[
            pltpu.VMEM((len(blocks) * tokens, model), jnp.bfloat16),
            pltpu.VMEM((rows, model), jnp.float32),
            pltpu.SemaphoreType.DMA((steps, len(blocks))),
            pltpu.SemaphoreType.DMA((steps, per_dev)),
        ],
        compiler_params=pltpu.CompilerParams(vmem_limit_bytes=32 * 2**20),
        name="tiles",
    )(weighted, *blocks)


def swapped(value):
    return lax.all_to_all(value, "exp", split_axis=0, concat_axis=0, tiled=True)


def source_rows(expert_ids, route_probs, shadow_list, stored_hidden_state):
    owners = lax.axis_size("exp")
    tokens = expert_ids.shape[0]
    count = shadow_list.shape[0]
    per_dev = count // owners
    capacity, units = stored_hidden_state.shape[3:]
    hit = expert_ids[:, None, :] == jnp.arange(count, dtype=jnp.int32)[None, :, None]
    table = jnp.sum(
        jnp.where(hit, route_probs[:, None, :].astype(jnp.float32), 0.0), axis=2
    ).astype(jnp.bfloat16)
    table = table.T.reshape(owners, per_dev, tokens)
    used = min(capacity, tokens // 2)
    limit = -(-used // 16) * 16
    lanes = max(units, tokens)
    rows = jnp.pad(
        stored_hidden_state[0, per_dev, :, :used],
        ((0, 0), (0, limit - used), (0, lanes - units)),
    )
    mixed = jnp.concatenate([rows, jnp.pad(table, ((0, 0), (0, 0), (0, lanes - tokens)))], axis=1)
    mixed = swapped(mixed)
    return mixed, picked_rows(shadow_list, mixed, limit)


def expert_rows(mixed, shadow_rows, shadow_list, stored_hidden_state, tokens):
    steps = block_steps(lax.axis_size("exp"))
    orders = [
        [step ^ turn for pair in zip(steps[core], steps[1 - core]) for step, turn in zip(pair, (0, 1))]
        for core in range(2)
    ]
    own_index = lax.axis_index("exp")
    return weighted_rows(
        own_index, shadow_list, mixed, stored_hidden_state, shadow_rows, tokens, orders
    )


def block_steps(owners):
    masks = [1 << bit for bit in range(1, owners.bit_length() - 1)]
    steps = []
    for core in range(2):
        first, second = masks[1 - core], masks[core]
        held = [0, first, second, first ^ second]
        for mask in masks[2:]:
            held = held + [step ^ mask for step in held]
        steps.append(held)
    return steps


def moved(value, steps):
    owners = lax.axis_size("exp")
    return lax.ppermute(value, "exp", [(e, e ^ steps[e % 2]) for e in range(owners)])


def expert_tiles(weighted, near, anchor, per_dev):
    owners = lax.axis_size("exp")
    steps = block_steps(owners)
    far = moved(near[1], [held[2] for held in steps])
    held = list(near)
    blocks = [block for part in held for block in (part, moved(part, (1, 1)))]
    far, _ = lax.optimization_barrier((far, (weighted, anchor)))
    held = held + [far]
    rest = [far]
    for turn in range(len(steps[0]).bit_length() - 3):
        mask = steps[0][4 << turn]
        more = [moved(part, (mask, mask)) for part in held]
        held, rest = held + more, rest + more
    rest = [block for part in rest for block in (part, moved(part, (1, 1)))]
    return tile_sums(weighted, blocks + rest, per_dev)


def local(
    queries,
    keys,
    values,
    attn_out,
    attn_out_grad,
    lse_excess,
    block_mask,
    expert_ids,
    route_probs,
    moe_grad,
    shadow_list,
    stored_hidden_state,
):
    steps = block_steps(lax.axis_size("exp"))
    first = moved(moe_grad, [held[1] for held in steps])
    arrived = key_blocks(keys, values, queries.shape[1] // lse_excess.shape[0])
    mixed, sent = source_rows(expert_ids, route_probs, shadow_list, stored_hidden_state)
    shadow_rows = swapped(sent)
    ready, first, _ = lax.optimization_barrier((moe_grad, first, shadow_rows))
    second = moved(ready, [held[2] for held in steps])
    arrived, _ = lax.optimization_barrier((arrived, shadow_rows))
    query_grad, terms = attention(
        queries, arrived, attn_out, attn_out_grad, lse_excess, block_mask
    )
    weighted = expert_rows(
        mixed, shadow_rows, shadow_list, stored_hidden_state, expert_ids.shape[0]
    )
    per_dev = shadow_list.shape[0] // lax.axis_size("exp")
    tiles = expert_tiles(weighted, (moe_grad, first, second), query_grad, per_dev)
    key_grad, value_grad, expert_grad = summed_terms(terms, keys.shape[1], tiles)
    return (query_grad, key_grad, value_grad, expert_grad)


def solution(mesh):
    placed = (
        P("ctx", "exp"),
        P("ctx", None),
        P("ctx", None),
        P("ctx", "exp"),
        P("ctx", "exp"),
        P("exp", "ctx"),
        P(),
        P("exp", None),
        P("exp", None),
        P("exp", None),
        P(),
        P("exp", None, None, None, "ctx"),
    )
    return jax.shard_map(
        local,
        mesh=mesh,
        in_specs=placed,
        out_specs=(
            P("ctx", "exp"),
            P(("ctx", "exp"), None),
            P(("ctx", "exp"), None),
            P("exp", "ctx", None),
        ),
        check_vma=False,
    )
```

```python
import functools
import math

import jax
import jax.numpy as jnp
from jax import lax
from jax.experimental import pallas as pl
from jax.experimental.pallas import tpu as pltpu
from jax.sharding import PartitionSpec as P

LAST = (((1,), (1,)), ((), ()))
FIRST = (((0,), (0,)), ((), ()))


def full(shape):
    return pl.BlockSpec(shape, lambda *at: (0,) * len(shape))


def attention_kernel(
    place_ref, mask_ref, query_ref, grad_ref, out_ref, lse_ref, *rest
):
    cycle = mask_ref.shape[0]
    pair_refs, (query_grad_ref, terms_ref, sums_ref, pairs_ref) = rest[:cycle], rest[cycle:]
    rows, width = pairs_ref.shape[1], pairs_ref.shape[2] // 2
    heads = lse_ref.shape[0]
    scale = 1.0 / math.sqrt(width)
    mine = place_ref[0]
    offset = 0.5 * math.log(rows) + lse_ref[...]
    spans = [slice(h * width, (h + 1) * width) for h in range(heads)]
    for step, pair_ref in enumerate(pair_refs):
        pairs_ref[step] = pair_ref[...]
    delta = []
    for span in spans:
        both = grad_ref[:, span].astype(jnp.float32) * out_ref[:, span].astype(jnp.float32)
        delta.append(jnp.sum(both.T, axis=0, keepdims=True))

    def block(step, diagonal):
        key, value = pairs_ref[step, :, :width], pairs_ref[step, :, width:]
        probs, slopes = [], []
        for h, span in enumerate(spans):
            query, grad = query_ref[:, span], grad_ref[:, span]
            scores = lax.dot_general(key, query, LAST, preferred_element_type=jnp.float32)
            prob = jnp.exp(scores * scale - offset[h : h + 1])
            if diagonal:
                at_key = lax.broadcasted_iota(jnp.int32, (rows, rows), 0)
                at_query = lax.broadcasted_iota(jnp.int32, (rows, rows), 1)
                prob = jnp.where(at_key <= at_query, prob, 0.0)
            prob_grad = lax.dot_general(value, grad, LAST, preferred_element_type=jnp.float32)
            slope = (prob * (prob_grad - delta[h]) * scale).astype(jnp.bfloat16)
            probs.append(prob.astype(jnp.bfloat16))
            slopes.append(slope)
            query_term = lax.dot_general(slope, key, FIRST, preferred_element_type=jnp.float32)
            if diagonal:
                sums_ref[:, span] = query_term
            else:
                sums_ref[:, span] += query_term
        queries = jnp.concatenate([query_ref[:, span] for span in spans], axis=0)
        grads = jnp.concatenate([grad_ref[:, span] for span in spans], axis=0)
        key_term = jnp.dot(
            jnp.concatenate(slopes, axis=1), queries, preferred_element_type=jnp.float32
        )
        value_term = jnp.dot(
            jnp.concatenate(probs, axis=1), grads, preferred_element_type=jnp.float32
        )
        terms_ref[mine - step, :, :width] = key_term.astype(jnp.bfloat16)
        terms_ref[mine - step, :, width:] = value_term.astype(jnp.bfloat16)

    block(0, True)

    @pl.loop(0, cycle)
    def _(source):
        seen = jnp.logical_and(source < mine, mask_ref[mine, source] > 0)

        @pl.when(seen)
        def _():
            block(mine - source, False)

        @pl.when(jnp.logical_and(source != mine, jnp.logical_not(seen)))
        def _():
            terms_ref[source] = jnp.zeros_like(terms_ref[source])

    query_grad_ref[...] = sums_ref[...].astype(jnp.bfloat16)


def key_blocks(keys, values, width):
    cycle = lax.axis_size("ctx")
    owners = lax.axis_size("exp")
    kv_count = keys.shape[1] // width
    kv_head = lax.axis_index("exp") * kv_count // owners
    pair = jnp.concatenate(
        [
            lax.dynamic_slice_in_dim(keys, kv_head * width, width, 1),
            lax.dynamic_slice_in_dim(values, kv_head * width, width, 1),
        ],
        axis=1,
    )
    return [pair] + [
        lax.ppermute(pair, "ctx", [(c, c + step) for c in range(cycle - step)])
        for step in range(1, cycle)
    ]


def attention(queries, arrived, attn_out, attn_out_grad, lse_excess, block_mask):
    cycle = lax.axis_size("ctx")
    mine = lax.axis_index("ctx")
    pair = arrived[0]
    operands = (queries, attn_out_grad, attn_out, lse_excess, *arrived)
    return pl.pallas_call(
        attention_kernel,
        out_shape=(
            jax.ShapeDtypeStruct(queries.shape, jnp.bfloat16),
            jax.ShapeDtypeStruct((cycle,) + pair.shape, jnp.bfloat16),
        ),
        grid_spec=pltpu.PrefetchScalarGridSpec(
            num_scalar_prefetch=2,
            grid=(1,),
            in_specs=[full(operand.shape) for operand in operands],
            out_specs=(full(queries.shape), full((cycle,) + pair.shape)),
            scratch_shapes=[
                pltpu.VMEM(queries.shape, jnp.float32),
                pltpu.VMEM((cycle,) + pair.shape, jnp.bfloat16),
            ],
        ),
        compiler_params=pltpu.CompilerParams(vmem_limit_bytes=32 * 2**20),
        name="attention",
    )(mine.astype(jnp.int32)[None], block_mask, *operands)


def sum_kernel(parts_ref, key_ref, value_ref):
    cycle, owners, rows, columns = parts_ref.shape
    kv_count = key_ref.shape[1] * 2 // columns
    group = owners // kv_count
    width = columns // 2
    for k in range(kv_count):
        total = jnp.zeros((rows, columns), jnp.float32)
        for c in range(cycle):
            for e in range(k * group, (k + 1) * group):
                total += parts_ref[c, e].astype(jnp.float32)
        key_ref[:, k * width : (k + 1) * width] = total[:, :width].astype(jnp.bfloat16)
        value_ref[:, k * width : (k + 1) * width] = total[:, width:].astype(jnp.bfloat16)


def summed_terms(terms, kv_columns, tiles):
    cycle, owners = lax.axis_size("ctx"), lax.axis_size("exp")
    rows, columns = terms.shape[1:]
    parts = lax.all_to_all(
        terms.reshape(cycle * owners, rows // owners, columns),
        ("ctx", "exp"),
        split_axis=0,
        concat_axis=0,
        tiled=True,
    ).reshape(cycle, owners, rows // owners, columns)
    parts, tiles = lax.optimization_barrier((parts, tiles))
    shape = (rows // owners, kv_columns)
    out = jax.ShapeDtypeStruct(shape, jnp.bfloat16)
    key_grad, value_grad = pl.pallas_call(
        sum_kernel,
        out_shape=(out, out),
        grid=(1,),
        in_specs=[full(parts.shape)],
        out_specs=(full(shape), full(shape)),
        compiler_params=pltpu.CompilerParams(vmem_limit_bytes=16 * 2**20),
        name="sums",
    )(parts)
    return key_grad, value_grad, tiles


def pick_kernel(per_dev, shadow_ref, mixed_ref, sent_ref):
    for owner in range(sent_ref.shape[0]):
        host = shadow_ref[owner * per_dev]
        for j in range(1, per_dev):
            host = jnp.maximum(host, shadow_ref[owner * per_dev + j])
        sent_ref[owner] = mixed_ref[host, : sent_ref.shape[1]]


def picked_rows(shadow_list, mixed, limit):
    owners = mixed.shape[0]
    whole = pl.BlockSpec(memory_space=pltpu.VMEM)
    return pl.pallas_call(
        functools.partial(pick_kernel, shadow_list.shape[0] // owners),
        out_shape=jax.ShapeDtypeStruct((owners, limit, mixed.shape[2]), jnp.bfloat16),
        in_specs=[pl.BlockSpec(memory_space=pltpu.SMEM), whole],
        out_specs=whole,
        compiler_params=pltpu.CompilerParams(vmem_limit_bytes=4 * 2**20),
        name="picked",
    )(shadow_list, mixed)


def weight_kernel(orders, own_ref, shadow_ref, mixed_ref, hidden_ref, side_ref, weight_ref):
    owners = mixed_ref.shape[0]
    per_dev, units = hidden_ref.shape[1], hidden_ref.shape[4]
    tokens = weight_ref.shape[1] // owners
    limit = side_ref.shape[1]
    own = own_ref[0]
    earlier = (
        lax.broadcasted_iota(jnp.int32, (tokens, tokens), 0)
        < lax.broadcasted_iota(jnp.int32, (tokens, tokens), 1)
    ).astype(jnp.bfloat16)
    odd = lax.broadcasted_iota(jnp.int32, (1, tokens), 1) % 2 == 1

    def rows_at(named, rows):
        rank = jnp.dot(
            jnp.broadcast_to(named.astype(jnp.float32), (8, tokens)).astype(jnp.bfloat16),
            earlier,
            preferred_element_type=jnp.float32,
        )[:1]
        place = lax.broadcasted_iota(jnp.int32, (rows.shape[0], tokens), 0).astype(jnp.float32)
        chosen = jnp.where(jnp.logical_and(named, rank == place), 1.0, 0.0).astype(jnp.bfloat16)
        return lax.dot_general(rows, chosen, FIRST, preferred_element_type=jnp.float32)

    for i in range(owners):
        source = own ^ jnp.where(own % 2 == 0, orders[0][i], orders[1][i])
        for j in range(per_dev):
            prob = mixed_ref[source, limit + j : limit + j + 1, :tokens].astype(jnp.float32)
            named = prob > 0
            flag = shadow_ref[own * per_dev + j] >= 0
            side = jnp.logical_and(jnp.logical_and(named, odd), flag)
            here = jnp.logical_and(named, jnp.logical_not(side))
            rows = rows_at(here, hidden_ref[0, j, source]) + rows_at(
                side, side_ref[source, :, :units]
            )
            weight_ref[j * units : (j + 1) * units, i * tokens : (i + 1) * tokens] = (
                rows * prob
            ).astype(jnp.bfloat16)


def weighted_rows(own_index, shadow_list, mixed, hidden, shadow_rows, tokens, orders):
    owners = mixed.shape[0]
    per_dev, units = shadow_list.shape[0] // owners, hidden.shape[4]
    shape = (per_dev * units, owners * tokens)
    return pl.pallas_call(
        functools.partial(weight_kernel, orders),
        out_shape=jax.ShapeDtypeStruct(shape, jnp.bfloat16),
        grid_spec=pltpu.PrefetchScalarGridSpec(
            num_scalar_prefetch=2,
            grid=(1,),
            in_specs=[
                full(mixed.shape),
                full((1, per_dev) + hidden.shape[2:]),
                full(shadow_rows.shape),
            ],
            out_specs=full(shape),
        ),
        compiler_params=pltpu.CompilerParams(vmem_limit_bytes=32 * 2**20),
        name="weighted",
    )(own_index.astype(jnp.int32)[None], shadow_list, mixed, hidden, shadow_rows)


def tile_kernel(weight_ref, *refs):
    *block_refs, tile_ref, gathered_ref, held_ref, in_sems, out_sems = refs
    per_dev, units, model = tile_ref.shape
    tokens = block_refs[0].shape[0]
    steps = in_sems.shape[0]
    step = model // steps
    arriving, leaving = [], []
    for i in range(steps):
        columns = pl.ds(i * step, step)
        arriving.append(
            [
                pltpu.make_async_copy(
                    ref.at[:, columns],
                    gathered_ref.at[pl.ds(n * tokens, tokens), columns],
                    in_sems.at[i, n],
                )
                for n, ref in enumerate(block_refs)
            ]
        )
    for copy in arriving[0] + arriving[1]:
        copy.start()
    for i in range(steps):
        for copy in arriving[i]:
            copy.wait()
        for copy in arriving[i + 2] if i + 2 < steps else []:
            copy.start()
        columns = slice(i * step, (i + 1) * step)
        held_ref[:, columns] = jnp.dot(
            weight_ref[...], gathered_ref[:, columns], preferred_element_type=jnp.float32
        )
        for j in range(per_dev):
            leaving.append(
                pltpu.make_async_copy(
                    held_ref.at[pl.ds(j * units, units), pl.ds(i * step, step)],
                    tile_ref.at[j, :, pl.ds(i * step, step)],
                    out_sems.at[i, j],
                )
            )
            leaving[-1].start()
    for copy in leaving:
        copy.wait()


def tile_sums(weighted, blocks, per_dev):
    tokens, model = blocks[0].shape
    rows = weighted.shape[0]
    steps = model // 1024
    anywhere = pl.BlockSpec(memory_space=pl.ANY)
    return pl.pallas_call(
        tile_kernel,
        out_shape=jax.ShapeDtypeStruct((per_dev, rows // per_dev, model), jnp.float32),
        in_specs=[pl.BlockSpec(memory_space=pltpu.VMEM)] + [anywhere] * len(blocks),
        out_specs=anywhere,
        scratch_shapes=[
            pltpu.VMEM((len(blocks) * tokens, model), jnp.bfloat16),
            pltpu.VMEM((rows, model), jnp.float32),
            pltpu.SemaphoreType.DMA((steps, len(blocks))),
            pltpu.SemaphoreType.DMA((steps, per_dev)),
        ],
        compiler_params=pltpu.CompilerParams(vmem_limit_bytes=32 * 2**20),
        name="tiles",
    )(weighted, *blocks)


def swapped(value):
    return lax.all_to_all(value, "exp", split_axis=0, concat_axis=0, tiled=True)


def source_rows(expert_ids, route_probs, shadow_list, stored_hidden_state):
    owners = lax.axis_size("exp")
    tokens = expert_ids.shape[0]
    count = shadow_list.shape[0]
    per_dev = count // owners
    capacity, units = stored_hidden_state.shape[3:]
    hit = expert_ids[:, None, :] == jnp.arange(count, dtype=jnp.int32)[None, :, None]
    table = jnp.sum(
        jnp.where(hit, route_probs[:, None, :].astype(jnp.float32), 0.0), axis=2
    ).astype(jnp.bfloat16)
    table = table.T.reshape(owners, per_dev, tokens)
    used = min(capacity, tokens // 2)
    limit = -(-used // 16) * 16
    lanes = max(units, tokens)
    rows = jnp.pad(
        stored_hidden_state[0, per_dev, :, :used],
        ((0, 0), (0, limit - used), (0, lanes - units)),
    )
    mixed = jnp.concatenate([rows, jnp.pad(table, ((0, 0), (0, 0), (0, lanes - tokens)))], axis=1)
    return mixed


def expert_rows(mixed, shadow_rows, shadow_list, stored_hidden_state, tokens):
    steps = block_steps(lax.axis_size("exp"))
    orders = [
        [step ^ turn for pair in zip(steps[core], steps[1 - core]) for step, turn in zip(pair, (0, 1))]
        for core in range(2)
    ]
    own_index = lax.axis_index("exp")
    return weighted_rows(
        own_index, shadow_list, mixed, stored_hidden_state, shadow_rows, tokens, orders
    )


def block_steps(owners):
    masks = [1 << bit for bit in range(1, owners.bit_length() - 1)]
    steps = []
    for core in range(2):
        first, second = masks[1 - core], masks[core]
        held = [0, first, second, first ^ second]
        for mask in masks[2:]:
            held = held + [step ^ mask for step in held]
        steps.append(held)
    return steps


def moved(value, steps):
    owners = lax.axis_size("exp")
    return lax.ppermute(value, "exp", [(e, e ^ steps[e % 2]) for e in range(owners)])


def paired_half(block):
    rows = block.shape[0] // 2
    return lax.dynamic_slice_in_dim(block, lax.axis_index("ctx") % 2 * rows, rows, 0)


def paired_whole(half):
    other = lax.ppermute(half, "ctx", [(c, c ^ 1) for c in range(lax.axis_size("ctx"))])
    lower = lax.axis_index("ctx") % 2 == 0
    return jnp.where(
        lower, jnp.concatenate([half, other], axis=0), jnp.concatenate([other, half], axis=0)
    )


def expert_tiles(weighted, near, anchor, per_dev):
    owners = lax.axis_size("exp")
    steps = block_steps(owners)
    far = moved(near[1], [held[2] for held in steps])
    held = list(near)
    blocks = [block for part in held for block in (part, moved(part, (1, 1)))]
    far, _ = lax.optimization_barrier((far, (weighted, anchor)))
    held = held + [far]
    rest = [far]
    for turn in range(len(steps[0]).bit_length() - 3):
        mask = steps[0][4 << turn]
        more = [moved(part, (mask, mask)) for part in held]
        held, rest = held + more, rest + more
    rest = [block for part in rest for block in (part, moved(part, (1, 1)))]
    return tile_sums(weighted, blocks + rest, per_dev)


def local(
    queries,
    keys,
    values,
    attn_out,
    attn_out_grad,
    lse_excess,
    block_mask,
    expert_ids,
    route_probs,
    moe_grad,
    shadow_list,
    stored_hidden_state,
):
    steps = block_steps(lax.axis_size("exp"))
    half = paired_half(moe_grad)
    first = moved(half, [held[1] for held in steps])
    second = moved(half, [held[2] for held in steps])
    arrived = key_blocks(keys, values, queries.shape[1] // lse_excess.shape[0])
    payload = source_rows(expert_ids, route_probs, shadow_list, stored_hidden_state)
    mixed, arrived = lax.optimization_barrier((swapped(payload), arrived))
    per_dev = shadow_list.shape[0] // lax.axis_size("exp")
    sent = picked_rows(shadow_list, mixed, payload.shape[1] - per_dev)
    sent, first, second = lax.optimization_barrier((sent, first, second))
    first, second = paired_whole(first), paired_whole(second)
    shadow_rows = swapped(sent)
    arrived, _ = lax.optimization_barrier((arrived, sent))
    query_grad, terms = attention(
        queries, arrived, attn_out, attn_out_grad, lse_excess, block_mask
    )
    first, shadow_rows = lax.optimization_barrier((first, shadow_rows))
    weighted = expert_rows(
        mixed, shadow_rows, shadow_list, stored_hidden_state, expert_ids.shape[0]
    )
    tiles = expert_tiles(weighted, (moe_grad, first, second), query_grad, per_dev)
    key_grad, value_grad, expert_grad = summed_terms(terms, keys.shape[1], tiles)
    return (query_grad, key_grad, value_grad, expert_grad)


def solution(mesh):
    placed = (
        P("ctx", "exp"),
        P("ctx", None),
        P("ctx", None),
        P("ctx", "exp"),
        P("ctx", "exp"),
        P("exp", "ctx"),
        P(),
        P("exp", None),
        P("exp", None),
        P("exp", None),
        P(),
        P("exp", None, None, None, "ctx"),
    )
    return jax.shard_map(
        local,
        mesh=mesh,
        in_specs=placed,
        out_specs=(
            P("ctx", "exp"),
            P(("ctx", "exp"), None),
            P(("ctx", "exp"), None),
            P("exp", "ctx", None),
        ),
        check_vma=False,
    )
```

```python
import functools
import math

import jax
import jax.numpy as jnp
from jax import lax
from jax.experimental import pallas as pl
from jax.experimental.pallas import tpu as pltpu
from jax.sharding import PartitionSpec as P

LAST = (((1,), (1,)), ((), ()))
FIRST = (((0,), (0,)), ((), ()))


def full(shape):
    return pl.BlockSpec(shape, lambda *at: (0,) * len(shape))


def attention_kernel(
    place_ref, mask_ref, query_ref, grad_ref, out_ref, lse_ref, *rest
):
    cycle = mask_ref.shape[0]
    pair_refs, (query_grad_ref, terms_ref, sums_ref, pairs_ref) = rest[:cycle], rest[cycle:]
    rows, width = pairs_ref.shape[1], pairs_ref.shape[2] // 2
    heads = lse_ref.shape[0]
    scale = 1.0 / math.sqrt(width)
    mine = place_ref[0]
    offset = 0.5 * math.log(rows) + lse_ref[...]
    spans = [slice(h * width, (h + 1) * width) for h in range(heads)]
    for step, pair_ref in enumerate(pair_refs):
        pairs_ref[step] = pair_ref[...]
    delta = []
    for span in spans:
        both = grad_ref[:, span].astype(jnp.float32) * out_ref[:, span].astype(jnp.float32)
        delta.append(jnp.sum(both.T, axis=0, keepdims=True))

    def block(step, diagonal):
        key, value = pairs_ref[step, :, :width], pairs_ref[step, :, width:]
        probs, slopes = [], []
        for h, span in enumerate(spans):
            query, grad = query_ref[:, span], grad_ref[:, span]
            scores = lax.dot_general(key, query, LAST, preferred_element_type=jnp.float32)
            prob = jnp.exp(scores * scale - offset[h : h + 1])
            if diagonal:
                at_key = lax.broadcasted_iota(jnp.int32, (rows, rows), 0)
                at_query = lax.broadcasted_iota(jnp.int32, (rows, rows), 1)
                prob = jnp.where(at_key <= at_query, prob, 0.0)
            prob_grad = lax.dot_general(value, grad, LAST, preferred_element_type=jnp.float32)
            slope = (prob * (prob_grad - delta[h]) * scale).astype(jnp.bfloat16)
            probs.append(prob.astype(jnp.bfloat16))
            slopes.append(slope)
            query_term = lax.dot_general(slope, key, FIRST, preferred_element_type=jnp.float32)
            if diagonal:
                sums_ref[:, span] = query_term
            else:
                sums_ref[:, span] += query_term
        queries = jnp.concatenate([query_ref[:, span] for span in spans], axis=0)
        grads = jnp.concatenate([grad_ref[:, span] for span in spans], axis=0)
        key_term = jnp.dot(
            jnp.concatenate(slopes, axis=1), queries, preferred_element_type=jnp.float32
        )
        value_term = jnp.dot(
            jnp.concatenate(probs, axis=1), grads, preferred_element_type=jnp.float32
        )
        terms_ref[mine - step, :, :width] = key_term.astype(jnp.bfloat16)
        terms_ref[mine - step, :, width:] = value_term.astype(jnp.bfloat16)

    block(0, True)

    @pl.loop(0, cycle)
    def _(source):
        seen = jnp.logical_and(source < mine, mask_ref[mine, source] > 0)

        @pl.when(seen)
        def _():
            block(mine - source, False)

        @pl.when(jnp.logical_and(source != mine, jnp.logical_not(seen)))
        def _():
            terms_ref[source] = jnp.zeros_like(terms_ref[source])

    query_grad_ref[...] = sums_ref[...].astype(jnp.bfloat16)


def key_blocks(keys, values, width):
    cycle = lax.axis_size("ctx")
    owners = lax.axis_size("exp")
    kv_count = keys.shape[1] // width
    kv_head = lax.axis_index("exp") * kv_count // owners
    pair = jnp.concatenate(
        [
            lax.dynamic_slice_in_dim(keys, kv_head * width, width, 1),
            lax.dynamic_slice_in_dim(values, kv_head * width, width, 1),
        ],
        axis=1,
    )
    return [pair] + [
        lax.ppermute(pair, "ctx", [(c, c + step) for c in range(cycle - step)])
        for step in range(1, cycle)
    ]


def attention(queries, arrived, attn_out, attn_out_grad, lse_excess, block_mask):
    cycle = lax.axis_size("ctx")
    mine = lax.axis_index("ctx")
    pair = arrived[0]
    operands = (queries, attn_out_grad, attn_out, lse_excess, *arrived)
    return pl.pallas_call(
        attention_kernel,
        out_shape=(
            jax.ShapeDtypeStruct(queries.shape, jnp.bfloat16),
            jax.ShapeDtypeStruct((cycle,) + pair.shape, jnp.bfloat16),
        ),
        grid_spec=pltpu.PrefetchScalarGridSpec(
            num_scalar_prefetch=2,
            grid=(1,),
            in_specs=[full(operand.shape) for operand in operands],
            out_specs=(full(queries.shape), full((cycle,) + pair.shape)),
            scratch_shapes=[
                pltpu.VMEM(queries.shape, jnp.float32),
                pltpu.VMEM((cycle,) + pair.shape, jnp.bfloat16),
            ],
        ),
        compiler_params=pltpu.CompilerParams(vmem_limit_bytes=32 * 2**20),
        name="attention",
    )(mine.astype(jnp.int32)[None], block_mask, *operands)


def sum_kernel(parts_ref, key_ref, value_ref):
    cycle, owners, rows, columns = parts_ref.shape
    kv_count = key_ref.shape[1] * 2 // columns
    group = owners // kv_count
    width = columns // 2
    for k in range(kv_count):
        total = jnp.zeros((rows, columns), jnp.float32)
        for c in range(cycle):
            for e in range(k * group, (k + 1) * group):
                total += parts_ref[c, e].astype(jnp.float32)
        key_ref[:, k * width : (k + 1) * width] = total[:, :width].astype(jnp.bfloat16)
        value_ref[:, k * width : (k + 1) * width] = total[:, width:].astype(jnp.bfloat16)


def summed_terms(terms, kv_columns, tiles):
    cycle, owners = lax.axis_size("ctx"), lax.axis_size("exp")
    rows, columns = terms.shape[1:]
    parts = lax.all_to_all(
        terms.reshape(cycle * owners, rows // owners, columns),
        ("ctx", "exp"),
        split_axis=0,
        concat_axis=0,
        tiled=True,
    ).reshape(cycle, owners, rows // owners, columns)
    parts, tiles = lax.optimization_barrier((parts, tiles))
    shape = (rows // owners, kv_columns)
    out = jax.ShapeDtypeStruct(shape, jnp.bfloat16)
    key_grad, value_grad = pl.pallas_call(
        sum_kernel,
        out_shape=(out, out),
        grid=(1,),
        in_specs=[full(parts.shape)],
        out_specs=(full(shape), full(shape)),
        compiler_params=pltpu.CompilerParams(vmem_limit_bytes=16 * 2**20),
        name="sums",
    )(parts)
    return key_grad, value_grad, tiles


def pick_kernel(per_dev, shadow_ref, mixed_ref, sent_ref):
    for owner in range(sent_ref.shape[0]):
        host = shadow_ref[owner * per_dev]
        for j in range(1, per_dev):
            host = jnp.maximum(host, shadow_ref[owner * per_dev + j])
        sent_ref[owner] = mixed_ref[host, : sent_ref.shape[1]]


def picked_rows(shadow_list, mixed, limit):
    owners = mixed.shape[0]
    whole = pl.BlockSpec(memory_space=pltpu.VMEM)
    return pl.pallas_call(
        functools.partial(pick_kernel, shadow_list.shape[0] // owners),
        out_shape=jax.ShapeDtypeStruct((owners, limit, mixed.shape[2]), jnp.bfloat16),
        in_specs=[pl.BlockSpec(memory_space=pltpu.SMEM), whole],
        out_specs=whole,
        compiler_params=pltpu.CompilerParams(vmem_limit_bytes=4 * 2**20),
        name="picked",
    )(shadow_list, mixed)


def weight_kernel(orders, own_ref, shadow_ref, mixed_ref, hidden_ref, side_ref, weight_ref):
    owners = mixed_ref.shape[0]
    per_dev, units = hidden_ref.shape[1], hidden_ref.shape[4]
    tokens = weight_ref.shape[1] // owners
    limit = side_ref.shape[1]
    own = own_ref[0]
    earlier = (
        lax.broadcasted_iota(jnp.int32, (tokens, tokens), 0)
        < lax.broadcasted_iota(jnp.int32, (tokens, tokens), 1)
    ).astype(jnp.bfloat16)
    odd = lax.broadcasted_iota(jnp.int32, (1, tokens), 1) % 2 == 1

    def rows_at(named, rows):
        rank = jnp.dot(
            jnp.broadcast_to(named.astype(jnp.float32), (8, tokens)).astype(jnp.bfloat16),
            earlier,
            preferred_element_type=jnp.float32,
        )[:1]
        place = lax.broadcasted_iota(jnp.int32, (rows.shape[0], tokens), 0).astype(jnp.float32)
        chosen = jnp.where(jnp.logical_and(named, rank == place), 1.0, 0.0).astype(jnp.bfloat16)
        return lax.dot_general(rows, chosen, FIRST, preferred_element_type=jnp.float32)

    for i in range(owners):
        source = own ^ jnp.where(own % 2 == 0, orders[0][i], orders[1][i])
        for j in range(per_dev):
            prob = mixed_ref[source, limit + j : limit + j + 1, :tokens].astype(jnp.float32)
            named = prob > 0
            flag = shadow_ref[own * per_dev + j] >= 0
            side = jnp.logical_and(jnp.logical_and(named, odd), flag)
            here = jnp.logical_and(named, jnp.logical_not(side))
            rows = rows_at(here, hidden_ref[0, j, source]) + rows_at(
                side, side_ref[source, :, :units]
            )
            weight_ref[j * units : (j + 1) * units, i * tokens : (i + 1) * tokens] = (
                rows * prob
            ).astype(jnp.bfloat16)


def weighted_rows(own_index, shadow_list, mixed, hidden, shadow_rows, tokens, orders):
    owners = mixed.shape[0]
    per_dev, units = shadow_list.shape[0] // owners, hidden.shape[4]
    shape = (per_dev * units, owners * tokens)
    return pl.pallas_call(
        functools.partial(weight_kernel, orders),
        out_shape=jax.ShapeDtypeStruct(shape, jnp.bfloat16),
        grid_spec=pltpu.PrefetchScalarGridSpec(
            num_scalar_prefetch=2,
            grid=(1,),
            in_specs=[
                full(mixed.shape),
                full((1, per_dev) + hidden.shape[2:]),
                full(shadow_rows.shape),
            ],
            out_specs=full(shape),
        ),
        compiler_params=pltpu.CompilerParams(vmem_limit_bytes=32 * 2**20),
        name="weighted",
    )(own_index.astype(jnp.int32)[None], shadow_list, mixed, hidden, shadow_rows)


def tile_kernel(halves, parity_ref, weight_ref, *refs):
    *part_refs, tile_ref, gathered_ref, held_ref, in_sems, out_sems = refs
    per_dev, units, model = tile_ref.shape
    steps = in_sems.shape[0]
    tokens = gathered_ref.shape[0] // len(halves)
    parity = parity_ref[0]
    places = []
    for n, count in enumerate(halves):
        if count == 1:
            places.append(n * tokens)
        else:
            places.append(pl.multiple_of(n * tokens + parity * (tokens // 2), 16))
            places.append(pl.multiple_of(n * tokens + (1 - parity) * (tokens // 2), 16))
    step = model // steps
    arriving, leaving = [], []
    for i in range(steps):
        columns = pl.ds(i * step, step)
        arriving.append(
            [
                pltpu.make_async_copy(
                    ref.at[:, columns],
                    gathered_ref.at[pl.ds(place, ref.shape[0]), columns],
                    in_sems.at[i, n],
                )
                for n, (place, ref) in enumerate(zip(places, part_refs))
            ]
        )
    for copy in arriving[0] + arriving[1]:
        copy.start()
    for i in range(steps):
        for copy in arriving[i]:
            copy.wait()
        for copy in arriving[i + 2] if i + 2 < steps else []:
            copy.start()
        columns = slice(i * step, (i + 1) * step)
        held_ref[:, columns] = jnp.dot(
            weight_ref[...], gathered_ref[:, columns], preferred_element_type=jnp.float32
        )
        for j in range(per_dev):
            leaving.append(
                pltpu.make_async_copy(
                    held_ref.at[pl.ds(j * units, units), pl.ds(i * step, step)],
                    tile_ref.at[j, :, pl.ds(i * step, step)],
                    out_sems.at[i, j],
                )
            )
            leaving[-1].start()
    for copy in leaving:
        copy.wait()


def tile_sums(weighted, blocks, per_dev):
    tokens, model = blocks[0][0].shape
    rows = weighted.shape[0]
    steps = model // 1024
    halves = [len(block) for block in blocks]
    parts = [part for block in blocks for part in block]
    parity = (lax.axis_index("ctx") % 2).astype(jnp.int32)[None]
    anywhere = pl.BlockSpec(memory_space=pl.ANY)
    return pl.pallas_call(
        functools.partial(tile_kernel, halves),
        out_shape=jax.ShapeDtypeStruct((per_dev, rows // per_dev, model), jnp.float32),
        in_specs=[pl.BlockSpec(memory_space=pltpu.SMEM), pl.BlockSpec(memory_space=pltpu.VMEM)]
        + [anywhere] * len(parts),
        out_specs=anywhere,
        scratch_shapes=[
            pltpu.VMEM((len(blocks) * tokens, model), jnp.bfloat16),
            pltpu.VMEM((rows, model), jnp.float32),
            pltpu.SemaphoreType.DMA((steps, len(parts))),
            pltpu.SemaphoreType.DMA((steps, per_dev)),
        ],
        compiler_params=pltpu.CompilerParams(vmem_limit_bytes=32 * 2**20),
        name="tiles",
    )(parity, weighted, *parts)


def swapped(value):
    return lax.all_to_all(value, "exp", split_axis=0, concat_axis=0, tiled=True)


def source_rows(expert_ids, route_probs, shadow_list, stored_hidden_state):
    owners = lax.axis_size("exp")
    tokens = expert_ids.shape[0]
    count = shadow_list.shape[0]
    per_dev = count // owners
    capacity, units = stored_hidden_state.shape[3:]
    hit = expert_ids[:, None, :] == jnp.arange(count, dtype=jnp.int32)[None, :, None]
    table = jnp.sum(
        jnp.where(hit, route_probs[:, None, :].astype(jnp.float32), 0.0), axis=2
    ).astype(jnp.bfloat16)
    table = table.T.reshape(owners, per_dev, tokens)
    used = min(capacity, tokens // 2)
    limit = -(-used // 16) * 16
    lanes = max(units, tokens)
    rows = jnp.pad(
        stored_hidden_state[0, per_dev, :, :used],
        ((0, 0), (0, limit - used), (0, lanes - units)),
    )
    mixed = jnp.concatenate([rows, jnp.pad(table, ((0, 0), (0, 0), (0, lanes - tokens)))], axis=1)
    return mixed


def expert_rows(mixed, shadow_rows, shadow_list, stored_hidden_state, tokens):
    steps = block_steps(lax.axis_size("exp"))
    orders = [
        [step ^ turn for pair in zip(steps[core], steps[1 - core]) for step, turn in zip(pair, (0, 1))]
        for core in range(2)
    ]
    own_index = lax.axis_index("exp")
    return weighted_rows(
        own_index, shadow_list, mixed, stored_hidden_state, shadow_rows, tokens, orders
    )


def block_steps(owners):
    masks = [1 << bit for bit in range(1, owners.bit_length() - 1)]
    steps = []
    for core in range(2):
        first, second = masks[1 - core], masks[core]
        held = [0, first, second, first ^ second]
        for mask in masks[2:]:
            held = held + [step ^ mask for step in held]
        steps.append(held)
    return steps


def moved(value, steps):
    owners = lax.axis_size("exp")
    return lax.ppermute(value, "exp", [(e, e ^ steps[e % 2]) for e in range(owners)])


def paired_half(block):
    rows = block.shape[0] // 2
    return lax.dynamic_slice_in_dim(block, lax.axis_index("ctx") % 2 * rows, rows, 0)


def from_pair(half):
    return lax.ppermute(half, "ctx", [(c, c ^ 1) for c in range(lax.axis_size("ctx"))])


def beside(block):
    return [moved(part, (1, 1)) for part in block]


def all_blocks(held):
    steps = block_steps(lax.axis_size("exp"))[0]
    for turn in range(len(steps).bit_length() - 3):
        mask = steps[4 << turn]
        more = [[moved(part, (mask, mask)) for part in block] for block, _ in held]
        held = held + [(block, beside(block)) for block in more]
    return [block for pair in held for block in pair]


def local(
    queries,
    keys,
    values,
    attn_out,
    attn_out_grad,
    lse_excess,
    block_mask,
    expert_ids,
    route_probs,
    moe_grad,
    shadow_list,
    stored_hidden_state,
):
    steps = block_steps(lax.axis_size("exp"))
    first = moved(moe_grad, [held[1] for held in steps])
    second = moved(paired_half(moe_grad), [held[2] for held in steps])
    arrived = key_blocks(keys, values, queries.shape[1] // lse_excess.shape[0])
    payload = source_rows(expert_ids, route_probs, shadow_list, stored_hidden_state)
    mixed, arrived = lax.optimization_barrier((swapped(payload), arrived))
    per_dev = shadow_list.shape[0] // lax.axis_size("exp")
    sent = picked_rows(shadow_list, mixed, payload.shape[1] - per_dev)
    sent, second = lax.optimization_barrier((sent, second))
    second = [second, from_pair(second)]
    shadow_rows = swapped(sent)
    arrived, _ = lax.optimization_barrier((arrived, sent))
    query_grad, terms = attention(
        queries, arrived, attn_out, attn_out_grad, lse_excess, block_mask
    )
    first, shadow_rows = lax.optimization_barrier((first, shadow_rows))
    far = moved(first, [held[2] for held in steps])
    weighted = expert_rows(
        mixed, shadow_rows, shadow_list, stored_hidden_state, expert_ids.shape[0]
    )
    near = [(block, beside(block)) for block in ([moe_grad], [first], second)]
    far, _ = lax.optimization_barrier((far, (weighted, query_grad)))
    tiles = tile_sums(weighted, all_blocks(near + [([far], beside([far]))]), per_dev)
    key_grad, value_grad, expert_grad = summed_terms(terms, keys.shape[1], tiles)
    return (query_grad, key_grad, value_grad, expert_grad)


def solution(mesh):
    placed = (
        P("ctx", "exp"),
        P("ctx", None),
        P("ctx", None),
        P("ctx", "exp"),
        P("ctx", "exp"),
        P("exp", "ctx"),
        P(),
        P("exp", None),
        P("exp", None),
        P("exp", None),
        P(),
        P("exp", None, None, None, "ctx"),
    )
    return jax.shard_map(
        local,
        mesh=mesh,
        in_specs=placed,
        out_specs=(
            P("ctx", "exp"),
            P(("ctx", "exp"), None),
            P(("ctx", "exp"), None),
            P("exp", "ctx", None),
        ),
        check_vma=False,
    )
```

```python
import functools
import math

import jax
import jax.numpy as jnp
from jax import lax
from jax.experimental import pallas as pl
from jax.experimental.pallas import tpu as pltpu
from jax.sharding import PartitionSpec as P

LAST = (((1,), (1,)), ((), ()))
FIRST = (((0,), (0,)), ((), ()))


def full(shape):
    return pl.BlockSpec(shape, lambda *at: (0,) * len(shape))


def attention_kernel(
    place_ref, mask_ref, query_ref, grad_ref, out_ref, lse_ref, *rest
):
    cycle = mask_ref.shape[0]
    pair_ref, fetched_ref, swapped_ref, query_grad_ref, terms_ref, sums_ref, pairs_ref = rest
    rows, width = pairs_ref.shape[1], pairs_ref.shape[2] // 2
    heads = lse_ref.shape[0]
    scale = 1.0 / math.sqrt(width)
    mine = place_ref[0]
    offset = 0.5 * math.log(rows) + lse_ref[...]
    spans = [slice(h * width, (h + 1) * width) for h in range(heads)]
    pairs_ref[0] = pair_ref[...]
    for core, (key_ref, value_ref) in enumerate(
        ((fetched_ref, swapped_ref), (swapped_ref, fetched_ref))
    ):

        @pl.when(place_ref[1] == core)
        def _(key_ref=key_ref, value_ref=value_ref):
            pairs_ref[1:, :, :width] = key_ref[...]
            pairs_ref[1:, :, width:] = value_ref[...]

    delta = []
    for span in spans:
        both = grad_ref[:, span].astype(jnp.float32) * out_ref[:, span].astype(jnp.float32)
        delta.append(jnp.sum(both.T, axis=0, keepdims=True))

    def block(step, diagonal):
        key, value = pairs_ref[step, :, :width], pairs_ref[step, :, width:]
        probs, slopes = [], []
        for h, span in enumerate(spans):
            query, grad = query_ref[:, span], grad_ref[:, span]
            scores = lax.dot_general(key, query, LAST, preferred_element_type=jnp.float32)
            prob = jnp.exp(scores * scale - offset[h : h + 1])
            if diagonal:
                at_key = lax.broadcasted_iota(jnp.int32, (rows, rows), 0)
                at_query = lax.broadcasted_iota(jnp.int32, (rows, rows), 1)
                prob = jnp.where(at_key <= at_query, prob, 0.0)
            prob_grad = lax.dot_general(value, grad, LAST, preferred_element_type=jnp.float32)
            slope = (prob * (prob_grad - delta[h]) * scale).astype(jnp.bfloat16)
            probs.append(prob.astype(jnp.bfloat16))
            slopes.append(slope)
            query_term = lax.dot_general(slope, key, FIRST, preferred_element_type=jnp.float32)
            if diagonal:
                sums_ref[:, span] = query_term
            else:
                sums_ref[:, span] += query_term
        queries = jnp.concatenate([query_ref[:, span] for span in spans], axis=0)
        grads = jnp.concatenate([grad_ref[:, span] for span in spans], axis=0)
        key_term = jnp.dot(
            jnp.concatenate(slopes, axis=1), queries, preferred_element_type=jnp.float32
        )
        value_term = jnp.dot(
            jnp.concatenate(probs, axis=1), grads, preferred_element_type=jnp.float32
        )
        terms_ref[mine - step, :, :width] = key_term.astype(jnp.bfloat16)
        terms_ref[mine - step, :, width:] = value_term.astype(jnp.bfloat16)

    block(0, True)

    @pl.loop(0, cycle)
    def _(source):
        seen = jnp.logical_and(source < mine, mask_ref[mine, source] > 0)

        @pl.when(seen)
        def _():
            block(mine - source, False)

        @pl.when(jnp.logical_and(source != mine, jnp.logical_not(seen)))
        def _():
            terms_ref[source] = jnp.zeros_like(terms_ref[source])

    query_grad_ref[...] = sums_ref[...].astype(jnp.bfloat16)


def key_blocks(keys, values, width):
    cycle = lax.axis_size("ctx")
    owners = lax.axis_size("exp")
    kv_count = keys.shape[1] // width
    kv_head = lax.axis_index("exp") * kv_count // owners
    key = lax.dynamic_slice_in_dim(keys, kv_head * width, width, 1)
    value = lax.dynamic_slice_in_dim(values, kv_head * width, width, 1)
    half = jnp.where(lax.axis_index("exp") % 2 == 0, key, value)
    fetched = jnp.stack(
        [
            lax.ppermute(half, "ctx", [(c, c + step) for c in range(cycle - step)])
            for step in range(1, cycle)
        ]
    )
    return jnp.concatenate([key, value], axis=1), fetched


def attention(queries, arrived, attn_out, attn_out_grad, lse_excess, block_mask):
    cycle = lax.axis_size("ctx")
    mine = lax.axis_index("ctx")
    pair, fetched = arrived
    arrived = (pair, fetched, moved(fetched, (1, 1)))
    operands = (queries, attn_out_grad, attn_out, lse_excess, *arrived)
    return pl.pallas_call(
        attention_kernel,
        out_shape=(
            jax.ShapeDtypeStruct(queries.shape, jnp.bfloat16),
            jax.ShapeDtypeStruct((cycle,) + pair.shape, jnp.bfloat16),
        ),
        grid_spec=pltpu.PrefetchScalarGridSpec(
            num_scalar_prefetch=2,
            grid=(1,),
            in_specs=[full(operand.shape) for operand in operands],
            out_specs=(full(queries.shape), full((cycle,) + pair.shape)),
            scratch_shapes=[
                pltpu.VMEM(queries.shape, jnp.float32),
                pltpu.VMEM((cycle,) + pair.shape, jnp.bfloat16),
            ],
        ),
        compiler_params=pltpu.CompilerParams(vmem_limit_bytes=32 * 2**20),
        name="attention",
    )(jnp.stack([mine, lax.axis_index("exp") % 2]).astype(jnp.int32), block_mask, *operands)


def sum_kernel(parts_ref, key_ref, value_ref):
    cycle, owners, rows, columns = parts_ref.shape
    kv_count = key_ref.shape[1] * 2 // columns
    group = owners // kv_count
    width = columns // 2
    for k in range(kv_count):
        total = jnp.zeros((rows, columns), jnp.float32)
        for c in range(cycle):
            for e in range(k * group, (k + 1) * group):
                total += parts_ref[c, e].astype(jnp.float32)
        key_ref[:, k * width : (k + 1) * width] = total[:, :width].astype(jnp.bfloat16)
        value_ref[:, k * width : (k + 1) * width] = total[:, width:].astype(jnp.bfloat16)


def summed_terms(terms, kv_columns, tiles):
    cycle, owners = lax.axis_size("ctx"), lax.axis_size("exp")
    rows, columns = terms.shape[1:]
    parts = lax.all_to_all(
        terms.reshape(cycle * owners, rows // owners, columns),
        ("ctx", "exp"),
        split_axis=0,
        concat_axis=0,
        tiled=True,
    ).reshape(cycle, owners, rows // owners, columns)
    parts, tiles = lax.optimization_barrier((parts, tiles))
    shape = (rows // owners, kv_columns)
    out = jax.ShapeDtypeStruct(shape, jnp.bfloat16)
    key_grad, value_grad = pl.pallas_call(
        sum_kernel,
        out_shape=(out, out),
        grid=(1,),
        in_specs=[full(parts.shape)],
        out_specs=(full(shape), full(shape)),
        compiler_params=pltpu.CompilerParams(vmem_limit_bytes=16 * 2**20),
        name="sums",
    )(parts)
    return key_grad, value_grad, tiles


def pick_kernel(per_dev, shadow_ref, mixed_ref, sent_ref):
    for owner in range(sent_ref.shape[0]):
        host = shadow_ref[owner * per_dev]
        for j in range(1, per_dev):
            host = jnp.maximum(host, shadow_ref[owner * per_dev + j])
        sent_ref[owner] = mixed_ref[host, : sent_ref.shape[1]]


def picked_rows(shadow_list, mixed, limit):
    owners = mixed.shape[0]
    whole = pl.BlockSpec(memory_space=pltpu.VMEM)
    return pl.pallas_call(
        functools.partial(pick_kernel, shadow_list.shape[0] // owners),
        out_shape=jax.ShapeDtypeStruct((owners, limit, mixed.shape[2]), jnp.bfloat16),
        in_specs=[pl.BlockSpec(memory_space=pltpu.SMEM), whole],
        out_specs=whole,
        compiler_params=pltpu.CompilerParams(vmem_limit_bytes=4 * 2**20),
        name="picked",
    )(shadow_list, mixed)


def weight_kernel(orders, own_ref, shadow_ref, mixed_ref, hidden_ref, side_ref, weight_ref):
    owners = mixed_ref.shape[0]
    per_dev, units = hidden_ref.shape[1], hidden_ref.shape[4]
    tokens = weight_ref.shape[1] // owners
    limit = side_ref.shape[1]
    own = own_ref[0]
    earlier = (
        lax.broadcasted_iota(jnp.int32, (tokens, tokens), 0)
        < lax.broadcasted_iota(jnp.int32, (tokens, tokens), 1)
    ).astype(jnp.bfloat16)
    odd = lax.broadcasted_iota(jnp.int32, (1, tokens), 1) % 2 == 1

    def rows_at(named, rows):
        rank = jnp.dot(
            jnp.broadcast_to(named.astype(jnp.float32), (8, tokens)).astype(jnp.bfloat16),
            earlier,
            preferred_element_type=jnp.float32,
        )[:1]
        place = lax.broadcasted_iota(jnp.int32, (rows.shape[0], tokens), 0).astype(jnp.float32)
        chosen = jnp.where(jnp.logical_and(named, rank == place), 1.0, 0.0).astype(jnp.bfloat16)
        return lax.dot_general(rows, chosen, FIRST, preferred_element_type=jnp.float32)

    for i in range(owners):
        source = own ^ jnp.where(own % 2 == 0, orders[0][i], orders[1][i])
        for j in range(per_dev):
            prob = mixed_ref[source, limit + j : limit + j + 1, :tokens].astype(jnp.float32)
            named = prob > 0
            flag = shadow_ref[own * per_dev + j] >= 0
            side = jnp.logical_and(jnp.logical_and(named, odd), flag)
            here = jnp.logical_and(named, jnp.logical_not(side))
            rows = rows_at(here, hidden_ref[0, j, source]) + rows_at(
                side, side_ref[source, :, :units]
            )
            weight_ref[j * units : (j + 1) * units, i * tokens : (i + 1) * tokens] = (
                rows * prob
            ).astype(jnp.bfloat16)


def weighted_rows(own_index, shadow_list, mixed, hidden, shadow_rows, tokens, orders):
    owners = mixed.shape[0]
    per_dev, units = shadow_list.shape[0] // owners, hidden.shape[4]
    shape = (per_dev * units, owners * tokens)
    return pl.pallas_call(
        functools.partial(weight_kernel, orders),
        out_shape=jax.ShapeDtypeStruct(shape, jnp.bfloat16),
        grid_spec=pltpu.PrefetchScalarGridSpec(
            num_scalar_prefetch=2,
            grid=(1,),
            in_specs=[
                full(mixed.shape),
                full((1, per_dev) + hidden.shape[2:]),
                full(shadow_rows.shape),
            ],
            out_specs=full(shape),
        ),
        compiler_params=pltpu.CompilerParams(vmem_limit_bytes=32 * 2**20),
        name="weighted",
    )(own_index.astype(jnp.int32)[None], shadow_list, mixed, hidden, shadow_rows)


def tile_kernel(halves, parity_ref, weight_ref, *refs):
    *part_refs, tile_ref, gathered_ref, held_ref, in_sems, out_sems = refs
    per_dev, units, model = tile_ref.shape
    steps = in_sems.shape[0]
    tokens = gathered_ref.shape[0] // len(halves)
    parity = parity_ref[0]
    places = []
    for n, count in enumerate(halves):
        if count == 1:
            places.append(n * tokens)
        else:
            places.append(pl.multiple_of(n * tokens + parity * (tokens // 2), 16))
            places.append(pl.multiple_of(n * tokens + (1 - parity) * (tokens // 2), 16))
    step = model // steps
    arriving, leaving = [], []
    for i in range(steps):
        columns = pl.ds(i * step, step)
        arriving.append(
            [
                pltpu.make_async_copy(
                    ref.at[:, columns],
                    gathered_ref.at[pl.ds(place, ref.shape[0]), columns],
                    in_sems.at[i, n],
                )
                for n, (place, ref) in enumerate(zip(places, part_refs))
            ]
        )
    for copy in arriving[0] + arriving[1]:
        copy.start()
    for i in range(steps):
        for copy in arriving[i]:
            copy.wait()
        for copy in arriving[i + 2] if i + 2 < steps else []:
            copy.start()
        columns = slice(i * step, (i + 1) * step)
        held_ref[:, columns] = jnp.dot(
            weight_ref[...], gathered_ref[:, columns], preferred_element_type=jnp.float32
        )
        for j in range(per_dev):
            leaving.append(
                pltpu.make_async_copy(
                    held_ref.at[pl.ds(j * units, units), pl.ds(i * step, step)],
                    tile_ref.at[j, :, pl.ds(i * step, step)],
                    out_sems.at[i, j],
                )
            )
            leaving[-1].start()
    for copy in leaving:
        copy.wait()


def tile_sums(weighted, blocks, per_dev):
    tokens, model = blocks[0][0].shape
    rows = weighted.shape[0]
    steps = model // 1024
    halves = [len(block) for block in blocks]
    parts = [part for block in blocks for part in block]
    parity = (lax.axis_index("ctx") % 2).astype(jnp.int32)[None]
    anywhere = pl.BlockSpec(memory_space=pl.ANY)
    return pl.pallas_call(
        functools.partial(tile_kernel, halves),
        out_shape=jax.ShapeDtypeStruct((per_dev, rows // per_dev, model), jnp.float32),
        in_specs=[pl.BlockSpec(memory_space=pltpu.SMEM), pl.BlockSpec(memory_space=pltpu.VMEM)]
        + [anywhere] * len(parts),
        out_specs=anywhere,
        scratch_shapes=[
            pltpu.VMEM((len(blocks) * tokens, model), jnp.bfloat16),
            pltpu.VMEM((rows, model), jnp.float32),
            pltpu.SemaphoreType.DMA((steps, len(parts))),
            pltpu.SemaphoreType.DMA((steps, per_dev)),
        ],
        compiler_params=pltpu.CompilerParams(vmem_limit_bytes=32 * 2**20),
        name="tiles",
    )(parity, weighted, *parts)


def swapped(value):
    return lax.all_to_all(value, "exp", split_axis=0, concat_axis=0, tiled=True)


def source_rows(expert_ids, route_probs, shadow_list, stored_hidden_state):
    owners = lax.axis_size("exp")
    tokens = expert_ids.shape[0]
    count = shadow_list.shape[0]
    per_dev = count // owners
    capacity, units = stored_hidden_state.shape[3:]
    hit = expert_ids[:, None, :] == jnp.arange(count, dtype=jnp.int32)[None, :, None]
    table = jnp.sum(
        jnp.where(hit, route_probs[:, None, :].astype(jnp.float32), 0.0), axis=2
    ).astype(jnp.bfloat16)
    table = table.T.reshape(owners, per_dev, tokens)
    used = min(capacity, tokens // 2)
    limit = -(-used // 16) * 16
    lanes = max(units, tokens)
    rows = jnp.pad(
        stored_hidden_state[0, per_dev, :, :used],
        ((0, 0), (0, limit - used), (0, lanes - units)),
    )
    mixed = jnp.concatenate([rows, jnp.pad(table, ((0, 0), (0, 0), (0, lanes - tokens)))], axis=1)
    return mixed


def expert_rows(mixed, shadow_rows, shadow_list, stored_hidden_state, tokens):
    steps = block_steps(lax.axis_size("exp"))
    orders = [
        [step ^ turn for pair in zip(steps[core], steps[1 - core]) for step, turn in zip(pair, (0, 1))]
        for core in range(2)
    ]
    own_index = lax.axis_index("exp")
    return weighted_rows(
        own_index, shadow_list, mixed, stored_hidden_state, shadow_rows, tokens, orders
    )


def block_steps(owners):
    masks = [1 << bit for bit in range(1, owners.bit_length() - 1)]
    steps = []
    for core in range(2):
        first, second = masks[1 - core], masks[core]
        held = [0, first, second, first ^ second]
        for mask in masks[2:]:
            held = held + [step ^ mask for step in held]
        steps.append(held)
    return steps


def moved(value, steps):
    owners = lax.axis_size("exp")
    return lax.ppermute(value, "exp", [(e, e ^ steps[e % 2]) for e in range(owners)])


def paired_half(block):
    rows = block.shape[0] // 2
    return lax.dynamic_slice_in_dim(block, lax.axis_index("ctx") % 2 * rows, rows, 0)


def from_pair(half):
    return lax.ppermute(half, "ctx", [(c, c ^ 1) for c in range(lax.axis_size("ctx"))])


def beside(block):
    return [moved(part, (1, 1)) for part in block]


def all_blocks(held):
    steps = block_steps(lax.axis_size("exp"))[0]
    for turn in range(len(steps).bit_length() - 3):
        mask = steps[4 << turn]
        more = [[moved(part, (mask, mask)) for part in block] for block, _ in held]
        held = held + [(block, beside(block)) for block in more]
    return [block for pair in held for block in pair]


def local(
    queries,
    keys,
    values,
    attn_out,
    attn_out_grad,
    lse_excess,
    block_mask,
    expert_ids,
    route_probs,
    moe_grad,
    shadow_list,
    stored_hidden_state,
):
    steps = block_steps(lax.axis_size("exp"))
    first = moved(moe_grad, [held[1] for held in steps])
    second = moved(paired_half(moe_grad), [held[2] for held in steps])
    arrived = key_blocks(keys, values, queries.shape[1] // lse_excess.shape[0])
    payload = source_rows(expert_ids, route_probs, shadow_list, stored_hidden_state)
    mixed, arrived = lax.optimization_barrier((swapped(payload), arrived))
    per_dev = shadow_list.shape[0] // lax.axis_size("exp")
    sent = picked_rows(shadow_list, mixed, payload.shape[1] - per_dev)
    sent, second = lax.optimization_barrier((sent, second))
    second = [second, from_pair(second)]
    shadow_rows = swapped(sent)
    arrived, _ = lax.optimization_barrier((arrived, sent))
    query_grad, terms = attention(
        queries, arrived, attn_out, attn_out_grad, lse_excess, block_mask
    )
    first, shadow_rows, query_grad = lax.optimization_barrier((first, shadow_rows, query_grad))
    far = moved(first, [held[2] for held in steps])
    weighted = expert_rows(
        mixed, shadow_rows, shadow_list, stored_hidden_state, expert_ids.shape[0]
    )
    near = [(block, beside(block)) for block in ([moe_grad], [first], second)]
    far, _ = lax.optimization_barrier((far, (weighted, query_grad)))
    tiles = tile_sums(weighted, all_blocks(near + [([far], beside([far]))]), per_dev)
    key_grad, value_grad, expert_grad = summed_terms(terms, keys.shape[1], tiles)
    return (query_grad, key_grad, value_grad, expert_grad)


def solution(mesh):
    placed = (
        P("ctx", "exp"),
        P("ctx", None),
        P("ctx", None),
        P("ctx", "exp"),
        P("ctx", "exp"),
        P("exp", "ctx"),
        P(),
        P("exp", None),
        P("exp", None),
        P("exp", None),
        P(),
        P("exp", None, None, None, "ctx"),
    )
    return jax.shard_map(
        local,
        mesh=mesh,
        in_specs=placed,
        out_specs=(
            P("ctx", "exp"),
            P(("ctx", "exp"), None),
            P(("ctx", "exp"), None),
            P("exp", "ctx", None),
        ),
        check_vma=False,
    )
```

```python
import functools
import math

import jax
import jax.numpy as jnp
from jax import lax
from jax.experimental import pallas as pl
from jax.experimental.pallas import tpu as pltpu
from jax.sharding import PartitionSpec as P

LAST = (((1,), (1,)), ((), ()))
FIRST = (((0,), (0,)), ((), ()))


def full(shape):
    return pl.BlockSpec(shape, lambda *at: (0,) * len(shape))


def attention_kernel(
    place_ref, mask_ref, query_ref, grad_ref, out_ref, lse_ref, *rest
):
    cycle = mask_ref.shape[0]
    pair_ref, fetched_ref, swapped_ref, query_grad_ref = rest[:4]
    *term_refs, sums_ref, pairs_ref, terms_ref = rest[4:]
    rows, width = pairs_ref.shape[1], pairs_ref.shape[2] // 2
    heads = lse_ref.shape[0]
    scale = 1.0 / math.sqrt(width)
    mine = place_ref[0]
    offset = 0.5 * math.log(rows) + lse_ref[...]
    spans = [slice(h * width, (h + 1) * width) for h in range(heads)]
    pairs_ref[0] = pair_ref[...]
    for core, (key_ref, value_ref) in enumerate(
        ((fetched_ref, swapped_ref), (swapped_ref, fetched_ref))
    ):

        @pl.when(place_ref[1] == core)
        def _(key_ref=key_ref, value_ref=value_ref):
            pairs_ref[1:, :, :width] = key_ref[...]
            pairs_ref[1:, :, width:] = value_ref[...]

    delta = []
    for span in spans:
        both = grad_ref[:, span].astype(jnp.float32) * out_ref[:, span].astype(jnp.float32)
        delta.append(jnp.sum(both.T, axis=0, keepdims=True))

    def block(step, diagonal):
        key, value = pairs_ref[step, :, :width], pairs_ref[step, :, width:]
        probs, slopes = [], []
        for h, span in enumerate(spans):
            query, grad = query_ref[:, span], grad_ref[:, span]
            scores = lax.dot_general(key, query, LAST, preferred_element_type=jnp.float32)
            prob = jnp.exp(scores * scale - offset[h : h + 1])
            if diagonal:
                at_key = lax.broadcasted_iota(jnp.int32, (rows, rows), 0)
                at_query = lax.broadcasted_iota(jnp.int32, (rows, rows), 1)
                prob = jnp.where(at_key <= at_query, prob, 0.0)
            prob_grad = lax.dot_general(value, grad, LAST, preferred_element_type=jnp.float32)
            slope = (prob * (prob_grad - delta[h]) * scale).astype(jnp.bfloat16)
            probs.append(prob.astype(jnp.bfloat16))
            slopes.append(slope)
            query_term = lax.dot_general(slope, key, FIRST, preferred_element_type=jnp.float32)
            if diagonal:
                sums_ref[:, span] = query_term
            else:
                sums_ref[:, span] += query_term
        queries = jnp.concatenate([query_ref[:, span] for span in spans], axis=0)
        grads = jnp.concatenate([grad_ref[:, span] for span in spans], axis=0)
        key_term = jnp.dot(
            jnp.concatenate(slopes, axis=1), queries, preferred_element_type=jnp.float32
        )
        value_term = jnp.dot(
            jnp.concatenate(probs, axis=1), grads, preferred_element_type=jnp.float32
        )
        terms_ref[step, :, :width] = key_term.astype(jnp.bfloat16)
        terms_ref[step, :, width:] = value_term.astype(jnp.bfloat16)

    block(0, True)

    @pl.loop(1, cycle)
    def _(step):
        source = mine - step
        seen = jnp.logical_and(source >= 0, mask_ref[mine, jnp.maximum(source, 0)] > 0)

        @pl.when(seen)
        def _():
            block(step, False)

        @pl.when(jnp.logical_not(seen))
        def _():
            terms_ref[step] = jnp.zeros_like(terms_ref[step])

    for step, term_ref in enumerate(term_refs):
        term_ref[...] = terms_ref[step]
    query_grad_ref[...] = sums_ref[...].astype(jnp.bfloat16)


def key_blocks(keys, values, width):
    cycle = lax.axis_size("ctx")
    owners = lax.axis_size("exp")
    kv_count = keys.shape[1] // width
    kv_head = lax.axis_index("exp") * kv_count // owners
    key = lax.dynamic_slice_in_dim(keys, kv_head * width, width, 1)
    value = lax.dynamic_slice_in_dim(values, kv_head * width, width, 1)
    half = jnp.where(lax.axis_index("exp") % 2 == 0, key, value)
    fetched = jnp.stack(
        [
            lax.ppermute(half, "ctx", [(c, c + step) for c in range(cycle - step)])
            for step in range(1, cycle)
        ]
    )
    return jnp.concatenate([key, value], axis=1), fetched


def attention(queries, arrived, attn_out, attn_out_grad, lse_excess, block_mask):
    cycle = lax.axis_size("ctx")
    mine = lax.axis_index("ctx")
    pair, fetched = arrived
    arrived = (pair, fetched, moved(fetched, (1, 1)))
    operands = (queries, attn_out_grad, attn_out, lse_excess, *arrived)
    query_grad, *terms = pl.pallas_call(
        attention_kernel,
        out_shape=[jax.ShapeDtypeStruct(queries.shape, jnp.bfloat16)]
        + [jax.ShapeDtypeStruct(pair.shape, jnp.bfloat16)] * cycle,
        grid_spec=pltpu.PrefetchScalarGridSpec(
            num_scalar_prefetch=2,
            grid=(1,),
            in_specs=[full(operand.shape) for operand in operands],
            out_specs=[full(queries.shape)] + [full(pair.shape)] * cycle,
            scratch_shapes=[
                pltpu.VMEM(queries.shape, jnp.float32),
                pltpu.VMEM((cycle,) + pair.shape, jnp.bfloat16),
                pltpu.VMEM((cycle,) + pair.shape, jnp.bfloat16),
            ],
        ),
        compiler_params=pltpu.CompilerParams(vmem_limit_bytes=32 * 2**20),
        name="attention",
    )(jnp.stack([mine, lax.axis_index("exp") % 2]).astype(jnp.int32), block_mask, *operands)
    return query_grad, terms


def sum_kernel(parts_ref, key_ref, value_ref):
    owners, rows, columns = parts_ref.shape
    kv_count = key_ref.shape[1] * 2 // columns
    group = owners // kv_count
    width = columns // 2
    for k in range(kv_count):
        total = jnp.zeros((rows, columns), jnp.float32)
        for e in range(k * group, (k + 1) * group):
            total += parts_ref[e].astype(jnp.float32)
        key_ref[:, k * width : (k + 1) * width] = total[:, :width].astype(jnp.bfloat16)
        value_ref[:, k * width : (k + 1) * width] = total[:, width:].astype(jnp.bfloat16)


def block_terms(terms):
    cycle = lax.axis_size("ctx")
    total = terms[0].astype(jnp.float32)
    for step in range(1, cycle):
        pairs = [(c, c - step) for c in range(step, cycle)]
        total = total + lax.ppermute(terms[step], "ctx", pairs).astype(jnp.float32)
    return total.astype(jnp.bfloat16)


def summed_terms(total, kv_columns, tiles):
    owners = lax.axis_size("exp")
    rows, columns = total.shape
    parts = lax.all_to_all(
        total.reshape(owners, rows // owners, columns),
        "exp",
        split_axis=0,
        concat_axis=0,
        tiled=True,
    )
    parts, tiles = lax.optimization_barrier((parts, tiles))
    shape = (rows // owners, kv_columns)
    out = jax.ShapeDtypeStruct(shape, jnp.bfloat16)
    key_grad, value_grad = pl.pallas_call(
        sum_kernel,
        out_shape=(out, out),
        grid=(1,),
        in_specs=[full(parts.shape)],
        out_specs=(full(shape), full(shape)),
        compiler_params=pltpu.CompilerParams(vmem_limit_bytes=16 * 2**20),
        name="sums",
    )(parts)
    return key_grad, value_grad, tiles


def pick_kernel(per_dev, shadow_ref, mixed_ref, sent_ref):
    for owner in range(sent_ref.shape[0]):
        host = shadow_ref[owner * per_dev]
        for j in range(1, per_dev):
            host = jnp.maximum(host, shadow_ref[owner * per_dev + j])
        sent_ref[owner] = mixed_ref[host, : sent_ref.shape[1]]


def picked_rows(shadow_list, mixed, limit):
    owners = mixed.shape[0]
    whole = pl.BlockSpec(memory_space=pltpu.VMEM)
    return pl.pallas_call(
        functools.partial(pick_kernel, shadow_list.shape[0] // owners),
        out_shape=jax.ShapeDtypeStruct((owners, limit, mixed.shape[2]), jnp.bfloat16),
        in_specs=[pl.BlockSpec(memory_space=pltpu.SMEM), whole],
        out_specs=whole,
        compiler_params=pltpu.CompilerParams(vmem_limit_bytes=4 * 2**20),
        name="picked",
    )(shadow_list, mixed)


def weight_kernel(orders, own_ref, shadow_ref, mixed_ref, hidden_ref, side_ref, weight_ref):
    owners = mixed_ref.shape[0]
    per_dev, units = hidden_ref.shape[1], hidden_ref.shape[4]
    tokens = weight_ref.shape[1] // owners
    limit = side_ref.shape[1]
    own = own_ref[0]
    earlier = (
        lax.broadcasted_iota(jnp.int32, (tokens, tokens), 0)
        < lax.broadcasted_iota(jnp.int32, (tokens, tokens), 1)
    ).astype(jnp.bfloat16)
    odd = lax.broadcasted_iota(jnp.int32, (1, tokens), 1) % 2 == 1

    def rows_at(named, rows):
        rank = jnp.dot(
            jnp.broadcast_to(named.astype(jnp.float32), (8, tokens)).astype(jnp.bfloat16),
            earlier,
            preferred_element_type=jnp.float32,
        )[:1]
        place = lax.broadcasted_iota(jnp.int32, (rows.shape[0], tokens), 0).astype(jnp.float32)
        chosen = jnp.where(jnp.logical_and(named, rank == place), 1.0, 0.0).astype(jnp.bfloat16)
        return lax.dot_general(rows, chosen, FIRST, preferred_element_type=jnp.float32)

    for i in range(owners):
        source = own ^ jnp.where(own % 2 == 0, orders[0][i], orders[1][i])
        for j in range(per_dev):
            prob = mixed_ref[source, limit + j : limit + j + 1, :tokens].astype(jnp.float32)
            named = prob > 0
            flag = shadow_ref[own * per_dev + j] >= 0
            side = jnp.logical_and(jnp.logical_and(named, odd), flag)
            here = jnp.logical_and(named, jnp.logical_not(side))
            rows = rows_at(here, hidden_ref[0, j, source]) + rows_at(
                side, side_ref[source, :, :units]
            )
            weight_ref[j * units : (j + 1) * units, i * tokens : (i + 1) * tokens] = (
                rows * prob
            ).astype(jnp.bfloat16)


def weighted_rows(own_index, shadow_list, mixed, hidden, shadow_rows, tokens, orders):
    owners = mixed.shape[0]
    per_dev, units = shadow_list.shape[0] // owners, hidden.shape[4]
    shape = (per_dev * units, owners * tokens)
    return pl.pallas_call(
        functools.partial(weight_kernel, orders),
        out_shape=jax.ShapeDtypeStruct(shape, jnp.bfloat16),
        grid_spec=pltpu.PrefetchScalarGridSpec(
            num_scalar_prefetch=2,
            grid=(1,),
            in_specs=[
                full(mixed.shape),
                full((1, per_dev) + hidden.shape[2:]),
                full(shadow_rows.shape),
            ],
            out_specs=full(shape),
        ),
        compiler_params=pltpu.CompilerParams(vmem_limit_bytes=32 * 2**20),
        name="weighted",
    )(own_index.astype(jnp.int32)[None], shadow_list, mixed, hidden, shadow_rows)


def tile_kernel(halves, parity_ref, weight_ref, *refs):
    *part_refs, tile_ref, gathered_ref, held_ref, in_sems, out_sems = refs
    per_dev, units, model = tile_ref.shape
    steps = in_sems.shape[0]
    tokens = gathered_ref.shape[0] // len(halves)
    parity = parity_ref[0]
    places = []
    for n, count in enumerate(halves):
        if count == 1:
            places.append(n * tokens)
        else:
            places.append(pl.multiple_of(n * tokens + parity * (tokens // 2), 16))
            places.append(pl.multiple_of(n * tokens + (1 - parity) * (tokens // 2), 16))
    step = model // steps
    arriving, leaving = [], []
    for i in range(steps):
        columns = pl.ds(i * step, step)
        arriving.append(
            [
                pltpu.make_async_copy(
                    ref.at[:, columns],
                    gathered_ref.at[pl.ds(place, ref.shape[0]), columns],
                    in_sems.at[i, n],
                )
                for n, (place, ref) in enumerate(zip(places, part_refs))
            ]
        )
    for copy in arriving[0] + arriving[1]:
        copy.start()
    for i in range(steps):
        for copy in arriving[i]:
            copy.wait()
        for copy in arriving[i + 2] if i + 2 < steps else []:
            copy.start()
        columns = slice(i * step, (i + 1) * step)
        held_ref[:, columns] = jnp.dot(
            weight_ref[...], gathered_ref[:, columns], preferred_element_type=jnp.float32
        )
        for j in range(per_dev):
            leaving.append(
                pltpu.make_async_copy(
                    held_ref.at[pl.ds(j * units, units), pl.ds(i * step, step)],
                    tile_ref.at[j, :, pl.ds(i * step, step)],
                    out_sems.at[i, j],
                )
            )
            leaving[-1].start()
    for copy in leaving:
        copy.wait()


def tile_sums(weighted, blocks, per_dev):
    tokens, model = blocks[0][0].shape
    rows = weighted.shape[0]
    steps = model // 1024
    halves = [len(block) for block in blocks]
    parts = [part for block in blocks for part in block]
    parity = (lax.axis_index("ctx") % 2).astype(jnp.int32)[None]
    anywhere = pl.BlockSpec(memory_space=pl.ANY)
    return pl.pallas_call(
        functools.partial(tile_kernel, halves),
        out_shape=jax.ShapeDtypeStruct((per_dev, rows // per_dev, model), jnp.float32),
        in_specs=[pl.BlockSpec(memory_space=pltpu.SMEM), pl.BlockSpec(memory_space=pltpu.VMEM)]
        + [anywhere] * len(parts),
        out_specs=anywhere,
        scratch_shapes=[
            pltpu.VMEM((len(blocks) * tokens, model), jnp.bfloat16),
            pltpu.VMEM((rows, model), jnp.float32),
            pltpu.SemaphoreType.DMA((steps, len(parts))),
            pltpu.SemaphoreType.DMA((steps, per_dev)),
        ],
        compiler_params=pltpu.CompilerParams(vmem_limit_bytes=32 * 2**20),
        name="tiles",
    )(parity, weighted, *parts)


def swapped(value):
    return lax.all_to_all(value, "exp", split_axis=0, concat_axis=0, tiled=True)


def source_rows(expert_ids, route_probs, shadow_list, stored_hidden_state):
    owners = lax.axis_size("exp")
    tokens = expert_ids.shape[0]
    count = shadow_list.shape[0]
    per_dev = count // owners
    capacity, units = stored_hidden_state.shape[3:]
    hit = expert_ids[:, None, :] == jnp.arange(count, dtype=jnp.int32)[None, :, None]
    table = jnp.sum(
        jnp.where(hit, route_probs[:, None, :].astype(jnp.float32), 0.0), axis=2
    ).astype(jnp.bfloat16)
    table = table.T.reshape(owners, per_dev, tokens)
    used = min(capacity, tokens // 2)
    limit = -(-used // 16) * 16
    lanes = max(units, tokens)
    rows = jnp.pad(
        stored_hidden_state[0, per_dev, :, :used],
        ((0, 0), (0, limit - used), (0, lanes - units)),
    )
    mixed = jnp.concatenate([rows, jnp.pad(table, ((0, 0), (0, 0), (0, lanes - tokens)))], axis=1)
    return mixed


def expert_rows(mixed, shadow_rows, shadow_list, stored_hidden_state, tokens):
    steps = block_steps(lax.axis_size("exp"))
    orders = [
        [step ^ turn for pair in zip(steps[core], steps[1 - core]) for step, turn in zip(pair, (0, 1))]
        for core in range(2)
    ]
    own_index = lax.axis_index("exp")
    return weighted_rows(
        own_index, shadow_list, mixed, stored_hidden_state, shadow_rows, tokens, orders
    )


def block_steps(owners):
    masks = [1 << bit for bit in range(1, owners.bit_length() - 1)]
    steps = []
    for core in range(2):
        first, second = masks[1 - core], masks[core]
        held = [0, first, second, first ^ second]
        for mask in masks[2:]:
            held = held + [step ^ mask for step in held]
        steps.append(held)
    return steps


def moved(value, steps):
    owners = lax.axis_size("exp")
    return lax.ppermute(value, "exp", [(e, e ^ steps[e % 2]) for e in range(owners)])


def paired_half(block):
    rows = block.shape[0] // 2
    return lax.dynamic_slice_in_dim(block, lax.axis_index("ctx") % 2 * rows, rows, 0)


def from_pair(half):
    return lax.ppermute(half, "ctx", [(c, c ^ 1) for c in range(lax.axis_size("ctx"))])


def beside(block):
    return [moved(part, (1, 1)) for part in block]


def all_blocks(held):
    steps = block_steps(lax.axis_size("exp"))[0]
    for turn in range(len(steps).bit_length() - 3):
        mask = steps[4 << turn]
        more = [[moved(part, (mask, mask)) for part in block] for block, _ in held]
        held = held + [(block, beside(block)) for block in more]
    return [block for pair in held for block in pair]


def local(
    queries,
    keys,
    values,
    attn_out,
    attn_out_grad,
    lse_excess,
    block_mask,
    expert_ids,
    route_probs,
    moe_grad,
    shadow_list,
    stored_hidden_state,
):
    steps = block_steps(lax.axis_size("exp"))
    first = moved(moe_grad, [held[1] for held in steps])
    second = moved(paired_half(moe_grad), [held[2] for held in steps])
    arrived = key_blocks(keys, values, queries.shape[1] // lse_excess.shape[0])
    payload = source_rows(expert_ids, route_probs, shadow_list, stored_hidden_state)
    mixed, arrived = lax.optimization_barrier((swapped(payload), arrived))
    per_dev = shadow_list.shape[0] // lax.axis_size("exp")
    sent = picked_rows(shadow_list, mixed, payload.shape[1] - per_dev)
    sent, second = lax.optimization_barrier((sent, second))
    own, first, _ = lax.optimization_barrier((moe_grad, first, sent))
    second = [second, from_pair(second)]
    own_beside, first_beside = beside([own]), beside([first])
    shadow_rows = swapped(sent)
    arrived, _ = lax.optimization_barrier((arrived, sent))
    query_grad, terms = attention(
        queries, arrived, attn_out, attn_out_grad, lse_excess, block_mask
    )
    first, second, shadow_rows, terms, own_beside, first_beside = lax.optimization_barrier(
        (first, second, shadow_rows, terms, own_beside, first_beside)
    )
    far = moved(first, [held[2] for held in steps])
    total = block_terms(terms)
    weighted = expert_rows(
        mixed, shadow_rows, shadow_list, stored_hidden_state, expert_ids.shape[0]
    )
    far, total, _ = lax.optimization_barrier((far, total, weighted))
    near = [([moe_grad], own_beside), ([first], first_beside), (second, beside(second))]
    tiles = tile_sums(weighted, all_blocks(near + [([far], beside([far]))]), per_dev)
    key_grad, value_grad, expert_grad = summed_terms(total, keys.shape[1], tiles)
    return (query_grad, key_grad, value_grad, expert_grad)


def solution(mesh):
    placed = (
        P("ctx", "exp"),
        P("ctx", None),
        P("ctx", None),
        P("ctx", "exp"),
        P("ctx", "exp"),
        P("exp", "ctx"),
        P(),
        P("exp", None),
        P("exp", None),
        P("exp", None),
        P(),
        P("exp", None, None, None, "ctx"),
    )
    return jax.shard_map(
        local,
        mesh=mesh,
        in_specs=placed,
        out_specs=(
            P("ctx", "exp"),
            P(("ctx", "exp"), None),
            P(("ctx", "exp"), None),
            P("exp", "ctx", None),
        ),
        check_vma=False,
    )
```

```python
import functools
import math

import jax
import jax.numpy as jnp
from jax import lax
from jax.experimental import pallas as pl
from jax.experimental.pallas import tpu as pltpu
from jax.sharding import PartitionSpec as P

LAST = (((1,), (1,)), ((), ()))
FIRST = (((0,), (0,)), ((), ()))


def full(shape):
    return pl.BlockSpec(shape, lambda *at: (0,) * len(shape))


def attention_kernel(
    place_ref, mask_ref, query_ref, grad_ref, out_ref, lse_ref, *rest
):
    cycle = mask_ref.shape[0]
    pair_ref, fetched_ref, swapped_ref, query_grad_ref, terms_ref, sums_ref, pairs_ref = rest
    rows, width = pairs_ref.shape[1], pairs_ref.shape[2] // 2
    heads = lse_ref.shape[0]
    scale = 1.0 / math.sqrt(width)
    mine = place_ref[0]
    offset = 0.5 * math.log(rows) + lse_ref[...]
    spans = [slice(h * width, (h + 1) * width) for h in range(heads)]
    pairs_ref[0] = pair_ref[...]
    for core, (key_ref, value_ref) in enumerate(
        ((fetched_ref, swapped_ref), (swapped_ref, fetched_ref))
    ):

        @pl.when(place_ref[1] == core)
        def _(key_ref=key_ref, value_ref=value_ref):
            pairs_ref[1:, :, :width] = key_ref[...]
            pairs_ref[1:, :, width:] = value_ref[...]

    delta = []
    for span in spans:
        both = grad_ref[:, span].astype(jnp.float32) * out_ref[:, span].astype(jnp.float32)
        delta.append(jnp.sum(both.T, axis=0, keepdims=True))

    def block(step, diagonal):
        key, value = pairs_ref[step, :, :width], pairs_ref[step, :, width:]
        probs, slopes = [], []
        for h, span in enumerate(spans):
            query, grad = query_ref[:, span], grad_ref[:, span]
            scores = lax.dot_general(key, query, LAST, preferred_element_type=jnp.float32)
            prob = jnp.exp(scores * scale - offset[h : h + 1])
            if diagonal:
                at_key = lax.broadcasted_iota(jnp.int32, (rows, rows), 0)
                at_query = lax.broadcasted_iota(jnp.int32, (rows, rows), 1)
                prob = jnp.where(at_key <= at_query, prob, 0.0)
            prob_grad = lax.dot_general(value, grad, LAST, preferred_element_type=jnp.float32)
            slope = (prob * (prob_grad - delta[h]) * scale).astype(jnp.bfloat16)
            probs.append(prob.astype(jnp.bfloat16))
            slopes.append(slope)
            query_term = lax.dot_general(slope, key, FIRST, preferred_element_type=jnp.float32)
            if diagonal:
                sums_ref[:, span] = query_term
            else:
                sums_ref[:, span] += query_term
        queries = jnp.concatenate([query_ref[:, span] for span in spans], axis=0)
        grads = jnp.concatenate([grad_ref[:, span] for span in spans], axis=0)
        key_term = jnp.dot(
            jnp.concatenate(slopes, axis=1), queries, preferred_element_type=jnp.float32
        )
        value_term = jnp.dot(
            jnp.concatenate(probs, axis=1), grads, preferred_element_type=jnp.float32
        )
        terms_ref[mine - step, :, :width] = key_term.astype(jnp.bfloat16)
        terms_ref[mine - step, :, width:] = value_term.astype(jnp.bfloat16)

    block(0, True)

    @pl.loop(0, cycle)
    def _(source):
        seen = jnp.logical_and(source < mine, mask_ref[mine, source] > 0)

        @pl.when(seen)
        def _():
            block(mine - source, False)

        @pl.when(jnp.logical_and(source != mine, jnp.logical_not(seen)))
        def _():
            terms_ref[source] = jnp.zeros_like(terms_ref[source])

    query_grad_ref[...] = sums_ref[...].astype(jnp.bfloat16)


def key_blocks(keys, values, width):
    cycle = lax.axis_size("ctx")
    owners = lax.axis_size("exp")
    kv_count = keys.shape[1] // width
    kv_head = lax.axis_index("exp") * kv_count // owners
    key = lax.dynamic_slice_in_dim(keys, kv_head * width, width, 1)
    value = lax.dynamic_slice_in_dim(values, kv_head * width, width, 1)
    half = jnp.where(lax.axis_index("exp") % 2 == 0, key, value)
    fetched = jnp.stack(
        [
            lax.ppermute(half, "ctx", [(c, c + step) for c in range(cycle - step)])
            for step in range(1, cycle)
        ]
    )
    return jnp.concatenate([key, value], axis=1), fetched


def attention(queries, arrived, attn_out, attn_out_grad, lse_excess, block_mask):
    cycle = lax.axis_size("ctx")
    mine = lax.axis_index("ctx")
    pair, fetched = arrived
    arrived = (pair, fetched, moved(fetched, (1, 1)))
    operands = (queries, attn_out_grad, attn_out, lse_excess, *arrived)
    return pl.pallas_call(
        attention_kernel,
        out_shape=(
            jax.ShapeDtypeStruct(queries.shape, jnp.bfloat16),
            jax.ShapeDtypeStruct((cycle,) + pair.shape, jnp.bfloat16),
        ),
        grid_spec=pltpu.PrefetchScalarGridSpec(
            num_scalar_prefetch=2,
            grid=(1,),
            in_specs=[full(operand.shape) for operand in operands],
            out_specs=(full(queries.shape), full((cycle,) + pair.shape)),
            scratch_shapes=[
                pltpu.VMEM(queries.shape, jnp.float32),
                pltpu.VMEM((cycle,) + pair.shape, jnp.bfloat16),
            ],
        ),
        compiler_params=pltpu.CompilerParams(vmem_limit_bytes=32 * 2**20),
        name="attention",
    )(jnp.stack([mine, lax.axis_index("exp") % 2]).astype(jnp.int32), block_mask, *operands)


def sum_kernel(parts_ref, key_ref, value_ref):
    cycle, owners, rows, columns = parts_ref.shape
    kv_count = key_ref.shape[1] * 2 // columns
    group = owners // kv_count
    width = columns // 2
    for k in range(kv_count):
        total = jnp.zeros((rows, columns), jnp.float32)
        for c in range(cycle):
            for e in range(k * group, (k + 1) * group):
                total += parts_ref[c, e].astype(jnp.float32)
        key_ref[:, k * width : (k + 1) * width] = total[:, :width].astype(jnp.bfloat16)
        value_ref[:, k * width : (k + 1) * width] = total[:, width:].astype(jnp.bfloat16)


def summed_terms(terms, kv_columns, tiles):
    cycle, owners = lax.axis_size("ctx"), lax.axis_size("exp")
    rows, columns = terms.shape[1:]
    parts = lax.all_to_all(
        terms.reshape(cycle * owners, rows // owners, columns),
        ("ctx", "exp"),
        split_axis=0,
        concat_axis=0,
        tiled=True,
    ).reshape(cycle, owners, rows // owners, columns)
    parts, tiles = lax.optimization_barrier((parts, tiles))
    shape = (rows // owners, kv_columns)
    out = jax.ShapeDtypeStruct(shape, jnp.bfloat16)
    key_grad, value_grad = pl.pallas_call(
        sum_kernel,
        out_shape=(out, out),
        grid=(1,),
        in_specs=[full(parts.shape)],
        out_specs=(full(shape), full(shape)),
        compiler_params=pltpu.CompilerParams(vmem_limit_bytes=16 * 2**20),
        name="sums",
    )(parts)
    return key_grad, value_grad, tiles


def pick_kernel(per_dev, shadow_ref, mixed_ref, sent_ref):
    for owner in range(sent_ref.shape[0]):
        host = shadow_ref[owner * per_dev]
        for j in range(1, per_dev):
            host = jnp.maximum(host, shadow_ref[owner * per_dev + j])
        sent_ref[owner] = mixed_ref[host, : sent_ref.shape[1]]


def picked_rows(shadow_list, mixed, limit):
    owners = mixed.shape[0]
    whole = pl.BlockSpec(memory_space=pltpu.VMEM)
    return pl.pallas_call(
        functools.partial(pick_kernel, shadow_list.shape[0] // owners),
        out_shape=jax.ShapeDtypeStruct((owners, limit, mixed.shape[2]), jnp.bfloat16),
        in_specs=[pl.BlockSpec(memory_space=pltpu.SMEM), whole],
        out_specs=whole,
        compiler_params=pltpu.CompilerParams(vmem_limit_bytes=4 * 2**20),
        name="picked",
    )(shadow_list, mixed)


def weight_kernel(orders, own_ref, shadow_ref, mixed_ref, hidden_ref, side_ref, weight_ref):
    owners = mixed_ref.shape[0]
    per_dev, units = hidden_ref.shape[1], hidden_ref.shape[4]
    tokens = weight_ref.shape[1] // owners
    limit = side_ref.shape[1]
    own = own_ref[0]
    earlier = (
        lax.broadcasted_iota(jnp.int32, (tokens, tokens), 0)
        < lax.broadcasted_iota(jnp.int32, (tokens, tokens), 1)
    ).astype(jnp.bfloat16)
    odd = lax.broadcasted_iota(jnp.int32, (1, tokens), 1) % 2 == 1

    def rows_at(named, rows):
        rank = jnp.dot(
            jnp.broadcast_to(named.astype(jnp.float32), (8, tokens)).astype(jnp.bfloat16),
            earlier,
            preferred_element_type=jnp.float32,
        )[:1]
        place = lax.broadcasted_iota(jnp.int32, (rows.shape[0], tokens), 0).astype(jnp.float32)
        chosen = jnp.where(jnp.logical_and(named, rank == place), 1.0, 0.0).astype(jnp.bfloat16)
        return lax.dot_general(rows, chosen, FIRST, preferred_element_type=jnp.float32)

    for i in range(owners):
        source = own ^ jnp.where(own % 2 == 0, orders[0][i], orders[1][i])
        for j in range(per_dev):
            prob = mixed_ref[source, limit + j : limit + j + 1, :tokens].astype(jnp.float32)
            named = prob > 0
            flag = shadow_ref[own * per_dev + j] >= 0
            side = jnp.logical_and(jnp.logical_and(named, odd), flag)
            here = jnp.logical_and(named, jnp.logical_not(side))
            rows = rows_at(here, hidden_ref[0, j, source]) + rows_at(
                side, side_ref[source, :, :units]
            )
            weight_ref[j * units : (j + 1) * units, i * tokens : (i + 1) * tokens] = (
                rows * prob
            ).astype(jnp.bfloat16)


def weighted_rows(own_index, shadow_list, mixed, hidden, shadow_rows, tokens, orders):
    owners = mixed.shape[0]
    per_dev, units = shadow_list.shape[0] // owners, hidden.shape[4]
    shape = (per_dev * units, owners * tokens)
    return pl.pallas_call(
        functools.partial(weight_kernel, orders),
        out_shape=jax.ShapeDtypeStruct(shape, jnp.bfloat16),
        grid_spec=pltpu.PrefetchScalarGridSpec(
            num_scalar_prefetch=2,
            grid=(1,),
            in_specs=[
                full(mixed.shape),
                full((1, per_dev) + hidden.shape[2:]),
                full(shadow_rows.shape),
            ],
            out_specs=full(shape),
        ),
        compiler_params=pltpu.CompilerParams(vmem_limit_bytes=32 * 2**20),
        name="weighted",
    )(own_index.astype(jnp.int32)[None], shadow_list, mixed, hidden, shadow_rows)


def tile_kernel(halves, parity_ref, weight_ref, *refs):
    *part_refs, tile_ref, gathered_ref, held_ref, in_sems, out_sems = refs
    per_dev, units, model = tile_ref.shape
    steps = in_sems.shape[0]
    tokens = gathered_ref.shape[0] // len(halves)
    parity = parity_ref[0]
    places = []
    for n, count in enumerate(halves):
        if count == 1:
            places.append(n * tokens)
        else:
            places.append(pl.multiple_of(n * tokens + parity * (tokens // 2), 16))
            places.append(pl.multiple_of(n * tokens + (1 - parity) * (tokens // 2), 16))
    step = model // steps
    arriving, leaving = [], []
    for i in range(steps):
        columns = pl.ds(i * step, step)
        arriving.append(
            [
                pltpu.make_async_copy(
                    ref.at[:, columns],
                    gathered_ref.at[pl.ds(place, ref.shape[0]), columns],
                    in_sems.at[i, n],
                )
                for n, (place, ref) in enumerate(zip(places, part_refs))
            ]
        )
    for copy in arriving[0] + arriving[1]:
        copy.start()
    for i in range(steps):
        for copy in arriving[i]:
            copy.wait()
        for copy in arriving[i + 2] if i + 2 < steps else []:
            copy.start()
        columns = slice(i * step, (i + 1) * step)
        held_ref[:, columns] = jnp.dot(
            weight_ref[...], gathered_ref[:, columns], preferred_element_type=jnp.float32
        )
        for j in range(per_dev):
            leaving.append(
                pltpu.make_async_copy(
                    held_ref.at[pl.ds(j * units, units), pl.ds(i * step, step)],
                    tile_ref.at[j, :, pl.ds(i * step, step)],
                    out_sems.at[i, j],
                )
            )
            leaving[-1].start()
    for copy in leaving:
        copy.wait()


def tile_sums(weighted, blocks, per_dev):
    tokens, model = blocks[0][0].shape
    rows = weighted.shape[0]
    steps = model // 1024
    halves = [len(block) for block in blocks]
    parts = [part for block in blocks for part in block]
    parity = (lax.axis_index("ctx") % 2).astype(jnp.int32)[None]
    anywhere = pl.BlockSpec(memory_space=pl.ANY)
    return pl.pallas_call(
        functools.partial(tile_kernel, halves),
        out_shape=jax.ShapeDtypeStruct((per_dev, rows // per_dev, model), jnp.float32),
        in_specs=[pl.BlockSpec(memory_space=pltpu.SMEM), pl.BlockSpec(memory_space=pltpu.VMEM)]
        + [anywhere] * len(parts),
        out_specs=anywhere,
        scratch_shapes=[
            pltpu.VMEM((len(blocks) * tokens, model), jnp.bfloat16),
            pltpu.VMEM((rows, model), jnp.float32),
            pltpu.SemaphoreType.DMA((steps, len(parts))),
            pltpu.SemaphoreType.DMA((steps, per_dev)),
        ],
        compiler_params=pltpu.CompilerParams(vmem_limit_bytes=32 * 2**20),
        name="tiles",
    )(parity, weighted, *parts)


def swapped(value):
    return lax.all_to_all(value, "exp", split_axis=0, concat_axis=0, tiled=True)


def source_rows(expert_ids, route_probs, shadow_list, stored_hidden_state):
    owners = lax.axis_size("exp")
    tokens = expert_ids.shape[0]
    count = shadow_list.shape[0]
    per_dev = count // owners
    capacity, units = stored_hidden_state.shape[3:]
    hit = expert_ids[:, None, :] == jnp.arange(count, dtype=jnp.int32)[None, :, None]
    table = jnp.sum(
        jnp.where(hit, route_probs[:, None, :].astype(jnp.float32), 0.0), axis=2
    ).astype(jnp.bfloat16)
    table = table.T.reshape(owners, per_dev, tokens)
    used = min(capacity, tokens // 2)
    limit = -(-used // 16) * 16
    lanes = max(units, tokens)
    rows = jnp.pad(
        stored_hidden_state[0, per_dev, :, :used],
        ((0, 0), (0, limit - used), (0, lanes - units)),
    )
    mixed = jnp.concatenate([rows, jnp.pad(table, ((0, 0), (0, 0), (0, lanes - tokens)))], axis=1)
    return mixed


def expert_rows(mixed, shadow_rows, shadow_list, stored_hidden_state, tokens):
    steps = block_steps(lax.axis_size("exp"))
    orders = [
        [step ^ turn for pair in zip(steps[core], steps[1 - core]) for step, turn in zip(pair, (0, 1))]
        for core in range(2)
    ]
    own_index = lax.axis_index("exp")
    return weighted_rows(
        own_index, shadow_list, mixed, stored_hidden_state, shadow_rows, tokens, orders
    )


def block_steps(owners):
    masks = [1 << bit for bit in range(1, owners.bit_length() - 1)]
    steps = []
    for core in range(2):
        first, second = masks[1 - core], masks[core]
        held = [0, first, second, first ^ second]
        for mask in masks[2:]:
            held = held + [step ^ mask for step in held]
        steps.append(held)
    return steps


def moved(value, steps):
    owners = lax.axis_size("exp")
    return lax.ppermute(value, "exp", [(e, e ^ steps[e % 2]) for e in range(owners)])


def paired_half(block):
    rows = block.shape[0] // 2
    return lax.dynamic_slice_in_dim(block, lax.axis_index("ctx") % 2 * rows, rows, 0)


def from_pair(half):
    return lax.ppermute(half, "ctx", [(c, c ^ 1) for c in range(lax.axis_size("ctx"))])


def beside(block):
    return [moved(part, (1, 1)) for part in block]


def all_blocks(held):
    steps = block_steps(lax.axis_size("exp"))[0]
    for turn in range(len(steps).bit_length() - 3):
        mask = steps[4 << turn]
        more = [[moved(part, (mask, mask)) for part in block] for block, _ in held]
        held = held + [(block, beside(block)) for block in more]
    return [block for pair in held for block in pair]


def local(
    queries,
    keys,
    values,
    attn_out,
    attn_out_grad,
    lse_excess,
    block_mask,
    expert_ids,
    route_probs,
    moe_grad,
    shadow_list,
    stored_hidden_state,
):
    steps = block_steps(lax.axis_size("exp"))
    first = moved(moe_grad, [held[1] for held in steps])
    arrived = key_blocks(keys, values, queries.shape[1] // lse_excess.shape[0])
    payload = source_rows(expert_ids, route_probs, shadow_list, stored_hidden_state)
    mixed, arrived = lax.optimization_barrier((swapped(payload), arrived))
    per_dev = shadow_list.shape[0] // lax.axis_size("exp")
    sent = picked_rows(shadow_list, mixed, payload.shape[1] - per_dev)
    half, _ = lax.optimization_barrier((paired_half(moe_grad), mixed))
    second = moved(half, [held[2] for held in steps])
    shadow_rows = swapped(sent)
    arrived, _ = lax.optimization_barrier((arrived, sent))
    query_grad, terms = attention(
        queries, arrived, attn_out, attn_out_grad, lse_excess, block_mask
    )
    first, second, shadow_rows, query_grad = lax.optimization_barrier(
        (first, second, shadow_rows, query_grad)
    )
    second = [second, from_pair(second)]
    far = moved(first, [held[2] for held in steps])
    weighted = expert_rows(
        mixed, shadow_rows, shadow_list, stored_hidden_state, expert_ids.shape[0]
    )
    near = [(block, beside(block)) for block in ([moe_grad], [first], second)]
    far, _ = lax.optimization_barrier((far, (weighted, query_grad)))
    tiles = tile_sums(weighted, all_blocks(near + [([far], beside([far]))]), per_dev)
    key_grad, value_grad, expert_grad = summed_terms(terms, keys.shape[1], tiles)
    return (query_grad, key_grad, value_grad, expert_grad)


def solution(mesh):
    placed = (
        P("ctx", "exp"),
        P("ctx", None),
        P("ctx", None),
        P("ctx", "exp"),
        P("ctx", "exp"),
        P("exp", "ctx"),
        P(),
        P("exp", None),
        P("exp", None),
        P("exp", None),
        P(),
        P("exp", None, None, None, "ctx"),
    )
    return jax.shard_map(
        local,
        mesh=mesh,
        in_specs=placed,
        out_specs=(
            P("ctx", "exp"),
            P(("ctx", "exp"), None),
            P(("ctx", "exp"), None),
            P("exp", "ctx", None),
        ),
        check_vma=False,
    )
```

```python
import functools
import math

import jax
import jax.numpy as jnp
from jax import lax
from jax.experimental import pallas as pl
from jax.experimental.pallas import tpu as pltpu
from jax.sharding import PartitionSpec as P

LAST = (((1,), (1,)), ((), ()))
FIRST = (((0,), (0,)), ((), ()))


def full(shape):
    return pl.BlockSpec(shape, lambda *at: (0,) * len(shape))


def attention_kernel(
    place_ref, mask_ref, query_ref, grad_ref, out_ref, lse_ref, *rest
):
    cycle = mask_ref.shape[0]
    pair_refs, (query_grad_ref, terms_ref, sums_ref, pairs_ref) = rest[:cycle], rest[cycle:]
    rows, width = pairs_ref.shape[1], pairs_ref.shape[2] // 2
    heads = lse_ref.shape[0]
    scale = 1.0 / math.sqrt(width)
    mine = place_ref[0]
    offset = 0.5 * math.log(rows) + lse_ref[...]
    spans = [slice(h * width, (h + 1) * width) for h in range(heads)]
    for step, pair_ref in enumerate(pair_refs):
        pairs_ref[step] = pair_ref[...]
    delta = []
    for span in spans:
        both = grad_ref[:, span].astype(jnp.float32) * out_ref[:, span].astype(jnp.float32)
        delta.append(jnp.sum(both.T, axis=0, keepdims=True))

    def block(step, diagonal):
        key, value = pairs_ref[step, :, :width], pairs_ref[step, :, width:]
        probs, slopes = [], []
        for h, span in enumerate(spans):
            query, grad = query_ref[:, span], grad_ref[:, span]
            scores = lax.dot_general(key, query, LAST, preferred_element_type=jnp.float32)
            prob = jnp.exp(scores * scale - offset[h : h + 1])
            if diagonal:
                at_key = lax.broadcasted_iota(jnp.int32, (rows, rows), 0)
                at_query = lax.broadcasted_iota(jnp.int32, (rows, rows), 1)
                prob = jnp.where(at_key <= at_query, prob, 0.0)
            prob_grad = lax.dot_general(value, grad, LAST, preferred_element_type=jnp.float32)
            slope = (prob * (prob_grad - delta[h]) * scale).astype(jnp.bfloat16)
            probs.append(prob.astype(jnp.bfloat16))
            slopes.append(slope)
            query_term = lax.dot_general(slope, key, FIRST, preferred_element_type=jnp.float32)
            if diagonal:
                sums_ref[:, span] = query_term
            else:
                sums_ref[:, span] += query_term
        queries = jnp.concatenate([query_ref[:, span] for span in spans], axis=0)
        grads = jnp.concatenate([grad_ref[:, span] for span in spans], axis=0)
        key_term = jnp.dot(
            jnp.concatenate(slopes, axis=1), queries, preferred_element_type=jnp.float32
        )
        value_term = jnp.dot(
            jnp.concatenate(probs, axis=1), grads, preferred_element_type=jnp.float32
        )
        terms_ref[mine - step, :, :width] = key_term.astype(jnp.bfloat16)
        terms_ref[mine - step, :, width:] = value_term.astype(jnp.bfloat16)

    block(0, True)

    @pl.loop(0, cycle)
    def _(source):
        seen = jnp.logical_and(source < mine, mask_ref[mine, source] > 0)

        @pl.when(seen)
        def _():
            block(mine - source, False)

        @pl.when(jnp.logical_and(source != mine, jnp.logical_not(seen)))
        def _():
            terms_ref[source] = jnp.zeros_like(terms_ref[source])

    query_grad_ref[...] = sums_ref[...].astype(jnp.bfloat16)


def key_blocks(keys, values, width):
    cycle = lax.axis_size("ctx")
    owners = lax.axis_size("exp")
    kv_count = keys.shape[1] // width
    kv_head = lax.axis_index("exp") * kv_count // owners
    pair = jnp.concatenate(
        [
            lax.dynamic_slice_in_dim(keys, kv_head * width, width, 1),
            lax.dynamic_slice_in_dim(values, kv_head * width, width, 1),
        ],
        axis=1,
    )
    return [pair] + [
        lax.ppermute(pair, "ctx", [(c, c + step) for c in range(cycle - step)])
        for step in range(1, cycle)
    ]


def attention(queries, arrived, attn_out, attn_out_grad, lse_excess, block_mask):
    cycle = lax.axis_size("ctx")
    mine = lax.axis_index("ctx")
    pair = arrived[0]
    operands = (queries, attn_out_grad, attn_out, lse_excess, *arrived)
    return pl.pallas_call(
        attention_kernel,
        out_shape=(
            jax.ShapeDtypeStruct(queries.shape, jnp.bfloat16),
            jax.ShapeDtypeStruct((cycle,) + pair.shape, jnp.bfloat16),
        ),
        grid_spec=pltpu.PrefetchScalarGridSpec(
            num_scalar_prefetch=2,
            grid=(1,),
            in_specs=[full(operand.shape) for operand in operands],
            out_specs=(full(queries.shape), full((cycle,) + pair.shape)),
            scratch_shapes=[
                pltpu.VMEM(queries.shape, jnp.float32),
                pltpu.VMEM((cycle,) + pair.shape, jnp.bfloat16),
            ],
        ),
        compiler_params=pltpu.CompilerParams(vmem_limit_bytes=32 * 2**20),
        name="attention",
    )(mine.astype(jnp.int32)[None], block_mask, *operands)


def sum_kernel(parts_ref, key_ref, value_ref):
    cycle, owners, rows, columns = parts_ref.shape
    kv_count = key_ref.shape[1] * 2 // columns
    group = owners // kv_count
    width = columns // 2
    for k in range(kv_count):
        total = jnp.zeros((rows, columns), jnp.float32)
        for c in range(cycle):
            for e in range(k * group, (k + 1) * group):
                total += parts_ref[c, e].astype(jnp.float32)
        key_ref[:, k * width : (k + 1) * width] = total[:, :width].astype(jnp.bfloat16)
        value_ref[:, k * width : (k + 1) * width] = total[:, width:].astype(jnp.bfloat16)


def summed_terms(terms, kv_columns, tiles):
    cycle, owners = lax.axis_size("ctx"), lax.axis_size("exp")
    rows, columns = terms.shape[1:]
    parts = lax.all_to_all(
        terms.reshape(cycle * owners, rows // owners, columns),
        ("ctx", "exp"),
        split_axis=0,
        concat_axis=0,
        tiled=True,
    ).reshape(cycle, owners, rows // owners, columns)
    parts, tiles = lax.optimization_barrier((parts, tiles))
    shape = (rows // owners, kv_columns)
    out = jax.ShapeDtypeStruct(shape, jnp.bfloat16)
    key_grad, value_grad = pl.pallas_call(
        sum_kernel,
        out_shape=(out, out),
        grid=(1,),
        in_specs=[full(parts.shape)],
        out_specs=(full(shape), full(shape)),
        compiler_params=pltpu.CompilerParams(vmem_limit_bytes=16 * 2**20),
        name="sums",
    )(parts)
    return key_grad, value_grad, tiles


def pick_kernel(per_dev, shadow_ref, mixed_ref, sent_ref):
    for owner in range(sent_ref.shape[0]):
        host = shadow_ref[owner * per_dev]
        for j in range(1, per_dev):
            host = jnp.maximum(host, shadow_ref[owner * per_dev + j])
        sent_ref[owner] = mixed_ref[host, : sent_ref.shape[1]]


def picked_rows(shadow_list, mixed, limit):
    owners = mixed.shape[0]
    whole = pl.BlockSpec(memory_space=pltpu.VMEM)
    return pl.pallas_call(
        functools.partial(pick_kernel, shadow_list.shape[0] // owners),
        out_shape=jax.ShapeDtypeStruct((owners, limit, mixed.shape[2]), jnp.bfloat16),
        in_specs=[pl.BlockSpec(memory_space=pltpu.SMEM), whole],
        out_specs=whole,
        compiler_params=pltpu.CompilerParams(vmem_limit_bytes=4 * 2**20),
        name="picked",
    )(shadow_list, mixed)


def weight_kernel(orders, own_ref, shadow_ref, mixed_ref, hidden_ref, side_ref, weight_ref):
    owners = mixed_ref.shape[0]
    per_dev, units = hidden_ref.shape[1], hidden_ref.shape[4]
    tokens = weight_ref.shape[1] // owners
    limit = side_ref.shape[1]
    own = own_ref[0]
    earlier = (
        lax.broadcasted_iota(jnp.int32, (tokens, tokens), 0)
        < lax.broadcasted_iota(jnp.int32, (tokens, tokens), 1)
    ).astype(jnp.bfloat16)
    odd = lax.broadcasted_iota(jnp.int32, (1, tokens), 1) % 2 == 1

    def rows_at(named, rows):
        rank = jnp.dot(
            jnp.broadcast_to(named.astype(jnp.float32), (8, tokens)).astype(jnp.bfloat16),
            earlier,
            preferred_element_type=jnp.float32,
        )[:1]
        place = lax.broadcasted_iota(jnp.int32, (rows.shape[0], tokens), 0).astype(jnp.float32)
        chosen = jnp.where(jnp.logical_and(named, rank == place), 1.0, 0.0).astype(jnp.bfloat16)
        return lax.dot_general(rows, chosen, FIRST, preferred_element_type=jnp.float32)

    for i in range(owners):
        source = own ^ jnp.where(own % 2 == 0, orders[0][i], orders[1][i])
        for j in range(per_dev):
            prob = mixed_ref[source, limit + j : limit + j + 1, :tokens].astype(jnp.float32)
            named = prob > 0
            flag = shadow_ref[own * per_dev + j] >= 0
            side = jnp.logical_and(jnp.logical_and(named, odd), flag)
            here = jnp.logical_and(named, jnp.logical_not(side))
            rows = rows_at(here, hidden_ref[0, j, source]) + rows_at(
                side, side_ref[source, :, :units]
            )
            weight_ref[j * units : (j + 1) * units, i * tokens : (i + 1) * tokens] = (
                rows * prob
            ).astype(jnp.bfloat16)


def weighted_rows(own_index, shadow_list, mixed, hidden, shadow_rows, tokens, orders):
    owners = mixed.shape[0]
    per_dev, units = shadow_list.shape[0] // owners, hidden.shape[4]
    shape = (per_dev * units, owners * tokens)
    return pl.pallas_call(
        functools.partial(weight_kernel, orders),
        out_shape=jax.ShapeDtypeStruct(shape, jnp.bfloat16),
        grid_spec=pltpu.PrefetchScalarGridSpec(
            num_scalar_prefetch=2,
            grid=(1,),
            in_specs=[
                full(mixed.shape),
                full((1, per_dev) + hidden.shape[2:]),
                full(shadow_rows.shape),
            ],
            out_specs=full(shape),
        ),
        compiler_params=pltpu.CompilerParams(vmem_limit_bytes=32 * 2**20),
        name="weighted",
    )(own_index.astype(jnp.int32)[None], shadow_list, mixed, hidden, shadow_rows)


def tile_kernel(halves, parity_ref, weight_ref, *refs):
    *part_refs, tile_ref, gathered_ref, held_ref, in_sems, out_sems = refs
    per_dev, units, model = tile_ref.shape
    steps = in_sems.shape[0]
    tokens = gathered_ref.shape[0] // len(halves)
    parity = parity_ref[0]
    places = []
    for n, count in enumerate(halves):
        if count == 1:
            places.append(n * tokens)
        else:
            places.append(pl.multiple_of(n * tokens + parity * (tokens // 2), 16))
            places.append(pl.multiple_of(n * tokens + (1 - parity) * (tokens // 2), 16))
    step = model // steps
    arriving, leaving = [], []
    for i in range(steps):
        columns = pl.ds(i * step, step)
        arriving.append(
            [
                pltpu.make_async_copy(
                    ref.at[:, columns],
                    gathered_ref.at[pl.ds(place, ref.shape[0]), columns],
                    in_sems.at[i, n],
                )
                for n, (place, ref) in enumerate(zip(places, part_refs))
            ]
        )
    for copy in arriving[0] + arriving[1]:
        copy.start()
    for i in range(steps):
        for copy in arriving[i]:
            copy.wait()
        for copy in arriving[i + 2] if i + 2 < steps else []:
            copy.start()
        columns = slice(i * step, (i + 1) * step)
        for j in range(per_dev):
            expert = slice(j * units, (j + 1) * units)
            held_ref[expert, columns] = jnp.dot(
                weight_ref[expert], gathered_ref[:, columns], preferred_element_type=jnp.float32
            )
            leaving.append(
                pltpu.make_async_copy(
                    held_ref.at[pl.ds(j * units, units), pl.ds(i * step, step)],
                    tile_ref.at[j, :, pl.ds(i * step, step)],
                    out_sems.at[i, j],
                )
            )
            leaving[-1].start()
    for copy in leaving:
        copy.wait()


def tile_sums(weighted, blocks, per_dev):
    tokens, model = blocks[0][0].shape
    rows = weighted.shape[0]
    steps = model // 1024
    halves = [len(block) for block in blocks]
    parts = [part for block in blocks for part in block]
    parity = (lax.axis_index("ctx") % 2).astype(jnp.int32)[None]
    anywhere = pl.BlockSpec(memory_space=pl.ANY)
    return pl.pallas_call(
        functools.partial(tile_kernel, halves),
        out_shape=jax.ShapeDtypeStruct((per_dev, rows // per_dev, model), jnp.float32),
        in_specs=[pl.BlockSpec(memory_space=pltpu.SMEM), pl.BlockSpec(memory_space=pltpu.VMEM)]
        + [anywhere] * len(parts),
        out_specs=anywhere,
        scratch_shapes=[
            pltpu.VMEM((len(blocks) * tokens, model), jnp.bfloat16),
            pltpu.VMEM((rows, model), jnp.float32),
            pltpu.SemaphoreType.DMA((steps, len(parts))),
            pltpu.SemaphoreType.DMA((steps, per_dev)),
        ],
        compiler_params=pltpu.CompilerParams(vmem_limit_bytes=32 * 2**20),
        name="tiles",
    )(parity, weighted, *parts)


def swapped(value):
    return lax.all_to_all(value, "exp", split_axis=0, concat_axis=0, tiled=True)


def source_rows(expert_ids, route_probs, shadow_list, stored_hidden_state):
    owners = lax.axis_size("exp")
    tokens = expert_ids.shape[0]
    count = shadow_list.shape[0]
    per_dev = count // owners
    capacity, units = stored_hidden_state.shape[3:]
    hit = expert_ids[:, None, :] == jnp.arange(count, dtype=jnp.int32)[None, :, None]
    table = jnp.sum(
        jnp.where(hit, route_probs[:, None, :].astype(jnp.float32), 0.0), axis=2
    ).astype(jnp.bfloat16)
    table = table.T.reshape(owners, per_dev, tokens)
    used = min(capacity, tokens // 2)
    limit = -(-used // 16) * 16
    lanes = max(units, tokens)
    rows = jnp.pad(
        stored_hidden_state[0, per_dev, :, :used],
        ((0, 0), (0, limit - used), (0, lanes - units)),
    )
    mixed = jnp.concatenate([rows, jnp.pad(table, ((0, 0), (0, 0), (0, lanes - tokens)))], axis=1)
    return mixed


def expert_rows(mixed, shadow_rows, shadow_list, stored_hidden_state, tokens):
    steps = block_steps(lax.axis_size("exp"))
    orders = [
        [step ^ turn for pair in zip(steps[core], steps[1 - core]) for step, turn in zip(pair, (0, 1))]
        for core in range(2)
    ]
    own_index = lax.axis_index("exp")
    return weighted_rows(
        own_index, shadow_list, mixed, stored_hidden_state, shadow_rows, tokens, orders
    )


def block_steps(owners):
    masks = [1 << bit for bit in range(1, owners.bit_length() - 1)]
    steps = []
    for core in range(2):
        first, second = masks[1 - core], masks[core]
        held = [0, first, second, first ^ second]
        for mask in masks[2:]:
            held = held + [step ^ mask for step in held]
        steps.append(held)
    return steps


def moved(value, steps):
    owners = lax.axis_size("exp")
    return lax.ppermute(value, "exp", [(e, e ^ steps[e % 2]) for e in range(owners)])


def paired_half(block):
    rows = block.shape[0] // 2
    return lax.dynamic_slice_in_dim(block, lax.axis_index("ctx") % 2 * rows, rows, 0)


def from_pair(half):
    return lax.ppermute(half, "ctx", [(c, c ^ 1) for c in range(lax.axis_size("ctx"))])


def beside(block):
    return [moved(part, (1, 1)) for part in block]


def all_blocks(held):
    steps = block_steps(lax.axis_size("exp"))[0]
    for turn in range(len(steps).bit_length() - 3):
        mask = steps[4 << turn]
        more = [[moved(part, (mask, mask)) for part in block] for block, _ in held]
        held = held + [(block, beside(block)) for block in more]
    return [block for pair in held for block in pair]


def local(
    queries,
    keys,
    values,
    attn_out,
    attn_out_grad,
    lse_excess,
    block_mask,
    expert_ids,
    route_probs,
    moe_grad,
    shadow_list,
    stored_hidden_state,
):
    steps = block_steps(lax.axis_size("exp"))
    first = moved(moe_grad, [held[1] for held in steps])
    second = moved(paired_half(moe_grad), [held[2] for held in steps])
    arrived = key_blocks(keys, values, queries.shape[1] // lse_excess.shape[0])
    payload = source_rows(expert_ids, route_probs, shadow_list, stored_hidden_state)
    mixed, arrived = lax.optimization_barrier((swapped(payload), arrived))
    per_dev = shadow_list.shape[0] // lax.axis_size("exp")
    sent = picked_rows(shadow_list, mixed, payload.shape[1] - per_dev)
    sent, second = lax.optimization_barrier((sent, second))
    second = [second, from_pair(second)]
    shadow_rows = swapped(sent)
    arrived, _ = lax.optimization_barrier((arrived, sent))
    query_grad, terms = attention(
        queries, arrived, attn_out, attn_out_grad, lse_excess, block_mask
    )
    first, shadow_rows = lax.optimization_barrier((first, shadow_rows))
    far = moved(first, [held[2] for held in steps])
    weighted = expert_rows(
        mixed, shadow_rows, shadow_list, stored_hidden_state, expert_ids.shape[0]
    )
    near = [(block, beside(block)) for block in ([moe_grad], [first], second)]
    far, _ = lax.optimization_barrier((far, (weighted, query_grad)))
    tiles = tile_sums(weighted, all_blocks(near + [([far], beside([far]))]), per_dev)
    key_grad, value_grad, expert_grad = summed_terms(terms, keys.shape[1], tiles)
    return (query_grad, key_grad, value_grad, expert_grad)


def solution(mesh):
    placed = (
        P("ctx", "exp"),
        P("ctx", None),
        P("ctx", None),
        P("ctx", "exp"),
        P("ctx", "exp"),
        P("exp", "ctx"),
        P(),
        P("exp", None),
        P("exp", None),
        P("exp", None),
        P(),
        P("exp", None, None, None, "ctx"),
    )
    return jax.shard_map(
        local,
        mesh=mesh,
        in_specs=placed,
        out_specs=(
            P("ctx", "exp"),
            P(("ctx", "exp"), None),
            P(("ctx", "exp"), None),
            P("exp", "ctx", None),
        ),
        check_vma=False,
    )
```
